32 devices in a mesh: slab: 16 (over z, y, x), tile: 2 (over core).
Axes of the slice: x: 2, y: 2, z: 4, core: 2. Of those that a mesh axis runs over, the one named last changes fastest.
Arguments:
- charges: bfloat16 [64, 8192], P(None, ('slab', 'tile')), may hold values from -6 to 6
- live_count: int32 [32], P(('slab', 'tile')), may hold values from 32 to 256, as said below
- slot_brick: int32 [8192], P(('slab', 'tile')), may hold values from 0 to 4095
- slot_stencil: int32 [8192], P(('slab', 'tile')), may hold values from 0 to 15
- stencils: bfloat16 [16, 64, 512], replicated, may hold values from -0.75 to 0.75
- near_source: int32 [8192, 8], P(('slab', 'tile')), may hold values from 0 to 2303
- near_block: int32 [8192, 8], P(('slab', 'tile')), may hold values from 0 to 15
- near_blocks: bfloat16 [64, 16, 64], replicated, may hold values from -0.25 to 0.25
- kernel_hat: float32 [512, 64, 256], P(('slab', 'tile')), may hold values from 0 to 1, as said below
Outputs:
- potentials: float32 [64, 8192], P(None, ('slab', 'tile'))
The draws below stay inside these ranges and needn't reach their ends.
Inputs may be any that keep to these rules, and one draw needn't show every extreme that they name: `live_count`: some device has all 256 slots live in every draw. kernel_hat is even: its entry at (kz, kx, ky) equals the one at ((-kz) mod 512, (-kx) mod 64, (-ky) mod 256). It is zero on the plane kz = 256 and at least 0.05 elsewhere.
All inputs are finite; a program needn't handle non-finite values.
Results may differ from the reference program's by a relative error of at most 0.0011.
Values may be sent and summed in bfloat16 or wider, within the bound.
No kernel may reach another device: no remote copies, remote signals or barrier semaphores. Data moves between devices by JAX's collectives and lax.ppermute only.
A program may use at most 64 MiB of HBM per device.

```python
import math
import jax
import jax.numpy as jnp
from jax import lax

PANELS = 64
POINTS = 512
NY = 256
NZ = 512
SLOTS = 256
KS = 16
KN = 16
FANOUT = 8
NX = 64
BRICKS_DEV = 4096
TOTAL_SLOTS = 8192
N_SLAB = 16
N_TILE = 2


def draw_live_count(key, part):
    key = jax.random.fold_in(key, 11)
    count_key, busy_key = jax.random.split(key)
    device_total = TOTAL_SLOTS // SLOTS
    counts = jax.random.randint(count_key, (device_total,), SLOTS // 8, SLOTS // 2 + 1)
    busiest = jax.random.randint(busy_key, (), 0, device_total)
    return jnp.where(jnp.arange(device_total) == busiest, SLOTS, counts).astype(jnp.int32)


def draw_kernel_hat(key, part):
    key = jax.random.fold_in(key, 23)
    sample_grid = jnp.exp(jax.random.uniform(key, (NZ, NX, NY), jnp.float32, math.log(0.05), 0.0))
    mirrored = sample_grid
    for dimension in range(3):
        mirrored = jnp.roll(jnp.flip(mirrored, dimension), 1, dimension)
    symmetric = jnp.sqrt(sample_grid * mirrored)
    planes = jnp.arange(NZ, dtype=jnp.int32)
    return jnp.where((planes == NZ // 2)[:, None, None], 0.0, symmetric).astype(jnp.float32)


def place_ends(result, own_key, smallest, top_value):
    place = [jax.random.randint(jax.random.fold_in(own_key, axis), (), 0, length) for axis, length in enumerate(result.shape)]
    main_axis = result.shape.index(max(result.shape))
    beside = place[:main_axis] + [(place[main_axis] + 1) % result.shape[main_axis]] + place[main_axis + 1:]
    return result.at[tuple(place)].set(smallest).at[tuple(beside)].set(top_value)


def levels(rng, shape, shards, low, top_value):
    def one(dim, parts):
        steps = jax.random.uniform(jax.random.fold_in(jax.random.fold_in(rng, 6), dim), (parts,), jnp.float32, low / len(shards), top_value / len(shards))
        return jnp.repeat(jnp.exp(steps), shape[dim] // parts).reshape((-1,) + (1,) * (len(shape) - dim - 1))

    factor_of = one(*shards[0])
    for cut in shards[1:]:
        factor_of = factor_of * one(*cut)
    return factor_of


def normal_values(own_key, dims, deviation, limit, cuts=(), held_as=jnp.bfloat16):
    entries = deviation * jax.random.normal(own_key, dims, jnp.float32)
    if cuts:
        entries = entries * levels(own_key, dims, cuts, -0.22, 0.18)
    return jnp.clip(entries, -limit, limit).astype(held_as)


def setup_inputs(seed: int = 0) -> dict:
    key_of = jax.random.split(jax.random.key(seed), 10)
    return {
        "charges": normal_values(key_of[0], (PANELS, TOTAL_SLOTS), 1.0, 6.0, ((1, 32),)),
        "live_count": draw_live_count(jax.random.fold_in(key_of[9], 71), 0),
        "slot_brick": place_ends(jax.random.randint(key_of[2], (TOTAL_SLOTS,), 0, BRICKS_DEV), jax.random.fold_in(key_of[2], 1), 0, BRICKS_DEV - 1).astype(jnp.int32),
        "slot_stencil": place_ends(jax.random.randint(key_of[3], (TOTAL_SLOTS,), 0, KS), jax.random.fold_in(key_of[3], 1), 0, KS - 1).astype(jnp.int32),
        "stencils": normal_values(key_of[4], (KS, PANELS, POINTS), PANELS ** -0.5, 0.75),
        "near_source": place_ends(jax.random.randint(key_of[5], (TOTAL_SLOTS, FANOUT), 0, 9 * SLOTS), jax.random.fold_in(key_of[5], 1), 0, (9 * SLOTS) - 1).astype(jnp.int32),
        "near_block": place_ends(jax.random.randint(key_of[6], (TOTAL_SLOTS, FANOUT), 0, KN), jax.random.fold_in(key_of[6], 1), 0, KN - 1).astype(jnp.int32),
        "near_blocks": normal_values(key_of[7], (PANELS, KN, PANELS), (PANELS * FANOUT) ** -0.5, 0.25),
        "kernel_hat": draw_kernel_hat(jax.random.fold_in(key_of[9], 71), 0),
    }


def footprint_points():
    points = jnp.arange(POINTS, dtype=jnp.int32)
    return points // 64, (points // 8) % 8, points % 8


def one_hot_rows(kind_rows, kinds_count, out_type):
    return (kind_rows[None, :] == jnp.arange(kinds_count, dtype=jnp.int32)[:, None]).astype(out_type)


def spread_rows(values, kind_rows, kinds_count):
    selector = one_hot_rows(kind_rows, kinds_count, values.dtype)
    return (selector[:, None, :] * values[None, :, :]).reshape(kinds_count * values.shape[0], values.shape[1])


def reference(charges, live_count, slot_brick, slot_stencil, stencils, near_source, near_block, near_blocks, kernel_hat):
    devices = N_SLAB * N_TILE
    local_y = NY // N_TILE
    zbricks = NZ // 4
    point_x, point_y, point_z = footprint_points()
    columns = jnp.arange(TOTAL_SLOTS, dtype=jnp.int32)
    alive_mask = live_count[columns // SLOTS] > columns % SLOTS
    masked = jnp.where(alive_mask[None, :], charges, jnp.zeros((), charges.dtype))
    stencil_rows = stencils.reshape(KS * PANELS, POINTS)
    near_table = near_blocks.reshape(PANELS, KN * PANELS)
    slot_lane = jnp.arange(SLOTS, dtype=jnp.int32)

    def places_of(device):
        slab_index = device // N_TILE
        tile_index = device % N_TILE
        bricks = lax.dynamic_slice_in_dim(slot_brick, device * SLOTS, SLOTS, 0)
        brick_y = bricks // zbricks
        brick_z = bricks % zbricks
        grid_x = (4 * slab_index - 2 + point_x[:, None]) % NX
        grid_y = (local_y * tile_index + 4 * brick_y[None, :] - 2 + point_y[:, None]) % NY
        grid_z = (4 * brick_z[None, :] - 2 + point_z[:, None]) % NZ
        return (grid_x * NY + grid_y) * NZ + grid_z

    def project(charge_grid, device):
        device_charges = lax.dynamic_slice_in_dim(masked, device * SLOTS, SLOTS, 1)
        device_kinds = lax.dynamic_slice_in_dim(slot_stencil, device * SLOTS, SLOTS, 0)
        footprint = lax.dot_general(stencil_rows, spread_rows(device_charges, device_kinds, KS), (((0,), (0,)), ((), ())), preferred_element_type=jnp.float32)
        return charge_grid.at[places_of(device).reshape(-1)].add(footprint.reshape(-1)), None

    device_list = jnp.arange(devices, dtype=jnp.int32)
    charge_grid, unused = lax.scan(project, jnp.zeros((NX * NY * NZ,), jnp.float32), device_list)
    spectrum = jnp.fft.fftn(charge_grid.reshape(NX, NY, NZ))
    weighted = spectrum * jnp.transpose(kernel_hat, (1, 2, 0))
    potential = jnp.real(jnp.fft.ifftn(weighted)).astype(jnp.float32)
    sampled = potential.astype(jnp.bfloat16).reshape(-1)

    def sample(state_value, device):
        slab_index = device // N_TILE
        tile_index = device % N_TILE
        device_kinds = lax.dynamic_slice_in_dim(slot_stencil, device * SLOTS, SLOTS, 0)
        samples = sampled[places_of(device)]
        stencil_sums = jnp.dot(stencil_rows, samples, preferred_element_type=jnp.float32)
        picked = jnp.sum(stencil_sums.reshape(KS, PANELS, SLOTS) * one_hot_rows(device_kinds, KS, jnp.float32)[:, None, :], axis=0)
        sources = lax.dynamic_slice_in_dim(near_source, device * SLOTS, SLOTS, 0)
        blocks = lax.dynamic_slice_in_dim(near_block, device * SLOTS, SLOTS, 0)
        offset_dir = sources // SLOTS
        step_x = offset_dir // 3 - 1
        step_y = offset_dir % 3 - 1
        owners = ((slab_index + step_x) % N_SLAB) * N_TILE + (tile_index + step_y) % N_TILE
        gathered = jnp.take(masked, (owners * SLOTS + sources % SLOTS).reshape(-1), axis=1)
        near_sums = jnp.dot(near_table, spread_rows(gathered, blocks.reshape(-1), KN), preferred_element_type=jnp.float32)
        near_terms = jnp.sum(near_sums.reshape(PANELS, SLOTS, FANOUT), axis=2)
        alive_here = slot_lane < live_count[device]
        return state_value, jnp.where(alive_here[None, :], picked + near_terms, 0.0)

    unused, outputs = lax.scan(sample, jnp.zeros((), jnp.float32), device_list)
    return jnp.transpose(outputs, (1, 0, 2)).reshape(PANELS, TOTAL_SLOTS)
```

```python
import functools

import jax
import jax.numpy as jnp
import ml_dtypes
import numpy as np
from jax import lax
from jax.experimental import pallas as pl
from jax.experimental.pallas import tpu as pltpu
from jax.sharding import PartitionSpec as P

PANELS = 64
POINTS = 512
NY = 256
NZ = 512
KS = 16
KN = 16
LANES = 128
ZROWS = NZ + 8
UNROLL = 4
F32 = jnp.float32
BF16 = jnp.bfloat16
SMEM = pl.BlockSpec(memory_space=pltpu.SMEM)
VMEM = pl.BlockSpec(memory_space=pltpu.VMEM)
PARAMS = pltpu.CompilerParams(vmem_limit_bytes=48 * 1024 * 1024)


def halves(table):
    high = table.astype(ml_dtypes.bfloat16)
    low = (table - high.astype(np.float64)).astype(ml_dtypes.bfloat16)
    return high, low


def owner_frequencies(slabs, tiles):
    devices = slabs * tiles
    planes = NZ // devices
    owner = np.array([a * tiles + b for b in range(tiles) for a in range(slabs)])
    plane = np.arange(planes // 2)
    return (owner[None, :] * planes + plane[:, None] + (owner[None, :] >= devices // 2)).reshape(-1)


def z_tables(slabs, tiles):
    freq = owner_frequencies(slabs, tiles)
    cell = np.arange(NZ) - 2
    angle = (freq[:, None] * cell[None, :] % NZ) * (2 * np.pi / NZ)
    forward = np.concatenate([np.cos(angle), -np.sin(angle)], axis=0)
    weight = np.where(freq % NZ == 0, 1.0, 2.0)[:, None] / NZ
    inverse = np.concatenate([weight * np.cos(angle), -weight * np.sin(angle)], axis=0).T
    return forward, inverse


def y_tables(cells):
    angle = (np.arange(NY)[:, None] * np.arange(NY)[None, :] % NY) * (2 * np.pi / NY)
    cosine, sine = np.cos(angle), np.sin(angle)
    forward = np.block([[cosine, -sine], [sine, cosine]])
    inverse = np.block([[cosine, sine], [-sine, cosine]]) / cells
    return forward, inverse


def x_tables(length):
    angle = (np.arange(length)[:, None] * np.arange(length)[None, :] % length) * (2 * np.pi / length)
    cosine, sine = np.cos(angle), np.sin(angle)
    forward = np.block([[cosine, sine], [-sine, cosine]])
    inverse = np.block([[cosine, -sine], [sine, cosine]])
    return forward, inverse


def point_order():
    point = np.arange(POINTS)
    target = (point % 8) * 64 + point // 8
    table = np.zeros((POINTS, POINTS), ml_dtypes.bfloat16)
    table[point, target] = 1
    return table


def split(values):
    high = values.astype(BF16)
    return high, (values - high.astype(F32)).astype(BF16)


def dot(a, b):
    return jnp.dot(a, b, preferred_element_type=F32)


def dot3(a, b):
    return dot(a[0], b[0]) + (dot(a[0], b[1]) + dot(a[1], b[0]))


def lane_of(shape):
    return lax.broadcasted_iota(jnp.int32, shape, 1)


def by_kind(values, kinds):
    zero = jnp.zeros_like(values)
    return jnp.concatenate(
        [jnp.where(kinds == kind, values, zero) for kind in range(KS)], axis=0
    )


def footprints(charges_ref, kinds_ref, stk_ref, fp_ref, first, count):
    columns = slice(first, first + count)
    spread = by_kind(charges_ref[:, columns].astype(F32), kinds_ref[0:1, columns]).astype(BF16)
    for pair in range(4):
        part = lax.dot_general(
            spread,
            stk_ref[:, pair * LANES : (pair + 1) * LANES],
            (((0,), (0,)), ((), ())),
            preferred_element_type=F32,
        )
        fp_ref[pl.ds(first * 8 + 2 * pair, count, stride=8), :] = part
        fp_ref[pl.ds(first * 8 + 2 * pair + 1, count, stride=8), :] = pltpu.roll(part, 64, 1)


def scatter_columns(fp_ref, by_ref, bz_ref, grids, edge_ref, first, live, planes, shift_i):
    lane = lane_of((8, LANES))
    in_planes = (lane >= 8 * planes[0]) & (lane < 8 * (planes[-1] + 1))

    def step(index, carry):
        for inner in range(UNROLL):
            column = first + index * UNROLL + inner
            by = by_ref[column]
            row = 4 * bz_ref[column]
            value = fp_ref[pl.ds(pl.multiple_of(column * 8, 8), 8), :]
            begin = 4 * by - 2
            offset = lane - begin
            mask = (offset >= 0) & (offset < 8)
            for plane in planes:
                turned = pltpu.roll(value, (begin - 8 * (plane + shift_i) + 2 * LANES) & (LANES - 1), 1)
                where = pl.ds(row, 8)
                grids[plane][where, :] += jnp.where(mask, turned, 0.0)
            is_first = (by == 0).astype(jnp.int32)
            is_last = (by == NY // 8 - 1).astype(jnp.int32)
            turned = pltpu.roll(value, (2 * LANES - 8 * shift_i - 4 * is_last) & (LANES - 1), 1)
            low = jnp.where(is_first + is_last > 0, 2 * is_last, 8)
            place = (lane & 7) - low
            edge_ref[pl.ds(row, 8), :] += jnp.where(
                in_planes & (place >= 0) & (place < 2), turned, 0.0
            )
        return carry

    lax.fori_loop(0, (live + UNROLL - 1) // UNROLL, step, 0)


def sample_columns(pot_refs, edge_ref, by_ref, bz_ref, sp_ref, first, live, planes, shift_i):
    lane = lane_of((8, LANES))
    point_j = lane & 7

    def step(index, carry):
        for inner in range(UNROLL):
            column = first + index * UNROLL + inner
            by = by_ref[column]
            row = 4 * bz_ref[column]
            begin = 4 * by - 2
            result = jnp.zeros((8, LANES), F32)
            for plane in planes:
                low = 8 * (plane + shift_i)
                turned = pltpu.roll(
                    pot_refs[plane][pl.ds(row, 8), :], (low - begin + 2 * LANES) & (LANES - 1), 1
                )
                result = jnp.where((lane >= low) & (lane < low + 8), turned, result)
            is_first = (by == 0).astype(jnp.int32)
            is_last = (by == NY // 8 - 1).astype(jnp.int32)
            turned = pltpu.roll(
                edge_ref[pl.ds(row, 8), :], (8 * shift_i + 4 * is_last + 2 * LANES) & (LANES - 1), 1
            )
            low = jnp.where(is_first + is_last > 0, 6 * is_last, 8)
            place = point_j - low
            inside = (lane >= 8 * (planes[0] + shift_i)) & (lane < 8 * (planes[-1] + shift_i + 1))
            result = jnp.where(inside & (place >= 0) & (place < 2), turned, result)
            sp_ref[pl.ds(pl.multiple_of(column * 8, 8), 8), :] = result
        return carry

    lax.fori_loop(0, (live + UNROLL - 1) // UNROLL, step, 0)


def far_sums(sp_ref, kinds_ref, stk_ref, first, count):
    lane = lane_of((count, LANES))
    pairs = []
    for pair in range(4):
        even = sp_ref[pl.ds(first * 8 + 2 * pair, count, stride=8), :]
        odd = sp_ref[pl.ds(first * 8 + 2 * pair + 1, count, stride=8), :]
        pairs.append(jnp.where(lane < 64, even, pltpu.roll(odd, 64, 1)).astype(BF16))
    samples = jnp.concatenate(pairs, axis=1)
    sums = lax.dot_general(
        stk_ref[...], samples, (((1,), (1,)), ((), ())), preferred_element_type=F32
    )
    kinds = kinds_ref[0:1, first : first + count]
    result = jnp.zeros((PANELS, count), F32)
    for kind in range(KS):
        result += jnp.where(kinds == kind, sums[kind * PANELS : (kind + 1) * PANELS, :], 0.0)
    return result


def own_kernel(by_ref, bz_ref, live_ref, charges_ref, kinds_ref, stencil_ref, order_ref,
               g0, g1, g2, g3, edge_ref, stk_ref, fp_ref):
    stk_ref[...] = dot(stencil_ref[...], order_ref[...]).astype(BF16)
    for ref in (g0, g1, g2, g3, edge_ref):
        ref[...] = jnp.zeros_like(ref)
    slots = charges_ref.shape[1]
    live = live_ref[0]
    for first in range(0, slots, LANES):
        @pl.when(live > first)
        def _(first=first):
            footprints(charges_ref, kinds_ref, stk_ref, fp_ref, first, LANES)
    scatter_columns(fp_ref, by_ref, bz_ref, (g0, g1, g2, g3), edge_ref, 0, live, (0, 1, 2, 3), 2)


def beside_kernel(by_ref, bz_ref, live_ref, charges_ref, kinds_ref, stk_ref,
                  i0, i1, i2, i3, iedge, g0, g1, g2, g3, out_edge, edge_ref, fp_ref):
    for ref, source in ((g0, i0), (g1, i1), (g2, i2), (g3, i3), (edge_ref, iedge)):
        ref[...] = source[...]
    slots = charges_ref.shape[1] // 2
    for side in range(2):
        live = live_ref[side]
        for first in range(0, slots, LANES):
            @pl.when(live > first)
            def _(first=side * slots + first):
                footprints(charges_ref, kinds_ref, stk_ref, fp_ref, first, LANES)
    for side, planes, shift_i in ((0, (0, 1), 6), (1, (2, 3), -2)):
        scatter_columns(fp_ref, by_ref, bz_ref, (g0, g1, g2, g3), edge_ref,
                        side * slots, live_ref[side], planes, shift_i)
    edge_ref[0:8, :] += edge_ref[NZ:ZROWS, :]
    total = edge_ref[0:LANES, :]
    for block in range(1, 4):
        total += pltpu.roll(edge_ref[block * LANES : (block + 1) * LANES, :], 32 * block, 1)
    out_edge[...] = total


def z_kernel(owners, g0, g1, g2, g3, edge_ref, wh_ref, wl_ref, out_ref):
    lane = lane_of((LANES, LANES))
    at_edge = (lane < 2) | (lane >= LANES - 2)
    parts = NZ // owners
    for plane, grid in enumerate((g0, g1, g2, g3)):
        blocks = []
        for block in range(4):
            turned = pltpu.roll(edge_ref[...], (LANES - 2 - 32 * block - 8 * plane) % LANES, 1)
            blocks.append(
                grid[block * LANES : (block + 1) * LANES, :] + jnp.where(at_edge, turned, 0.0)
            )
        blocks[0] = jnp.concatenate([blocks[0][0:8] + grid[NZ:ZROWS, :], blocks[0][8:]], axis=0)
        values = split(jnp.concatenate(blocks, axis=0))
        result = dot3((wh_ref[...], wl_ref[...]), values)
        for part in range(parts):
            out_ref[pl.ds(plane * parts + part, owners, stride=4 * parts), :] = result[
                part * owners : (part + 1) * owners, :
            ]


def plane_kernel(length, planes, offset_ref, in_ref, hat_ref, yfh, yfl, yih, yil, xfh, xfl, xih, xil,
                 out_ref, ah_ref, al_ref):
    rows = planes * length
    offset = offset_ref[0]
    for part in range(2):
        for tile in range(2):
            block = slice((2 * part + tile) * LANES, (2 * part + tile + 1) * LANES)
            for plane in range(planes):
                values = in_ref[
                    pl.ds(tile * length * 2 * planes + part * planes + plane, length, stride=2 * planes), :
                ]
                high, low = split(values)
                ah_ref[plane * length : (plane + 1) * length, block] = high
                al_ref[plane * length : (plane + 1) * length, block] = low
    along_y = dot3((ah_ref[...], al_ref[...]), (yfh[...], yfl[...]))
    forward = (xfh[...], xfl[...])
    inverse = (xih[...], xil[...])
    for plane in range(planes):
        here = slice(plane * length, (plane + 1) * length)
        values = along_y[here, :]
        values = jnp.concatenate([values[:, :NY], values[:, NY:]], axis=0)
        values = dot3(forward, split(values))
        hat = hat_ref[offset + plane]
        values = values * jnp.concatenate([hat, hat], axis=0)
        values = dot3(inverse, split(values))
        high, low = split(values)
        ah_ref[here, 0:NY] = high[:length]
        ah_ref[here, NY : 2 * NY] = high[length:]
        al_ref[here, 0:NY] = low[:length]
        al_ref[here, NY : 2 * NY] = low[length:]
    result = dot3((ah_ref[...], al_ref[...]), (yih[...], yil[...]))
    for part in range(2):
        for tile in range(2):
            block = slice((2 * part + tile) * LANES, (2 * part + tile + 1) * LANES)
            for plane in range(planes):
                out_ref[
                    pl.ds(tile * length * 2 * planes + part * planes + plane, length, stride=2 * planes), :
                ] = result[plane * length : (plane + 1) * length, block]


def potential_kernel(owners, in_ref, vh_ref, vl_ref, p0, p1, p2, p3, edge_ref):
    parts = NZ // owners
    lane = lane_of((LANES, LANES))
    edge = jnp.zeros((LANES, LANES), F32)
    for plane, pot in enumerate((p0, p1, p2, p3)):
        values = split(jnp.concatenate(
            [in_ref[pl.ds(plane * parts + part, owners, stride=4 * parts), :] for part in range(parts)],
            axis=0,
        ))
        result = dot3((vh_ref[...], vl_ref[...]), values).astype(BF16).astype(F32)
        pot[0:NZ, :] = result
        pot[NZ:ZROWS, :] = result[0:8, :]
        for block in range(4):
            low = 32 * block + 8 * plane
            turned = pltpu.roll(result[block * LANES : (block + 1) * LANES, :], low + 2, 1)
            edge = jnp.where((lane >= low) & (lane < low + 4), turned, edge)
    edge_ref[...] = edge.astype(BF16)


def widen_edge(edge_ref, wide_ref):
    for block in range(4):
        wide_ref[block * LANES : (block + 1) * LANES, :] = pltpu.roll(
            edge_ref[...].astype(F32), (LANES - 32 * block) % LANES, 1
        )
    wide_ref[NZ:ZROWS, :] = wide_ref[0:8, :]


def sample_kernel(sides, by_ref, bz_ref, live_ref, p0, p1, p2, p3, edge_ref, kinds_ref, stk_ref,
                  out_ref, wide_ref, sp_ref):
    widen_edge(edge_ref, wide_ref)
    slots = kinds_ref.shape[1] // len(sides)
    for side, (planes, shift_i) in enumerate(sides):
        live = live_ref[side]
        sample_columns((p0, p1, p2, p3), wide_ref, by_ref, bz_ref, sp_ref,
                       side * slots, live, planes, shift_i)
        for first in range(0, slots, LANES):
            where = slice(side * slots + first, side * slots + first + LANES)

            @pl.when(live > first)
            def _(side=side, first=first, where=where, live=live):
                result = far_sums(sp_ref, kinds_ref, stk_ref, side * slots + first, LANES)
                column = first + lane_of((PANELS, LANES))
                out_ref[:, where] = jnp.where(column < live, result, 0.0)

            @pl.when(live <= first)
            def _(where=where):
                out_ref[:, where] = jnp.zeros((PANELS, LANES), F32)


def near_kernel(live_ref, pool_ref, source_ref, block_ref, table_ref, out_ref):
    live = live_ref[0]
    fanout, slots = source_ref.shape
    total = pool_ref.shape[1]
    for first in range(0, slots, LANES):
        where = slice(first, first + LANES)

        @pl.when(live > first)
        def _(where=where, first=first):
            index = lax.broadcasted_iota(jnp.int32, (total, LANES), 0)
            result = jnp.zeros((PANELS, LANES), F32)
            for j in range(fanout):
                chosen = jnp.where(index == source_ref[j : j + 1, where], 1.0, 0.0).astype(BF16)
                gathered = dot(pool_ref[...], chosen)
                result += dot(
                    table_ref[...], by_kind(gathered, block_ref[j : j + 1, where]).astype(BF16)
                )
            column = first + lane_of((PANELS, LANES))
            out_ref[:, where] = jnp.where(column < live, result, 0.0)

        @pl.when(live <= first)
        def _(where=where):
            out_ref[:, where] = jnp.zeros((PANELS, LANES), F32)


def shape_of(*dims, dtype=F32):
    return jax.ShapeDtypeStruct(dims, dtype)


def body(slabs, tiles, charges, live_count, slot_brick, slot_stencil, stencils, near_source,
         near_block, near_blocks, kernel_hat):
    slots = charges.shape[1]
    owners = slabs * tiles
    planes = kernel_hat.shape[0] // 2
    length = kernel_hat.shape[1]
    parts = NZ // owners
    axes = ("tile", "slab")
    both = ("slab", "tile")

    def moved(values, step, swap):
        pairs = [
            (a * tiles + b, (a + step) % slabs * tiles + (b + swap) % tiles)
            for a in range(slabs)
            for b in range(tiles)
        ]
        return lax.ppermute(values, both, pairs)

    live = live_count[0]
    slot = jnp.arange(slots, dtype=jnp.int32)
    held = jnp.where((slot < live)[None, :], charges, jnp.zeros((), charges.dtype))
    zbricks = NZ // 4
    brick_y = slot_brick // zbricks
    brick_z = slot_brick % zbricks
    facts = jnp.stack([brick_y, brick_z, slot_stencil, jnp.full((slots,), live)], axis=0)
    packed = jnp.concatenate(
        [held, facts.astype(BF16), jnp.zeros((12, slots), BF16)], axis=0
    )
    from_prev = moved(packed, 1, 0)
    from_next = moved(packed, -1, 0)

    grid = shape_of(ZROWS, LANES)
    g = pl.pallas_call(
        own_kernel,
        out_shape=(grid,) * 5 + (shape_of(KS * PANELS, POINTS, dtype=BF16),),
        in_specs=[SMEM] * 3 + [VMEM] * 4,
        out_specs=(VMEM,) * 6,
        scratch_shapes=[pltpu.VMEM((slots * 8, LANES), F32)],
        compiler_params=PARAMS,
        name="own_scatter",
    )(brick_y, brick_z, live_count, held, slot_stencil[None, :],
      stencils.reshape(KS * PANELS, POINTS), jnp.asarray(point_order()))
    grids, stk = g[:5], g[5]

    beside = jnp.concatenate([from_prev, from_next], axis=1)
    facts2 = beside[PANELS : PANELS + 4].astype(jnp.int32)
    by2, bz2, kinds2 = facts2[0], facts2[1], facts2[2:3]
    live2 = jnp.stack([facts2[3, 0], facts2[3, slots]])
    g = pl.pallas_call(
        beside_kernel,
        out_shape=(grid,) * 4 + (shape_of(LANES, LANES),),
        in_specs=[SMEM] * 3 + [VMEM] * 8,
        out_specs=(VMEM,) * 5,
        scratch_shapes=[pltpu.VMEM((ZROWS, LANES), F32), pltpu.VMEM((2 * slots * 8, LANES), F32)],
        compiler_params=PARAMS,
        name="beside_scatter",
    )(by2, bz2, live2, beside[:PANELS], kinds2, stk, *grids)
    edge = moved(g[4], 0, 1)

    forward, inverse = z_tables(slabs, tiles)
    sent = pl.pallas_call(
        functools.partial(z_kernel, owners),
        out_shape=shape_of(owners * 4 * parts, LANES),
        in_specs=[VMEM] * 7,
        out_specs=VMEM,
        compiler_params=PARAMS,
        name="z_forward",
    )(*g[:4], edge, *map(jnp.asarray, halves(forward)))

    def exchanged(values):
        values = values.reshape(owners, 4 * parts, LANES)
        return lax.all_to_all(values, axes, 0, 0, tiled=True).reshape(owners * 4 * parts, LANES)

    got = exchanged(sent)

    swapped = moved(held, 0, 1)
    pool = jnp.concatenate(
        [from_prev[:PANELS], moved(swapped, 1, 0), held, swapped, from_next[:PANELS], moved(swapped, -1, 0)],
        axis=1,
    )
    direction = near_source // slots
    pool_index = (direction // 3 * 2 + (direction % 3 != 1).astype(jnp.int32)) * slots + near_source % slots
    near = pl.pallas_call(
        near_kernel,
        out_shape=shape_of(PANELS, slots),
        in_specs=[SMEM] + [VMEM] * 4,
        out_specs=VMEM,
        compiler_params=PARAMS,
        name="near_field",
    )(live_count, pool, pool_index.T, near_block.T, near_blocks.reshape(PANELS, KN * PANELS))

    me = lax.axis_index("slab") * tiles + lax.axis_index("tile")
    offset = (me >= owners // 2).astype(jnp.int32)[None]
    y_forward, y_inverse = y_tables(length * NY)
    x_forward, x_inverse = x_tables(length)
    tables = [jnp.asarray(t) for pair in map(halves, (y_forward, y_inverse, x_forward, x_inverse)) for t in pair]
    back = pl.pallas_call(
        functools.partial(plane_kernel, length, planes),
        out_shape=shape_of(owners * 4 * parts, LANES),
        in_specs=[SMEM] + [VMEM] * 10,
        out_specs=VMEM,
        scratch_shapes=[pltpu.VMEM((planes * length, 2 * NY), BF16)] * 2,
        compiler_params=PARAMS,
        name="plane_filter",
    )(offset, got, kernel_hat, *tables)
    back = exchanged(back)

    pot = pl.pallas_call(
        functools.partial(potential_kernel, owners),
        out_shape=(grid,) * 4 + (shape_of(LANES, LANES, dtype=BF16),),
        in_specs=[VMEM] * 3,
        out_specs=(VMEM,) * 5,
        compiler_params=PARAMS,
        name="z_inverse",
    )(back, *map(jnp.asarray, halves(inverse)))
    edge = moved(pot[4], 0, 1)

    def sampled(sides, by, bz, counts, kinds, name):
        width = kinds.shape[1]
        return pl.pallas_call(
            functools.partial(sample_kernel, sides),
            out_shape=shape_of(PANELS, width),
            in_specs=[SMEM] * 3 + [VMEM] * 7,
            out_specs=VMEM,
            scratch_shapes=[pltpu.VMEM((ZROWS, LANES), F32), pltpu.VMEM((width * 8, LANES), F32)],
            compiler_params=PARAMS,
            name=name,
        )(by, bz, counts, *pot[:4], edge, kinds, stk)

    others = sampled((((0, 1), 6), ((2, 3), -2)), by2, bz2, live2, kinds2, "beside_sample")
    to_prev = moved(others[:, :slots], -1, 0)
    to_next = moved(others[:, slots:], 1, 0)
    own = sampled((((0, 1, 2, 3), 2),), brick_y, brick_z, live_count, slot_stencil[None, :], "own_sample")
    return own + near + to_prev + to_next


def solution(mesh):
    both = ("slab", "tile")
    in_specs = (
        P(None, both),
        P(both),
        P(both),
        P(both),
        P(),
        P(both, None),
        P(both, None),
        P(),
        P(both, None, None),
    )
    return jax.shard_map(
        functools.partial(body, mesh.shape["slab"], mesh.shape["tile"]),
        mesh=mesh,
        in_specs=in_specs,
        out_specs=P(None, both),
        check_vma=False,
    )
```

```python
import functools

import jax
import jax.numpy as jnp
import ml_dtypes
import numpy as np
from jax import lax
from jax.experimental import pallas as pl
from jax.experimental.pallas import tpu as pltpu
from jax.sharding import PartitionSpec as P

PANELS = 64
POINTS = 512
NY = 256
NZ = 512
KS = 16
KN = 16
LANES = 128
ZROWS = NZ + 8
UNROLL = 8
SCALE_ROWS = 8
F32 = jnp.float32
BF16 = jnp.bfloat16
SMEM = pl.BlockSpec(memory_space=pltpu.SMEM)
VMEM = pl.BlockSpec(memory_space=pltpu.VMEM)
PARAMS = pltpu.CompilerParams(vmem_limit_bytes=48 * 1024 * 1024)


def halves(*tables):
    parts = []
    for table in tables:
        high = table.astype(ml_dtypes.bfloat16)
        parts += [high, (table - high.astype(np.float64)).astype(ml_dtypes.bfloat16)]
    return np.concatenate(parts, axis=0)


def owner_frequencies(slabs, tiles):
    devices = slabs * tiles
    planes = NZ // devices
    owner = np.array([a * tiles + b for b in range(tiles) for a in range(slabs)])
    plane = np.arange(planes // 2)
    return (owner[None, :] * planes + plane[:, None] + (owner[None, :] >= devices // 2)).reshape(-1)


def z_tables(slabs, tiles):
    freq = owner_frequencies(slabs, tiles)
    cell = np.arange(NZ) - 2
    angle = (freq[:, None] * cell[None, :] % NZ) * (2 * np.pi / NZ)
    forward = np.concatenate([np.cos(angle), -np.sin(angle)], axis=0)
    weight = np.where(freq % NZ == 0, 1.0, 2.0)[:, None] / NZ
    inverse = np.concatenate([weight * np.cos(angle), -weight * np.sin(angle)], axis=0).T
    return forward, inverse


def y_table():
    angle = (np.arange(NY)[:, None] * np.arange(NY)[None, :] % NY) * (2 * np.pi / NY)
    return np.concatenate([np.cos(angle), np.sin(angle)], axis=1)


def x_tables(slabs):
    length = 4 * slabs
    cell = (np.arange(4)[:, None] + 4 * np.arange(slabs)[None, :]).reshape(-1)
    angle = (np.arange(length)[:, None] * cell[None, :] % length) * (2 * np.pi / length)
    cosine, sine = np.cos(angle), np.sin(angle)
    forward = np.block([[cosine, sine], [-sine, cosine]])
    inverse = np.block([[cosine.T, -sine.T], [sine.T, cosine.T]])
    return forward, inverse


def point_order():
    point = np.arange(POINTS)
    target = (point % 8) * 64 + point // 8
    table = np.zeros((POINTS, POINTS), ml_dtypes.bfloat16)
    table[point, target] = 1
    return table


def split(values):
    high = values.astype(BF16)
    return high, (values - high.astype(F32)).astype(BF16)


def dot(a, b):
    return jnp.dot(a, b, preferred_element_type=F32)


def dot3(a, b):
    return dot(a[0], b[0]) + (dot(a[0], b[1]) + dot(a[1], b[0]))


def lane_of(shape):
    return lax.broadcasted_iota(jnp.int32, shape, 1)


def by_kind(values, kinds):
    zero = jnp.zeros_like(values)
    return jnp.concatenate(
        [jnp.where(kinds == kind, values, zero) for kind in range(KS)], axis=0
    )


def footprints(charges, kinds, stk_ref, fp_ref, first):
    count = charges.shape[1]
    spread = by_kind(charges.astype(F32), kinds).astype(BF16)
    for pair in range(4):
        part = lax.dot_general(
            spread,
            stk_ref[:, pair * LANES : (pair + 1) * LANES],
            (((0,), (0,)), ((), ())),
            preferred_element_type=F32,
        )
        fp_ref[pl.ds(first * 8 + 2 * pair, count, stride=8), :] = part
        fp_ref[pl.ds(first * 8 + 2 * pair + 1, count, stride=8), :] = pltpu.roll(part, 64, 1)


def scatter_columns(fp_ref, place_of, grids, edge_ref, first, live, planes, shift_i):
    lane = lane_of((8, LANES))
    in_planes = (lane >= 8 * planes[0]) & (lane < 8 * (planes[-1] + 1))
    point_j = lane & 7

    def step(index, carry):
        updates = []
        for inner in range(UNROLL):
            column = first + index * UNROLL + inner
            by, bz = place_of(column)
            value = fp_ref[pl.ds(pl.multiple_of(column * 8, 8), 8), :]
            begin = 4 * by - 2
            mask = ((lane - begin) & -8) == 0
            terms = []
            for plane in planes:
                turned = pltpu.roll(value, (begin - 8 * (plane + shift_i)) & (LANES - 1), 1)
                terms.append(jnp.where(mask, turned, 0.0))
            is_last = (by == NY // 8 - 1).astype(jnp.int32)
            low = jnp.where(by == 0, 0, jnp.where(by == NY // 8 - 1, 2, 8))
            turned = pltpu.roll(value, (-8 * shift_i - 4 * is_last) & (LANES - 1), 1)
            mask = in_planes & (((point_j - low) & -2) == 0)
            terms.append(jnp.where(mask, turned, 0.0))
            updates.append((pl.ds(4 * bz, 8), terms))
        refs = [grids[plane] for plane in planes] + [edge_ref]
        for where, terms in updates:
            sums = [ref[where, :] + term for ref, term in zip(refs, terms)]
            for ref, total in zip(refs, sums):
                ref[where, :] = total
        return carry

    lax.fori_loop(0, (live + UNROLL - 1) // UNROLL, step, 0)


def sample_columns(pot_refs, edge_ref, place_of, sp_ref, first, live, planes, shift_i):
    lane = lane_of((8, LANES))
    point_j = lane & 7
    inside = (lane >= 8 * (planes[0] + shift_i)) & (lane < 8 * (planes[-1] + shift_i + 1))

    def step(index, carry):
        results = []
        for inner in range(UNROLL):
            column = first + index * UNROLL + inner
            by, bz = place_of(column)
            where = pl.ds(4 * bz, 8)
            begin = 4 * by - 2
            result = jnp.zeros((8, LANES), F32)
            for plane in planes:
                low = 8 * (plane + shift_i)
                turned = pltpu.roll(pot_refs[plane][where, :], (low - begin) & (LANES - 1), 1)
                result = jnp.where(((lane - low) & -8) == 0, turned, result)
            is_last = (by == NY // 8 - 1).astype(jnp.int32)
            low = jnp.where(by == 0, 0, jnp.where(by == NY // 8 - 1, 6, 8))
            turned = pltpu.roll(edge_ref[where, :], (8 * shift_i + 4 * is_last) & (LANES - 1), 1)
            mask = inside & (((point_j - low) & -2) == 0)
            results.append((pl.ds(pl.multiple_of(column * 8, 8), 8), jnp.where(mask, turned, result)))
        for where, result in results:
            sp_ref[where, :] = result
        return carry

    lax.fori_loop(0, (live + UNROLL - 1) // UNROLL, step, 0)


def far_sums(sp_ref, kinds, stk_ref, first):
    count = kinds.shape[1]
    lane = lane_of((count, LANES))
    pairs = []
    for pair in range(4):
        even = sp_ref[pl.ds(first * 8 + 2 * pair, count, stride=8), :]
        odd = sp_ref[pl.ds(first * 8 + 2 * pair + 1, count, stride=8), :]
        pairs.append(jnp.where(lane < 64, even, pltpu.roll(odd, 64, 1)).astype(BF16))
    samples = jnp.concatenate(pairs, axis=1)
    sums = lax.dot_general(
        stk_ref[...], samples, (((1,), (1,)), ((), ())), preferred_element_type=F32
    )
    result = jnp.zeros((PANELS, count), F32)
    for kind in range(KS):
        result += jnp.where(kinds == kind, sums[kind * PANELS : (kind + 1) * PANELS, :], 0.0)
    return result


def place_in_brick(brick_ref):
    zbricks = NZ // 4

    def place_of(column):
        brick = brick_ref[column]
        return brick // zbricks, brick % zbricks

    return place_of


def place_in_facts(facts_ref):
    return lambda column: (facts_ref[0, column], facts_ref[1, column])


def own_kernel(brick_ref, live_ref, charges_ref, kinds_ref, stencil_ref, order_ref,
               g0, g1, g2, g3, edge_ref, stk_ref, fp_ref):
    stk_ref[...] = dot(stencil_ref[...], order_ref[...]).astype(BF16)
    for ref in (g0, g1, g2, g3, edge_ref):
        ref[...] = jnp.zeros_like(ref)
    slots = charges_ref.shape[1]
    live = live_ref[0]
    for first in range(0, slots, LANES):
        @pl.when(live > first)
        def _(columns=slice(first, first + LANES)):
            footprints(charges_ref[:, columns], kinds_ref[0:1, columns], stk_ref, fp_ref, columns.start)
    scatter_columns(fp_ref, place_in_brick(brick_ref), (g0, g1, g2, g3), edge_ref, 0, live, (0, 1, 2, 3), 2)


def beside_kernel(prev_ref, next_ref, stk_ref, i0, i1, i2, i3, iedge,
                  g0, g1, g2, g3, out_edge, out_facts, edge_ref, fp_ref, facts_ref, sem):
    slots = prev_ref.shape[1]
    for side, source in enumerate((prev_ref, next_ref)):
        facts = source[PANELS : PANELS + 8, :].astype(F32)
        out_facts[:, side * slots : (side + 1) * slots] = facts.astype(jnp.int32)
    copy = pltpu.make_async_copy(out_facts, facts_ref, sem)
    copy.start()
    for ref, source in ((g0, i0), (g1, i1), (g2, i2), (g3, i3), (edge_ref, iedge)):
        ref[...] = source[...]
    copy.wait()
    sides = ((prev_ref, (0, 1), 6), (next_ref, (2, 3), -2))
    for side, (source, planes, shift_i) in enumerate(sides):
        start = side * slots
        live = facts_ref[3, start]
        for first in range(0, slots, LANES):
            @pl.when(live > first)
            def _(source=source, start=start, first=first):
                here = slice(first, first + LANES)
                kinds = out_facts[2:3, start + first : start + first + LANES]
                footprints(source[0:PANELS, here], kinds, stk_ref, fp_ref, start + first)
        scatter_columns(fp_ref, place_in_facts(facts_ref), (g0, g1, g2, g3), edge_ref,
                        start, live, planes, shift_i)
    edge_ref[0:8, :] += edge_ref[NZ:ZROWS, :]
    total = edge_ref[0:LANES, :]
    for block in range(1, 4):
        total += pltpu.roll(edge_ref[block * LANES : (block + 1) * LANES, :], 32 * block, 1)
    out_edge[...] = total


def exponent_of(values):
    top = functools.reduce(jnp.maximum, [jnp.max(jnp.abs(v), axis=0, keepdims=True) for v in values])
    top = jnp.maximum(jnp.max(top, axis=1, keepdims=True), 2.0**-100)
    return jnp.ceil(jnp.log2(top)) - 12.0


def z_kernel(owners, g0, g1, g2, g3, edge_ref, w_ref, out_ref):
    lane = lane_of((LANES, LANES))
    at_edge = (lane < 2) | (lane >= LANES - 2)
    parts = NZ // owners
    stride = 4 * parts + SCALE_ROWS
    results = []
    for plane, grid in enumerate((g0, g1, g2, g3)):
        blocks = []
        for block in range(4):
            turned = pltpu.roll(edge_ref[...], (LANES - 2 - 32 * block - 8 * plane) % LANES, 1)
            blocks.append(
                grid[block * LANES : (block + 1) * LANES, :] + jnp.where(at_edge, turned, 0.0)
            )
        blocks[0] = jnp.concatenate([blocks[0][0:8] + grid[NZ:ZROWS, :], blocks[0][8:]], axis=0)
        values = split(jnp.concatenate(blocks, axis=0))
        results.append(dot3((w_ref[0:NZ, :], w_ref[NZ : 2 * NZ, :]), values))
    exponent = exponent_of(results)
    scale = jnp.exp2(-exponent)
    for plane, result in enumerate(results):
        result = result * scale
        for part in range(parts):
            out_ref[pl.ds(plane * parts + part, owners, stride=stride), :] = result[
                part * owners : (part + 1) * owners, :
            ]
    for row in range(SCALE_ROWS):
        out_ref[pl.ds(4 * parts + row, owners, stride=stride), :] = jnp.broadcast_to(
            exponent, (owners, LANES)
        )


def plane_kernel(slabs, planes, offset_ref, in_ref, hat_ref, y_ref, x_ref, out_ref, ah_ref, al_ref):
    length = 4 * slabs
    rows = planes * length
    parts = 2 * planes
    stride = 4 * parts + SCALE_ROWS
    offset = offset_ref[0]

    def pieces():
        for tile in range(2):
            for part in range(2):
                for xi in range(4):
                    for plane in range(planes):
                        start = tile * slabs * stride + xi * parts + part * planes + plane
                        row = (part * planes + plane) * length + xi * slabs
                        yield tile, part, pl.ds(start, slabs, stride=stride), row

    scales = [
        jnp.exp2(in_ref[pl.ds(tile * slabs * stride + 4 * parts, slabs, stride=stride), :])
        for tile in range(2)
    ]
    for tile, part, where, row in pieces():
        high, low = split(in_ref[where, :] * scales[tile])
        ah_ref[row : row + slabs, tile * LANES : (tile + 1) * LANES] = high
        al_ref[row : row + slabs, tile * LANES : (tile + 1) * LANES] = low
    along_y = (y_ref[0:NY, :], y_ref[NY : 2 * NY, :])
    turned = dot3((ah_ref[...], al_ref[...]), along_y)
    real = turned[:rows, :NY] + turned[rows:, NY:]
    imag = turned[rows:, :NY] - turned[:rows, NY:]
    size = 2 * length
    forward = (x_ref[0:size, :], x_ref[size : 2 * size, :])
    inverse = (x_ref[2 * size : 3 * size, :], x_ref[3 * size : 4 * size, :])
    for plane in range(planes):
        here = slice(plane * length, (plane + 1) * length)
        there = slice(rows + plane * length, rows + (plane + 1) * length)
        values = dot3(forward, split(jnp.concatenate([real[here], imag[here]], axis=0)))
        hat = hat_ref[offset + plane] * (1.0 / (length * NY))
        values = values * jnp.concatenate([hat, hat], axis=0)
        high, low = split(dot3(inverse, split(values)))
        ah_ref[here, :] = high[:length]
        ah_ref[there, :] = high[length:]
        al_ref[here, :] = low[:length]
        al_ref[there, :] = low[length:]
    turned = dot3((ah_ref[...], al_ref[...]), along_y)
    results = (turned[:rows, :NY] - turned[rows:, NY:], turned[rows:, :NY] + turned[:rows, NY:])
    exponent = exponent_of(results)
    scale = jnp.exp2(-exponent)
    results = [result * scale for result in results]
    for tile, part, where, row in pieces():
        row -= part * rows
        out_ref[where, :] = results[part][row : row + slabs, tile * LANES : (tile + 1) * LANES]
    for row in range(SCALE_ROWS):
        out_ref[pl.ds(4 * parts + row, 2 * slabs, stride=stride), :] = jnp.broadcast_to(
            exponent, (2 * slabs, LANES)
        )


def potential_kernel(owners, in_ref, v_ref, p0, p1, p2, p3, edge_ref):
    parts = NZ // owners
    stride = 4 * parts + SCALE_ROWS
    lane = lane_of((LANES, LANES))
    edge = jnp.zeros((LANES, LANES), F32)
    scale = jnp.exp2(in_ref[pl.ds(4 * parts, owners, stride=stride), :])
    for plane, pot in enumerate((p0, p1, p2, p3)):
        values = split(jnp.concatenate(
            [in_ref[pl.ds(plane * parts + part, owners, stride=stride), :] * scale for part in range(parts)],
            axis=0,
        ))
        result = dot3((v_ref[0:NZ, :], v_ref[NZ : 2 * NZ, :]), values).astype(BF16).astype(F32)
        pot[0:NZ, :] = result
        pot[NZ:ZROWS, :] = result[0:8, :]
        for block in range(4):
            low = 32 * block + 8 * plane
            turned = pltpu.roll(result[block * LANES : (block + 1) * LANES, :], low + 2, 1)
            edge = jnp.where((lane >= low) & (lane < low + 4), turned, edge)
    edge_ref[...] = edge.astype(BF16)


def widen_edge(edge_ref, wide_ref):
    for block in range(4):
        wide_ref[block * LANES : (block + 1) * LANES, :] = pltpu.roll(
            edge_ref[...].astype(F32), (LANES - 32 * block) % LANES, 1
        )
    wide_ref[NZ:ZROWS, :] = wide_ref[0:8, :]


def sampled_sums(place_of, pots, wide_ref, kinds, stk_ref, out_ref, sp_ref, start, slots, live, planes, shift_i):
    sample_columns(pots, wide_ref, place_of, sp_ref, start, live, planes, shift_i)
    for first in range(0, slots, LANES):
        where = slice(start + first, start + first + LANES)

        @pl.when(live > first)
        def _(first=first, where=where):
            result = far_sums(sp_ref, kinds[0:1, where], stk_ref, where.start)
            column = first + lane_of((PANELS, LANES))
            out_ref[:, where] = jnp.where(column < live, result, 0.0)

        @pl.when(live <= first)
        def _(where=where):
            out_ref[:, where] = jnp.zeros((PANELS, LANES), F32)


def own_sample_kernel(brick_ref, live_ref, p0, p1, p2, p3, edge_ref, kinds_ref, stk_ref, out_ref, wide_ref, sp_ref):
    widen_edge(edge_ref, wide_ref)
    sampled_sums(place_in_brick(brick_ref), (p0, p1, p2, p3), wide_ref, kinds_ref, stk_ref, out_ref, sp_ref,
                 0, kinds_ref.shape[1], live_ref[0], (0, 1, 2, 3), 2)


def beside_sample_kernel(facts_ref, p0, p1, p2, p3, edge_ref, kinds_ref, stk_ref, out_ref, wide_ref, sp_ref):
    widen_edge(edge_ref, wide_ref)
    slots = kinds_ref.shape[1] // 2
    for side, (planes, shift_i) in enumerate((((0, 1), 6), ((2, 3), -2))):
        sampled_sums(place_in_facts(facts_ref), (p0, p1, p2, p3), wide_ref, kinds_ref.at[2:3, :], stk_ref, out_ref,
                     sp_ref, side * slots, slots, facts_ref[3, side * slots], planes, shift_i)


def near_kernel(live_ref, a0, a1, a2, a3, a4, a5, source_ref, block_ref, table_ref, out_ref):
    live = live_ref[0]
    fanout, slots = source_ref.shape
    pool = jnp.concatenate([ref[0:PANELS, :] for ref in (a0, a1, a2, a3, a4, a5)], axis=1)
    total = pool.shape[1]
    for first in range(0, slots, LANES):
        where = slice(first, first + LANES)

        @pl.when(live > first)
        def _(where=where, first=first):
            index = lax.broadcasted_iota(jnp.int32, (total, LANES), 0)
            result = jnp.zeros((PANELS, LANES), F32)
            for j in range(fanout):
                chosen = jnp.where(index == source_ref[j : j + 1, where], 1.0, 0.0).astype(BF16)
                gathered = dot(pool, chosen)
                result += dot(
                    table_ref[...], by_kind(gathered, block_ref[j : j + 1, where]).astype(BF16)
                )
            column = first + lane_of((PANELS, LANES))
            out_ref[:, where] = jnp.where(column < live, result, 0.0)

        @pl.when(live <= first)
        def _(where=where):
            out_ref[:, where] = jnp.zeros((PANELS, LANES), F32)


def shape_of(*dims, dtype=F32):
    return jax.ShapeDtypeStruct(dims, dtype)


def body(slabs, tiles, charges, live_count, slot_brick, slot_stencil, stencils, near_source,
         near_block, near_blocks, kernel_hat):
    slots = charges.shape[1]
    owners = slabs * tiles
    planes = kernel_hat.shape[0] // 2
    length = kernel_hat.shape[1]
    parts = NZ // owners
    axes = ("tile", "slab")
    both = ("slab", "tile")

    def moved(values, step, swap):
        pairs = [
            (a * tiles + b, (a + step) % slabs * tiles + (b + swap) % tiles)
            for a in range(slabs)
            for b in range(tiles)
        ]
        return lax.ppermute(values, both, pairs)

    live = live_count[0]
    slot = jnp.arange(slots, dtype=jnp.int32)
    held = jnp.where((slot < live)[None, :], charges, jnp.zeros((), charges.dtype))
    zbricks = NZ // 4
    kinds = slot_stencil[None, :]
    facts = jnp.stack(
        [slot_brick // zbricks, slot_brick % zbricks, slot_stencil, jnp.full((slots,), live)], axis=0
    )
    packed = jnp.concatenate(
        [held, facts.astype(BF16), jnp.zeros((12, slots), BF16)], axis=0
    )
    from_prev = moved(packed, 1, 0)
    from_next = moved(packed, -1, 0)
    swapped = moved(held, 0, 1)

    grid = shape_of(ZROWS, LANES)
    g = pl.pallas_call(
        own_kernel,
        out_shape=(grid,) * 5 + (shape_of(KS * PANELS, POINTS, dtype=BF16),),
        in_specs=[SMEM] * 2 + [VMEM] * 4,
        out_specs=(VMEM,) * 6,
        scratch_shapes=[pltpu.VMEM((slots * 8, LANES), F32)],
        compiler_params=PARAMS,
        name="own_scatter",
    )(slot_brick, live_count, held, kinds, stencils.reshape(KS * PANELS, POINTS), jnp.asarray(point_order()))
    grids, stk = g[:5], g[5]

    g = pl.pallas_call(
        beside_kernel,
        out_shape=(grid,) * 4 + (shape_of(LANES, LANES), shape_of(8, 2 * slots, dtype=jnp.int32)),
        in_specs=[VMEM] * 8,
        out_specs=(VMEM,) * 6,
        scratch_shapes=[
            pltpu.VMEM((ZROWS, LANES), F32),
            pltpu.VMEM((2 * slots * 8, LANES), F32),
            pltpu.SMEM((8, 2 * slots), jnp.int32),
            pltpu.SemaphoreType.DMA,
        ],
        compiler_params=PARAMS,
        name="beside_scatter",
    )(from_prev, from_next, stk, *grids)
    facts2 = g[5]
    edge = moved(g[4], 0, 1)

    forward, inverse = z_tables(slabs, tiles)
    rows = owners * (4 * parts + SCALE_ROWS)
    sent = pl.pallas_call(
        functools.partial(z_kernel, owners),
        out_shape=shape_of(rows, LANES),
        in_specs=[VMEM] * 6,
        out_specs=VMEM,
        compiler_params=PARAMS,
        name="z_forward",
    )(*g[:4], edge, jnp.asarray(halves(forward)))

    def exchanged(values):
        values = values.astype(jnp.float16).reshape(owners, 4 * parts + SCALE_ROWS, LANES)
        values = lax.all_to_all(values, axes, 0, 0, tiled=True)
        return values

    def widened(values):
        return values.astype(F32).reshape(rows, LANES)

    got = exchanged(sent)

    pool = [from_prev, moved(swapped, 1, 0), held, swapped, from_next, moved(swapped, -1, 0)]
    direction = near_source // slots
    pool_index = (direction // 3 * 2 + (direction % 3 != 1).astype(jnp.int32)) * slots + near_source % slots
    near = pl.pallas_call(
        near_kernel,
        out_shape=shape_of(PANELS, slots),
        in_specs=[SMEM] + [VMEM] * 9,
        out_specs=VMEM,
        compiler_params=PARAMS,
        name="near_field",
    )(live_count, *pool, pool_index.T, near_block.T, near_blocks.reshape(PANELS, KN * PANELS))

    me = lax.axis_index("slab") * tiles + lax.axis_index("tile")
    offset = (me >= owners // 2).astype(jnp.int32)[None]
    back = pl.pallas_call(
        functools.partial(plane_kernel, slabs, planes),
        out_shape=shape_of(rows, LANES),
        in_specs=[SMEM] + [VMEM] * 4,
        out_specs=VMEM,
        scratch_shapes=[pltpu.VMEM((2 * planes * length, NY), BF16)] * 2,
        compiler_params=PARAMS,
        name="plane_filter",
    )(offset, widened(got), kernel_hat, jnp.asarray(halves(y_table())), jnp.asarray(halves(*x_tables(slabs))))
    back, near = lax.optimization_barrier((exchanged(back), near))

    pot = pl.pallas_call(
        functools.partial(potential_kernel, owners),
        out_shape=(grid,) * 4 + (shape_of(LANES, LANES, dtype=BF16),),
        in_specs=[VMEM] * 2,
        out_specs=(VMEM,) * 5,
        compiler_params=PARAMS,
        name="z_inverse",
    )(widened(back), jnp.asarray(halves(inverse)))
    edge = moved(pot[4], 0, 1)

    def sampling(width):
        return dict(
            out_shape=shape_of(PANELS, width),
            out_specs=VMEM,
            scratch_shapes=[pltpu.VMEM((ZROWS, LANES), F32), pltpu.VMEM((width * 8, LANES), F32)],
            compiler_params=PARAMS,
        )

    others = pl.pallas_call(
        beside_sample_kernel, in_specs=[SMEM] + [VMEM] * 7, name="beside_sample", **sampling(2 * slots)
    )(facts2, *pot[:4], edge, facts2, stk)
    to_prev = moved(others[:, :slots], -1, 0)
    to_next = moved(others[:, slots:], 1, 0)
    own = pl.pallas_call(
        own_sample_kernel, in_specs=[SMEM] * 2 + [VMEM] * 7, name="own_sample", **sampling(slots)
    )(slot_brick, live_count, *pot[:4], edge, kinds, stk)
    return own + near + to_prev + to_next


def solution(mesh):
    both = ("slab", "tile")
    in_specs = (
        P(None, both),
        P(both),
        P(both),
        P(both),
        P(),
        P(both, None),
        P(both, None),
        P(),
        P(both, None, None),
    )
    return jax.shard_map(
        functools.partial(body, mesh.shape["slab"], mesh.shape["tile"]),
        mesh=mesh,
        in_specs=in_specs,
        out_specs=P(None, both),
        check_vma=False,
    )
```

```python
import functools

import jax
import jax.numpy as jnp
import ml_dtypes
import numpy as np
from jax import lax
from jax.experimental import pallas as pl
from jax.experimental.pallas import tpu as pltpu
from jax.sharding import PartitionSpec as P

PANELS = 64
POINTS = 512
NY = 256
NZ = 512
KS = 16
KN = 16
LANES = 128
ZROWS = NZ + 8
UNROLL = 16
HALF = NY // 2
SCALE_ROWS = 8
F32 = jnp.float32
BF16 = jnp.bfloat16
SMEM = pl.BlockSpec(memory_space=pltpu.SMEM)
VMEM = pl.BlockSpec(memory_space=pltpu.VMEM)
PARAMS = pltpu.CompilerParams(vmem_limit_bytes=48 * 1024 * 1024)


def halves(*tables):
    parts = []
    for table in tables:
        high = table.astype(ml_dtypes.bfloat16)
        parts += [high, (table - high.astype(np.float64)).astype(ml_dtypes.bfloat16)]
    return np.concatenate(parts, axis=0)


def owner_frequencies(slabs, tiles):
    devices = slabs * tiles
    planes = NZ // devices
    owner = np.array([a * tiles + b for b in range(tiles) for a in range(slabs)])
    plane = np.arange(planes // 2)
    return (owner[None, :] * planes + plane[:, None] + (owner[None, :] >= devices // 2)).reshape(-1)


def z_tables(slabs, tiles):
    freq = owner_frequencies(slabs, tiles)
    cell = np.arange(NZ) - 2
    angle = (freq[:, None] * cell[None, :] % NZ) * (2 * np.pi / NZ)
    forward = np.concatenate([np.cos(angle), -np.sin(angle)], axis=0)
    weight = np.where(freq % NZ == 0, 1.0, 2.0)[:, None] / NZ
    inverse = np.concatenate([weight * np.cos(angle), -weight * np.sin(angle)], axis=0).T
    return forward, inverse


def y_table():
    angle = (np.arange(NY)[:, None] * np.arange(HALF + 1)[None, :] % NY) * (2 * np.pi / NY)
    return np.concatenate([np.cos(angle[:, :HALF]), np.cos(angle[:, HALF:]), np.sin(angle[:, 1:HALF])], axis=1)


def reversal():
    table = np.zeros((HALF, HALF), ml_dtypes.bfloat16)
    lane = np.arange(HALF)
    table[lane, (HALF - lane) % HALF] = 1
    return table


def x_tables(slabs):
    length = 4 * slabs
    cell = (np.arange(4)[:, None] + 4 * np.arange(slabs)[None, :]).reshape(-1)
    angle = (np.arange(length)[:, None] * cell[None, :] % length) * (2 * np.pi / length)
    cosine, sine = np.cos(angle), np.sin(angle)
    forward = np.block([[cosine, sine], [-sine, cosine]])
    inverse = np.block([[cosine.T, -sine.T], [sine.T, cosine.T]])
    return forward, inverse


def split(values):
    high = values.astype(BF16)
    return high, (values - high.astype(F32)).astype(BF16)


def dot(a, b):
    return jnp.dot(a, b, preferred_element_type=F32)


def dot3(a, b):
    return dot(a[0], b[0]) + (dot(a[0], b[1]) + dot(a[1], b[0]))


def lane_of(shape):
    return lax.broadcasted_iota(jnp.int32, shape, 1)


def by_kind(values, kinds):
    zero = jnp.zeros_like(values)
    return jnp.concatenate(
        [jnp.where(kinds == kind, values, zero) for kind in range(KS)], axis=0
    )


def footprints(charges, kinds, stk_ref, fp_ref, first):
    count = charges.shape[1]
    spread = by_kind(charges.astype(F32), kinds).astype(BF16)
    for pair in range(4):
        part = lax.dot_general(
            spread,
            stk_ref[:, pair * LANES : (pair + 1) * LANES],
            (((0,), (0,)), ((), ())),
            preferred_element_type=F32,
        )
        fp_ref[pl.ds(first * 8 + 2 * pair, count, stride=8), :] = part
        fp_ref[pl.ds(first * 8 + 2 * pair + 1, count, stride=8), :] = pltpu.roll(part, 64, 1)


def scatter_columns(fp_ref, first, place_of, count, grids, edge_ref, planes, shift_i):
    lane = lane_of((8, LANES))
    in_planes = (lane >= 8 * planes[0]) & (lane < 8 * (planes[-1] + 1))
    point_j = lane & 7

    def step(index, carry):
        updates = []
        for inner in range(UNROLL):
            column = index * UNROLL + inner
            by, bz = place_of(column)
            value = fp_ref[pl.ds(pl.multiple_of((first + column) * 8, 8), 8), :]
            begin = 4 * by - 2
            mask = ((lane - begin) & -8) == 0
            terms = []
            for plane in planes:
                turned = pltpu.roll(value, (begin - 8 * (plane + shift_i)) & (LANES - 1), 1)
                terms.append(jnp.where(mask, turned, 0.0))
            is_last = (by == NY // 8 - 1).astype(jnp.int32)
            low = jnp.where(by == 0, 0, jnp.where(by == NY // 8 - 1, 2, 8))
            turned = pltpu.roll(value, (-8 * shift_i - 4 * is_last) & (LANES - 1), 1)
            mask = in_planes & (((point_j - low) & -2) == 0)
            terms.append(jnp.where(mask, turned, 0.0))
            updates.append((pl.ds(4 * bz, 8), terms))
        refs = [grids[plane] for plane in planes] + [edge_ref]
        for where, terms in updates:
            sums = [ref[where, :] + term for ref, term in zip(refs, terms)]
            for ref, total in zip(refs, sums):
                ref[where, :] = total
        return carry

    lax.fori_loop(0, lax.shift_right_logical(count + UNROLL - 1, 4), step, 0)


def sample_columns(pot_refs, edge_ref, place_of, count, sp_ref, first, planes, shift_i):
    lane = lane_of((8, LANES))
    point_j = lane & 7
    inside = (lane >= 8 * (planes[0] + shift_i)) & (lane < 8 * (planes[-1] + shift_i + 1))

    def step(index, carry):
        results = []
        for inner in range(UNROLL):
            column = index * UNROLL + inner
            by, bz = place_of(column)
            where = pl.ds(4 * bz, 8)
            begin = 4 * by - 2
            result = jnp.zeros((8, LANES), F32)
            for plane in planes:
                low = 8 * (plane + shift_i)
                turned = pltpu.roll(pot_refs[plane][where, :], (low - begin) & (LANES - 1), 1)
                result = jnp.where(((lane - low) & -8) == 0, turned, result)
            is_last = (by == NY // 8 - 1).astype(jnp.int32)
            low = jnp.where(by == 0, 0, jnp.where(by == NY // 8 - 1, 6, 8))
            turned = pltpu.roll(edge_ref[where, :], (8 * shift_i + 4 * is_last) & (LANES - 1), 1)
            mask = inside & (((point_j - low) & -2) == 0)
            results.append((pl.ds(pl.multiple_of((first + column) * 8, 8), 8), jnp.where(mask, turned, result)))
        for where, result in results:
            sp_ref[where, :] = result
        return carry

    lax.fori_loop(0, lax.shift_right_logical(count + UNROLL - 1, 4), step, 0)


def far_sums(sp_ref, kinds, stk_ref, first):
    count = kinds.shape[1]
    lane = lane_of((count, LANES))
    pairs = []
    for pair in range(4):
        even = sp_ref[pl.ds(first * 8 + 2 * pair, count, stride=8), :]
        odd = sp_ref[pl.ds(first * 8 + 2 * pair + 1, count, stride=8), :]
        pairs.append(jnp.where(lane < 64, even, pltpu.roll(odd, 64, 1)).astype(BF16))
    samples = jnp.concatenate(pairs, axis=1)
    sums = lax.dot_general(
        stk_ref[...], samples, (((1,), (1,)), ((), ())), preferred_element_type=F32
    )
    result = jnp.zeros((PANELS, count), F32)
    for kind in range(KS):
        result += jnp.where(kinds == kind, sums[kind * PANELS : (kind + 1) * PANELS, :], 0.0)
    return result


def place_in_brick(brick_ref):
    def place_of(column):
        brick = brick_ref[column]
        return lax.shift_right_logical(brick, 7), brick & (NZ // 4 - 1)

    return place_of


def place_in_facts(facts_ref, start):
    return lambda column: (facts_ref[0, start + column], facts_ref[1, start + column])


def pack_kernel(live_ref, charges_ref, brick_ref, stencil_ref, out_ref):
    slots = charges_ref.shape[1]
    charges = charges_ref[...].astype(F32)
    held = jnp.where(lane_of(charges.shape) < live_ref[0], charges, 0.0)
    row = lax.broadcasted_iota(jnp.int32, (16, slots), 0)
    brick = jnp.broadcast_to(brick_ref[...], (16, slots))
    facts = jnp.where(row == 0, lax.shift_right_logical(brick, 7), brick & (NZ // 4 - 1))
    facts = jnp.where(row == 2, stencil_ref[...], jnp.where(row == 3, live_ref[0], facts))
    out_ref[...] = jnp.concatenate([held, facts.astype(F32)], axis=0).astype(BF16)


def facts_of(packed_ref):
    return packed_ref[PANELS : PANELS + 8, :].astype(F32).astype(jnp.int32)


def own_kernel(brick_ref, live_ref, packed_ref, stencil_ref,
               g0, g1, g2, g3, edge_ref, stk_ref, fp_ref, rows_ref, sem):
    copy = pltpu.make_async_copy(stencil_ref, rows_ref, sem)
    copy.start()
    for ref in (g0, g1, g2, g3, edge_ref):
        ref[...] = jnp.zeros_like(ref)
    shape = (POINTS, POINTS)
    point = lax.broadcasted_iota(jnp.int32, shape, 0)
    target = (point & 7) * 64 + lax.shift_right_logical(point, 3)
    order = jnp.where(lane_of(shape) == target, 1.0, 0.0).astype(BF16)
    kinds = facts_of(packed_ref)[2:3, :]
    slots = packed_ref.shape[1]
    live = live_ref[0]
    copy.wait()
    stk_ref[...] = dot(rows_ref[...], order).astype(BF16)

    @pl.when(live > LANES)
    def _():
        footprints(packed_ref[0:PANELS, :], kinds, stk_ref, fp_ref, 0)

    @pl.when(live <= LANES)
    def _():
        footprints(packed_ref[0:PANELS, 0:LANES], kinds[:, 0:LANES], stk_ref, fp_ref, 0)

    scatter_columns(fp_ref, 0, place_in_brick(brick_ref), live, (g0, g1, g2, g3), edge_ref, (0, 1, 2, 3), 2)


BESIDE = (((0, 1), 6), ((2, 3), -2))


def chunks_beside(facts_ref, slots):
    for first in range(0, slots, LANES):
        counts = [jnp.clip(facts_ref[3, side * slots] - first, 0, LANES) for side in range(2)]
        yield first, counts


def both_sides(ref, slots, first):
    return jnp.concatenate(
        [ref[:, side * slots + first : side * slots + first + LANES] for side in range(2)], axis=1
    )


def beside_kernel(prev_ref, next_ref, stk_ref, i0, i1, i2, i3, iedge,
                  g0, g1, g2, g3, edge_ref, out_edge, out_facts, fp_ref, facts_ref, sem):
    slots = prev_ref.shape[1]
    for side, source in enumerate((prev_ref, next_ref)):
        out_facts[:, side * slots : (side + 1) * slots] = facts_of(source)
    copy = pltpu.make_async_copy(out_facts, facts_ref, sem)
    copy.start()
    copy.wait()
    for first, counts in chunks_beside(facts_ref, slots):
        @pl.when(counts[0] + counts[1] > 0)
        def _(first=first):
            here = slice(first, first + LANES)
            charges = jnp.concatenate([prev_ref[0:PANELS, here], next_ref[0:PANELS, here]], axis=1)
            kinds = both_sides(out_facts.at[2:3, :], slots, first)
            footprints(charges, kinds, stk_ref, fp_ref, 2 * first)

        for side, (planes, shift_i) in enumerate(BESIDE):
            scatter_columns(fp_ref, 2 * first + side * LANES, place_in_facts(facts_ref, side * slots + first),
                            counts[side], (g0, g1, g2, g3), edge_ref, planes, shift_i)
    edge_ref[0:8, :] += edge_ref[NZ:ZROWS, :]
    total = edge_ref[0:LANES, :]
    for block in range(1, 4):
        total += pltpu.roll(edge_ref[block * LANES : (block + 1) * LANES, :], 32 * block, 1)
    out_edge[...] = total


def exponent_of(values):
    top = functools.reduce(jnp.maximum, [jnp.max(jnp.abs(v), axis=0, keepdims=True) for v in values])
    top = jnp.maximum(jnp.max(top, axis=1, keepdims=True), 2.0**-100)
    return jnp.ceil(jnp.log2(top)) - 12.0


def z_kernel(owners, g0, g1, g2, g3, edge_ref, w_ref, out_ref):
    lane = lane_of((LANES, LANES))
    at_edge = (lane < 2) | (lane >= LANES - 2)
    parts = NZ // owners
    stride = 4 * parts + SCALE_ROWS
    results = []
    for plane, grid in enumerate((g0, g1, g2, g3)):
        blocks = []
        for block in range(4):
            turned = pltpu.roll(edge_ref[...], (LANES - 2 - 32 * block - 8 * plane) % LANES, 1)
            blocks.append(
                grid[block * LANES : (block + 1) * LANES, :] + jnp.where(at_edge, turned, 0.0)
            )
        blocks[0] = jnp.concatenate([blocks[0][0:8] + grid[NZ:ZROWS, :], blocks[0][8:]], axis=0)
        values = split(jnp.concatenate(blocks, axis=0))
        results.append(dot3((w_ref[0:NZ, :], w_ref[NZ : 2 * NZ, :]), values))
    exponent = exponent_of(results)
    scale = jnp.exp2(-exponent)
    for plane, result in enumerate(results):
        result = result * scale
        for part in range(parts):
            out_ref[pl.ds(plane * parts + part, owners, stride=stride), :] = result[
                part * owners : (part + 1) * owners, :
            ]
    for row in range(SCALE_ROWS):
        out_ref[pl.ds(4 * parts + row, owners, stride=stride), :] = jnp.broadcast_to(
            exponent, (owners, LANES)
        )


def hat_kernel(planes, offset_ref, hat_ref, turn_ref, out_ref):
    length = hat_ref.shape[1]
    values = jnp.concatenate([hat_ref[offset_ref[0] + plane] for plane in range(planes)], axis=0)
    values = values * (1.0 / (length * NY))
    upper = values[:, HALF:]
    high, low = split(upper)
    rest = (upper - high.astype(F32) - low.astype(F32)).astype(BF16)
    turn = turn_ref[...]
    upper = dot(high, turn) + (dot(low, turn) + dot(rest, turn))
    for plane in range(planes):
        here = slice(plane * length, (plane + 1) * length)
        out_ref[plane] = jnp.concatenate([values[here, :HALF], upper[here, :]], axis=1)


def plane_kernel(slabs, planes, in_ref, hat_ref, y_ref, x_ref, out_ref, ah_ref, al_ref):
    length = 4 * slabs
    rows = planes * length
    parts = 2 * planes
    stride = 4 * parts + SCALE_ROWS

    def pieces():
        for tile in range(2):
            for part in range(2):
                for xi in range(4):
                    for plane in range(planes):
                        start = tile * slabs * stride + xi * parts + part * planes + plane
                        row = (part * planes + plane) * length + xi * slabs
                        yield tile, part, pl.ds(start, slabs, stride=stride), row

    scales = [
        jnp.exp2(in_ref[pl.ds(tile * slabs * stride + 4 * parts, slabs, stride=stride), :])
        for tile in range(2)
    ]
    for tile, part, where, row in pieces():
        high, low = split(in_ref[where, :] * scales[tile])
        ah_ref[row : row + slabs, tile * LANES : (tile + 1) * LANES] = high
        al_ref[row : row + slabs, tile * LANES : (tile + 1) * LANES] = low
    first_lane = lane_of((rows, HALF)) == 0
    turned = dot3((ah_ref[...], al_ref[...]), (y_ref[0:NY, :], y_ref[NY : 2 * NY, :]))
    even = (turned[:rows, :HALF], turned[rows:, :HALF])
    odd = (turned[:rows, HALF:], turned[rows:, HALF:])
    zero_odd = [jnp.where(first_lane, 0.0, values) for values in odd]
    real = jnp.concatenate(
        [even[0] + zero_odd[1], jnp.where(first_lane, odd[0], even[0] - zero_odd[1])], axis=1
    )
    imag = jnp.concatenate(
        [even[1] - zero_odd[0], jnp.where(first_lane, odd[1], even[1] + zero_odd[0])], axis=1
    )
    size = 2 * length
    forward = (x_ref[0:size, :], x_ref[size : 2 * size, :])
    inverse = (x_ref[2 * size : 3 * size, :], x_ref[3 * size : 4 * size, :])
    for plane in range(planes):
        here = slice(plane * length, (plane + 1) * length)
        there = slice(rows + plane * length, rows + (plane + 1) * length)
        values = dot3(forward, split(jnp.concatenate([real[here], imag[here]], axis=0)))
        values = values * jnp.concatenate([hat_ref[plane], hat_ref[plane]], axis=0)
        values = dot3(inverse, split(values))
        low, high = values[:, :HALF], values[:, HALF:]
        lane = first_lane[:length]
        even_r = jnp.where(lane, low[:length], low[:length] + high[:length])
        even_i = jnp.where(lane, low[length:], low[length:] + high[length:])
        odd_r = jnp.where(lane, high[:length], high[length:] - low[length:])
        odd_i = jnp.where(lane, high[length:], low[:length] - high[:length])
        ah_ref[here, :], al_ref[here, :] = split(jnp.concatenate([even_r, odd_r], axis=1))
        ah_ref[there, :], al_ref[there, :] = split(jnp.concatenate([even_i, odd_i], axis=1))
    turned = dot3((ah_ref[...], al_ref[...]), (y_ref[2 * NY : 3 * NY, :], y_ref[3 * NY : 4 * NY, :]))
    results = (turned[:rows], turned[rows:])
    exponent = exponent_of(results)
    scale = jnp.exp2(-exponent)
    results = [result * scale for result in results]
    for tile, part, where, row in pieces():
        row -= part * rows
        out_ref[where, :] = results[part][row : row + slabs, tile * LANES : (tile + 1) * LANES]
    for row in range(SCALE_ROWS):
        out_ref[pl.ds(4 * parts + row, 2 * slabs, stride=stride), :] = jnp.broadcast_to(
            exponent, (2 * slabs, LANES)
        )


def potential_kernel(owners, in_ref, v_ref, p0, p1, p2, p3, edge_ref):
    parts = NZ // owners
    stride = 4 * parts + SCALE_ROWS
    lane = lane_of((LANES, LANES))
    edge = jnp.zeros((LANES, LANES), F32)
    scale = jnp.exp2(in_ref[pl.ds(4 * parts, owners, stride=stride), :])
    for plane, pot in enumerate((p0, p1, p2, p3)):
        values = split(jnp.concatenate(
            [in_ref[pl.ds(plane * parts + part, owners, stride=stride), :] * scale for part in range(parts)],
            axis=0,
        ))
        result = dot3((v_ref[0:NZ, :], v_ref[NZ : 2 * NZ, :]), values).astype(BF16).astype(F32)
        pot[0:NZ, :] = result
        pot[NZ:ZROWS, :] = result[0:8, :]
        for block in range(4):
            low = 32 * block + 8 * plane
            turned = pltpu.roll(result[block * LANES : (block + 1) * LANES, :], low + 2, 1)
            edge = jnp.where((lane >= low) & (lane < low + 4), turned, edge)
    edge_ref[...] = edge.astype(BF16)


def widen_edge(edge_ref, wide_ref):
    for block in range(4):
        wide_ref[block * LANES : (block + 1) * LANES, :] = pltpu.roll(
            edge_ref[...].astype(F32), (LANES - 32 * block) % LANES, 1
        )
    wide_ref[NZ:ZROWS, :] = wide_ref[0:8, :]


def masked(values, live):
    return jnp.where(lane_of(values.shape) < live, values, 0.0)


def own_sample_kernel(brick_ref, live_ref, p0, p1, p2, p3, edge_ref, kinds_ref, stk_ref, out_ref, wide_ref, sp_ref):
    widen_edge(edge_ref, wide_ref)
    live = live_ref[0]
    slots = kinds_ref.shape[1]
    sample_columns((p0, p1, p2, p3), wide_ref, place_in_brick(brick_ref), live, sp_ref, 0, (0, 1, 2, 3), 2)

    @pl.when(live > LANES)
    def _():
        out_ref[...] = masked(far_sums(sp_ref, kinds_ref[...], stk_ref, 0), live)

    @pl.when(live <= LANES)
    def _():
        out_ref[:, 0:LANES] = masked(far_sums(sp_ref, kinds_ref[:, 0:LANES], stk_ref, 0), live)
        out_ref[:, LANES:slots] = jnp.zeros((PANELS, slots - LANES), F32)


def beside_sample_kernel(facts_ref, p0, p1, p2, p3, edge_ref, kinds_ref, stk_ref, out0, out1, wide_ref, sp_ref):
    widen_edge(edge_ref, wide_ref)
    slots = kinds_ref.shape[1] // 2
    outs = (out0, out1)
    for first, counts in chunks_beside(facts_ref, slots):
        here = slice(first, first + LANES)
        for side, (planes, shift_i) in enumerate(BESIDE):
            sample_columns((p0, p1, p2, p3), wide_ref, place_in_facts(facts_ref, side * slots + first),
                           counts[side], sp_ref, 2 * first + side * LANES, planes, shift_i)

        @pl.when(counts[0] + counts[1] > 0)
        def _(first=first, counts=counts, here=here):
            kinds = both_sides(kinds_ref.at[2:3, :], slots, first)
            result = far_sums(sp_ref, kinds, stk_ref, 2 * first)
            for side, out in enumerate(outs):
                out[:, here] = masked(result[:, side * LANES : (side + 1) * LANES], counts[side])

        @pl.when(counts[0] + counts[1] <= 0)
        def _(here=here):
            for out in outs:
                out[:, here] = jnp.zeros((PANELS, LANES), F32)


def near_kernel(live_ref, a0, a1, a2, a3, a4, a5, source_ref, block_ref, table_ref, out_ref):
    live = live_ref[0]
    fanout, slots = source_ref.shape
    pool = jnp.concatenate([ref[0:PANELS, :] for ref in (a0, a1, a2, a3, a4, a5)], axis=1)
    total = pool.shape[1]
    for first in range(0, slots, LANES):
        where = slice(first, first + LANES)

        @pl.when(live > first)
        def _(where=where, first=first):
            index = lax.broadcasted_iota(jnp.int32, (total, LANES), 0)
            result = jnp.zeros((PANELS, LANES), F32)
            for j in range(fanout):
                chosen = jnp.where(index == source_ref[j : j + 1, where], 1.0, 0.0).astype(BF16)
                gathered = dot(pool, chosen)
                result += dot(
                    table_ref[...], by_kind(gathered, block_ref[j : j + 1, where]).astype(BF16)
                )
            column = first + lane_of((PANELS, LANES))
            out_ref[:, where] = jnp.where(column < live, result, 0.0)

        @pl.when(live <= first)
        def _(where=where):
            out_ref[:, where] = jnp.zeros((PANELS, LANES), F32)


def shape_of(*dims, dtype=F32):
    return jax.ShapeDtypeStruct(dims, dtype)


def body(slabs, tiles, charges, live_count, slot_brick, slot_stencil, stencils, near_source,
         near_block, near_blocks, kernel_hat):
    slots = charges.shape[1]
    owners = slabs * tiles
    planes = kernel_hat.shape[0] // 2
    length = kernel_hat.shape[1]
    parts = NZ // owners
    axes = ("tile", "slab")
    both = ("slab", "tile")

    def moved(values, step, swap):
        pairs = [
            (a * tiles + b, (a + step) % slabs * tiles + (b + swap) % tiles)
            for a in range(slabs)
            for b in range(tiles)
        ]
        return lax.ppermute(values, both, pairs)

    kinds = slot_stencil[None, :]
    packed = pl.pallas_call(
        pack_kernel,
        out_shape=shape_of(PANELS + 16, slots, dtype=BF16),
        in_specs=[SMEM] + [VMEM] * 3,
        out_specs=VMEM,
        compiler_params=PARAMS,
        name="pack",
    )(live_count, charges, slot_brick[None, :], kinds)
    from_prev = moved(packed, 1, 0)
    from_next = moved(packed, -1, 0)
    swapped = moved(packed, 0, 1)

    grid = shape_of(ZROWS, LANES)
    g = pl.pallas_call(
        own_kernel,
        out_shape=(grid,) * 5 + (shape_of(KS * PANELS, POINTS, dtype=BF16),),
        in_specs=[SMEM] * 2 + [VMEM, pl.BlockSpec(memory_space=pl.ANY)],
        out_specs=(VMEM,) * 6,
        scratch_shapes=[
            pltpu.VMEM((slots * 8, LANES), F32),
            pltpu.VMEM((KS * PANELS, POINTS), BF16),
            pltpu.SemaphoreType.DMA,
        ],
        compiler_params=PARAMS,
        name="own_scatter",
    )(slot_brick, live_count, packed, stencils.reshape(KS * PANELS, POINTS))
    grids, stk = g[:5], g[5]

    g = pl.pallas_call(
        beside_kernel,
        out_shape=(grid,) * 5 + (shape_of(LANES, LANES), shape_of(8, 2 * slots, dtype=jnp.int32)),
        in_specs=[VMEM] * 8,
        out_specs=(VMEM,) * 7,
        scratch_shapes=[
            pltpu.VMEM((2 * slots * 8, LANES), F32),
            pltpu.SMEM((8, 2 * slots), jnp.int32),
            pltpu.SemaphoreType.DMA,
        ],
        input_output_aliases={3: 0, 4: 1, 5: 2, 6: 3, 7: 4},
        compiler_params=PARAMS,
        name="beside_scatter",
    )(from_prev, from_next, stk, *grids)
    facts2 = g[6]
    edge = moved(g[5], 0, 1)

    forward, inverse = z_tables(slabs, tiles)
    rows = owners * (4 * parts + SCALE_ROWS)
    sent = pl.pallas_call(
        functools.partial(z_kernel, owners),
        out_shape=shape_of(rows, LANES),
        in_specs=[VMEM] * 6,
        out_specs=VMEM,
        compiler_params=PARAMS,
        name="z_forward",
    )(*g[:4], edge, jnp.asarray(halves(forward)))

    def exchanged(values):
        values = values.astype(jnp.float16).reshape(owners, 4 * parts + SCALE_ROWS, LANES)
        values = lax.all_to_all(values, axes, 0, 0, tiled=True)
        return values

    def widened(values):
        return values.astype(F32).reshape(rows, LANES)

    hat, sent = lax.optimization_barrier((kernel_hat, sent))
    got = exchanged(sent)
    me = lax.axis_index("slab") * tiles + lax.axis_index("tile")
    offset = (me >= owners // 2).astype(jnp.int32)[None]
    hat = pl.pallas_call(
        functools.partial(hat_kernel, planes),
        out_shape=shape_of(planes, length, NY),
        in_specs=[SMEM] + [VMEM] * 2,
        out_specs=VMEM,
        compiler_params=PARAMS,
        name="hat_order",
    )(offset, hat, jnp.asarray(reversal()))

    swapped_prev = moved(swapped, 1, 0)
    swapped_next = moved(swapped, -1, 0)
    got, hat, swapped_prev, swapped_next = lax.optimization_barrier((got, hat, swapped_prev, swapped_next))
    pool = [from_prev, swapped_prev, packed, swapped, from_next, swapped_next]
    direction = near_source // slots
    pool_index = (direction // 3 * 2 + (direction % 3 != 1).astype(jnp.int32)) * slots + near_source % slots
    near = pl.pallas_call(
        near_kernel,
        out_shape=shape_of(PANELS, slots),
        in_specs=[SMEM] + [VMEM] * 9,
        out_specs=VMEM,
        compiler_params=PARAMS,
        name="near_field",
    )(live_count, *pool, pool_index.T, near_block.T, near_blocks.reshape(PANELS, KN * PANELS))

    back = pl.pallas_call(
        functools.partial(plane_kernel, slabs, planes),
        out_shape=shape_of(rows, LANES),
        in_specs=[VMEM] * 4,
        out_specs=VMEM,
        scratch_shapes=[pltpu.VMEM((2 * planes * length, NY), BF16)] * 2,
        compiler_params=PARAMS,
        name="plane_filter",
    )(widened(got), hat, jnp.asarray(halves(y_table(), y_table().T)), jnp.asarray(halves(*x_tables(slabs))))
    back, near = lax.optimization_barrier((exchanged(back), near))

    pot = pl.pallas_call(
        functools.partial(potential_kernel, owners),
        out_shape=(grid,) * 4 + (shape_of(LANES, LANES, dtype=BF16),),
        in_specs=[VMEM] * 2,
        out_specs=(VMEM,) * 5,
        compiler_params=PARAMS,
        name="z_inverse",
    )(widened(back), jnp.asarray(halves(inverse)))
    edge = moved(pot[4], 0, 1)

    def sample_scratch(width):
        return [pltpu.VMEM((ZROWS, LANES), F32), pltpu.VMEM((width * 8, LANES), F32)]

    sums = shape_of(PANELS, slots)
    others = pl.pallas_call(
        beside_sample_kernel,
        out_shape=(sums, sums),
        in_specs=[SMEM] + [VMEM] * 7,
        out_specs=(VMEM, VMEM),
        scratch_shapes=sample_scratch(2 * slots),
        compiler_params=PARAMS,
        name="beside_sample",
    )(facts2, *pot[:4], edge, facts2, stk)
    to_prev = moved(others[0], -1, 0)
    to_next = moved(others[1], 1, 0)
    own = pl.pallas_call(
        own_sample_kernel,
        out_shape=sums,
        in_specs=[SMEM] * 2 + [VMEM] * 7,
        out_specs=VMEM,
        scratch_shapes=sample_scratch(slots),
        compiler_params=PARAMS,
        name="own_sample",
    )(slot_brick, live_count, *pot[:4], edge, kinds, stk)
    return own + near + to_prev + to_next


def solution(mesh):
    both = ("slab", "tile")
    in_specs = (
        P(None, both),
        P(both),
        P(both),
        P(both),
        P(),
        P(both, None),
        P(both, None),
        P(),
        P(both, None, None),
    )
    return jax.shard_map(
        functools.partial(body, mesh.shape["slab"], mesh.shape["tile"]),
        mesh=mesh,
        in_specs=in_specs,
        out_specs=P(None, both),
        check_vma=False,
    )
```

```python
import functools

import jax
import jax.numpy as jnp
import ml_dtypes
import numpy as np
from jax import lax
from jax.experimental import pallas as pl
from jax.experimental.pallas import tpu as pltpu
from jax.sharding import PartitionSpec as P

PANELS = 64
POINTS = 512
NY = 256
NZ = 512
KS = 16
KN = 16
LANES = 128
ZROWS = NZ + 8
UNROLL = 16
HALF = NY // 2
SCALE_ROWS = 8
F32 = jnp.float32
BF16 = jnp.bfloat16
SMEM = pl.BlockSpec(memory_space=pltpu.SMEM)
VMEM = pl.BlockSpec(memory_space=pltpu.VMEM)
PARAMS = pltpu.CompilerParams(vmem_limit_bytes=48 * 1024 * 1024)


def halves(*tables):
    parts = []
    for table in tables:
        high = table.astype(ml_dtypes.bfloat16)
        parts += [high, (table - high.astype(np.float64)).astype(ml_dtypes.bfloat16)]
    return np.concatenate(parts, axis=0)


def owner_frequencies(slabs, tiles):
    devices = slabs * tiles
    planes = NZ // devices
    owner = np.array([a * tiles + b for b in range(tiles) for a in range(slabs)])
    plane = np.arange(planes // 2)
    return (owner[None, :] * planes + plane[:, None] + (owner[None, :] >= devices // 2)).reshape(-1)


def z_tables(slabs, tiles):
    freq = owner_frequencies(slabs, tiles)
    cell = np.arange(NZ) - 2
    angle = (freq[:, None] * cell[None, :] % NZ) * (2 * np.pi / NZ)
    forward = np.concatenate([np.cos(angle), -np.sin(angle)], axis=0)
    weight = np.where(freq % NZ == 0, 1.0, 2.0)[:, None] / NZ
    inverse = np.concatenate([weight * np.cos(angle), -weight * np.sin(angle)], axis=0).T
    return forward, inverse


def y_table():
    angle = (np.arange(NY)[:, None] * np.arange(HALF + 1)[None, :] % NY) * (2 * np.pi / NY)
    return np.concatenate([np.cos(angle[:, :HALF]), np.cos(angle[:, HALF:]), np.sin(angle[:, 1:HALF])], axis=1)


def reversal():
    table = np.zeros((HALF, HALF), ml_dtypes.bfloat16)
    lane = np.arange(HALF)
    table[lane, (HALF - lane) % HALF] = 1
    return table


def x_tables(slabs):
    length = 4 * slabs
    cell = (np.arange(4)[:, None] + 4 * np.arange(slabs)[None, :]).reshape(-1)
    angle = (np.arange(length)[:, None] * cell[None, :] % length) * (2 * np.pi / length)
    cosine, sine = np.cos(angle), np.sin(angle)
    forward = np.block([[cosine, sine], [-sine, cosine]])
    inverse = np.block([[cosine.T, -sine.T], [sine.T, cosine.T]])
    return forward, inverse


def split(values):
    high = values.astype(BF16)
    return high, (values - high.astype(F32)).astype(BF16)


def dot(a, b):
    return jnp.dot(a, b, preferred_element_type=F32)


def dot3(a, b):
    return dot(a[0], b[0]) + (dot(a[0], b[1]) + dot(a[1], b[0]))


def lane_of(shape):
    return lax.broadcasted_iota(jnp.int32, shape, 1)


def by_kind(values, kinds):
    zero = jnp.zeros_like(values)
    return jnp.concatenate(
        [jnp.where(kinds == kind, values, zero) for kind in range(KS)], axis=0
    )


def footprints(packed, stk_ref, fp_ref, first):
    count = packed.shape[1]
    turned = jnp.transpose(packed.astype(F32))
    kinds = turned[:, PANELS + 2 : PANELS + 3]
    charges = jnp.concatenate([turned[:, :PANELS], turned[:, :PANELS]], axis=1)
    offset = kinds - jnp.where(lane_of((count, LANES)) < PANELS, 0.0, 1.0)
    spread = jnp.concatenate(
        [jnp.where(offset == kind, charges, 0.0).astype(BF16) for kind in range(0, KS, 2)], axis=1
    )
    for pair in range(4):
        part = dot(spread, stk_ref[:, pair * LANES : (pair + 1) * LANES])
        fp_ref[pl.ds(first * 8 + 2 * pair, count, stride=8), :] = part
        fp_ref[pl.ds(first * 8 + 2 * pair + 1, count, stride=8), :] = pltpu.roll(part, 64, 1)


def scatter_columns(fp_ref, first, place_of, count, grids, edge_ref, planes, shift_i):
    lane = lane_of((8, LANES))
    in_planes = (lane >= 8 * planes[0]) & (lane < 8 * (planes[-1] + 1))
    point_j = lane & 7

    def step(index, carry):
        updates = []
        for inner in range(UNROLL):
            column = index * UNROLL + inner
            by, bz = place_of(column)
            value = fp_ref[pl.ds(pl.multiple_of((first + column) * 8, 8), 8), :]
            begin = 4 * by - 2
            mask = ((lane - begin) & -8) == 0
            terms = []
            for plane in planes:
                turned = pltpu.roll(value, (begin - 8 * (plane + shift_i)) & (LANES - 1), 1)
                terms.append(jnp.where(mask, turned, 0.0))
            is_last = (by == NY // 8 - 1).astype(jnp.int32)
            low = jnp.where(by == 0, 0, jnp.where(by == NY // 8 - 1, 2, 8))
            turned = pltpu.roll(value, (-8 * shift_i - 4 * is_last) & (LANES - 1), 1)
            mask = in_planes & (((point_j - low) & -2) == 0)
            terms.append(jnp.where(mask, turned, 0.0))
            updates.append((pl.ds(4 * bz, 8), terms))
        refs = [grids[plane] for plane in planes] + [edge_ref]
        for where, terms in updates:
            sums = [ref[where, :] + term for ref, term in zip(refs, terms)]
            for ref, total in zip(refs, sums):
                ref[where, :] = total
        return carry

    lax.fori_loop(0, lax.shift_right_logical(count + UNROLL - 1, 4), step, 0)


def sample_columns(pot_refs, edge_ref, place_of, count, sp_ref, first, planes, shift_i):
    lane = lane_of((8, LANES))
    point_j = lane & 7
    inside = (lane >= 8 * (planes[0] + shift_i)) & (lane < 8 * (planes[-1] + shift_i + 1))

    def step(index, carry):
        results = []
        for inner in range(UNROLL):
            column = index * UNROLL + inner
            by, bz = place_of(column)
            where = pl.ds(4 * bz, 8)
            begin = 4 * by - 2
            result = jnp.zeros((8, LANES), F32)
            for plane in planes:
                low = 8 * (plane + shift_i)
                turned = pltpu.roll(pot_refs[plane][where, :], (low - begin) & (LANES - 1), 1)
                result = jnp.where(((lane - low) & -8) == 0, turned, result)
            is_last = (by == NY // 8 - 1).astype(jnp.int32)
            low = jnp.where(by == 0, 0, jnp.where(by == NY // 8 - 1, 6, 8))
            turned = pltpu.roll(edge_ref[where, :], (8 * shift_i + 4 * is_last) & (LANES - 1), 1)
            mask = inside & (((point_j - low) & -2) == 0)
            results.append((pl.ds(pl.multiple_of((first + column) * 8, 8), 8), jnp.where(mask, turned, result)))
        for where, result in results:
            sp_ref[where, :] = result
        return carry

    lax.fori_loop(0, lax.shift_right_logical(count + UNROLL - 1, 4), step, 0)


def far_sums(sp_ref, kinds, stk_ref, first):
    count = kinds.shape[1]
    lane = lane_of((count, LANES))
    pairs = []
    for pair in range(4):
        even = sp_ref[pl.ds(first * 8 + 2 * pair, count, stride=8), :]
        odd = sp_ref[pl.ds(first * 8 + 2 * pair + 1, count, stride=8), :]
        pairs.append(jnp.where(lane < 64, even, pltpu.roll(odd, 64, 1)).astype(BF16))
    samples = jnp.concatenate(pairs, axis=1)
    sums = lax.dot_general(
        stk_ref[...], samples, (((1,), (1,)), ((), ())), preferred_element_type=F32
    )
    result = jnp.zeros((PANELS, count), F32)
    for kind in range(KS):
        result += jnp.where(kinds == kind, sums[kind * PANELS : (kind + 1) * PANELS, :], 0.0)
    return result


def place_in_brick(brick_ref):
    def place_of(column):
        brick = brick_ref[column]
        return lax.shift_right_logical(brick, 7), brick & (NZ // 4 - 1)

    return place_of


def place_in_facts(facts_ref, start):
    return lambda column: (facts_ref[0, start + column], facts_ref[1, start + column])


def pack_kernel(live_ref, charges_ref, brick_ref, stencil_ref, out_ref):
    slots = charges_ref.shape[1]
    charges = charges_ref[...].astype(F32)
    held = jnp.where(lane_of(charges.shape) < live_ref[0], charges, 0.0)
    row = lax.broadcasted_iota(jnp.int32, (16, slots), 0)
    brick = jnp.broadcast_to(brick_ref[...], (16, slots))
    facts = jnp.where(row == 0, lax.shift_right_logical(brick, 7), brick & (NZ // 4 - 1))
    facts = jnp.where(row == 2, stencil_ref[...], jnp.where(row == 3, live_ref[0], facts))
    out_ref[...] = jnp.concatenate([held, facts.astype(F32)], axis=0).astype(BF16)


def own_kernel(brick_ref, live_ref, packed_ref, stencil_ref,
               g0, g1, g2, g3, edge_ref, stk_ref, fp_ref, rows_ref, sem):
    copy = pltpu.make_async_copy(stencil_ref, rows_ref, sem)
    copy.start()
    for ref in (g0, g1, g2, g3, edge_ref):
        ref[...] = jnp.zeros_like(ref)
    shape = (POINTS, POINTS)
    point = lax.broadcasted_iota(jnp.int32, shape, 0)
    target = (point & 7) * 64 + lax.shift_right_logical(point, 3)
    order = jnp.where(lane_of(shape) == target, 1.0, 0.0).astype(BF16)
    live = live_ref[0]
    copy.wait()
    stk_ref[...] = dot(rows_ref[...], order).astype(BF16)

    @pl.when(live > LANES)
    def _():
        footprints(packed_ref[...], stk_ref, fp_ref, 0)

    @pl.when(live <= LANES)
    def _():
        footprints(packed_ref[:, 0:LANES], stk_ref, fp_ref, 0)

    scatter_columns(fp_ref, 0, place_in_brick(brick_ref), live, (g0, g1, g2, g3), edge_ref, (0, 1, 2, 3), 2)


BESIDE = (((0, 1), 6), ((2, 3), -2))


def chunks_beside(facts_ref, slots):
    for first in range(0, slots, LANES):
        counts = [jnp.clip(facts_ref[3, side * slots] - first, 0, LANES) for side in range(2)]
        yield first, counts


def both_sides(ref, slots, first):
    return jnp.concatenate(
        [ref[:, side * slots + first : side * slots + first + LANES] for side in range(2)], axis=1
    )


def beside_kernel(odd_ref, own_ref, first_ref, second_ref, stk_ref, i0, i1, i2, i3, iedge,
                  g0, g1, g2, g3, edge_ref, out_edge, out_facts, pool_ref, fp_ref, facts_ref, sem):
    height, slots = own_ref.shape
    before, after = pl.ds(0, height), pl.ds(2 * height, height)
    pool_ref[height : 2 * height, :] = own_ref[...]

    @pl.when(odd_ref[0] == 0)
    def _():
        pool_ref[after, :] = first_ref[...]
        pool_ref[before, :] = second_ref[...]

    @pl.when(odd_ref[0] != 0)
    def _():
        pool_ref[before, :] = first_ref[...]
        pool_ref[after, :] = second_ref[...]

    for side in range(2):
        row = 2 * side * height + PANELS
        facts = pool_ref[row : row + 16, :].astype(F32).astype(jnp.int32)
        out_facts[:, side * slots : (side + 1) * slots] = facts[0:8, :]
    copy = pltpu.make_async_copy(out_facts, facts_ref, sem)
    copy.start()

    def project(first):
        here = slice(first, first + LANES)
        packed = jnp.concatenate(
            [pool_ref[0:height, here], pool_ref[2 * height : 3 * height, here]], axis=1
        )
        footprints(packed, stk_ref, fp_ref, 2 * first)

    project(0)
    copy.wait()
    for first, counts in chunks_beside(facts_ref, slots):
        if first:
            @pl.when(counts[0] + counts[1] > 0)
            def _(first=first):
                project(first)

        for side, (planes, shift_i) in enumerate(BESIDE):
            scatter_columns(fp_ref, 2 * first + side * LANES, place_in_facts(facts_ref, side * slots + first),
                            counts[side], (g0, g1, g2, g3), edge_ref, planes, shift_i)
    edge_ref[0:8, :] += edge_ref[NZ:ZROWS, :]
    total = edge_ref[0:LANES, :]
    for block in range(1, 4):
        total += pltpu.roll(edge_ref[block * LANES : (block + 1) * LANES, :], 32 * block, 1)
    out_edge[...] = total


def exponent_of(values):
    top = functools.reduce(jnp.maximum, [jnp.max(jnp.abs(v), axis=0, keepdims=True) for v in values])
    top = jnp.maximum(jnp.max(top, axis=1, keepdims=True), 2.0**-100)
    return jnp.ceil(jnp.log2(top)) - 12.0


def z_kernel(owners, g0, g1, g2, g3, edge_ref, w_ref, out_ref):
    lane = lane_of((LANES, LANES))
    at_edge = (lane < 2) | (lane >= LANES - 2)
    parts = NZ // owners
    stride = 4 * parts + SCALE_ROWS
    results = []
    for plane, grid in enumerate((g0, g1, g2, g3)):
        blocks = []
        for block in range(4):
            turned = pltpu.roll(edge_ref[...], (LANES - 2 - 32 * block - 8 * plane) % LANES, 1)
            blocks.append(
                grid[block * LANES : (block + 1) * LANES, :] + jnp.where(at_edge, turned, 0.0)
            )
        blocks[0] = jnp.concatenate([blocks[0][0:8] + grid[NZ:ZROWS, :], blocks[0][8:]], axis=0)
        values = split(jnp.concatenate(blocks, axis=0))
        results.append(dot3((w_ref[0:NZ, :], w_ref[NZ : 2 * NZ, :]), values))
    exponent = exponent_of(results)
    scale = jnp.exp2(-exponent)
    for plane, result in enumerate(results):
        result = result * scale
        for part in range(parts):
            out_ref[pl.ds(plane * parts + part, owners, stride=stride), :] = result[
                part * owners : (part + 1) * owners, :
            ]
    for row in range(SCALE_ROWS):
        out_ref[pl.ds(4 * parts + row, owners, stride=stride), :] = jnp.broadcast_to(
            exponent, (owners, LANES)
        )


def hat_kernel(planes, offset_ref, hat_ref, turn_ref, out_ref):
    length = hat_ref.shape[1]
    values = jnp.concatenate([hat_ref[offset_ref[0] + plane] for plane in range(planes)], axis=0)
    values = values * (1.0 / (length * NY))
    upper = values[:, HALF:]
    high, low = split(upper)
    rest = (upper - high.astype(F32) - low.astype(F32)).astype(BF16)
    turn = turn_ref[...]
    upper = dot(high, turn) + (dot(low, turn) + dot(rest, turn))
    for plane in range(planes):
        here = slice(plane * length, (plane + 1) * length)
        out_ref[plane] = jnp.concatenate([values[here, :HALF], upper[here, :]], axis=1)


def plane_kernel(slabs, planes, in_ref, hat_ref, y_ref, x_ref, out_ref, ah_ref, al_ref):
    length = 4 * slabs
    rows = planes * length
    parts = 2 * planes
    stride = 4 * parts + SCALE_ROWS

    def pieces():
        for tile in range(2):
            for part in range(2):
                for xi in range(4):
                    for plane in range(planes):
                        start = tile * slabs * stride + xi * parts + part * planes + plane
                        row = (part * planes + plane) * length + xi * slabs
                        yield tile, part, pl.ds(start, slabs, stride=stride), row

    scales = [
        jnp.exp2(in_ref[pl.ds(tile * slabs * stride + 4 * parts, slabs, stride=stride), :])
        for tile in range(2)
    ]
    for tile, part, where, row in pieces():
        high, low = split(in_ref[where, :] * scales[tile])
        ah_ref[row : row + slabs, tile * LANES : (tile + 1) * LANES] = high
        al_ref[row : row + slabs, tile * LANES : (tile + 1) * LANES] = low
    first_lane = lane_of((rows, HALF)) == 0
    turned = dot3((ah_ref[...], al_ref[...]), (y_ref[0:NY, :], y_ref[NY : 2 * NY, :]))
    even = (turned[:rows, :HALF], turned[rows:, :HALF])
    odd = (turned[:rows, HALF:], turned[rows:, HALF:])
    zero_odd = [jnp.where(first_lane, 0.0, values) for values in odd]
    real = jnp.concatenate(
        [even[0] + zero_odd[1], jnp.where(first_lane, odd[0], even[0] - zero_odd[1])], axis=1
    )
    imag = jnp.concatenate(
        [even[1] - zero_odd[0], jnp.where(first_lane, odd[1], even[1] + zero_odd[0])], axis=1
    )
    size = 2 * length
    forward = (x_ref[0:size, :], x_ref[size : 2 * size, :])
    inverse = (x_ref[2 * size : 3 * size, :], x_ref[3 * size : 4 * size, :])
    for plane in range(planes):
        here = slice(plane * length, (plane + 1) * length)
        there = slice(rows + plane * length, rows + (plane + 1) * length)
        values = dot3(forward, split(jnp.concatenate([real[here], imag[here]], axis=0)))
        values = values * jnp.concatenate([hat_ref[plane], hat_ref[plane]], axis=0)
        values = dot3(inverse, split(values))
        low, high = values[:, :HALF], values[:, HALF:]
        lane = first_lane[:length]
        even_r = jnp.where(lane, low[:length], low[:length] + high[:length])
        even_i = jnp.where(lane, low[length:], low[length:] + high[length:])
        odd_r = jnp.where(lane, high[:length], high[length:] - low[length:])
        odd_i = jnp.where(lane, high[length:], low[:length] - high[:length])
        ah_ref[here, :], al_ref[here, :] = split(jnp.concatenate([even_r, odd_r], axis=1))
        ah_ref[there, :], al_ref[there, :] = split(jnp.concatenate([even_i, odd_i], axis=1))
    turned = dot3((ah_ref[...], al_ref[...]), (y_ref[2 * NY : 3 * NY, :], y_ref[3 * NY : 4 * NY, :]))
    results = (turned[:rows], turned[rows:])
    exponent = exponent_of(results)
    scale = jnp.exp2(-exponent)
    results = [result * scale for result in results]
    for tile, part, where, row in pieces():
        row -= part * rows
        out_ref[where, :] = results[part][row : row + slabs, tile * LANES : (tile + 1) * LANES]
    for row in range(SCALE_ROWS):
        out_ref[pl.ds(4 * parts + row, 2 * slabs, stride=stride), :] = jnp.broadcast_to(
            exponent, (2 * slabs, LANES)
        )


def potential_kernel(owners, in_ref, v_ref, p0, p1, p2, p3, edge_ref):
    parts = NZ // owners
    stride = 4 * parts + SCALE_ROWS
    lane = lane_of((LANES, LANES))
    edge = jnp.zeros((LANES, LANES), F32)
    scale = jnp.exp2(in_ref[pl.ds(4 * parts, owners, stride=stride), :])
    for plane, pot in enumerate((p0, p1, p2, p3)):
        values = split(jnp.concatenate(
            [in_ref[pl.ds(plane * parts + part, owners, stride=stride), :] * scale for part in range(parts)],
            axis=0,
        ))
        result = dot3((v_ref[0:NZ, :], v_ref[NZ : 2 * NZ, :]), values).astype(BF16).astype(F32)
        pot[0:NZ, :] = result
        pot[NZ:ZROWS, :] = result[0:8, :]
        for block in range(4):
            low = 32 * block + 8 * plane
            turned = pltpu.roll(result[block * LANES : (block + 1) * LANES, :], low + 2, 1)
            edge = jnp.where((lane >= low) & (lane < low + 4), turned, edge)
    edge_ref[...] = edge.astype(BF16)


def widen_edge(edge_ref, wide_ref):
    for block in range(4):
        wide_ref[block * LANES : (block + 1) * LANES, :] = pltpu.roll(
            edge_ref[...].astype(F32), (LANES - 32 * block) % LANES, 1
        )
    wide_ref[NZ:ZROWS, :] = wide_ref[0:8, :]


def masked(values, live):
    return jnp.where(lane_of(values.shape) < live, values, 0.0)


def own_sample_kernel(brick_ref, live_ref, p0, p1, p2, p3, edge_ref, kinds_ref, stk_ref, out_ref, wide_ref, sp_ref):
    widen_edge(edge_ref, wide_ref)
    live = live_ref[0]
    slots = kinds_ref.shape[1]
    sample_columns((p0, p1, p2, p3), wide_ref, place_in_brick(brick_ref), live, sp_ref, 0, (0, 1, 2, 3), 2)

    @pl.when(live > LANES)
    def _():
        out_ref[...] = masked(far_sums(sp_ref, kinds_ref[...], stk_ref, 0), live)

    @pl.when(live <= LANES)
    def _():
        out_ref[:, 0:LANES] = masked(far_sums(sp_ref, kinds_ref[:, 0:LANES], stk_ref, 0), live)
        out_ref[:, LANES:slots] = jnp.zeros((PANELS, slots - LANES), F32)


def beside_sample_kernel(odd_ref, facts_ref, p0, p1, p2, p3, edge_ref, kinds_ref, stk_ref, out0, out1, wide_ref, sp_ref):
    widen_edge(edge_ref, wide_ref)
    slots = kinds_ref.shape[1] // 2
    outs = (out0, out1)
    for first, counts in chunks_beside(facts_ref, slots):
        here = slice(first, first + LANES)
        for side, (planes, shift_i) in enumerate(BESIDE):
            sample_columns((p0, p1, p2, p3), wide_ref, place_in_facts(facts_ref, side * slots + first),
                           counts[side], sp_ref, 2 * first + side * LANES, planes, shift_i)

        @pl.when(counts[0] + counts[1] > 0)
        def _(first=first, counts=counts, here=here):
            kinds = both_sides(kinds_ref.at[2:3, :], slots, first)
            result = far_sums(sp_ref, kinds, stk_ref, 2 * first)
            sums = [masked(result[:, side * LANES : (side + 1) * LANES], counts[side]) for side in range(2)]
            even = jnp.broadcast_to(odd_ref[0], sums[0].shape) == 0
            out0[:, here] = jnp.where(even, sums[1], sums[0])
            out1[:, here] = jnp.where(even, sums[0], sums[1])

        @pl.when(counts[0] + counts[1] <= 0)
        def _(here=here):
            for out in outs:
                out[:, here] = jnp.zeros((PANELS, LANES), F32)


def near_kernel(live_ref, here_ref, there_ref, source_ref, block_ref, table_ref, out_ref):
    live = live_ref[0]
    fanout, slots = source_ref.shape
    height = here_ref.shape[0] // 3
    pool = jnp.concatenate(
        [ref[step * height : step * height + PANELS, :] for step in range(3) for ref in (here_ref, there_ref)],
        axis=1,
    )
    total = pool.shape[1]
    for first in range(0, slots, LANES):
        where = slice(first, first + LANES)

        @pl.when(live > first)
        def _(where=where, first=first):
            index = lax.broadcasted_iota(jnp.int32, (total, LANES), 0)
            result = jnp.zeros((PANELS, LANES), F32)
            for j in range(fanout):
                chosen = jnp.where(index == source_ref[j : j + 1, where], 1.0, 0.0).astype(BF16)
                gathered = dot(pool, chosen)
                result += dot(
                    table_ref[...], by_kind(gathered, block_ref[j : j + 1, where]).astype(BF16)
                )
            column = first + lane_of((PANELS, LANES))
            out_ref[:, where] = jnp.where(column < live, result, 0.0)

        @pl.when(live <= first)
        def _(where=where):
            out_ref[:, where] = jnp.zeros((PANELS, LANES), F32)


def shape_of(*dims, dtype=F32):
    return jax.ShapeDtypeStruct(dims, dtype)


def body(slabs, tiles, charges, live_count, slot_brick, slot_stencil, stencils, near_source,
         near_block, near_blocks, kernel_hat):
    slots = charges.shape[1]
    owners = slabs * tiles
    planes = kernel_hat.shape[0] // 2
    length = kernel_hat.shape[1]
    parts = NZ // owners
    axes = ("tile", "slab")
    both = ("slab", "tile")

    def moved(values, step_of, swap=0):
        pairs = [
            (a * tiles + b, (a + step_of(a)) % slabs * tiles + (b + swap) % tiles)
            for a in range(slabs)
            for b in range(tiles)
        ]
        return lax.ppermute(values, both, pairs)

    def to_first(values):
        return moved(values, lambda a: 1 - 2 * (a % 2))

    def to_second(values):
        return moved(values, lambda a: 2 * (a % 2) - 1)

    def to_other_tile(values):
        return moved(values, lambda a: 0, 1)

    odd = (lax.axis_index("slab") % 2)[None]
    kinds = slot_stencil[None, :]
    packed = pl.pallas_call(
        pack_kernel,
        out_shape=shape_of(PANELS + 16, slots, dtype=BF16),
        in_specs=[SMEM] + [VMEM] * 3,
        out_specs=VMEM,
        compiler_params=PARAMS,
        name="pack",
    )(live_count, charges, slot_brick[None, :], kinds)
    from_second = to_second(packed)
    from_first = to_first(packed)

    grid = shape_of(ZROWS, LANES)
    g = pl.pallas_call(
        own_kernel,
        out_shape=(grid,) * 5 + (shape_of(KS * PANELS, POINTS, dtype=BF16),),
        in_specs=[SMEM] * 2 + [VMEM, pl.BlockSpec(memory_space=pl.ANY)],
        out_specs=(VMEM,) * 6,
        scratch_shapes=[
            pltpu.VMEM((slots * 8, LANES), F32),
            pltpu.VMEM((KS * PANELS, POINTS), BF16),
            pltpu.SemaphoreType.DMA,
        ],
        compiler_params=PARAMS,
        name="own_scatter",
    )(slot_brick, live_count, packed, stencils.reshape(KS * PANELS, POINTS))
    grids, stk = g[:5], g[5]

    g = pl.pallas_call(
        beside_kernel,
        out_shape=(grid,) * 5
        + (
            shape_of(LANES, LANES),
            shape_of(8, 2 * slots, dtype=jnp.int32),
            shape_of(3 * (PANELS + 16), slots, dtype=BF16),
        ),
        in_specs=[SMEM] + [VMEM] * 9,
        out_specs=(VMEM,) * 8,
        scratch_shapes=[
            pltpu.VMEM((2 * slots * 8, LANES), F32),
            pltpu.SMEM((8, 2 * slots), jnp.int32),
            pltpu.SemaphoreType.DMA,
        ],
        input_output_aliases={5: 0, 6: 1, 7: 2, 8: 3, 9: 4},
        compiler_params=PARAMS,
        name="beside_scatter",
    )(odd, packed, from_first, from_second, stk, *grids)
    facts2 = g[6]
    edge = to_other_tile(g[5])

    forward, inverse = z_tables(slabs, tiles)
    rows = owners * (4 * parts + SCALE_ROWS)
    sent = pl.pallas_call(
        functools.partial(z_kernel, owners),
        out_shape=shape_of(rows, LANES),
        in_specs=[VMEM] * 6,
        out_specs=VMEM,
        compiler_params=PARAMS,
        name="z_forward",
    )(*g[:4], edge, jnp.asarray(halves(forward)))

    def exchanged(values):
        values = values.astype(jnp.float16).reshape(owners, 4 * parts + SCALE_ROWS, LANES)
        values = lax.all_to_all(values, axes, 0, 0, tiled=True)
        return values

    def widened(values):
        return values.astype(F32).reshape(rows, LANES)

    hat, sent = lax.optimization_barrier((kernel_hat, sent))
    got = exchanged(sent)
    me = lax.axis_index("slab") * tiles + lax.axis_index("tile")
    offset = (me >= owners // 2).astype(jnp.int32)[None]
    hat = pl.pallas_call(
        functools.partial(hat_kernel, planes),
        out_shape=shape_of(planes, length, NY),
        in_specs=[SMEM] + [VMEM] * 2,
        out_specs=VMEM,
        compiler_params=PARAMS,
        name="hat_order",
    )(offset, hat, jnp.asarray(reversal()))

    got, hat = lax.optimization_barrier((got, hat))
    pool = (g[7], to_other_tile(g[7]))
    direction = near_source // slots
    pool_index = (direction // 3 * 2 + (direction % 3 != 1).astype(jnp.int32)) * slots + near_source % slots
    near = pl.pallas_call(
        near_kernel,
        out_shape=shape_of(PANELS, slots),
        in_specs=[SMEM] + [VMEM] * 5,
        out_specs=VMEM,
        compiler_params=PARAMS,
        name="near_field",
    )(live_count, *pool, pool_index.T, near_block.T, near_blocks.reshape(PANELS, KN * PANELS))

    back = pl.pallas_call(
        functools.partial(plane_kernel, slabs, planes),
        out_shape=shape_of(rows, LANES),
        in_specs=[VMEM] * 4,
        out_specs=VMEM,
        scratch_shapes=[pltpu.VMEM((2 * planes * length, NY), BF16)] * 2,
        compiler_params=PARAMS,
        name="plane_filter",
    )(widened(got), hat, jnp.asarray(halves(y_table(), y_table().T)), jnp.asarray(halves(*x_tables(slabs))))
    back, near = lax.optimization_barrier((exchanged(back), near))

    pot = pl.pallas_call(
        functools.partial(potential_kernel, owners),
        out_shape=(grid,) * 4 + (shape_of(LANES, LANES, dtype=BF16),),
        in_specs=[VMEM] * 2,
        out_specs=(VMEM,) * 5,
        compiler_params=PARAMS,
        name="z_inverse",
    )(widened(back), jnp.asarray(halves(inverse)))
    edge = to_other_tile(pot[4])

    def sample_scratch(width):
        return [pltpu.VMEM((ZROWS, LANES), F32), pltpu.VMEM((width * 8, LANES), F32)]

    sums = shape_of(PANELS, slots)
    others = pl.pallas_call(
        beside_sample_kernel,
        out_shape=(sums, sums),
        in_specs=[SMEM] * 2 + [VMEM] * 7,
        out_specs=(VMEM, VMEM),
        scratch_shapes=sample_scratch(2 * slots),
        compiler_params=PARAMS,
        name="beside_sample",
    )(odd, facts2, *pot[:4], edge, facts2, stk)
    second = to_second(others[1])
    first = to_first(others[0])
    own = pl.pallas_call(
        own_sample_kernel,
        out_shape=sums,
        in_specs=[SMEM] * 2 + [VMEM] * 7,
        out_specs=VMEM,
        scratch_shapes=sample_scratch(slots),
        compiler_params=PARAMS,
        name="own_sample",
    )(slot_brick, live_count, *pot[:4], edge, kinds, stk)
    return own + near + first + second


def solution(mesh):
    both = ("slab", "tile")
    in_specs = (
        P(None, both),
        P(both),
        P(both),
        P(both),
        P(),
        P(both, None),
        P(both, None),
        P(),
        P(both, None, None),
    )
    return jax.shard_map(
        functools.partial(body, mesh.shape["slab"], mesh.shape["tile"]),
        mesh=mesh,
        in_specs=in_specs,
        out_specs=P(None, both),
        check_vma=False,
    )
```

```python
import functools

import jax
import jax.numpy as jnp
import ml_dtypes
import numpy as np
from jax import lax
from jax.experimental import pallas as pl
from jax.experimental.pallas import tpu as pltpu
from jax.sharding import PartitionSpec as P

PANELS = 64
POINTS = 512
NY = 256
NZ = 512
KS = 16
KN = 16
LANES = 128
ZROWS = NZ + 8
UNROLL = 16
HALF = NY // 2
SCALE_ROWS = 8
F32 = jnp.float32
BF16 = jnp.bfloat16
SMEM = pl.BlockSpec(memory_space=pltpu.SMEM)
VMEM = pl.BlockSpec(memory_space=pltpu.VMEM)
PARAMS = pltpu.CompilerParams(vmem_limit_bytes=48 * 1024 * 1024)


def halves(*tables):
    parts = []
    for table in tables:
        high = table.astype(ml_dtypes.bfloat16)
        parts += [high, (table - high.astype(np.float64)).astype(ml_dtypes.bfloat16)]
    return np.concatenate(parts, axis=0)


def owner_frequencies(slabs, tiles):
    devices = slabs * tiles
    planes = NZ // devices
    owner = np.array([a * tiles + b for b in range(tiles) for a in range(slabs)])
    plane = np.arange(planes // 2)
    return (owner[None, :] * planes + plane[:, None] + (owner[None, :] >= devices // 2)).reshape(-1)


def z_tables(slabs, tiles):
    freq = owner_frequencies(slabs, tiles)
    cell = np.arange(NZ) - 2
    angle = (freq[:, None] * cell[None, :] % NZ) * (2 * np.pi / NZ)
    forward = np.concatenate([np.cos(angle), -np.sin(angle)], axis=0)
    weight = np.where(freq % NZ == 0, 1.0, 2.0)[:, None] / NZ
    inverse = np.concatenate([weight * np.cos(angle), -weight * np.sin(angle)], axis=0).T
    return forward, inverse


def y_table():
    angle = (np.arange(NY)[:, None] * np.arange(HALF + 1)[None, :] % NY) * (2 * np.pi / NY)
    return np.concatenate([np.cos(angle[:, :HALF]), np.cos(angle[:, HALF:]), np.sin(angle[:, 1:HALF])], axis=1)


def reversal():
    table = np.zeros((HALF, HALF), ml_dtypes.bfloat16)
    lane = np.arange(HALF)
    table[lane, (HALF - lane) % HALF] = 1
    return table


def x_tables(slabs):
    length = 4 * slabs
    cell = (np.arange(4)[:, None] + 4 * np.arange(slabs)[None, :]).reshape(-1)
    angle = (np.arange(length)[:, None] * cell[None, :] % length) * (2 * np.pi / length)
    cosine, sine = np.cos(angle), np.sin(angle)
    forward = np.block([[cosine, sine], [-sine, cosine]])
    inverse = np.block([[cosine.T, -sine.T], [sine.T, cosine.T]])
    return forward, inverse


def split(values):
    high = values.astype(BF16)
    return high, (values - high.astype(F32)).astype(BF16)


def dot(a, b):
    return jnp.dot(a, b, preferred_element_type=F32)


def dot3(a, b):
    return dot(a[0], b[0]) + (dot(a[0], b[1]) + dot(a[1], b[0]))


def lane_of(shape):
    return lax.broadcasted_iota(jnp.int32, shape, 1)


def by_kind(values, kinds):
    zero = jnp.zeros_like(values)
    return jnp.concatenate(
        [jnp.where(kinds == kind, values, zero) for kind in range(KS)], axis=0
    )


def footprints(packed, stk_ref, fp_ref, first):
    count = packed.shape[1]
    turned = jnp.transpose(packed.astype(F32))
    kinds = turned[:, PANELS + 2 : PANELS + 3]
    charges = jnp.concatenate([turned[:, :PANELS], turned[:, :PANELS]], axis=1)
    offset = kinds - jnp.where(lane_of((count, LANES)) < PANELS, 0.0, 1.0)
    spread = jnp.concatenate(
        [jnp.where(offset == kind, charges, 0.0).astype(BF16) for kind in range(0, KS, 2)], axis=1
    )
    for pair in range(4):
        part = dot(spread, stk_ref[:, pair * LANES : (pair + 1) * LANES])
        fp_ref[pl.ds(first * 8 + 2 * pair, count, stride=8), :] = part
        fp_ref[pl.ds(first * 8 + 2 * pair + 1, count, stride=8), :] = pltpu.roll(part, 64, 1)


def scatter_columns(fp_ref, first, place_of, count, grids, edge_ref, planes, shift_i):
    lane = lane_of((8, LANES))
    in_planes = (lane >= 8 * planes[0]) & (lane < 8 * (planes[-1] + 1))
    point_j = lane & 7

    def step(index, carry):
        updates = []
        for inner in range(UNROLL):
            column = index * UNROLL + inner
            by, bz = place_of(column)
            value = fp_ref[pl.ds(pl.multiple_of((first + column) * 8, 8), 8), :]
            begin = 4 * by - 2
            mask = ((lane - begin) & -8) == 0
            terms = []
            for plane in planes:
                turned = pltpu.roll(value, (begin - 8 * (plane + shift_i)) & (LANES - 1), 1)
                terms.append(jnp.where(mask, turned, 0.0))
            is_last = (by == NY // 8 - 1).astype(jnp.int32)
            low = jnp.where(by == 0, 0, jnp.where(by == NY // 8 - 1, 2, 8))
            turned = pltpu.roll(value, (-8 * shift_i - 4 * is_last) & (LANES - 1), 1)
            mask = in_planes & (((point_j - low) & -2) == 0)
            terms.append(jnp.where(mask, turned, 0.0))
            updates.append((pl.ds(4 * bz, 8), terms))
        refs = [grids[plane] for plane in planes] + [edge_ref]
        for where, terms in updates:
            sums = [ref[where, :] + term for ref, term in zip(refs, terms)]
            for ref, total in zip(refs, sums):
                ref[where, :] = total
        return carry

    lax.fori_loop(0, lax.shift_right_logical(count + UNROLL - 1, 4), step, 0)


def sample_columns(pot_refs, edge_ref, place_of, count, sp_ref, first, planes, shift_i):
    lane = lane_of((8, LANES))
    point_j = lane & 7
    inside = (lane >= 8 * (planes[0] + shift_i)) & (lane < 8 * (planes[-1] + shift_i + 1))

    def step(index, carry):
        results = []
        for inner in range(UNROLL):
            column = index * UNROLL + inner
            by, bz = place_of(column)
            where = pl.ds(4 * bz, 8)
            begin = 4 * by - 2
            result = jnp.zeros((8, LANES), F32)
            for plane in planes:
                low = 8 * (plane + shift_i)
                turned = pltpu.roll(pot_refs[plane][where, :], (low - begin) & (LANES - 1), 1)
                result = jnp.where(((lane - low) & -8) == 0, turned, result)
            is_last = (by == NY // 8 - 1).astype(jnp.int32)
            low = jnp.where(by == 0, 0, jnp.where(by == NY // 8 - 1, 6, 8))
            turned = pltpu.roll(edge_ref[where, :], (8 * shift_i + 4 * is_last) & (LANES - 1), 1)
            mask = inside & (((point_j - low) & -2) == 0)
            results.append((pl.ds(pl.multiple_of((first + column) * 8, 8), 8), jnp.where(mask, turned, result)))
        for where, result in results:
            sp_ref[where, :] = result
        return carry

    lax.fori_loop(0, lax.shift_right_logical(count + UNROLL - 1, 4), step, 0)


def far_sums(sp_ref, kinds, stk_ref, first):
    count = kinds.shape[1]
    lane = lane_of((count, LANES))
    pairs = []
    for pair in range(4):
        even = sp_ref[pl.ds(first * 8 + 2 * pair, count, stride=8), :]
        odd = sp_ref[pl.ds(first * 8 + 2 * pair + 1, count, stride=8), :]
        pairs.append(jnp.where(lane < 64, even, pltpu.roll(odd, 64, 1)).astype(BF16))
    samples = jnp.concatenate(pairs, axis=1)
    sums = lax.dot_general(
        stk_ref[...], samples, (((1,), (1,)), ((), ())), preferred_element_type=F32
    )
    result = jnp.zeros((PANELS, count), F32)
    for kind in range(KS):
        result += jnp.where(kinds == kind, sums[kind * PANELS : (kind + 1) * PANELS, :], 0.0)
    return result


def place_in(facts_ref):
    return lambda column: (facts_ref[0, column], facts_ref[1, column])


def facts_copy(packed_ref, out_facts, facts_ref, sem):
    out_facts[...] = packed_ref[PANELS : PANELS + 16, :].astype(F32).astype(jnp.int32)[0:8, :]
    copy = pltpu.make_async_copy(out_facts, facts_ref, sem)
    copy.start()
    return copy


def own_kernel(packed_ref, stencil_ref,
               g0, g1, g2, g3, edge_ref, stk_ref, out_facts, fp_ref, rows_ref, facts_ref, sems):
    copy = pltpu.make_async_copy(stencil_ref, rows_ref, sems.at[0])
    copy.start()
    other_copy = facts_copy(packed_ref, out_facts, facts_ref, sems.at[1])
    for ref in (g0, g1, g2, g3, edge_ref):
        ref[...] = jnp.zeros_like(ref)
    shape = (POINTS, POINTS)
    point = lax.broadcasted_iota(jnp.int32, shape, 0)
    target = (point & 7) * 64 + lax.shift_right_logical(point, 3)
    order = jnp.where(lane_of(shape) == target, 1.0, 0.0).astype(BF16)
    other_copy.wait()
    copy.wait()
    stk_ref[...] = dot(rows_ref[...], order).astype(BF16)
    live = facts_ref[3, 0]

    @pl.when(live > LANES)
    def _():
        footprints(packed_ref[...], stk_ref, fp_ref, 0)

    @pl.when(live <= LANES)
    def _():
        footprints(packed_ref[:, 0:LANES], stk_ref, fp_ref, 0)

    scatter_columns(fp_ref, 0, place_in(facts_ref), live, (g0, g1, g2, g3), edge_ref, (0, 1, 2, 3), 2)


BEFORE = ((0, 1), 6)
AFTER = ((2, 3), -2)


def partner_kernel(is_second, odd_ref, packed_ref, stk_ref, i0, i1, i2, i3, iedge,
                   g0, g1, g2, g3, edge_ref, out_facts, *rest):
    fp_ref, facts_ref, sem = rest[-3:]
    slots = packed_ref.shape[1]
    copy = facts_copy(packed_ref, out_facts, facts_ref, sem)
    footprints(packed_ref[:, 0:LANES], stk_ref, fp_ref, 0)
    copy.wait()
    live = facts_ref[3, 0]

    @pl.when(live > LANES)
    def _():
        footprints(packed_ref[:, LANES:slots], stk_ref, fp_ref, LANES)

    for flag, (planes, shift_i) in enumerate((BEFORE, AFTER) if is_second else (AFTER, BEFORE)):
        @pl.when(odd_ref[0] == flag)
        def _(planes=planes, shift_i=shift_i):
            scatter_columns(fp_ref, 0, place_in(facts_ref), live, (g0, g1, g2, g3), edge_ref, planes, shift_i)

    if is_second:
        out_edge = rest[0]
        edge_ref[0:8, :] += edge_ref[NZ:ZROWS, :]
        total = edge_ref[0:LANES, :]
        for block in range(1, 4):
            total += pltpu.roll(edge_ref[block * LANES : (block + 1) * LANES, :], 32 * block, 1)
        out_edge[...] = total


def exponent_of(values):
    top = functools.reduce(jnp.maximum, [jnp.max(jnp.abs(v), axis=0, keepdims=True) for v in values])
    top = jnp.maximum(jnp.max(top, axis=1, keepdims=True), 2.0**-100)
    return jnp.ceil(jnp.log2(top)) - 12.0


def z_kernel(owners, g0, g1, g2, g3, edge_ref, w_ref, out_ref):
    lane = lane_of((LANES, LANES))
    at_edge = (lane < 2) | (lane >= LANES - 2)
    parts = NZ // owners
    stride = 4 * parts + SCALE_ROWS
    results = []
    for plane, grid in enumerate((g0, g1, g2, g3)):
        blocks = []
        for block in range(4):
            turned = pltpu.roll(edge_ref[...], (LANES - 2 - 32 * block - 8 * plane) % LANES, 1)
            blocks.append(
                grid[block * LANES : (block + 1) * LANES, :] + jnp.where(at_edge, turned, 0.0)
            )
        blocks[0] = jnp.concatenate([blocks[0][0:8] + grid[NZ:ZROWS, :], blocks[0][8:]], axis=0)
        values = split(jnp.concatenate(blocks, axis=0))
        results.append(dot3((w_ref[0:NZ, :], w_ref[NZ : 2 * NZ, :]), values))
    exponent = exponent_of(results)
    scale = jnp.exp2(-exponent)
    for plane, result in enumerate(results):
        result = result * scale
        for part in range(parts):
            out_ref[pl.ds(plane * parts + part, owners, stride=stride), :] = result[
                part * owners : (part + 1) * owners, :
            ]
    for row in range(SCALE_ROWS):
        out_ref[pl.ds(4 * parts + row, owners, stride=stride), :] = jnp.broadcast_to(
            exponent, (owners, LANES)
        )


def hat_kernel(planes, offset_ref, hat_ref, turn_ref, out_ref):
    length = hat_ref.shape[1]
    values = jnp.concatenate([hat_ref[offset_ref[0] + plane] for plane in range(planes)], axis=0)
    values = values * (1.0 / (length * NY))
    upper = values[:, HALF:]
    high, low = split(upper)
    rest = (upper - high.astype(F32) - low.astype(F32)).astype(BF16)
    turn = turn_ref[...]
    upper = dot(high, turn) + (dot(low, turn) + dot(rest, turn))
    for plane in range(planes):
        here = slice(plane * length, (plane + 1) * length)
        out_ref[plane] = jnp.concatenate([values[here, :HALF], upper[here, :]], axis=1)


def plane_kernel(slabs, planes, in_ref, hat_ref, y_ref, x_ref, out_ref, ah_ref, al_ref):
    length = 4 * slabs
    rows = planes * length
    parts = 2 * planes
    stride = 4 * parts + SCALE_ROWS

    def pieces():
        for tile in range(2):
            for part in range(2):
                for xi in range(4):
                    for plane in range(planes):
                        start = tile * slabs * stride + xi * parts + part * planes + plane
                        row = (part * planes + plane) * length + xi * slabs
                        yield tile, part, pl.ds(start, slabs, stride=stride), row

    scales = [
        jnp.exp2(in_ref[pl.ds(tile * slabs * stride + 4 * parts, slabs, stride=stride), :])
        for tile in range(2)
    ]
    for tile, part, where, row in pieces():
        high, low = split(in_ref[where, :] * scales[tile])
        ah_ref[row : row + slabs, tile * LANES : (tile + 1) * LANES] = high
        al_ref[row : row + slabs, tile * LANES : (tile + 1) * LANES] = low
    first_lane = lane_of((rows, HALF)) == 0
    turned = dot3((ah_ref[...], al_ref[...]), (y_ref[0:NY, :], y_ref[NY : 2 * NY, :]))
    even = (turned[:rows, :HALF], turned[rows:, :HALF])
    odd = (turned[:rows, HALF:], turned[rows:, HALF:])
    zero_odd = [jnp.where(first_lane, 0.0, values) for values in odd]
    real = jnp.concatenate(
        [even[0] + zero_odd[1], jnp.where(first_lane, odd[0], even[0] - zero_odd[1])], axis=1
    )
    imag = jnp.concatenate(
        [even[1] - zero_odd[0], jnp.where(first_lane, odd[1], even[1] + zero_odd[0])], axis=1
    )
    size = 2 * length
    forward = (x_ref[0:size, :], x_ref[size : 2 * size, :])
    inverse = (x_ref[2 * size : 3 * size, :], x_ref[3 * size : 4 * size, :])
    for plane in range(planes):
        here = slice(plane * length, (plane + 1) * length)
        there = slice(rows + plane * length, rows + (plane + 1) * length)
        values = dot3(forward, split(jnp.concatenate([real[here], imag[here]], axis=0)))
        values = values * jnp.concatenate([hat_ref[plane], hat_ref[plane]], axis=0)
        values = dot3(inverse, split(values))
        low, high = values[:, :HALF], values[:, HALF:]
        lane = first_lane[:length]
        even_r = jnp.where(lane, low[:length], low[:length] + high[:length])
        even_i = jnp.where(lane, low[length:], low[length:] + high[length:])
        odd_r = jnp.where(lane, high[:length], high[length:] - low[length:])
        odd_i = jnp.where(lane, high[length:], low[:length] - high[:length])
        ah_ref[here, :], al_ref[here, :] = split(jnp.concatenate([even_r, odd_r], axis=1))
        ah_ref[there, :], al_ref[there, :] = split(jnp.concatenate([even_i, odd_i], axis=1))
    turned = dot3((ah_ref[...], al_ref[...]), (y_ref[2 * NY : 3 * NY, :], y_ref[3 * NY : 4 * NY, :]))
    results = (turned[:rows], turned[rows:])
    exponent = exponent_of(results)
    scale = jnp.exp2(-exponent)
    results = [result * scale for result in results]
    for tile, part, where, row in pieces():
        row -= part * rows
        out_ref[where, :] = results[part][row : row + slabs, tile * LANES : (tile + 1) * LANES]
    for row in range(SCALE_ROWS):
        out_ref[pl.ds(4 * parts + row, 2 * slabs, stride=stride), :] = jnp.broadcast_to(
            exponent, (2 * slabs, LANES)
        )


def potential_kernel(owners, in_ref, v_ref, p0, p1, p2, p3, edge_ref):
    parts = NZ // owners
    stride = 4 * parts + SCALE_ROWS
    lane = lane_of((LANES, LANES))
    edge = jnp.zeros((LANES, LANES), F32)
    scale = jnp.exp2(in_ref[pl.ds(4 * parts, owners, stride=stride), :])
    for plane, pot in enumerate((p0, p1, p2, p3)):
        values = split(jnp.concatenate(
            [in_ref[pl.ds(plane * parts + part, owners, stride=stride), :] * scale for part in range(parts)],
            axis=0,
        ))
        result = dot3((v_ref[0:NZ, :], v_ref[NZ : 2 * NZ, :]), values).astype(BF16).astype(F32)
        pot[0:NZ, :] = result
        pot[NZ:ZROWS, :] = result[0:8, :]
        for block in range(4):
            low = 32 * block + 8 * plane
            turned = pltpu.roll(result[block * LANES : (block + 1) * LANES, :], low + 2, 1)
            edge = jnp.where((lane >= low) & (lane < low + 4), turned, edge)
    edge_ref[...] = edge.astype(BF16)


def widen_edge(edge_ref, wide_ref):
    for block in range(4):
        wide_ref[block * LANES : (block + 1) * LANES, :] = pltpu.roll(
            edge_ref[...].astype(F32), (LANES - 32 * block) % LANES, 1
        )
    wide_ref[NZ:ZROWS, :] = wide_ref[0:8, :]


def masked(values, live):
    return jnp.where(lane_of(values.shape) < live, values, 0.0)


def write_sums(live, sp_ref, kinds_ref, stk_ref, out_ref):
    slots = kinds_ref.shape[1]

    @pl.when(live > LANES)
    def _():
        out_ref[...] = masked(far_sums(sp_ref, kinds_ref[2:3, :], stk_ref, 0), live)

    @pl.when(live <= LANES)
    def _():
        out_ref[:, 0:LANES] = masked(far_sums(sp_ref, kinds_ref[2:3, 0:LANES], stk_ref, 0), live)
        out_ref[:, LANES:slots] = jnp.zeros((PANELS, slots - LANES), F32)


def own_sample_kernel(facts_ref, p0, p1, p2, p3, wide_ref, kinds_ref, stk_ref, out_ref, sp_ref):
    live = facts_ref[3, 0]
    sample_columns((p0, p1, p2, p3), wide_ref, place_in(facts_ref), live, sp_ref, 0, (0, 1, 2, 3), 2)
    write_sums(live, sp_ref, kinds_ref, stk_ref, out_ref)


def partner_sample_kernel(is_second, odd_ref, facts_ref, p0, p1, p2, p3, edge_ref, kinds_ref, stk_ref, out_ref, *rest):
    live = facts_ref[3, 0]
    wide_ref, sp_ref = rest if is_second else (edge_ref, rest[0])
    if is_second:
        widen_edge(edge_ref, wide_ref)
    for flag, (planes, shift_i) in enumerate((BEFORE, AFTER) if is_second else (AFTER, BEFORE)):
        @pl.when(odd_ref[0] == flag)
        def _(planes=planes, shift_i=shift_i):
            sample_columns((p0, p1, p2, p3), wide_ref, place_in(facts_ref), live, sp_ref, 0, planes, shift_i)

    write_sums(live, sp_ref, kinds_ref, stk_ref, out_ref)


def near_kernel(live_ref, a0, a1, a2, a3, a4, a5, source_ref, block_ref, table_ref, out_ref):
    live = live_ref[0]
    fanout, slots = source_ref.shape
    pool = jnp.concatenate([ref[0:PANELS, :] for ref in (a0, a1, a2, a3, a4, a5)], axis=1)
    total = pool.shape[1]
    for first in range(0, slots, LANES):
        where = slice(first, first + LANES)

        @pl.when(live > first)
        def _(where=where, first=first):
            index = lax.broadcasted_iota(jnp.int32, (total, LANES), 0)
            result = jnp.zeros((PANELS, LANES), F32)
            for j in range(fanout):
                chosen = jnp.where(index == source_ref[j : j + 1, where], 1.0, 0.0).astype(BF16)
                gathered = dot(pool, chosen)
                result += dot(
                    table_ref[...], by_kind(gathered, block_ref[j : j + 1, where]).astype(BF16)
                )
            column = first + lane_of((PANELS, LANES))
            out_ref[:, where] = jnp.where(column < live, result, 0.0)

        @pl.when(live <= first)
        def _(where=where):
            out_ref[:, where] = jnp.zeros((PANELS, LANES), F32)


def shape_of(*dims, dtype=F32):
    return jax.ShapeDtypeStruct(dims, dtype)


def body(slabs, tiles, charges, live_count, slot_brick, slot_stencil, stencils, near_source,
         near_block, near_blocks, kernel_hat):
    slots = charges.shape[1]
    owners = slabs * tiles
    planes = kernel_hat.shape[0] // 2
    length = kernel_hat.shape[1]
    parts = NZ // owners
    axes = ("tile", "slab")
    both = ("slab", "tile")

    def moved(values, step_of, swap=0):
        pairs = [
            (a * tiles + b, (a + step_of(a)) % slabs * tiles + (b + swap) % tiles)
            for a in range(slabs)
            for b in range(tiles)
        ]
        return lax.ppermute(values, both, pairs)

    def to_first(values):
        return moved(values, lambda a: 1 - 2 * (a % 2))

    def to_second(values):
        return moved(values, lambda a: 2 * (a % 2) - 1)

    def to_other_tile(values):
        return moved(values, lambda a: 0, 1)

    odd = (lax.axis_index("slab") % 2)[None]
    row = lax.broadcasted_iota(jnp.int32, (PANELS + 16, slots), 0)
    column = lax.broadcasted_iota(jnp.int32, (PANELS + 16, slots), 1)
    live = jnp.broadcast_to(live_count[0], row.shape)
    brick = jnp.broadcast_to(slot_brick[None, :], row.shape)
    facts = jnp.where(row == PANELS, lax.shift_right_logical(brick, 7), brick & (NZ // 4 - 1))
    facts = jnp.where(row == PANELS + 2, slot_stencil[None, :], jnp.where(row == PANELS + 3, live, facts))
    held = jnp.where(column < live, jnp.pad(charges, ((0, 16), (0, 0))), jnp.zeros((), BF16))
    packed = jnp.where(row < PANELS, held, facts.astype(BF16))
    from_first = to_first(packed)

    grid = shape_of(ZROWS, LANES)
    facts_shape = shape_of(8, slots, dtype=jnp.int32)
    scratch = [pltpu.VMEM((slots * 8, LANES), F32), pltpu.SMEM((8, slots), jnp.int32)]
    *grids, stk, facts = pl.pallas_call(
        own_kernel,
        out_shape=(grid,) * 5 + (shape_of(KS * PANELS, POINTS, dtype=BF16), facts_shape),
        in_specs=[VMEM, pl.BlockSpec(memory_space=pltpu.HBM)],
        out_specs=(VMEM,) * 7,
        scratch_shapes=[
            scratch[0], pltpu.VMEM((KS * PANELS, POINTS), BF16), scratch[1], pltpu.SemaphoreType.DMA((2,))
        ],
        compiler_params=PARAMS,
        name="own_scatter",
    )(packed, stencils.reshape(KS * PANELS, POINTS))

    def with_partner(is_second, values, grids):
        return pl.pallas_call(
            functools.partial(partner_kernel, is_second),
            out_shape=(grid,) * 5 + (facts_shape,) + (shape_of(LANES, LANES),) * is_second,
            in_specs=[SMEM] + [VMEM] * 7,
            out_specs=(VMEM,) * (6 + is_second),
            scratch_shapes=scratch + [pltpu.SemaphoreType.DMA],
            input_output_aliases={3: 0, 4: 1, 5: 2, 6: 3, 7: 4},
            compiler_params=PARAMS,
            name="second_scatter" if is_second else "first_scatter",
        )(odd, values, stk, *grids)

    packed, grids[4] = lax.optimization_barrier((packed, grids[4]))
    from_second = to_second(packed)
    *grids, first_facts = with_partner(0, from_first, grids)
    *grids, second_facts, edge = with_partner(1, from_second, grids)
    edge = to_other_tile(edge)

    forward, inverse = z_tables(slabs, tiles)
    rows = owners * (4 * parts + SCALE_ROWS)
    sent = pl.pallas_call(
        functools.partial(z_kernel, owners),
        out_shape=shape_of(rows, LANES),
        in_specs=[VMEM] * 6,
        out_specs=VMEM,
        compiler_params=PARAMS,
        name="z_forward",
    )(*grids[:4], edge, jnp.asarray(halves(forward)))

    def exchanged(values):
        values = values.astype(jnp.float16).reshape(owners, 4 * parts + SCALE_ROWS, LANES)
        values = lax.all_to_all(values, axes, 0, 0, tiled=True)
        return values

    def widened(values):
        return values.astype(F32).reshape(rows, LANES)

    hat, sent = lax.optimization_barrier((kernel_hat, sent))
    got = exchanged(sent)
    me = lax.axis_index("slab") * tiles + lax.axis_index("tile")
    offset = (me >= owners // 2).astype(jnp.int32)[None]
    hat = pl.pallas_call(
        functools.partial(hat_kernel, planes),
        out_shape=shape_of(planes, length, NY),
        in_specs=[SMEM] + [VMEM] * 2,
        out_specs=VMEM,
        compiler_params=PARAMS,
        name="hat_order",
    )(offset, hat, jnp.asarray(reversal()))

    got, hat = lax.optimization_barrier((got, hat))
    pool = []
    for values in (from_first, packed, from_second):
        pool += [values, to_other_tile(values)]
    direction = near_source // slots
    step = direction // 3 - 1
    partner = jnp.where(step == 0, 1, jnp.where((step > 0) == (odd[0] == 0), 0, 2))
    pool_index = (partner * 2 + (direction % 3 != 1).astype(jnp.int32)) * slots + near_source % slots
    near = pl.pallas_call(
        near_kernel,
        out_shape=shape_of(PANELS, slots),
        in_specs=[SMEM] + [VMEM] * 9,
        out_specs=VMEM,
        compiler_params=PARAMS,
        name="near_field",
    )(live_count, *pool, pool_index.T, near_block.T, near_blocks.reshape(PANELS, KN * PANELS))

    back = pl.pallas_call(
        functools.partial(plane_kernel, slabs, planes),
        out_shape=shape_of(rows, LANES),
        in_specs=[VMEM] * 4,
        out_specs=VMEM,
        scratch_shapes=[pltpu.VMEM((2 * planes * length, NY), BF16)] * 2,
        compiler_params=PARAMS,
        name="plane_filter",
    )(widened(got), hat, jnp.asarray(halves(y_table(), y_table().T)), jnp.asarray(halves(*x_tables(slabs))))
    back, near = lax.optimization_barrier((exchanged(back), near))

    pot = pl.pallas_call(
        functools.partial(potential_kernel, owners),
        out_shape=(grid,) * 4 + (shape_of(LANES, LANES, dtype=BF16),),
        in_specs=[VMEM] * 2,
        out_specs=(VMEM,) * 5,
        compiler_params=PARAMS,
        name="z_inverse",
    )(widened(back), jnp.asarray(halves(inverse)))
    edge = to_other_tile(pot[4])

    sums = shape_of(PANELS, slots)
    wide = shape_of(ZROWS, LANES)

    def sampled(kernel, name, facts, *edges, scalars=(), outs=(sums,)):
        return pl.pallas_call(
            kernel,
            out_shape=outs,
            in_specs=[SMEM] * (1 + len(scalars)) + [VMEM] * 7,
            out_specs=(VMEM,) * len(outs),
            scratch_shapes=[pltpu.VMEM((slots * 8, LANES), F32)],
            compiler_params=PARAMS,
            name=name,
        )(*scalars, facts, *pot[:4], *edges, facts, stk)

    second, edge = sampled(
        functools.partial(partner_sample_kernel, 1), "second_sample", second_facts, edge,
        scalars=(odd,), outs=(sums, wide),
    )
    second = to_second(second)
    first, = sampled(functools.partial(partner_sample_kernel, 0), "first_sample", first_facts, edge, scalars=(odd,))
    first = to_first(first)
    own, = sampled(own_sample_kernel, "own_sample", facts, edge)
    return own + near + first + second


def solution(mesh):
    both = ("slab", "tile")
    in_specs = (
        P(None, both),
        P(both),
        P(both),
        P(both),
        P(),
        P(both, None),
        P(both, None),
        P(),
        P(both, None, None),
    )
    return jax.shard_map(
        functools.partial(body, mesh.shape["slab"], mesh.shape["tile"]),
        mesh=mesh,
        in_specs=in_specs,
        out_specs=P(None, both),
        check_vma=False,
    )
```

```python
import functools
import math

import jax
import jax.numpy as jnp
import ml_dtypes
import numpy as np
from jax import lax
from jax.experimental import pallas as pl
from jax.experimental.pallas import tpu as pltpu
from jax.sharding import PartitionSpec as P

PANELS = 64
POINTS = 512
NY = 256
NZ = 512
KS = 16
KN = 16
LANES = 128
ZROWS = NZ + 8
UNROLL = 16
HALF = NY // 2
SCALE_ROWS = 8
BOUND = 12.0
HEADROOM = 15.0
F32 = jnp.float32
BF16 = jnp.bfloat16
SMEM = pl.BlockSpec(memory_space=pltpu.SMEM)
VMEM = pl.BlockSpec(memory_space=pltpu.VMEM)
PARAMS = pltpu.CompilerParams(vmem_limit_bytes=48 * 1024 * 1024)


def halves(*tables):
    parts = []
    for table in tables:
        high = table.astype(ml_dtypes.bfloat16)
        parts += [high, (table - high.astype(np.float64)).astype(ml_dtypes.bfloat16)]
    return np.concatenate(parts, axis=0)


def owner_frequencies(slabs, tiles):
    devices = slabs * tiles
    planes = NZ // devices
    owner = np.array([a * tiles + b for b in range(tiles) for a in range(slabs)])
    plane = np.arange(planes // 2)
    return (owner[None, :] * planes + plane[:, None] + (owner[None, :] >= devices // 2)).reshape(-1)


def z_tables(slabs, tiles):
    freq = owner_frequencies(slabs, tiles)
    cell = np.arange(NZ) - 2
    angle = (freq[:, None] * cell[None, :] % NZ) * (2 * np.pi / NZ)
    forward = np.concatenate([np.cos(angle), -np.sin(angle)], axis=0)
    weight = np.where(freq % NZ == 0, 1.0, 2.0)[:, None] / NZ
    inverse = np.concatenate([weight * np.cos(angle), -weight * np.sin(angle)], axis=0).T
    return forward, inverse


def y_table():
    angle = (np.arange(NY)[:, None] * np.arange(HALF + 1)[None, :] % NY) * (2 * np.pi / NY)
    return np.concatenate([np.cos(angle[:, :HALF]), np.cos(angle[:, HALF:]), np.sin(angle[:, 1:HALF])], axis=1)


def reversal():
    table = np.zeros((HALF, HALF), ml_dtypes.bfloat16)
    lane = np.arange(HALF)
    table[lane, (HALF - lane) % HALF] = 1
    return table


def x_tables(slabs):
    length = 4 * slabs
    cell = (np.arange(4)[:, None] + 4 * np.arange(slabs)[None, :]).reshape(-1)
    angle = (np.arange(length)[:, None] * cell[None, :] % length) * (2 * np.pi / length)
    cosine, sine = np.cos(angle), np.sin(angle)
    forward = np.block([[cosine, sine], [-sine, cosine]])
    inverse = np.block([[cosine.T, -sine.T], [sine.T, cosine.T]])
    return forward, inverse


def split(values):
    high = values.astype(BF16)
    return high, (values - high.astype(F32)).astype(BF16)


def dot(a, b):
    return jnp.dot(a, b, preferred_element_type=F32)


def dot3(a, b):
    return dot(a[0], b[0]) + (dot(a[0], b[1]) + dot(a[1], b[0]))


def lane_of(shape):
    return lax.broadcasted_iota(jnp.int32, shape, 1)


def by_kind(values, kinds):
    zero = jnp.zeros_like(values)
    return jnp.concatenate(
        [jnp.where(kinds == kind, values, zero) for kind in range(KS)], axis=0
    )


def footprints(packed, stk_ref, fp_ref, first):
    count = packed.shape[1]
    turned = jnp.transpose(packed.astype(F32))
    kinds = turned[:, PANELS + 2 : PANELS + 3]
    charges = jnp.concatenate([turned[:, :PANELS], turned[:, :PANELS]], axis=1)
    offset = kinds - jnp.where(lane_of((count, LANES)) < PANELS, 0.0, 1.0)
    spread = jnp.concatenate(
        [jnp.where(offset == kind, charges, 0.0).astype(BF16) for kind in range(0, KS, 2)], axis=1
    )
    for pair in range(4):
        part = dot(spread, stk_ref[:, pair * LANES : (pair + 1) * LANES])
        fp_ref[pl.ds(first * 8 + 2 * pair, count, stride=8), :] = part
        fp_ref[pl.ds(first * 8 + 2 * pair + 1, count, stride=8), :] = pltpu.roll(part, 64, 1)


def scatter_columns(fp_ref, first, place_of, count, grids, edge_ref, planes, shift_i):
    lane = lane_of((8, LANES))
    in_planes = (lane >= 8 * planes[0]) & (lane < 8 * (planes[-1] + 1))
    point_j = lane & 7

    def step(index, carry):
        updates = []
        for inner in range(UNROLL):
            column = index * UNROLL + inner
            by, bz = place_of(column)
            value = fp_ref[pl.ds(pl.multiple_of((first + column) * 8, 8), 8), :]
            begin = 4 * by - 2
            mask = ((lane - begin) & -8) == 0
            terms = []
            for plane in planes:
                turned = pltpu.roll(value, (begin - 8 * (plane + shift_i)) & (LANES - 1), 1)
                terms.append(jnp.where(mask, turned, 0.0))
            is_last = (by == NY // 8 - 1).astype(jnp.int32)
            low = jnp.where(by == 0, 0, jnp.where(by == NY // 8 - 1, 2, 8))
            turned = pltpu.roll(value, (-8 * shift_i - 4 * is_last) & (LANES - 1), 1)
            mask = in_planes & (((point_j - low) & -2) == 0)
            terms.append(jnp.where(mask, turned, 0.0))
            updates.append((pl.ds(4 * bz, 8), terms))
        refs = [grids[plane] for plane in planes] + [edge_ref]
        for where, terms in updates:
            sums = [ref[where, :] + term for ref, term in zip(refs, terms)]
            for ref, total in zip(refs, sums):
                ref[where, :] = total
        return carry

    lax.fori_loop(0, lax.shift_right_logical(count + UNROLL - 1, 4), step, 0)


def sample_columns(pot_refs, edge_ref, place_of, count, sp_ref, first, planes, shift_i):
    lane = lane_of((8, LANES))
    point_j = lane & 7
    inside = (lane >= 8 * (planes[0] + shift_i)) & (lane < 8 * (planes[-1] + shift_i + 1))

    def step(index, carry):
        results = []
        for inner in range(UNROLL):
            column = index * UNROLL + inner
            by, bz = place_of(column)
            where = pl.ds(4 * bz, 8)
            begin = 4 * by - 2
            result = jnp.zeros((8, LANES), F32)
            for plane in planes:
                low = 8 * (plane + shift_i)
                turned = pltpu.roll(pot_refs[plane][where, :], (low - begin) & (LANES - 1), 1)
                result = jnp.where(((lane - low) & -8) == 0, turned, result)
            is_last = (by == NY // 8 - 1).astype(jnp.int32)
            low = jnp.where(by == 0, 0, jnp.where(by == NY // 8 - 1, 6, 8))
            turned = pltpu.roll(edge_ref[where, :], (8 * shift_i + 4 * is_last) & (LANES - 1), 1)
            mask = inside & (((point_j - low) & -2) == 0)
            results.append((pl.ds(pl.multiple_of((first + column) * 8, 8), 8), jnp.where(mask, turned, result)))
        for where, result in results:
            sp_ref[where, :] = result
        return carry

    lax.fori_loop(0, lax.shift_right_logical(count + UNROLL - 1, 4), step, 0)


def far_sums(sp_ref, kinds, stk_ref, first):
    count = kinds.shape[1]
    lane = lane_of((count, LANES))
    pairs = []
    for pair in range(4):
        even = sp_ref[pl.ds(first * 8 + 2 * pair, count, stride=8), :]
        odd = sp_ref[pl.ds(first * 8 + 2 * pair + 1, count, stride=8), :]
        pairs.append(jnp.where(lane < 64, even, pltpu.roll(odd, 64, 1)).astype(BF16))
    samples = jnp.concatenate(pairs, axis=1)
    sums = lax.dot_general(
        stk_ref[...], samples, (((1,), (1,)), ((), ())), preferred_element_type=F32
    )
    result = jnp.zeros((PANELS, count), F32)
    for kind in range(KS):
        result += jnp.where(kinds == kind, sums[kind * PANELS : (kind + 1) * PANELS, :], 0.0)
    return result


def place_in_facts(facts_ref, start=0):
    return lambda column: (facts_ref[0, start + column], facts_ref[1, start + column])


def facts_of(packed_ref, row):
    return packed_ref[row : row + 16, :].astype(F32).astype(jnp.int32)[0:8, :]


def own_kernel(packed_ref, stencil_ref,
               g0, g1, g2, g3, edge_ref, stk_ref, out_facts, fp_ref, rows_ref, facts_ref, sems):
    copy = pltpu.make_async_copy(stencil_ref, rows_ref, sems.at[0])
    copy.start()
    out_facts[...] = facts_of(packed_ref, PANELS)
    facts_copy = pltpu.make_async_copy(out_facts, facts_ref, sems.at[1])
    facts_copy.start()
    for ref in (g0, g1, g2, g3, edge_ref):
        ref[...] = jnp.zeros_like(ref)
    shape = (POINTS, POINTS)
    point = lax.broadcasted_iota(jnp.int32, shape, 0)
    target = (point & 7) * 64 + lax.shift_right_logical(point, 3)
    order = jnp.where(lane_of(shape) == target, 1.0, 0.0).astype(BF16)
    facts_copy.wait()
    copy.wait()
    stk_ref[...] = dot(rows_ref[...], order).astype(BF16)
    live = facts_ref[3, 0]

    @pl.when(live > LANES)
    def _():
        footprints(packed_ref[...], stk_ref, fp_ref, 0)

    @pl.when(live <= LANES)
    def _():
        footprints(packed_ref[:, 0:LANES], stk_ref, fp_ref, 0)

    scatter_columns(fp_ref, 0, place_in_facts(facts_ref), live, (g0, g1, g2, g3), edge_ref, (0, 1, 2, 3), 2)


BESIDE = (((0, 1), 6), ((2, 3), -2))


def chunks_beside(facts_ref, slots):
    for first in range(0, slots, LANES):
        counts = [jnp.clip(facts_ref[3, side * slots] - first, 0, LANES) for side in range(2)]
        yield first, counts


def both_sides(ref, slots, first):
    return jnp.concatenate(
        [ref[:, side * slots + first : side * slots + first + LANES] for side in range(2)], axis=1
    )


def beside_kernel(odd_ref, own_ref, first_ref, second_ref, stk_ref, i0, i1, i2, i3, iedge,
                  g0, g1, g2, g3, edge_ref, out_edge, out_facts, pool_ref, fp_ref, facts_ref, sem):
    height, slots = own_ref.shape
    before, after = pl.ds(0, height), pl.ds(2 * height, height)
    pool_ref[height : 2 * height, :] = own_ref[...]

    @pl.when(odd_ref[0] == 0)
    def _():
        pool_ref[after, :] = first_ref[...]
        pool_ref[before, :] = second_ref[...]

    @pl.when(odd_ref[0] != 0)
    def _():
        pool_ref[before, :] = first_ref[...]
        pool_ref[after, :] = second_ref[...]

    for side in range(2):
        out_facts[:, side * slots : (side + 1) * slots] = facts_of(pool_ref, 2 * side * height + PANELS)
    copy = pltpu.make_async_copy(out_facts, facts_ref, sem)
    copy.start()

    def project(first):
        here = slice(first, first + LANES)
        packed = jnp.concatenate(
            [pool_ref[0:height, here], pool_ref[2 * height : 3 * height, here]], axis=1
        )
        footprints(packed, stk_ref, fp_ref, 2 * first)

    project(0)
    copy.wait()
    for first, counts in chunks_beside(facts_ref, slots):
        if first:
            @pl.when(counts[0] + counts[1] > 0)
            def _(first=first):
                project(first)

        for side, (planes, shift_i) in enumerate(BESIDE):
            scatter_columns(fp_ref, 2 * first + side * LANES, place_in_facts(facts_ref, side * slots + first),
                            counts[side], (g0, g1, g2, g3), edge_ref, planes, shift_i)
    edge_ref[0:8, :] += edge_ref[NZ:ZROWS, :]
    total = edge_ref[0:LANES, :]
    for block in range(1, 4):
        total += pltpu.roll(edge_ref[block * LANES : (block + 1) * LANES, :], 32 * block, 1)
    out_edge[...] = total


def exponent_of(values):
    top = functools.reduce(jnp.maximum, [jnp.max(jnp.abs(v), axis=0, keepdims=True) for v in values])
    top = jnp.maximum(jnp.max(top, axis=1, keepdims=True), 2.0**-100)
    return jnp.ceil(jnp.log2(top)) - BOUND


def z_kernel(owners, g0, g1, g2, g3, edge_ref, w_ref, out_ref):
    lane = lane_of((LANES, LANES))
    at_edge = (lane < 2) | (lane >= LANES - 2)
    parts = NZ // owners
    stride = 4 * parts + SCALE_ROWS
    results = []
    for plane, grid in enumerate((g0, g1, g2, g3)):
        blocks = []
        for block in range(4):
            turned = pltpu.roll(edge_ref[...], (LANES - 2 - 32 * block - 8 * plane) % LANES, 1)
            blocks.append(
                grid[block * LANES : (block + 1) * LANES, :] + jnp.where(at_edge, turned, 0.0)
            )
        blocks[0] = jnp.concatenate([blocks[0][0:8] + grid[NZ:ZROWS, :], blocks[0][8:]], axis=0)
        values = split(jnp.concatenate(blocks, axis=0))
        results.append(dot3((w_ref[0:NZ, :], w_ref[NZ : 2 * NZ, :]), values))
    exponent = exponent_of(results)
    scale = jnp.exp2(-exponent)
    for plane, result in enumerate(results):
        result = result * scale
        for part in range(parts):
            out_ref[pl.ds(plane * parts + part, owners, stride=stride), :] = result[
                part * owners : (part + 1) * owners, :
            ]
    for row in range(SCALE_ROWS):
        out_ref[pl.ds(4 * parts + row, owners, stride=stride), :] = jnp.broadcast_to(
            exponent, (owners, LANES)
        )


def hat_kernel(planes, offset_ref, hat_ref, turn_ref, out_ref):
    length = hat_ref.shape[1]
    values = jnp.concatenate([hat_ref[offset_ref[0] + plane] for plane in range(planes)], axis=0)
    values = values * (1.0 / (length * NY))
    upper = values[:, HALF:]
    high, low = split(upper)
    rest = (upper - high.astype(F32) - low.astype(F32)).astype(BF16)
    turn = turn_ref[...]
    upper = dot(high, turn) + (dot(low, turn) + dot(rest, turn))
    for plane in range(planes):
        here = slice(plane * length, (plane + 1) * length)
        out_ref[plane] = jnp.concatenate([values[here, :HALF], upper[here, :]], axis=1)


def plane_kernel(slabs, planes, in_ref, hat_ref, y_ref, x_ref, out_ref, exponent_ref, ah_ref, al_ref):
    length = 4 * slabs
    rows = planes * length
    parts = 2 * planes
    stride = 4 * parts + SCALE_ROWS

    def pieces():
        for tile in range(2):
            for part in range(2):
                for xi in range(4):
                    for plane in range(planes):
                        yield tile, part, plane, xi

    scales = [
        jnp.exp2(in_ref[pl.ds(tile * slabs * stride + 4 * parts, slabs, stride=stride), :])
        for tile in range(2)
    ]
    for tile, part, plane, xi in pieces():
        start = tile * slabs * stride + xi * parts + part * planes + plane
        row = (part * planes + plane) * length + xi * slabs
        high, low = split(in_ref[pl.ds(start, slabs, stride=stride), :] * scales[tile])
        ah_ref[row : row + slabs, tile * LANES : (tile + 1) * LANES] = high
        al_ref[row : row + slabs, tile * LANES : (tile + 1) * LANES] = low
    first_lane = lane_of((rows, HALF)) == 0
    turned = dot3((ah_ref[...], al_ref[...]), (y_ref[0:NY, :], y_ref[NY : 2 * NY, :]))
    even = (turned[:rows, :HALF], turned[rows:, :HALF])
    odd = (turned[:rows, HALF:], turned[rows:, HALF:])
    zero_odd = [jnp.where(first_lane, 0.0, values) for values in odd]
    real = jnp.concatenate(
        [even[0] + zero_odd[1], jnp.where(first_lane, odd[0], even[0] - zero_odd[1])], axis=1
    )
    imag = jnp.concatenate(
        [even[1] - zero_odd[0], jnp.where(first_lane, odd[1], even[1] + zero_odd[0])], axis=1
    )
    size = 2 * length
    forward = (x_ref[0:size, :], x_ref[size : 2 * size, :])
    inverse = (x_ref[2 * size : 3 * size, :], x_ref[3 * size : 4 * size, :])
    for plane in range(planes):
        here = slice(plane * length, (plane + 1) * length)
        there = slice(rows + plane * length, rows + (plane + 1) * length)
        values = dot3(forward, split(jnp.concatenate([real[here], imag[here]], axis=0)))
        values = values * jnp.concatenate([hat_ref[plane], hat_ref[plane]], axis=0)
        values = dot3(inverse, split(values))
        low, high = values[:, :HALF], values[:, HALF:]
        lane = first_lane[:length]
        even_r = jnp.where(lane, low[:length], low[:length] + high[:length])
        even_i = jnp.where(lane, low[length:], low[length:] + high[length:])
        odd_r = jnp.where(lane, high[:length], high[length:] - low[length:])
        odd_i = jnp.where(lane, high[length:], low[:length] - high[:length])
        ah_ref[here, :], al_ref[here, :] = split(jnp.concatenate([even_r, odd_r], axis=1))
        ah_ref[there, :], al_ref[there, :] = split(jnp.concatenate([even_i, odd_i], axis=1))
    turned = dot3((ah_ref[...], al_ref[...]), (y_ref[2 * NY : 3 * NY, :], y_ref[3 * NY : 4 * NY, :]))
    tops = [
        jnp.max(in_ref[pl.ds(tile * slabs * stride + 4 * parts, slabs, stride=stride), :], axis=0, keepdims=True)
        for tile in range(2)
    ]
    exponent = jnp.broadcast_to(jnp.maximum(*tops) + BOUND - HEADROOM + math.ceil(math.log2(length * NY) / 2), (8, LANES))
    exponent_ref[...] = exponent
    scale = jnp.exp2(-exponent[0:1, 0:1])
    for tile, part, plane, xi in pieces():
        here = slice((part * planes + plane) * length + xi * slabs, (part * planes + plane) * length + (xi + 1) * slabs)
        start = tile * slabs * 4 * parts + xi * parts + part * planes + plane
        out_ref[pl.ds(start, slabs, stride=4 * parts), :] = (
            turned[here, tile * LANES : (tile + 1) * LANES] * scale
        )


def potential_kernel(owners, in_ref, exponent_ref, v_ref, p0, p1, p2, p3, edge_ref):
    parts = NZ // owners
    lane = lane_of((LANES, LANES))
    edge = jnp.zeros((LANES, LANES), F32)
    scale = jnp.exp2(exponent_ref[0:1, 0:1])
    for plane, pot in enumerate((p0, p1, p2, p3)):
        values = split(jnp.concatenate(
            [in_ref[pl.ds(plane * parts + part, owners, stride=4 * parts), :] for part in range(parts)],
            axis=0,
        ))
        result = dot3((v_ref[0:NZ, :], v_ref[NZ : 2 * NZ, :]), values) * scale
        result = result.astype(BF16).astype(F32)
        pot[0:NZ, :] = result
        pot[NZ:ZROWS, :] = result[0:8, :]
        for block in range(4):
            low = 32 * block + 8 * plane
            turned = pltpu.roll(result[block * LANES : (block + 1) * LANES, :], low + 2, 1)
            edge = jnp.where((lane >= low) & (lane < low + 4), turned, edge)
    edge_ref[...] = edge.astype(BF16)


def widen_edge(edge_ref, wide_ref):
    for block in range(4):
        wide_ref[block * LANES : (block + 1) * LANES, :] = pltpu.roll(
            edge_ref[...].astype(F32), (LANES - 32 * block) % LANES, 1
        )
    wide_ref[NZ:ZROWS, :] = wide_ref[0:8, :]


def masked(values, live):
    return jnp.where(lane_of(values.shape) < live, values, 0.0)


def own_sample_kernel(facts_ref, p0, p1, p2, p3, edge_ref, kinds_ref, stk_ref, out_ref, wide_ref, sp_ref):
    widen_edge(edge_ref, wide_ref)
    live = facts_ref[3, 0]
    slots = kinds_ref.shape[1]
    sample_columns((p0, p1, p2, p3), wide_ref, place_in_facts(facts_ref), live, sp_ref, 0, (0, 1, 2, 3), 2)

    @pl.when(live > LANES)
    def _():
        out_ref[...] = masked(far_sums(sp_ref, kinds_ref[2:3, :], stk_ref, 0), live)

    @pl.when(live <= LANES)
    def _():
        out_ref[:, 0:LANES] = masked(far_sums(sp_ref, kinds_ref[2:3, 0:LANES], stk_ref, 0), live)
        out_ref[:, LANES:slots] = jnp.zeros((PANELS, slots - LANES), F32)


def beside_sample_kernel(odd_ref, facts_ref, p0, p1, p2, p3, edge_ref, kinds_ref, stk_ref, out0, out1, wide_ref, sp_ref):
    widen_edge(edge_ref, wide_ref)
    slots = kinds_ref.shape[1] // 2
    outs = (out0, out1)
    for first, counts in chunks_beside(facts_ref, slots):
        here = slice(first, first + LANES)
        for side, (planes, shift_i) in enumerate(BESIDE):
            sample_columns((p0, p1, p2, p3), wide_ref, place_in_facts(facts_ref, side * slots + first),
                           counts[side], sp_ref, 2 * first + side * LANES, planes, shift_i)

        @pl.when(counts[0] + counts[1] > 0)
        def _(first=first, counts=counts, here=here):
            kinds = both_sides(kinds_ref.at[2:3, :], slots, first)
            result = far_sums(sp_ref, kinds, stk_ref, 2 * first)
            sums = [masked(result[:, side * LANES : (side + 1) * LANES], counts[side]) for side in range(2)]
            even = jnp.broadcast_to(odd_ref[0], sums[0].shape) == 0
            out0[:, here] = jnp.where(even, sums[1], sums[0])
            out1[:, here] = jnp.where(even, sums[0], sums[1])

        @pl.when(counts[0] + counts[1] <= 0)
        def _(here=here):
            for out in outs:
                out[:, here] = jnp.zeros((PANELS, LANES), F32)


def near_kernel(live_ref, here_ref, there_ref, source_ref, block_ref, table_ref, out_ref):
    live = live_ref[0]
    fanout, slots = source_ref.shape
    height = here_ref.shape[0] // 3
    pool = jnp.concatenate(
        [ref[step * height : step * height + PANELS, :] for step in range(3) for ref in (here_ref, there_ref)],
        axis=1,
    )
    total = pool.shape[1]
    for first in range(0, slots, LANES):
        where = slice(first, first + LANES)

        @pl.when(live > first)
        def _(where=where, first=first):
            index = lax.broadcasted_iota(jnp.int32, (total, LANES), 0)
            result = jnp.zeros((PANELS, LANES), F32)
            for j in range(fanout):
                chosen = jnp.where(index == source_ref[j : j + 1, where], 1.0, 0.0).astype(BF16)
                gathered = dot(pool, chosen)
                result += dot(
                    table_ref[...], by_kind(gathered, block_ref[j : j + 1, where]).astype(BF16)
                )
            column = first + lane_of((PANELS, LANES))
            out_ref[:, where] = jnp.where(column < live, result, 0.0)

        @pl.when(live <= first)
        def _(where=where):
            out_ref[:, where] = jnp.zeros((PANELS, LANES), F32)


def shape_of(*dims, dtype=F32):
    return jax.ShapeDtypeStruct(dims, dtype)


def body(slabs, tiles, charges, live_count, slot_brick, slot_stencil, stencils, near_source,
         near_block, near_blocks, kernel_hat):
    slots = charges.shape[1]
    owners = slabs * tiles
    planes = kernel_hat.shape[0] // 2
    length = kernel_hat.shape[1]
    parts = NZ // owners
    axes = ("tile", "slab")
    both = ("slab", "tile")

    def moved(values, step_of, swap=0):
        pairs = [
            (a * tiles + b, (a + step_of(a)) % slabs * tiles + (b + swap) % tiles)
            for a in range(slabs)
            for b in range(tiles)
        ]
        return lax.ppermute(values, both, pairs)

    def to_first(values):
        return moved(values, lambda a: 1 - 2 * (a % 2))

    def to_second(values):
        return moved(values, lambda a: 2 * (a % 2) - 1)

    def to_other_tile(values):
        return moved(values, lambda a: 0, 1)

    odd = (lax.axis_index("slab") % 2)[None]
    row = lax.broadcasted_iota(jnp.int32, (PANELS + 16, slots), 0)
    column = lax.broadcasted_iota(jnp.int32, (PANELS + 16, slots), 1)
    live = jnp.broadcast_to(live_count[0], row.shape)
    brick = jnp.broadcast_to(slot_brick[None, :], row.shape)
    facts = jnp.where(row == PANELS, lax.shift_right_logical(brick, 7), brick & (NZ // 4 - 1))
    facts = jnp.where(row == PANELS + 2, slot_stencil[None, :], jnp.where(row == PANELS + 3, live, facts))
    held = jnp.where(column < live, jnp.pad(charges, ((0, 16), (0, 0))), jnp.zeros((), BF16))
    packed = jnp.where(row < PANELS, held, facts.astype(BF16))
    from_second = to_second(packed)
    from_first = to_first(packed)

    grid = shape_of(ZROWS, LANES)
    *grids, stk, facts = pl.pallas_call(
        own_kernel,
        out_shape=(grid,) * 5 + (shape_of(KS * PANELS, POINTS, dtype=BF16), shape_of(8, slots, dtype=jnp.int32)),
        in_specs=[VMEM, pl.BlockSpec(memory_space=pl.ANY)],
        out_specs=(VMEM,) * 7,
        scratch_shapes=[
            pltpu.VMEM((slots * 8, LANES), F32),
            pltpu.VMEM((KS * PANELS, POINTS), BF16),
            pltpu.SMEM((8, slots), jnp.int32),
            pltpu.SemaphoreType.DMA((2,)),
        ],
        compiler_params=PARAMS,
        name="own_scatter",
    )(packed, stencils.reshape(KS * PANELS, POINTS))

    g = pl.pallas_call(
        beside_kernel,
        out_shape=(grid,) * 5
        + (
            shape_of(LANES, LANES),
            shape_of(8, 2 * slots, dtype=jnp.int32),
            shape_of(3 * (PANELS + 16), slots, dtype=BF16),
        ),
        in_specs=[SMEM] + [VMEM] * 9,
        out_specs=(VMEM,) * 8,
        scratch_shapes=[
            pltpu.VMEM((2 * slots * 8, LANES), F32),
            pltpu.SMEM((8, 2 * slots), jnp.int32),
            pltpu.SemaphoreType.DMA,
        ],
        input_output_aliases={5: 0, 6: 1, 7: 2, 8: 3, 9: 4},
        compiler_params=PARAMS,
        name="beside_scatter",
    )(odd, packed, from_first, from_second, stk, *grids)
    facts2 = g[6]
    edge = to_other_tile(g[5])

    forward, inverse = z_tables(slabs, tiles)
    rows = owners * (4 * parts + SCALE_ROWS)
    sent = pl.pallas_call(
        functools.partial(z_kernel, owners),
        out_shape=shape_of(rows, LANES),
        in_specs=[VMEM] * 6,
        out_specs=VMEM,
        compiler_params=PARAMS,
        name="z_forward",
    )(*g[:4], edge, jnp.asarray(halves(forward)))

    def exchanged(values):
        values = values.astype(jnp.float16).reshape(owners, -1, LANES)
        values = lax.all_to_all(values, axes, 0, 0, tiled=True)
        return values

    def widened(values):
        return values.astype(F32).reshape(-1, LANES)

    hat, sent = lax.optimization_barrier((kernel_hat, sent))
    got = exchanged(sent)
    me = lax.axis_index("slab") * tiles + lax.axis_index("tile")
    offset = (me >= owners // 2).astype(jnp.int32)[None]
    hat = pl.pallas_call(
        functools.partial(hat_kernel, planes),
        out_shape=shape_of(planes, length, NY),
        in_specs=[SMEM] + [VMEM] * 2,
        out_specs=VMEM,
        compiler_params=PARAMS,
        name="hat_order",
    )(offset, hat, jnp.asarray(reversal()))

    got, hat = lax.optimization_barrier((got, hat))
    pool = (g[7], to_other_tile(g[7]))
    direction = near_source // slots
    pool_index = (direction // 3 * 2 + (direction % 3 != 1).astype(jnp.int32)) * slots + near_source % slots
    near = pl.pallas_call(
        near_kernel,
        out_shape=shape_of(PANELS, slots),
        in_specs=[SMEM] + [VMEM] * 5,
        out_specs=VMEM,
        compiler_params=PARAMS,
        name="near_field",
    )(live_count, *pool, pool_index.T, near_block.T, near_blocks.reshape(PANELS, KN * PANELS))

    back, exponent = pl.pallas_call(
        functools.partial(plane_kernel, slabs, planes),
        out_shape=(shape_of(owners * 4 * parts, LANES), shape_of(8, LANES)),
        in_specs=[VMEM] * 4,
        out_specs=(VMEM, VMEM),
        scratch_shapes=[pltpu.VMEM((2 * planes * length, NY), BF16)] * 2,
        compiler_params=PARAMS,
        name="plane_filter",
    )(widened(got), hat, jnp.asarray(halves(y_table(), y_table().T)), jnp.asarray(halves(*x_tables(slabs))))
    back, near = lax.optimization_barrier((exchanged(back), near))

    pot = pl.pallas_call(
        functools.partial(potential_kernel, owners),
        out_shape=(grid,) * 4 + (shape_of(LANES, LANES, dtype=BF16),),
        in_specs=[VMEM] * 3,
        out_specs=(VMEM,) * 5,
        compiler_params=PARAMS,
        name="z_inverse",
    )(widened(back), exponent, jnp.asarray(halves(inverse)))
    edge = to_other_tile(pot[4])

    def sample_scratch(width):
        return [pltpu.VMEM((ZROWS, LANES), F32), pltpu.VMEM((width * 8, LANES), F32)]

    sums = shape_of(PANELS, slots)
    others = pl.pallas_call(
        beside_sample_kernel,
        out_shape=(sums, sums),
        in_specs=[SMEM] * 2 + [VMEM] * 7,
        out_specs=(VMEM, VMEM),
        scratch_shapes=sample_scratch(2 * slots),
        compiler_params=PARAMS,
        name="beside_sample",
    )(odd, facts2, *pot[:4], edge, facts2, stk)
    second = to_second(others[1])
    first = to_first(others[0])
    own = pl.pallas_call(
        own_sample_kernel,
        out_shape=sums,
        in_specs=[SMEM] + [VMEM] * 7,
        out_specs=VMEM,
        scratch_shapes=sample_scratch(slots),
        compiler_params=PARAMS,
        name="own_sample",
    )(facts, *pot[:4], edge, facts, stk)
    return own + near + first + second


def solution(mesh):
    both = ("slab", "tile")
    in_specs = (
        P(None, both),
        P(both),
        P(both),
        P(both),
        P(),
        P(both, None),
        P(both, None),
        P(),
        P(both, None, None),
    )
    return jax.shard_map(
        functools.partial(body, mesh.shape["slab"], mesh.shape["tile"]),
        mesh=mesh,
        in_specs=in_specs,
        out_specs=P(None, both),
        check_vma=False,
    )
```

```python
import functools
import math

import jax
import jax.numpy as jnp
import ml_dtypes
import numpy as np
from jax import lax
from jax.experimental import pallas as pl
from jax.experimental.pallas import tpu as pltpu
from jax.sharding import PartitionSpec as P

PANELS = 64
POINTS = 512
NY = 256
NZ = 512
KS = 16
KN = 16
LANES = 128
ZROWS = NZ + 8
UNROLL = 16
HALF = NY // 2
SCALE_ROWS = 8
BOUND = 12.0
HEADROOM = 15.0
F32 = jnp.float32
BF16 = jnp.bfloat16
SMEM = pl.BlockSpec(memory_space=pltpu.SMEM)
VMEM = pl.BlockSpec(memory_space=pltpu.VMEM)
PARAMS = pltpu.CompilerParams(vmem_limit_bytes=48 * 1024 * 1024)


def halves(*tables):
    parts = []
    for table in tables:
        high = table.astype(ml_dtypes.bfloat16)
        parts += [high, (table - high.astype(np.float64)).astype(ml_dtypes.bfloat16)]
    return np.concatenate(parts, axis=0)


def owner_frequencies(slabs, tiles):
    devices = slabs * tiles
    planes = NZ // devices
    owner = np.array([a * tiles + b for b in range(tiles) for a in range(slabs)])
    plane = np.arange(planes // 2)
    return (owner[None, :] * planes + plane[:, None] + (owner[None, :] >= devices // 2)).reshape(-1)


def z_tables(slabs, tiles):
    freq = owner_frequencies(slabs, tiles)
    cell = np.arange(NZ) - 2
    angle = (freq[:, None] * cell[None, :] % NZ) * (2 * np.pi / NZ)
    forward = np.concatenate([np.cos(angle), -np.sin(angle)], axis=0)
    weight = np.where(freq % NZ == 0, 1.0, 2.0)[:, None] / NZ
    inverse = np.concatenate([weight * np.cos(angle), -weight * np.sin(angle)], axis=0).T
    return forward, inverse


def y_table():
    angle = (np.arange(NY)[:, None] * np.arange(HALF + 1)[None, :] % NY) * (2 * np.pi / NY)
    return np.concatenate([np.cos(angle[:, :HALF]), np.cos(angle[:, HALF:]), np.sin(angle[:, 1:HALF])], axis=1)


def reversal():
    table = np.zeros((HALF, HALF), ml_dtypes.bfloat16)
    lane = np.arange(HALF)
    table[lane, (HALF - lane) % HALF] = 1
    return table


def x_tables(slabs):
    length = 4 * slabs
    cell = (np.arange(4)[:, None] + 4 * np.arange(slabs)[None, :]).reshape(-1)
    angle = (np.arange(length)[:, None] * cell[None, :] % length) * (2 * np.pi / length)
    cosine, sine = np.cos(angle), np.sin(angle)
    forward = np.block([[cosine, sine], [-sine, cosine]])
    inverse = np.block([[cosine.T, -sine.T], [sine.T, cosine.T]])
    return forward, inverse


def split(values):
    high = values.astype(BF16)
    return high, (values - high.astype(F32)).astype(BF16)


def dot(a, b):
    return jnp.dot(a, b, preferred_element_type=F32)


def dot3(a, b):
    return dot(a[0], b[0]) + (dot(a[0], b[1]) + dot(a[1], b[0]))


def lane_of(shape):
    return lax.broadcasted_iota(jnp.int32, shape, 1)


def by_kind(values, kinds):
    zero = jnp.zeros_like(values)
    return jnp.concatenate(
        [jnp.where(kinds == kind, values, zero) for kind in range(KS)], axis=0
    )


def footprints(packed, stk_ref, fp_ref, first):
    count = packed.shape[1]
    turned = jnp.transpose(packed.astype(F32))
    kinds = turned[:, PANELS + 2 : PANELS + 3]
    charges = jnp.concatenate([turned[:, :PANELS], turned[:, :PANELS]], axis=1)
    offset = kinds - jnp.where(lane_of((count, LANES)) < PANELS, 0.0, 1.0)
    spread = jnp.concatenate(
        [jnp.where(offset == kind, charges, 0.0).astype(BF16) for kind in range(0, KS, 2)], axis=1
    )
    for pair in range(4):
        part = dot(spread, stk_ref[:, pair * LANES : (pair + 1) * LANES])
        fp_ref[pl.ds(first * 8 + 2 * pair, count, stride=8), :] = part
        fp_ref[pl.ds(first * 8 + 2 * pair + 1, count, stride=8), :] = pltpu.roll(part, 64, 1)


def lane_in(plane, shape):
    return (lane_of(shape) - 8 * plane) & (LANES - 1)


def edge_codes(planes, shape):
    code = jnp.full(shape, 3, jnp.int32)
    for plane in planes:
        lane = lane_in(plane, shape)
        code = jnp.where(lane >= LANES - 2, 0, jnp.where(lane < 2, 1, code))
    return code


def edge_of(by):
    return jnp.where(by == 0, 0, jnp.where(by == NY // 8 - 1, 1, 2))


def scatter_columns(fp_ref, first, place_of, count, grids, edge_ref, planes, shift_i):
    shape = (8, LANES)
    lanes = [lane_in(plane, shape) for plane in planes]
    codes = edge_codes(planes, shape)

    def step(index, carry):
        updates = []
        for inner in range(UNROLL):
            column = index * UNROLL + inner
            by, bz = place_of(column)
            value = fp_ref[pl.ds(pl.multiple_of((first + column) * 8, 8), 8), :]
            begin = 4 * by - 2
            turned = pltpu.roll(value, (begin - 8 * shift_i) & (LANES - 1), 1)
            terms = [jnp.where(((lane - begin) & -8) == 0, turned, 0.0) for lane in lanes]
            terms.append(jnp.where(codes == edge_of(by), turned, 0.0))
            updates.append((pl.ds(4 * bz, 8), terms))
        refs = [grids[plane] for plane in planes] + [edge_ref]
        for where, terms in updates:
            sums = [ref[where, :] + term for ref, term in zip(refs, terms)]
            for ref, total in zip(refs, sums):
                ref[where, :] = total
        return carry

    lax.fori_loop(0, lax.shift_right_logical(count + UNROLL - 1, 4), step, 0)


def sample_columns(pot_refs, edge_ref, place_of, count, sp_ref, first, planes, shift_i):
    shape = (8, LANES)
    lanes = [lane_in(plane, shape) for plane in planes]
    codes = edge_codes(planes, shape)

    def step(index, carry):
        results = []
        for inner in range(UNROLL):
            column = index * UNROLL + inner
            by, bz = place_of(column)
            where = pl.ds(4 * bz, 8)
            begin = 4 * by - 2
            result = jnp.where(codes == edge_of(by), edge_ref[where, :], 0.0)
            for plane, lane in zip(planes, lanes):
                result = jnp.where(((lane - begin) & -8) == 0, pot_refs[plane][where, :], result)
            turned = pltpu.roll(result, (8 * shift_i - begin) & (LANES - 1), 1)
            results.append((pl.ds(pl.multiple_of((first + column) * 8, 8), 8), turned))
        for where, result in results:
            sp_ref[where, :] = result
        return carry

    lax.fori_loop(0, lax.shift_right_logical(count + UNROLL - 1, 4), step, 0)


def far_sums(sp_ref, kinds, stk_ref, first):
    count = kinds.shape[1]
    lane = lane_of((count, LANES))
    pairs = []
    for pair in range(4):
        even = sp_ref[pl.ds(first * 8 + 2 * pair, count, stride=8), :]
        odd = sp_ref[pl.ds(first * 8 + 2 * pair + 1, count, stride=8), :]
        pairs.append(jnp.where(lane < 64, even, pltpu.roll(odd, 64, 1)).astype(BF16))
    samples = jnp.concatenate(pairs, axis=1)
    sums = lax.dot_general(
        stk_ref[...], samples, (((1,), (1,)), ((), ())), preferred_element_type=F32
    )
    result = jnp.zeros((PANELS, count), F32)
    for kind in range(KS):
        result += jnp.where(kinds == kind, sums[kind * PANELS : (kind + 1) * PANELS, :], 0.0)
    return result


def place_in_facts(facts_ref, start=0):
    return lambda column: (facts_ref[0, start + column], facts_ref[1, start + column])


def facts_of(packed_ref, row):
    return packed_ref[row : row + 16, :].astype(F32).astype(jnp.int32)[0:8, :]


def own_kernel(packed_ref, stencil_ref,
               g0, g1, g2, g3, edge_ref, stk_ref, out_facts, fp_ref, rows_ref, facts_ref, sems):
    copy = pltpu.make_async_copy(stencil_ref, rows_ref, sems.at[0])
    copy.start()
    out_facts[...] = facts_of(packed_ref, PANELS)
    facts_copy = pltpu.make_async_copy(out_facts, facts_ref, sems.at[1])
    facts_copy.start()
    for ref in (g0, g1, g2, g3, edge_ref):
        ref[...] = jnp.zeros_like(ref)
    shape = (POINTS, POINTS)
    point = lax.broadcasted_iota(jnp.int32, shape, 0)
    target = (point & 7) * 64 + lax.shift_right_logical(point, 3)
    order = jnp.where(lane_of(shape) == target, 1.0, 0.0).astype(BF16)
    facts_copy.wait()
    copy.wait()
    stk_ref[...] = dot(rows_ref[...], order).astype(BF16)
    live = facts_ref[3, 0]

    @pl.when(live > LANES)
    def _():
        footprints(packed_ref[...], stk_ref, fp_ref, 0)

    @pl.when(live <= LANES)
    def _():
        footprints(packed_ref[:, 0:LANES], stk_ref, fp_ref, 0)

    scatter_columns(fp_ref, 0, place_in_facts(facts_ref), live, (g0, g1, g2, g3), edge_ref, (0, 1, 2, 3), 2)


BESIDE = (((0, 1), 6), ((2, 3), -2))


def chunks_beside(facts_ref, slots):
    for first in range(0, slots, LANES):
        counts = [jnp.clip(facts_ref[3, side * slots] - first, 0, LANES) for side in range(2)]
        yield first, counts


def both_sides(ref, slots, first):
    return jnp.concatenate(
        [ref[:, side * slots + first : side * slots + first + LANES] for side in range(2)], axis=1
    )


def beside_kernel(odd_ref, own_ref, first_ref, second_ref, stk_ref, i0, i1, i2, i3, iedge,
                  g0, g1, g2, g3, edge_ref, out_edge, out_facts, pool_ref, fp_ref, facts_ref, sem):
    height, slots = own_ref.shape
    before, after = pl.ds(0, height), pl.ds(2 * height, height)
    pool_ref[height : 2 * height, :] = own_ref[...]

    @pl.when(odd_ref[0] == 0)
    def _():
        pool_ref[after, :] = first_ref[...]
        pool_ref[before, :] = second_ref[...]

    @pl.when(odd_ref[0] != 0)
    def _():
        pool_ref[before, :] = first_ref[...]
        pool_ref[after, :] = second_ref[...]

    for side in range(2):
        out_facts[:, side * slots : (side + 1) * slots] = facts_of(pool_ref, 2 * side * height + PANELS)
    copy = pltpu.make_async_copy(out_facts, facts_ref, sem)
    copy.start()

    def project(first):
        here = slice(first, first + LANES)
        packed = jnp.concatenate(
            [pool_ref[0:height, here], pool_ref[2 * height : 3 * height, here]], axis=1
        )
        footprints(packed, stk_ref, fp_ref, 2 * first)

    project(0)
    copy.wait()
    for first, counts in chunks_beside(facts_ref, slots):
        if first:
            @pl.when(counts[0] + counts[1] > 0)
            def _(first=first):
                project(first)

        for side, (planes, shift_i) in enumerate(BESIDE):
            scatter_columns(fp_ref, 2 * first + side * LANES, place_in_facts(facts_ref, side * slots + first),
                            counts[side], (g0, g1, g2, g3), edge_ref, planes, shift_i)
    edge_ref[0:8, :] += edge_ref[NZ:ZROWS, :]
    total = pltpu.roll(edge_ref[0:LANES, :], 2, 1)
    for block in range(1, 4):
        total += pltpu.roll(edge_ref[block * LANES : (block + 1) * LANES, :], 32 * block + 2, 1)
    out_edge[...] = total


def exponent_of(values):
    top = functools.reduce(jnp.maximum, [jnp.max(jnp.abs(v), axis=0, keepdims=True) for v in values])
    top = jnp.maximum(jnp.max(top, axis=1, keepdims=True), 2.0**-100)
    return jnp.ceil(jnp.log2(top)) - BOUND


def z_kernel(owners, g0, g1, g2, g3, edge_ref, w_ref, out_ref):
    shape = (LANES, LANES)
    parts = NZ // owners
    stride = 4 * parts + SCALE_ROWS
    edges = [pltpu.roll(edge_ref[...], (LANES - 2 - 32 * block) % LANES, 1) for block in range(4)]
    results = []
    for plane, grid in enumerate((g0, g1, g2, g3)):
        at_edge = edge_codes((plane,), shape) < 2
        blocks = [
            grid[block * LANES : (block + 1) * LANES, :] + jnp.where(at_edge, edges[block], 0.0)
            for block in range(4)
        ]
        blocks[0] = jnp.concatenate([blocks[0][0:8] + grid[NZ:ZROWS, :], blocks[0][8:]], axis=0)
        values = jnp.concatenate(blocks, axis=0)
        if plane:
            values = pltpu.roll(values, LANES - 8 * plane, 1)
        results.append(dot3((w_ref[0:NZ, :], w_ref[NZ : 2 * NZ, :]), split(values)))
    exponent = exponent_of(results)
    scale = jnp.exp2(-exponent)
    for plane, result in enumerate(results):
        result = result * scale
        for part in range(parts):
            out_ref[pl.ds(plane * parts + part, owners, stride=stride), :] = result[
                part * owners : (part + 1) * owners, :
            ]
    for row in range(SCALE_ROWS):
        out_ref[pl.ds(4 * parts + row, owners, stride=stride), :] = jnp.broadcast_to(
            exponent, (owners, LANES)
        )


def hat_kernel(planes, offset_ref, hat_ref, turn_ref, out_ref):
    length = hat_ref.shape[1]
    values = jnp.concatenate([hat_ref[offset_ref[0] + plane] for plane in range(planes)], axis=0)
    values = values * (1.0 / (length * NY))
    upper = values[:, HALF:]
    high, low = split(upper)
    rest = (upper - high.astype(F32) - low.astype(F32)).astype(BF16)
    turn = turn_ref[...]
    upper = dot(high, turn) + (dot(low, turn) + dot(rest, turn))
    for plane in range(planes):
        here = slice(plane * length, (plane + 1) * length)
        out_ref[plane] = jnp.concatenate([values[here, :HALF], upper[here, :]], axis=1)


def plane_kernel(slabs, planes, in_ref, hat_ref, y_ref, x_ref, out_ref, exponent_ref, ah_ref, al_ref):
    length = 4 * slabs
    rows = planes * length
    parts = 2 * planes
    stride = 4 * parts + SCALE_ROWS

    def pieces():
        for tile in range(2):
            for part in range(2):
                for xi in range(4):
                    for plane in range(planes):
                        yield tile, part, plane, xi

    scales = [
        jnp.exp2(in_ref[pl.ds(tile * slabs * stride + 4 * parts, slabs, stride=stride), :])
        for tile in range(2)
    ]
    for tile, part, plane, xi in pieces():
        start = tile * slabs * stride + xi * parts + part * planes + plane
        row = (part * planes + plane) * length + xi * slabs
        high, low = split(in_ref[pl.ds(start, slabs, stride=stride), :] * scales[tile])
        ah_ref[row : row + slabs, tile * LANES : (tile + 1) * LANES] = high
        al_ref[row : row + slabs, tile * LANES : (tile + 1) * LANES] = low
    first_lane = lane_of((rows, HALF)) == 0
    turned = dot3((ah_ref[...], al_ref[...]), (y_ref[0:NY, :], y_ref[NY : 2 * NY, :]))
    even = (turned[:rows, :HALF], turned[rows:, :HALF])
    odd = (turned[:rows, HALF:], turned[rows:, HALF:])
    zero_odd = [jnp.where(first_lane, 0.0, values) for values in odd]
    real = jnp.concatenate(
        [even[0] + zero_odd[1], jnp.where(first_lane, odd[0], even[0] - zero_odd[1])], axis=1
    )
    imag = jnp.concatenate(
        [even[1] - zero_odd[0], jnp.where(first_lane, odd[1], even[1] + zero_odd[0])], axis=1
    )
    size = 2 * length
    forward = (x_ref[0:size, :], x_ref[size : 2 * size, :])
    inverse = (x_ref[2 * size : 3 * size, :], x_ref[3 * size : 4 * size, :])
    for plane in range(planes):
        here = slice(plane * length, (plane + 1) * length)
        there = slice(rows + plane * length, rows + (plane + 1) * length)
        values = dot3(forward, split(jnp.concatenate([real[here], imag[here]], axis=0)))
        values = values * jnp.concatenate([hat_ref[plane], hat_ref[plane]], axis=0)
        values = dot3(inverse, split(values))
        low, high = values[:, :HALF], values[:, HALF:]
        lane = first_lane[:length]
        even_r = jnp.where(lane, low[:length], low[:length] + high[:length])
        even_i = jnp.where(lane, low[length:], low[length:] + high[length:])
        odd_r = jnp.where(lane, high[:length], high[length:] - low[length:])
        odd_i = jnp.where(lane, high[length:], low[:length] - high[:length])
        ah_ref[here, :], al_ref[here, :] = split(jnp.concatenate([even_r, odd_r], axis=1))
        ah_ref[there, :], al_ref[there, :] = split(jnp.concatenate([even_i, odd_i], axis=1))
    turned = dot3((ah_ref[...], al_ref[...]), (y_ref[2 * NY : 3 * NY, :], y_ref[3 * NY : 4 * NY, :]))
    tops = [
        jnp.max(in_ref[pl.ds(tile * slabs * stride + 4 * parts, slabs, stride=stride), :], axis=0, keepdims=True)
        for tile in range(2)
    ]
    exponent = jnp.broadcast_to(jnp.maximum(*tops) + BOUND - HEADROOM + math.ceil(math.log2(length * NY) / 2), (8, LANES))
    exponent_ref[...] = exponent
    scale = jnp.exp2(-exponent[0:1, 0:1])
    for tile, part, plane, xi in pieces():
        here = slice((part * planes + plane) * length + xi * slabs, (part * planes + plane) * length + (xi + 1) * slabs)
        start = tile * slabs * 4 * parts + xi * parts + part * planes + plane
        out_ref[pl.ds(start, slabs, stride=4 * parts), :] = (
            turned[here, tile * LANES : (tile + 1) * LANES] * scale
        )


def potential_kernel(owners, in_ref, exponent_ref, v_ref, p0, p1, p2, p3, edge_ref):
    parts = NZ // owners
    shape = (LANES, LANES)
    edges = [jnp.zeros(shape, F32)] * 4
    scale = jnp.exp2(exponent_ref[0:1, 0:1])
    for plane, pot in enumerate((p0, p1, p2, p3)):
        values = split(jnp.concatenate(
            [in_ref[pl.ds(plane * parts + part, owners, stride=4 * parts), :] for part in range(parts)],
            axis=0,
        ))
        result = dot3((v_ref[0:NZ, :], v_ref[NZ : 2 * NZ, :]), values) * scale
        result = result.astype(BF16).astype(F32)
        if plane:
            result = pltpu.roll(result, 8 * plane, 1)
        pot[0:NZ, :] = result
        pot[NZ:ZROWS, :] = result[0:8, :]
        at_edge = edge_codes((plane,), shape) < 2
        edges = [
            jnp.where(at_edge, result[block * LANES : (block + 1) * LANES, :], edge)
            for block, edge in enumerate(edges)
        ]
    edge = pltpu.roll(edges[0], 2, 1)
    for block in range(1, 4):
        edge += pltpu.roll(edges[block], 32 * block + 2, 1)
    edge_ref[...] = edge.astype(BF16)


def widen_edge(edge_ref, wide_ref):
    for block in range(4):
        wide_ref[block * LANES : (block + 1) * LANES, :] = pltpu.roll(
            edge_ref[...].astype(F32), (LANES - 2 - 32 * block) % LANES, 1
        )
    wide_ref[NZ:ZROWS, :] = wide_ref[0:8, :]


def masked(values, live):
    return jnp.where(lane_of(values.shape) < live, values, 0.0)


def own_sample_kernel(facts_ref, p0, p1, p2, p3, edge_ref, kinds_ref, stk_ref, out_ref, wide_ref, sp_ref):
    widen_edge(edge_ref, wide_ref)
    live = facts_ref[3, 0]
    slots = kinds_ref.shape[1]
    sample_columns((p0, p1, p2, p3), wide_ref, place_in_facts(facts_ref), live, sp_ref, 0, (0, 1, 2, 3), 2)

    @pl.when(live > LANES)
    def _():
        out_ref[...] = masked(far_sums(sp_ref, kinds_ref[2:3, :], stk_ref, 0), live)

    @pl.when(live <= LANES)
    def _():
        out_ref[:, 0:LANES] = masked(far_sums(sp_ref, kinds_ref[2:3, 0:LANES], stk_ref, 0), live)
        out_ref[:, LANES:slots] = jnp.zeros((PANELS, slots - LANES), F32)


def beside_sample_kernel(odd_ref, facts_ref, p0, p1, p2, p3, edge_ref, kinds_ref, stk_ref, out0, out1, wide_ref, sp_ref):
    widen_edge(edge_ref, wide_ref)
    slots = kinds_ref.shape[1] // 2
    outs = (out0, out1)
    for first, counts in chunks_beside(facts_ref, slots):
        here = slice(first, first + LANES)
        for side, (planes, shift_i) in enumerate(BESIDE):
            sample_columns((p0, p1, p2, p3), wide_ref, place_in_facts(facts_ref, side * slots + first),
                           counts[side], sp_ref, 2 * first + side * LANES, planes, shift_i)

        @pl.when(counts[0] + counts[1] > 0)
        def _(first=first, counts=counts, here=here):
            kinds = both_sides(kinds_ref.at[2:3, :], slots, first)
            result = far_sums(sp_ref, kinds, stk_ref, 2 * first)
            sums = [masked(result[:, side * LANES : (side + 1) * LANES], counts[side]) for side in range(2)]
            even = jnp.broadcast_to(odd_ref[0], sums[0].shape) == 0
            out0[:, here] = jnp.where(even, sums[1], sums[0])
            out1[:, here] = jnp.where(even, sums[0], sums[1])

        @pl.when(counts[0] + counts[1] <= 0)
        def _(here=here):
            for out in outs:
                out[:, here] = jnp.zeros((PANELS, LANES), F32)


def near_kernel(live_ref, here_ref, there_ref, source_ref, block_ref, table_ref, out_ref):
    live = live_ref[0]
    fanout, slots = source_ref.shape
    height = here_ref.shape[0] // 3
    pool = jnp.concatenate(
        [ref[step * height : step * height + PANELS, :] for step in range(3) for ref in (here_ref, there_ref)],
        axis=1,
    )
    total = pool.shape[1]
    for first in range(0, slots, LANES):
        where = slice(first, first + LANES)

        @pl.when(live > first)
        def _(where=where, first=first):
            index = lax.broadcasted_iota(jnp.int32, (total, LANES), 0)
            result = jnp.zeros((PANELS, LANES), F32)
            for j in range(fanout):
                chosen = jnp.where(index == source_ref[j : j + 1, where], 1.0, 0.0).astype(BF16)
                gathered = dot(pool, chosen)
                result += dot(
                    table_ref[...], by_kind(gathered, block_ref[j : j + 1, where]).astype(BF16)
                )
            column = first + lane_of((PANELS, LANES))
            out_ref[:, where] = jnp.where(column < live, result, 0.0)

        @pl.when(live <= first)
        def _(where=where):
            out_ref[:, where] = jnp.zeros((PANELS, LANES), F32)


def shape_of(*dims, dtype=F32):
    return jax.ShapeDtypeStruct(dims, dtype)


def body(slabs, tiles, charges, live_count, slot_brick, slot_stencil, stencils, near_source,
         near_block, near_blocks, kernel_hat):
    slots = charges.shape[1]
    owners = slabs * tiles
    planes = kernel_hat.shape[0] // 2
    length = kernel_hat.shape[1]
    parts = NZ // owners
    axes = ("tile", "slab")
    both = ("slab", "tile")

    def moved(values, step_of, swap=0):
        pairs = [
            (a * tiles + b, (a + step_of(a)) % slabs * tiles + (b + swap) % tiles)
            for a in range(slabs)
            for b in range(tiles)
        ]
        return lax.ppermute(values, both, pairs)

    def to_first(values):
        return moved(values, lambda a: 1 - 2 * (a % 2))

    def to_second(values):
        return moved(values, lambda a: 2 * (a % 2) - 1)

    def to_other_tile(values):
        return moved(values, lambda a: 0, 1)

    odd = (lax.axis_index("slab") % 2)[None]
    row = lax.broadcasted_iota(jnp.int32, (PANELS + 16, slots), 0)
    column = lax.broadcasted_iota(jnp.int32, (PANELS + 16, slots), 1)
    live = jnp.broadcast_to(live_count[0], row.shape)
    brick = jnp.broadcast_to(slot_brick[None, :], row.shape)
    facts = jnp.where(row == PANELS, lax.shift_right_logical(brick, 7), brick & (NZ // 4 - 1))
    facts = jnp.where(row == PANELS + 2, slot_stencil[None, :], jnp.where(row == PANELS + 3, live, facts))
    held = jnp.where(column < live, jnp.pad(charges, ((0, 16), (0, 0))), jnp.zeros((), BF16))
    packed = jnp.where(row < PANELS, held, facts.astype(BF16))
    from_second = to_second(packed)
    from_first = to_first(packed)

    grid = shape_of(ZROWS, LANES)
    *grids, stk, facts = pl.pallas_call(
        own_kernel,
        out_shape=(grid,) * 5 + (shape_of(KS * PANELS, POINTS, dtype=BF16), shape_of(8, slots, dtype=jnp.int32)),
        in_specs=[VMEM, pl.BlockSpec(memory_space=pl.ANY)],
        out_specs=(VMEM,) * 7,
        scratch_shapes=[
            pltpu.VMEM((slots * 8, LANES), F32),
            pltpu.VMEM((KS * PANELS, POINTS), BF16),
            pltpu.SMEM((8, slots), jnp.int32),
            pltpu.SemaphoreType.DMA((2,)),
        ],
        compiler_params=PARAMS,
        name="own_scatter",
    )(packed, stencils.reshape(KS * PANELS, POINTS))

    g = pl.pallas_call(
        beside_kernel,
        out_shape=(grid,) * 5
        + (
            shape_of(LANES, LANES),
            shape_of(8, 2 * slots, dtype=jnp.int32),
            shape_of(3 * (PANELS + 16), slots, dtype=BF16),
        ),
        in_specs=[SMEM] + [VMEM] * 9,
        out_specs=(VMEM,) * 8,
        scratch_shapes=[
            pltpu.VMEM((2 * slots * 8, LANES), F32),
            pltpu.SMEM((8, 2 * slots), jnp.int32),
            pltpu.SemaphoreType.DMA,
        ],
        input_output_aliases={5: 0, 6: 1, 7: 2, 8: 3, 9: 4},
        compiler_params=PARAMS,
        name="beside_scatter",
    )(odd, packed, from_first, from_second, stk, *grids)
    facts2 = g[6]
    edge = to_other_tile(g[5])

    forward, inverse = z_tables(slabs, tiles)
    rows = owners * (4 * parts + SCALE_ROWS)
    sent = pl.pallas_call(
        functools.partial(z_kernel, owners),
        out_shape=shape_of(rows, LANES),
        in_specs=[VMEM] * 6,
        out_specs=VMEM,
        compiler_params=PARAMS,
        name="z_forward",
    )(*g[:4], edge, jnp.asarray(halves(forward)))

    def exchanged(values):
        values = values.astype(jnp.float16).reshape(owners, -1, LANES)
        values = lax.all_to_all(values, axes, 0, 0, tiled=True)
        return values

    def widened(values):
        return values.astype(F32).reshape(-1, LANES)

    hat, sent = lax.optimization_barrier((kernel_hat, sent))
    got = exchanged(sent)
    me = lax.axis_index("slab") * tiles + lax.axis_index("tile")
    offset = (me >= owners // 2).astype(jnp.int32)[None]
    hat = pl.pallas_call(
        functools.partial(hat_kernel, planes),
        out_shape=shape_of(planes, length, NY),
        in_specs=[SMEM] + [VMEM] * 2,
        out_specs=VMEM,
        compiler_params=PARAMS,
        name="hat_order",
    )(offset, hat, jnp.asarray(reversal()))

    got, hat = lax.optimization_barrier((got, hat))
    pool = (g[7], to_other_tile(g[7]))
    direction = near_source // slots
    pool_index = (direction // 3 * 2 + (direction % 3 != 1).astype(jnp.int32)) * slots + near_source % slots
    near = pl.pallas_call(
        near_kernel,
        out_shape=shape_of(PANELS, slots),
        in_specs=[SMEM] + [VMEM] * 5,
        out_specs=VMEM,
        compiler_params=PARAMS,
        name="near_field",
    )(live_count, *pool, pool_index.T, near_block.T, near_blocks.reshape(PANELS, KN * PANELS))

    back, exponent = pl.pallas_call(
        functools.partial(plane_kernel, slabs, planes),
        out_shape=(shape_of(owners * 4 * parts, LANES), shape_of(8, LANES)),
        in_specs=[VMEM] * 4,
        out_specs=(VMEM, VMEM),
        scratch_shapes=[pltpu.VMEM((2 * planes * length, NY), BF16)] * 2,
        compiler_params=PARAMS,
        name="plane_filter",
    )(widened(got), hat, jnp.asarray(halves(y_table(), y_table().T)), jnp.asarray(halves(*x_tables(slabs))))
    back, near = lax.optimization_barrier((exchanged(back), near))

    pot = pl.pallas_call(
        functools.partial(potential_kernel, owners),
        out_shape=(grid,) * 4 + (shape_of(LANES, LANES, dtype=BF16),),
        in_specs=[VMEM] * 3,
        out_specs=(VMEM,) * 5,
        compiler_params=PARAMS,
        name="z_inverse",
    )(widened(back), exponent, jnp.asarray(halves(inverse)))
    edge = to_other_tile(pot[4])

    def sample_scratch(width):
        return [pltpu.VMEM((ZROWS, LANES), F32), pltpu.VMEM((width * 8, LANES), F32)]

    sums = shape_of(PANELS, slots)
    others = pl.pallas_call(
        beside_sample_kernel,
        out_shape=(sums, sums),
        in_specs=[SMEM] * 2 + [VMEM] * 7,
        out_specs=(VMEM, VMEM),
        scratch_shapes=sample_scratch(2 * slots),
        compiler_params=PARAMS,
        name="beside_sample",
    )(odd, facts2, *pot[:4], edge, facts2, stk)
    second = to_second(others[1])
    first = to_first(others[0])
    own = pl.pallas_call(
        own_sample_kernel,
        out_shape=sums,
        in_specs=[SMEM] + [VMEM] * 7,
        out_specs=VMEM,
        scratch_shapes=sample_scratch(slots),
        compiler_params=PARAMS,
        name="own_sample",
    )(facts, *pot[:4], edge, facts, stk)
    return own + near + first + second


def solution(mesh):
    both = ("slab", "tile")
    in_specs = (
        P(None, both),
        P(both),
        P(both),
        P(both),
        P(),
        P(both, None),
        P(both, None),
        P(),
        P(both, None, None),
    )
    return jax.shard_map(
        functools.partial(body, mesh.shape["slab"], mesh.shape["tile"]),
        mesh=mesh,
        in_specs=in_specs,
        out_specs=P(None, both),
        check_vma=False,
    )
```

```python
import functools
import math

import jax
import jax.numpy as jnp
import ml_dtypes
import numpy as np
from jax import lax
from jax.experimental import pallas as pl
from jax.experimental.pallas import tpu as pltpu
from jax.sharding import PartitionSpec as P

PANELS = 64
POINTS = 512
NY = 256
NZ = 512
KS = 16
KN = 16
LANES = 128
ZROWS = NZ + 8
UNROLL = 16
HALF = NY // 2
SCALE_ROWS = 8
BOUND = 12.0
HEADROOM = 15.0
F32 = jnp.float32
BF16 = jnp.bfloat16
SMEM = pl.BlockSpec(memory_space=pltpu.SMEM)
VMEM = pl.BlockSpec(memory_space=pltpu.VMEM)
PARAMS = pltpu.CompilerParams(vmem_limit_bytes=48 * 1024 * 1024)


def halves(*tables):
    parts = []
    for table in tables:
        high = table.astype(ml_dtypes.bfloat16)
        parts += [high, (table - high.astype(np.float64)).astype(ml_dtypes.bfloat16)]
    return np.concatenate(parts, axis=0)


def z_tables(slabs, tiles):
    half = slabs // 2
    planes = NZ // (slabs * tiles) // 2
    plane = np.arange(planes + 1)[:, None, None]
    tile = np.arange(tiles)[None, :, None]
    slab = np.arange(half)[None, None, :]
    owner = slab * tiles + tile
    freq = (owner * 2 * planes + plane).reshape(-1)
    forward, inverse = [], []
    for parity in range(2):
        cell = np.arange(parity, NZ, 2) - 2
        angle = (freq[:, None] * cell[None, :] % NZ) * (2 * np.pi / NZ)
        forward.append(np.concatenate([np.cos(angle), -np.sin(angle)], axis=0))
        upper = (plane[:-1] + parity) % 2
        back = ((upper * half * tiles + owner) * 2 * planes + plane[:-1] + upper).reshape(-1)
        cell = np.arange(NZ // 2) - 2
        angle = (back[:, None] * cell[None, :] % NZ) * (2 * np.pi / NZ)
        weight = np.where(back == 0, 1.0, 2.0)[:, None] / NZ
        inverse.append(np.concatenate([weight * np.cos(angle), -weight * np.sin(angle)], axis=0).T)
    return forward, inverse


def y_table():
    angle = (np.arange(NY)[:, None] * np.arange(HALF + 1)[None, :] % NY) * (2 * np.pi / NY)
    return np.concatenate([np.cos(angle[:, :HALF]), np.cos(angle[:, HALF:]), np.sin(angle[:, 1:HALF])], axis=1)


def reversal():
    table = np.zeros((HALF, HALF), ml_dtypes.bfloat16)
    lane = np.arange(HALF)
    table[lane, (HALF - lane) % HALF] = 1
    return table


def x_tables(slabs):
    length = 4 * slabs
    cell = (np.arange(4)[:, None] + 4 * np.arange(slabs)[None, :]).reshape(-1)
    angle = (np.arange(length)[:, None] * cell[None, :] % length) * (2 * np.pi / length)
    cosine, sine = np.cos(angle), np.sin(angle)
    forward = np.block([[cosine, sine], [-sine, cosine]])
    inverse = np.block([[cosine.T, -sine.T], [sine.T, cosine.T]])
    return forward, inverse


def split(values):
    high = values.astype(BF16)
    return high, (values - high.astype(F32)).astype(BF16)


def dot(a, b):
    return jnp.dot(a, b, preferred_element_type=F32)


def dot3(a, b):
    return dot(a[0], b[0]) + (dot(a[0], b[1]) + dot(a[1], b[0]))


def lane_of(shape):
    return lax.broadcasted_iota(jnp.int32, shape, 1)


def by_kind(values, kinds):
    zero = jnp.zeros_like(values)
    return jnp.concatenate(
        [jnp.where(kinds == kind, values, zero) for kind in range(KS)], axis=0
    )


def footprints(packed, stk_ref, fp_ref, first):
    count = packed.shape[1]
    turned = jnp.transpose(packed.astype(F32))
    kinds = turned[:, PANELS + 2 : PANELS + 3]
    charges = jnp.concatenate([turned[:, :PANELS], turned[:, :PANELS]], axis=1)
    offset = kinds - jnp.where(lane_of((count, LANES)) < PANELS, 0.0, 1.0)
    spread = jnp.concatenate(
        [jnp.where(offset == kind, charges, 0.0).astype(BF16) for kind in range(0, KS, 2)], axis=1
    )
    for pair in range(4):
        part = dot(spread, stk_ref[:, pair * LANES : (pair + 1) * LANES])
        fp_ref[pl.ds(first * 8 + 2 * pair, count, stride=8), :] = part
        fp_ref[pl.ds(first * 8 + 2 * pair + 1, count, stride=8), :] = pltpu.roll(part, 64, 1)


def lane_in(plane, shape):
    return (lane_of(shape) - 8 * plane) & (LANES - 1)


def edge_codes(planes, shape):
    code = jnp.full(shape, 3, jnp.int32)
    for plane in planes:
        lane = lane_in(plane, shape)
        code = jnp.where(lane >= LANES - 2, 0, jnp.where(lane < 2, 1, code))
    return code


def edge_of(by):
    return jnp.where(by == 0, 0, jnp.where(by == NY // 8 - 1, 1, 2))


def scatter_columns(fp_ref, first, place_of, count, grids, edge_ref, planes, shift_i):
    shape = (8, LANES)
    lanes = [lane_in(plane, shape) for plane in planes]
    codes = edge_codes(planes, shape)

    def step(index, carry):
        updates = []
        for inner in range(UNROLL):
            column = index * UNROLL + inner
            by, bz = place_of(column)
            value = fp_ref[pl.ds(pl.multiple_of((first + column) * 8, 8), 8), :]
            begin = 4 * by - 2
            turned = pltpu.roll(value, (begin - 8 * shift_i) & (LANES - 1), 1)
            terms = [jnp.where(((lane - begin) & -8) == 0, turned, 0.0) for lane in lanes]
            terms.append(jnp.where(codes == edge_of(by), turned, 0.0))
            updates.append((pl.ds(4 * bz, 8), terms))
        refs = [grids[plane] for plane in planes] + [edge_ref]
        for where, terms in updates:
            sums = [ref[where, :] + term for ref, term in zip(refs, terms)]
            for ref, total in zip(refs, sums):
                ref[where, :] = total
        return carry

    lax.fori_loop(0, lax.shift_right_logical(count + UNROLL - 1, 4), step, 0)


def sample_columns(pot_refs, edge_ref, place_of, count, sp_ref, first, planes, shift_i):
    shape = (8, LANES)
    lanes = [lane_in(plane, shape) for plane in planes]
    codes = edge_codes(planes, shape)

    def step(index, carry):
        results = []
        for inner in range(UNROLL):
            column = index * UNROLL + inner
            by, bz = place_of(column)
            where = pl.ds(4 * bz, 8)
            begin = 4 * by - 2
            result = jnp.where(codes == edge_of(by), edge_ref[where, :], 0.0)
            for plane, lane in zip(planes, lanes):
                result = jnp.where(((lane - begin) & -8) == 0, pot_refs[plane][where, :], result)
            turned = pltpu.roll(result, (8 * shift_i - begin) & (LANES - 1), 1)
            results.append((pl.ds(pl.multiple_of((first + column) * 8, 8), 8), turned))
        for where, result in results:
            sp_ref[where, :] = result
        return carry

    lax.fori_loop(0, lax.shift_right_logical(count + UNROLL - 1, 4), step, 0)


def far_sums(sp_ref, kinds, stk_ref, first):
    count = kinds.shape[1]
    lane = lane_of((count, LANES))
    pairs = []
    for pair in range(4):
        even = sp_ref[pl.ds(first * 8 + 2 * pair, count, stride=8), :]
        odd = sp_ref[pl.ds(first * 8 + 2 * pair + 1, count, stride=8), :]
        pairs.append(jnp.where(lane < 64, even, pltpu.roll(odd, 64, 1)).astype(BF16))
    samples = jnp.concatenate(pairs, axis=1)
    sums = lax.dot_general(
        stk_ref[...], samples, (((1,), (1,)), ((), ())), preferred_element_type=F32
    )
    result = jnp.zeros((PANELS, count), F32)
    for kind in range(KS):
        result += jnp.where(kinds == kind, sums[kind * PANELS : (kind + 1) * PANELS, :], 0.0)
    return result


def place_in_facts(facts_ref, start=0):
    return lambda column: (facts_ref[0, start + column], facts_ref[1, start + column])


def facts_of(packed_ref, row):
    return packed_ref[row : row + 16, :].astype(F32).astype(jnp.int32)[0:8, :]


def own_kernel(packed_ref, stencil_ref,
               g0, g1, g2, g3, edge_ref, stk_ref, out_facts, fp_ref, rows_ref, facts_ref, sems):
    copy = pltpu.make_async_copy(stencil_ref, rows_ref, sems.at[0])
    copy.start()
    out_facts[...] = facts_of(packed_ref, PANELS)
    facts_copy = pltpu.make_async_copy(out_facts, facts_ref, sems.at[1])
    facts_copy.start()
    for ref in (g0, g1, g2, g3, edge_ref):
        ref[...] = jnp.zeros_like(ref)
    shape = (POINTS, POINTS)
    point = lax.broadcasted_iota(jnp.int32, shape, 0)
    target = (point & 7) * 64 + lax.shift_right_logical(point, 3)
    order = jnp.where(lane_of(shape) == target, 1.0, 0.0).astype(BF16)
    facts_copy.wait()
    copy.wait()
    stk_ref[...] = dot(rows_ref[...], order).astype(BF16)
    live = facts_ref[3, 0]

    @pl.when(live > LANES)
    def _():
        footprints(packed_ref[...], stk_ref, fp_ref, 0)

    @pl.when(live <= LANES)
    def _():
        footprints(packed_ref[:, 0:LANES], stk_ref, fp_ref, 0)

    scatter_columns(fp_ref, 0, place_in_facts(facts_ref), live, (g0, g1, g2, g3), edge_ref, (0, 1, 2, 3), 2)


BESIDE = (((0, 1), 6), ((2, 3), -2))


def chunks_beside(facts_ref, slots):
    for first in range(0, slots, LANES):
        counts = [jnp.clip(facts_ref[3, side * slots] - first, 0, LANES) for side in range(2)]
        yield first, counts


def both_sides(ref, slots, first):
    return jnp.concatenate(
        [ref[:, side * slots + first : side * slots + first + LANES] for side in range(2)], axis=1
    )


def beside_kernel(odd_ref, own_ref, first_ref, second_ref, stk_ref, i0, i1, i2, i3, iedge,
                  g0, g1, g2, g3, edge_ref, out_edge, out_facts, pool_ref, fp_ref, facts_ref, sem):
    height, slots = own_ref.shape
    before, after = pl.ds(0, height), pl.ds(2 * height, height)
    pool_ref[height : 2 * height, :] = own_ref[...]

    @pl.when(odd_ref[0] == 0)
    def _():
        pool_ref[after, :] = first_ref[...]
        pool_ref[before, :] = second_ref[...]

    @pl.when(odd_ref[0] != 0)
    def _():
        pool_ref[before, :] = first_ref[...]
        pool_ref[after, :] = second_ref[...]

    for side in range(2):
        out_facts[:, side * slots : (side + 1) * slots] = facts_of(pool_ref, 2 * side * height + PANELS)
    copy = pltpu.make_async_copy(out_facts, facts_ref, sem)
    copy.start()

    def project(first):
        here = slice(first, first + LANES)
        packed = jnp.concatenate(
            [pool_ref[0:height, here], pool_ref[2 * height : 3 * height, here]], axis=1
        )
        footprints(packed, stk_ref, fp_ref, 2 * first)

    project(0)
    copy.wait()
    for first, counts in chunks_beside(facts_ref, slots):
        if first:
            @pl.when(counts[0] + counts[1] > 0)
            def _(first=first):
                project(first)

        for side, (planes, shift_i) in enumerate(BESIDE):
            scatter_columns(fp_ref, 2 * first + side * LANES, place_in_facts(facts_ref, side * slots + first),
                            counts[side], (g0, g1, g2, g3), edge_ref, planes, shift_i)
    for ref in (g0, g1, g2, g3, edge_ref):
        ref[0:8, :] += ref[NZ:ZROWS, :]
    total = pltpu.roll(edge_ref[0:LANES, :], 2, 1)
    for block in range(1, 4):
        total += pltpu.roll(edge_ref[block * LANES : (block + 1) * LANES, :], 32 * block + 2, 1)
    out_edge[...] = total


def exponent_of(values):
    top = functools.reduce(jnp.maximum, [jnp.max(jnp.abs(v), axis=0, keepdims=True) for v in values])
    top = jnp.maximum(jnp.max(top, axis=1, keepdims=True), 2.0**-100)
    return jnp.ceil(jnp.log2(top)) - BOUND


def quarter(table_ref, index):
    rows = table_ref.shape[0] // 4
    return tuple(table_ref[part * rows : (part + 1) * rows, :] for part in (2 * index, 2 * index + 1))


def z_kernel(slabs, g0, g1, g2, g3, edge_ref, w_ref, out_ref, wide_ref):
    widen_edge(edge_ref, wide_ref)
    half = slabs // 2
    parts = NZ // (2 * slabs)
    planes = parts // 2
    stride = 4 * parts + SCALE_ROWS
    sums = []
    for parity in range(2):
        where = pl.ds(parity, NZ // 2, stride=2)
        columns = []
        for plane, grid in enumerate((g0, g1, g2, g3)):
            at_edge = edge_codes((plane,), (NZ // 2, LANES)) < 2
            values = grid[where, :] + jnp.where(at_edge, wide_ref[where, :], 0.0)
            columns.append(pltpu.roll(values, LANES - 8 * plane, 1) if plane else values)
        sums.append(dot3(quarter(w_ref, parity), split(jnp.concatenate(columns, axis=1))))
    results = (sums[0] + sums[1], sums[0] - sums[1])
    exponent = exponent_of(results)
    scale = jnp.exp2(-exponent)
    results = [result * scale for result in results]
    for upper, result in enumerate(results):
        for part in range(parts):
            index = part // planes * (planes + 1) + part % planes + upper
            for tile in range(2):
                rows = result[(index * 2 + tile) * half : (index * 2 + tile + 1) * half, :]
                start = (tile * slabs + upper * half) * stride + part
                for plane in range(4):
                    out_ref[pl.ds(start + plane * parts, half, stride=stride), :] = rows[
                        :, plane * LANES : (plane + 1) * LANES
                    ]
    for row in range(SCALE_ROWS):
        out_ref[pl.ds(4 * parts + row, 2 * slabs, stride=stride), :] = jnp.broadcast_to(
            exponent, (2 * slabs, LANES)
        )


def hat_kernel(planes, offset_ref, hat_ref, turn_ref, out_ref):
    length = hat_ref.shape[1]
    values = jnp.concatenate([hat_ref[offset_ref[0] + plane] for plane in range(planes)], axis=0)
    values = values * (1.0 / (length * NY))
    upper = values[:, HALF:]
    high, low = split(upper)
    rest = (upper - high.astype(F32) - low.astype(F32)).astype(BF16)
    turn = turn_ref[...]
    upper = dot(high, turn) + (dot(low, turn) + dot(rest, turn))
    for plane in range(planes):
        here = slice(plane * length, (plane + 1) * length)
        out_ref[plane] = jnp.concatenate([values[here, :HALF], upper[here, :]], axis=1)


def plane_kernel(slabs, planes, in_ref, hat_ref, y_ref, x_ref, out_ref, exponent_ref, ah_ref, al_ref):
    length = 4 * slabs
    rows = planes * length
    parts = 2 * planes
    stride = 4 * parts + SCALE_ROWS

    def pieces():
        for tile in range(2):
            for part in range(2):
                for xi in range(4):
                    for plane in range(planes):
                        yield tile, part, plane, xi

    scales = [
        jnp.exp2(in_ref[pl.ds(tile * slabs * stride + 4 * parts, slabs, stride=stride), :])
        for tile in range(2)
    ]
    for tile, part, plane, xi in pieces():
        start = tile * slabs * stride + xi * parts + part * planes + plane
        row = (part * planes + plane) * length + xi * slabs
        high, low = split(in_ref[pl.ds(start, slabs, stride=stride), :] * scales[tile])
        ah_ref[row : row + slabs, tile * LANES : (tile + 1) * LANES] = high
        al_ref[row : row + slabs, tile * LANES : (tile + 1) * LANES] = low
    first_lane = lane_of((rows, HALF)) == 0
    turned = dot3((ah_ref[...], al_ref[...]), (y_ref[0:NY, :], y_ref[NY : 2 * NY, :]))
    even = (turned[:rows, :HALF], turned[rows:, :HALF])
    odd = (turned[:rows, HALF:], turned[rows:, HALF:])
    zero_odd = [jnp.where(first_lane, 0.0, values) for values in odd]
    real = jnp.concatenate(
        [even[0] + zero_odd[1], jnp.where(first_lane, odd[0], even[0] - zero_odd[1])], axis=1
    )
    imag = jnp.concatenate(
        [even[1] - zero_odd[0], jnp.where(first_lane, odd[1], even[1] + zero_odd[0])], axis=1
    )
    size = 2 * length

    def along_x(values, first):
        high, low = split(values)
        table = x_ref[first * size : (first + 1) * size, :]
        rest = x_ref[(first + 1) * size : (first + 2) * size, :]
        both = dot(jnp.concatenate([table, table], axis=1), jnp.concatenate([high, low], axis=0))
        return both + dot(rest, high)

    for plane in range(planes):
        here = slice(plane * length, (plane + 1) * length)
        there = slice(rows + plane * length, rows + (plane + 1) * length)
        values = along_x(jnp.concatenate([real[here], imag[here]], axis=0), 0)
        values = values * jnp.concatenate([hat_ref[plane], hat_ref[plane]], axis=0)
        values = along_x(values, 2)
        low, high = values[:, :HALF], values[:, HALF:]
        lane = first_lane[:length]
        even_r = jnp.where(lane, low[:length], low[:length] + high[:length])
        even_i = jnp.where(lane, low[length:], low[length:] + high[length:])
        odd_r = jnp.where(lane, high[:length], high[length:] - low[length:])
        odd_i = jnp.where(lane, high[length:], low[:length] - high[:length])
        ah_ref[here, :], al_ref[here, :] = split(jnp.concatenate([even_r, odd_r], axis=1))
        ah_ref[there, :], al_ref[there, :] = split(jnp.concatenate([even_i, odd_i], axis=1))
    turned = dot3((ah_ref[...], al_ref[...]), (y_ref[2 * NY : 3 * NY, :], y_ref[3 * NY : 4 * NY, :]))
    tops = [
        jnp.max(in_ref[pl.ds(tile * slabs * stride + 4 * parts, slabs, stride=stride), :], axis=0, keepdims=True)
        for tile in range(2)
    ]
    exponent = jnp.broadcast_to(jnp.maximum(*tops) + BOUND - HEADROOM + math.ceil(math.log2(length * NY) / 2), (8, LANES))
    exponent_ref[...] = exponent
    scale = jnp.exp2(-exponent[0:1, 0:1])
    for tile, part, plane, xi in pieces():
        here = slice((part * planes + plane) * length + xi * slabs, (part * planes + plane) * length + (xi + 1) * slabs)
        start = tile * slabs * stride + xi * parts + part * planes + plane
        out_ref[pl.ds(start, slabs, stride=stride), :] = (
            turned[here, tile * LANES : (tile + 1) * LANES] * scale
        )


def potential_kernel(slabs, in_ref, exponent_ref, v_ref, p0, p1, p2, p3, edge_ref):
    half = slabs // 2
    parts = NZ // (2 * slabs)
    planes = parts // 2
    stride = 4 * parts
    sums = []
    for parity in range(2):
        columns = []
        for plane in range(4):
            rows = []
            for part in range(parts):
                upper = (part % planes + parity) % 2
                for tile in range(2):
                    start = (tile * slabs + upper * half) * stride + plane * parts + part
                    rows.append(in_ref[pl.ds(start, half, stride=stride), :])
            columns.append(jnp.concatenate(rows, axis=0))
        sums.append(dot3(quarter(v_ref, parity), split(jnp.concatenate(columns, axis=1))))
    scale = jnp.exp2(exponent_ref[0:1, 0:1])
    shape = (LANES, LANES)
    edges = [jnp.zeros(shape, F32)] * 4
    halves_of_z = [((sums[0] + sums[1]) * scale), ((sums[0] - sums[1]) * scale)]
    for plane, pot in enumerate((p0, p1, p2, p3)):
        at_edge = edge_codes((plane,), shape) < 2
        for upper in range(2):
            result = halves_of_z[upper][:, plane * LANES : (plane + 1) * LANES].astype(BF16).astype(F32)
            if plane:
                result = pltpu.roll(result, 8 * plane, 1)
            pot[upper * (NZ // 2) : (upper + 1) * (NZ // 2), :] = result
            for block in range(2):
                edges[2 * upper + block] = jnp.where(
                    at_edge, result[block * LANES : (block + 1) * LANES, :], edges[2 * upper + block]
                )
        pot[NZ:ZROWS, :] = pot[0:8, :]
    edge = pltpu.roll(edges[0], 2, 1)
    for block in range(1, 4):
        edge += pltpu.roll(edges[block], 32 * block + 2, 1)
    edge_ref[...] = edge.astype(BF16)


def widen_edge(edge_ref, wide_ref):
    for block in range(4):
        wide_ref[block * LANES : (block + 1) * LANES, :] = pltpu.roll(
            edge_ref[...].astype(F32), (LANES - 2 - 32 * block) % LANES, 1
        )
    wide_ref[NZ:ZROWS, :] = wide_ref[0:8, :]


def masked(values, live):
    return jnp.where(lane_of(values.shape) < live, values, 0.0)


def own_sample_kernel(facts_ref, p0, p1, p2, p3, edge_ref, kinds_ref, stk_ref, out_ref, wide_ref, sp_ref):
    widen_edge(edge_ref, wide_ref)
    live = facts_ref[3, 0]
    slots = kinds_ref.shape[1]
    sample_columns((p0, p1, p2, p3), wide_ref, place_in_facts(facts_ref), live, sp_ref, 0, (0, 1, 2, 3), 2)

    @pl.when(live > LANES)
    def _():
        out_ref[...] = masked(far_sums(sp_ref, kinds_ref[2:3, :], stk_ref, 0), live)

    @pl.when(live <= LANES)
    def _():
        out_ref[:, 0:LANES] = masked(far_sums(sp_ref, kinds_ref[2:3, 0:LANES], stk_ref, 0), live)
        out_ref[:, LANES:slots] = jnp.zeros((PANELS, slots - LANES), F32)


def beside_sample_kernel(odd_ref, facts_ref, p0, p1, p2, p3, edge_ref, kinds_ref, stk_ref, out0, out1, wide_ref, sp_ref):
    widen_edge(edge_ref, wide_ref)
    slots = kinds_ref.shape[1] // 2
    outs = (out0, out1)
    for first, counts in chunks_beside(facts_ref, slots):
        here = slice(first, first + LANES)
        for side, (planes, shift_i) in enumerate(BESIDE):
            sample_columns((p0, p1, p2, p3), wide_ref, place_in_facts(facts_ref, side * slots + first),
                           counts[side], sp_ref, 2 * first + side * LANES, planes, shift_i)

        @pl.when(counts[0] + counts[1] > 0)
        def _(first=first, counts=counts, here=here):
            kinds = both_sides(kinds_ref.at[2:3, :], slots, first)
            result = far_sums(sp_ref, kinds, stk_ref, 2 * first)
            sums = [masked(result[:, side * LANES : (side + 1) * LANES], counts[side]) for side in range(2)]
            even = jnp.broadcast_to(odd_ref[0], sums[0].shape) == 0
            out0[:, here] = jnp.where(even, sums[1], sums[0])
            out1[:, here] = jnp.where(even, sums[0], sums[1])

        @pl.when(counts[0] + counts[1] <= 0)
        def _(here=here):
            for out in outs:
                out[:, here] = jnp.zeros((PANELS, LANES), F32)


def near_kernel(live_ref, here_ref, there_ref, source_ref, block_ref, table_ref, out_ref):
    live = live_ref[0]
    fanout, slots = source_ref.shape
    height = here_ref.shape[0] // 3
    pool = jnp.concatenate(
        [ref[step * height : step * height + PANELS, :] for step in range(3) for ref in (here_ref, there_ref)],
        axis=1,
    )
    total = pool.shape[1]
    for first in range(0, slots, LANES):
        where = slice(first, first + LANES)

        @pl.when(live > first)
        def _(where=where, first=first):
            index = lax.broadcasted_iota(jnp.int32, (total, LANES), 0)
            result = jnp.zeros((PANELS, LANES), F32)
            for j in range(fanout):
                chosen = jnp.where(index == source_ref[j : j + 1, where], 1.0, 0.0).astype(BF16)
                gathered = dot(pool, chosen)
                result += dot(
                    table_ref[...], by_kind(gathered, block_ref[j : j + 1, where]).astype(BF16)
                )
            column = first + lane_of((PANELS, LANES))
            out_ref[:, where] = jnp.where(column < live, result, 0.0)

        @pl.when(live <= first)
        def _(where=where):
            out_ref[:, where] = jnp.zeros((PANELS, LANES), F32)


def shape_of(*dims, dtype=F32):
    return jax.ShapeDtypeStruct(dims, dtype)


def body(slabs, tiles, charges, live_count, slot_brick, slot_stencil, stencils, near_source,
         near_block, near_blocks, kernel_hat):
    slots = charges.shape[1]
    owners = slabs * tiles
    planes = kernel_hat.shape[0] // 2
    length = kernel_hat.shape[1]
    parts = NZ // owners
    axes = ("tile", "slab")
    both = ("slab", "tile")

    def moved(values, step_of, swap=0):
        pairs = [
            (a * tiles + b, (a + step_of(a)) % slabs * tiles + (b + swap) % tiles)
            for a in range(slabs)
            for b in range(tiles)
        ]
        return lax.ppermute(values, both, pairs)

    def to_first(values):
        return moved(values, lambda a: 1 - 2 * (a % 2))

    def to_second(values):
        return moved(values, lambda a: 2 * (a % 2) - 1)

    def to_other_tile(values):
        return moved(values, lambda a: 0, 1)

    odd = (lax.axis_index("slab") % 2)[None]
    row = lax.broadcasted_iota(jnp.int32, (PANELS + 16, slots), 0)
    column = lax.broadcasted_iota(jnp.int32, (PANELS + 16, slots), 1)
    live = jnp.broadcast_to(live_count[0], row.shape)
    brick = jnp.broadcast_to(slot_brick[None, :], row.shape)
    facts = lax.shift_right_logical(brick, jnp.where(row == PANELS, 7, 0)) & (NZ // 4 - 1)
    facts = jnp.where(row == PANELS + 2, slot_stencil[None, :], jnp.where(row == PANELS + 3, live, facts))
    held = jnp.where(column < live, jnp.pad(charges, ((0, 16), (0, 0))), jnp.zeros((), BF16))
    packed = jnp.where(row < PANELS, held, facts.astype(BF16))
    from_second = to_second(packed)
    from_first = to_first(packed)

    grid = shape_of(ZROWS, LANES)
    *grids, stk, facts = pl.pallas_call(
        own_kernel,
        out_shape=(grid,) * 5 + (shape_of(KS * PANELS, POINTS, dtype=BF16), shape_of(8, slots, dtype=jnp.int32)),
        in_specs=[VMEM, pl.BlockSpec(memory_space=pl.ANY)],
        out_specs=(VMEM,) * 7,
        scratch_shapes=[
            pltpu.VMEM((slots * 8, LANES), F32),
            pltpu.VMEM((KS * PANELS, POINTS), BF16),
            pltpu.SMEM((8, slots), jnp.int32),
            pltpu.SemaphoreType.DMA((2,)),
        ],
        compiler_params=PARAMS,
        name="own_scatter",
    )(packed, stencils.reshape(KS * PANELS, POINTS))

    g = pl.pallas_call(
        beside_kernel,
        out_shape=(grid,) * 5
        + (
            shape_of(LANES, LANES),
            shape_of(8, 2 * slots, dtype=jnp.int32),
            shape_of(3 * (PANELS + 16), slots, dtype=BF16),
        ),
        in_specs=[SMEM] + [VMEM] * 9,
        out_specs=(VMEM,) * 8,
        scratch_shapes=[
            pltpu.VMEM((2 * slots * 8, LANES), F32),
            pltpu.SMEM((8, 2 * slots), jnp.int32),
            pltpu.SemaphoreType.DMA,
        ],
        input_output_aliases={5: 0, 6: 1, 7: 2, 8: 3, 9: 4},
        compiler_params=PARAMS,
        name="beside_scatter",
    )(odd, packed, from_first, from_second, stk, *grids)
    facts2 = g[6]
    edge = to_other_tile(g[5])

    forward, inverse = z_tables(slabs, tiles)
    rows = owners * (4 * parts + SCALE_ROWS)
    sent = pl.pallas_call(
        functools.partial(z_kernel, slabs),
        out_shape=shape_of(rows, LANES),
        in_specs=[VMEM] * 6,
        out_specs=VMEM,
        scratch_shapes=[pltpu.VMEM((ZROWS, LANES), F32)],
        compiler_params=PARAMS,
        name="z_forward",
    )(*g[:4], edge, jnp.asarray(halves(*forward)))

    def exchanged(values, kept):
        values = values.reshape(owners, -1, LANES)[:, :kept].astype(jnp.float16)
        values = lax.all_to_all(values, axes, 0, 0, tiled=True)
        return values

    def widened(values):
        return values.astype(F32).reshape(-1, LANES)

    hat, sent = lax.optimization_barrier((kernel_hat, sent))
    got = exchanged(sent, 4 * parts + SCALE_ROWS)
    me = lax.axis_index("slab") * tiles + lax.axis_index("tile")
    offset = (me >= owners // 2).astype(jnp.int32)[None]
    hat = pl.pallas_call(
        functools.partial(hat_kernel, planes),
        out_shape=shape_of(planes, length, NY),
        in_specs=[SMEM] + [VMEM] * 2,
        out_specs=VMEM,
        compiler_params=PARAMS,
        name="hat_order",
    )(offset, hat, jnp.asarray(reversal()))

    got, hat = lax.optimization_barrier((got, hat))
    pool = (g[7], to_other_tile(g[7]))
    direction = near_source // slots
    pool_index = (direction // 3 * 2 + (direction % 3 != 1).astype(jnp.int32)) * slots + near_source % slots
    near = pl.pallas_call(
        near_kernel,
        out_shape=shape_of(PANELS, slots),
        in_specs=[SMEM] + [VMEM] * 5,
        out_specs=VMEM,
        compiler_params=PARAMS,
        name="near_field",
    )(live_count, *pool, pool_index.T, near_block.T, near_blocks.reshape(PANELS, KN * PANELS))

    back, exponent = pl.pallas_call(
        functools.partial(plane_kernel, slabs, planes),
        out_shape=(shape_of(rows, LANES), shape_of(8, LANES)),
        in_specs=[VMEM] * 4,
        out_specs=(VMEM, VMEM),
        scratch_shapes=[pltpu.VMEM((2 * planes * length, NY), BF16)] * 2,
        compiler_params=PARAMS,
        name="plane_filter",
    )(widened(got), hat, jnp.asarray(halves(y_table(), y_table().T)), jnp.asarray(halves(*x_tables(slabs))))
    back, near = lax.optimization_barrier((exchanged(back, 4 * parts), near))

    pot = pl.pallas_call(
        functools.partial(potential_kernel, slabs),
        out_shape=(grid,) * 4 + (shape_of(LANES, LANES, dtype=BF16),),
        in_specs=[VMEM] * 3,
        out_specs=(VMEM,) * 5,
        compiler_params=PARAMS,
        name="z_inverse",
    )(widened(back), exponent, jnp.asarray(halves(*inverse)))
    edge = to_other_tile(pot[4])

    def sample_scratch(width):
        return [pltpu.VMEM((ZROWS, LANES), F32), pltpu.VMEM((width * 8, LANES), F32)]

    sums = shape_of(PANELS, slots)
    others = pl.pallas_call(
        beside_sample_kernel,
        out_shape=(sums, sums),
        in_specs=[SMEM] * 2 + [VMEM] * 7,
        out_specs=(VMEM, VMEM),
        scratch_shapes=sample_scratch(2 * slots),
        compiler_params=PARAMS,
        name="beside_sample",
    )(odd, facts2, *pot[:4], edge, facts2, stk)
    second = to_second(others[1])
    first = to_first(others[0])
    own = pl.pallas_call(
        own_sample_kernel,
        out_shape=sums,
        in_specs=[SMEM] + [VMEM] * 7,
        out_specs=VMEM,
        scratch_shapes=sample_scratch(slots),
        compiler_params=PARAMS,
        name="own_sample",
    )(facts, *pot[:4], edge, facts, stk)
    return own + near + first + second


def solution(mesh):
    both = ("slab", "tile")
    in_specs = (
        P(None, both),
        P(both),
        P(both),
        P(both),
        P(),
        P(both, None),
        P(both, None),
        P(),
        P(both, None, None),
    )
    return jax.shard_map(
        functools.partial(body, mesh.shape["slab"], mesh.shape["tile"]),
        mesh=mesh,
        in_specs=in_specs,
        out_specs=P(None, both),
        check_vma=False,
    )
```

```python
import functools
import math

import jax
import jax.numpy as jnp
import ml_dtypes
import numpy as np
from jax import lax
from jax.experimental import pallas as pl
from jax.experimental.pallas import tpu as pltpu
from jax.sharding import PartitionSpec as P

PANELS = 64
POINTS = 512
NY = 256
NZ = 512
KS = 16
KN = 16
LANES = 128
ZROWS = NZ + 8
UNROLL = 16
HALF = NY // 2
SCALE_ROWS = 8
BOUND = 12.0
HEADROOM = 15.0
F32 = jnp.float32
BF16 = jnp.bfloat16
SMEM = pl.BlockSpec(memory_space=pltpu.SMEM)
VMEM = pl.BlockSpec(memory_space=pltpu.VMEM)
PARAMS = pltpu.CompilerParams(vmem_limit_bytes=48 * 1024 * 1024)


def halves(*tables):
    parts = []
    for table in tables:
        high = table.astype(ml_dtypes.bfloat16)
        parts += [high, (table - high.astype(np.float64)).astype(ml_dtypes.bfloat16)]
    return np.concatenate(parts, axis=0)


def z_tables(slabs, tiles):
    half = slabs // 2
    planes = NZ // (slabs * tiles) // 2
    plane = np.arange(planes + 1)[:, None, None]
    tile = np.arange(tiles)[None, :, None]
    slab = np.arange(half)[None, None, :]
    owner = slab * tiles + tile
    freq = (owner * 2 * planes + plane).reshape(-1)
    forward, inverse = [], []
    for parity in range(2):
        cell = np.arange(parity, NZ, 2) - 2
        angle = (freq[:, None] * cell[None, :] % NZ) * (2 * np.pi / NZ)
        forward.append(np.concatenate([np.cos(angle), -np.sin(angle)], axis=0))
        upper = (plane[:-1] + parity) % 2
        back = ((upper * half * tiles + owner) * 2 * planes + plane[:-1] + upper).reshape(-1)
        cell = np.arange(NZ // 2) - 2
        angle = (back[:, None] * cell[None, :] % NZ) * (2 * np.pi / NZ)
        weight = np.where(back == 0, 1.0, 2.0)[:, None] / NZ
        inverse.append(np.concatenate([weight * np.cos(angle), -weight * np.sin(angle)], axis=0).T)
    return forward, inverse


def y_table():
    angle = (np.arange(NY)[:, None] * np.arange(HALF + 1)[None, :] % NY) * (2 * np.pi / NY)
    return np.concatenate([np.cos(angle[:, :HALF]), np.cos(angle[:, HALF:]), np.sin(angle[:, 1:HALF])], axis=1)


def reversal():
    table = np.zeros((HALF, HALF), ml_dtypes.bfloat16)
    lane = np.arange(HALF)
    table[lane, (HALF - lane) % HALF] = 1
    return table


def x_tables(slabs):
    length = 4 * slabs
    cell = (np.arange(4)[:, None] + 4 * np.arange(slabs)[None, :]).reshape(-1)
    angle = (np.arange(length)[:, None] * cell[None, :] % length) * (2 * np.pi / length)
    cosine, sine = np.cos(angle), np.sin(angle)
    forward = np.block([[cosine, sine], [-sine, cosine]])
    inverse = np.block([[cosine.T, -sine.T], [sine.T, cosine.T]])
    return forward, inverse


def split(values):
    high = values.astype(BF16)
    return high, (values - high.astype(F32)).astype(BF16)


def dot(a, b):
    return jnp.dot(a, b, preferred_element_type=F32)


def dot3(a, b):
    return dot(a[0], b[0]) + (dot(a[0], b[1]) + dot(a[1], b[0]))


def lane_of(shape):
    return lax.broadcasted_iota(jnp.int32, shape, 1)


def by_kind(values, kinds):
    zero = jnp.zeros_like(values)
    return jnp.concatenate(
        [jnp.where(kinds == kind, values, zero) for kind in range(KS)], axis=0
    )


def footprints(packed, stk_ref, fp_ref, first):
    count = packed.shape[1]
    turned = jnp.transpose(packed.astype(F32))
    kinds = turned[:, PANELS + 2 : PANELS + 3]
    charges = jnp.concatenate([turned[:, :PANELS], turned[:, :PANELS]], axis=1)
    offset = kinds - jnp.where(lane_of((count, LANES)) < PANELS, 0.0, 1.0)
    spread = jnp.concatenate(
        [jnp.where(offset == kind, charges, 0.0).astype(BF16) for kind in range(0, KS, 2)], axis=1
    )
    for pair in range(4):
        part = dot(spread, stk_ref[:, pair * LANES : (pair + 1) * LANES])
        fp_ref[pl.ds(first * 8 + 2 * pair, count, stride=8), :] = part
        fp_ref[pl.ds(first * 8 + 2 * pair + 1, count, stride=8), :] = pltpu.roll(part, 64, 1)


def lane_in(plane, shape):
    return (lane_of(shape) - 8 * plane) & (LANES - 1)


def edge_codes(planes, shape):
    code = jnp.full(shape, 3, jnp.int32)
    for plane in planes:
        lane = lane_in(plane, shape)
        code = jnp.where(lane >= LANES - 2, 0, jnp.where(lane < 2, 1, code))
    return code


def scatter_columns(fp_ref, first, place_of, count, grids, edge_ref, planes):
    shape = (8, LANES)
    lanes = [lane_in(plane, shape) for plane in planes]
    codes = edge_codes(planes, shape)

    def step(index, carry):
        updates = []
        for inner in range(UNROLL):
            column = index * UNROLL + inner
            row, begin, edge, turn, _ = place_of(column)
            value = fp_ref[pl.ds(pl.multiple_of((first + column) * 8, 8), 8), :]
            turned = pltpu.roll(value, turn, 1)
            terms = [jnp.where(((lane - begin) & -8) == 0, turned, 0.0) for lane in lanes]
            terms.append(jnp.where(codes == edge, turned, 0.0))
            updates.append((pl.ds(row, 8), terms))
        refs = [grids[plane] for plane in planes] + [edge_ref]
        for where, terms in updates:
            sums = [ref[where, :] + term for ref, term in zip(refs, terms)]
            for ref, total in zip(refs, sums):
                ref[where, :] = total
        return carry

    lax.fori_loop(0, lax.shift_right_logical(count + UNROLL - 1, 4), step, 0)


def sample_columns(pot_refs, edge_ref, place_of, count, sp_ref, first, planes):
    shape = (8, LANES)
    lanes = [lane_in(plane, shape) for plane in planes]
    codes = edge_codes(planes, shape)

    def step(index, carry):
        results = []
        for inner in range(UNROLL):
            column = index * UNROLL + inner
            row, begin, edge, _, turn = place_of(column)
            where = pl.ds(row, 8)
            result = jnp.where(codes == edge, edge_ref[where, :], 0.0)
            for plane, lane in zip(planes, lanes):
                result = jnp.where(((lane - begin) & -8) == 0, pot_refs[plane][where, :], result)
            turned = pltpu.roll(result, turn, 1)
            results.append((pl.ds(pl.multiple_of((first + column) * 8, 8), 8), turned))
        for where, result in results:
            sp_ref[where, :] = result
        return carry

    lax.fori_loop(0, lax.shift_right_logical(count + UNROLL - 1, 4), step, 0)


def far_sums(sp_ref, kinds, stk_ref, first):
    count = kinds.shape[1]
    lane = lane_of((count, LANES))
    pairs = []
    for pair in range(4):
        even = sp_ref[pl.ds(first * 8 + 2 * pair, count, stride=8), :]
        odd = sp_ref[pl.ds(first * 8 + 2 * pair + 1, count, stride=8), :]
        pairs.append(jnp.where(lane < 64, even, pltpu.roll(odd, 64, 1)).astype(BF16))
    samples = jnp.concatenate(pairs, axis=1)
    sums = lax.dot_general(
        stk_ref[...], samples, (((1,), (1,)), ((), ())), preferred_element_type=F32
    )
    result = jnp.zeros((PANELS, count), F32)
    for kind in range(KS):
        result += jnp.where(kinds == kind, sums[kind * PANELS : (kind + 1) * PANELS, :], 0.0)
    return result


OWN = ((0, 1, 2, 3), 2)
BESIDE = (((0, 1), 6), ((2, 3), -2))


def place_in_facts(facts_ref, start=0):
    return lambda column: [facts_ref[row, start + column] for row in (0, 1, 4, 5, 6)]


def facts_of(packed_ref, row, shift_i):
    facts = packed_ref[row : row + 16, :].astype(F32).astype(jnp.int32)
    by, bz, kinds, live = (facts[index : index + 1, :] for index in range(4))
    begin = 4 * by - 2
    edge = jnp.where(by == 0, 0, jnp.where(by == NY // 8 - 1, 1, 2))
    turn = begin - 8 * shift_i
    rows = [4 * bz, begin, kinds, live, edge, turn & (LANES - 1), -turn & (LANES - 1), by]
    return jnp.concatenate(rows, axis=0)


def own_kernel(packed_ref, stencil_ref,
               g0, g1, g2, g3, edge_ref, stk_ref, out_facts, fp_ref, rows_ref, facts_ref, sems):
    copy = pltpu.make_async_copy(stencil_ref, rows_ref, sems.at[0])
    copy.start()
    out_facts[...] = facts_of(packed_ref, PANELS, OWN[1])
    facts_copy = pltpu.make_async_copy(out_facts, facts_ref, sems.at[1])
    facts_copy.start()
    for ref in (g0, g1, g2, g3, edge_ref):
        ref[...] = jnp.zeros_like(ref)
    shape = (POINTS, POINTS)
    point = lax.broadcasted_iota(jnp.int32, shape, 0)
    target = (point & 7) * 64 + lax.shift_right_logical(point, 3)
    order = jnp.where(lane_of(shape) == target, 1.0, 0.0).astype(BF16)
    facts_copy.wait()
    copy.wait()
    stk_ref[...] = dot(rows_ref[...], order).astype(BF16)
    live = facts_ref[3, 0]

    @pl.when(live > LANES)
    def _():
        footprints(packed_ref[...], stk_ref, fp_ref, 0)

    @pl.when(live <= LANES)
    def _():
        footprints(packed_ref[:, 0:LANES], stk_ref, fp_ref, 0)

    scatter_columns(fp_ref, 0, place_in_facts(facts_ref), live, (g0, g1, g2, g3), edge_ref, OWN[0])


def chunks_beside(facts_ref, slots):
    for first in range(0, slots, LANES):
        counts = [jnp.clip(facts_ref[3, side * slots] - first, 0, LANES) for side in range(2)]
        yield first, counts


def both_sides(ref, slots, first):
    return jnp.concatenate(
        [ref[:, side * slots + first : side * slots + first + LANES] for side in range(2)], axis=1
    )


def beside_kernel(odd_ref, own_ref, first_ref, second_ref, stk_ref, i0, i1, i2, i3, iedge,
                  g0, g1, g2, g3, edge_ref, out_edge, out_facts, pool_ref, fp_ref, facts_ref, sem):
    height, slots = own_ref.shape
    before, after = pl.ds(0, height), pl.ds(2 * height, height)
    pool_ref[height : 2 * height, :] = own_ref[...]

    @pl.when(odd_ref[0] == 0)
    def _():
        pool_ref[after, :] = first_ref[...]
        pool_ref[before, :] = second_ref[...]

    @pl.when(odd_ref[0] != 0)
    def _():
        pool_ref[before, :] = first_ref[...]
        pool_ref[after, :] = second_ref[...]

    for side, (_, shift_i) in enumerate(BESIDE):
        out_facts[:, side * slots : (side + 1) * slots] = facts_of(pool_ref, 2 * side * height + PANELS, shift_i)
    copy = pltpu.make_async_copy(out_facts, facts_ref, sem)
    copy.start()

    def project(first):
        here = slice(first, first + LANES)
        packed = jnp.concatenate(
            [pool_ref[0:height, here], pool_ref[2 * height : 3 * height, here]], axis=1
        )
        footprints(packed, stk_ref, fp_ref, 2 * first)

    project(0)
    copy.wait()
    for first, counts in chunks_beside(facts_ref, slots):
        if first:
            @pl.when(counts[0] + counts[1] > 0)
            def _(first=first):
                project(first)

        for side, (planes, _) in enumerate(BESIDE):
            scatter_columns(fp_ref, 2 * first + side * LANES, place_in_facts(facts_ref, side * slots + first),
                            counts[side], (g0, g1, g2, g3), edge_ref, planes)
    for ref in (g0, g1, g2, g3, edge_ref):
        ref[0:8, :] += ref[NZ:ZROWS, :]
    total = pltpu.roll(edge_ref[0:LANES, :], 2, 1)
    for block in range(1, 4):
        total += pltpu.roll(edge_ref[block * LANES : (block + 1) * LANES, :], 32 * block + 2, 1)
    out_edge[...] = total


def exponent_of(values):
    top = functools.reduce(jnp.maximum, [jnp.max(jnp.abs(v), axis=0, keepdims=True) for v in values])
    top = jnp.maximum(jnp.max(top, axis=1, keepdims=True), 2.0**-100)
    return jnp.ceil(jnp.log2(top)) - BOUND


def quarter(table_ref, index):
    rows = table_ref.shape[0] // 4
    return tuple(table_ref[part * rows : (part + 1) * rows, :] for part in (2 * index, 2 * index + 1))


def z_kernel(slabs, g0, g1, g2, g3, edge_ref, w_ref, out_ref, wide_ref):
    widen_edge(edge_ref, wide_ref)
    half = slabs // 2
    parts = NZ // (2 * slabs)
    planes = parts // 2
    stride = 4 * parts + SCALE_ROWS
    sums = []
    for parity in range(2):
        where = pl.ds(parity, NZ // 2, stride=2)
        columns = []
        for plane, grid in enumerate((g0, g1, g2, g3)):
            at_edge = edge_codes((plane,), (NZ // 2, LANES)) < 2
            values = grid[where, :] + jnp.where(at_edge, wide_ref[where, :], 0.0)
            columns.append(pltpu.roll(values, LANES - 8 * plane, 1) if plane else values)
        sums.append(dot3(quarter(w_ref, parity), split(jnp.concatenate(columns, axis=1))))
    results = (sums[0] + sums[1], sums[0] - sums[1])
    exponent = exponent_of(results)
    scale = jnp.exp2(-exponent)
    results = [result * scale for result in results]
    for upper, result in enumerate(results):
        for part in range(parts):
            index = part // planes * (planes + 1) + part % planes + upper
            for tile in range(2):
                rows = result[(index * 2 + tile) * half : (index * 2 + tile + 1) * half, :]
                start = (tile * slabs + upper * half) * stride + part
                for plane in range(4):
                    out_ref[pl.ds(start + plane * parts, half, stride=stride), :] = rows[
                        :, plane * LANES : (plane + 1) * LANES
                    ]
    for row in range(SCALE_ROWS):
        out_ref[pl.ds(4 * parts + row, 2 * slabs, stride=stride), :] = jnp.broadcast_to(
            exponent, (2 * slabs, LANES)
        )


def hat_kernel(planes, offset_ref, hat_ref, turn_ref, out_ref):
    length = hat_ref.shape[1]
    values = jnp.concatenate([hat_ref[offset_ref[0] + plane] for plane in range(planes)], axis=0)
    values = values * (1.0 / (length * NY))
    upper = values[:, HALF:]
    high, low = split(upper)
    rest = (upper - high.astype(F32) - low.astype(F32)).astype(BF16)
    turn = turn_ref[...]
    upper = dot(high, turn) + (dot(low, turn) + dot(rest, turn))
    for plane in range(planes):
        here = slice(plane * length, (plane + 1) * length)
        out_ref[plane] = jnp.concatenate([values[here, :HALF], upper[here, :]], axis=1)


def plane_kernel(slabs, planes, in_ref, hat_ref, y_ref, x_ref, out_ref, exponent_ref, ah_ref, al_ref):
    length = 4 * slabs
    rows = planes * length
    parts = 2 * planes
    stride = 4 * parts + SCALE_ROWS

    def pieces():
        for tile in range(2):
            for part in range(2):
                for xi in range(4):
                    for plane in range(planes):
                        yield tile, part, plane, xi

    scales = [
        jnp.exp2(in_ref[pl.ds(tile * slabs * stride + 4 * parts, slabs, stride=stride), :])
        for tile in range(2)
    ]
    for tile, part, plane, xi in pieces():
        start = tile * slabs * stride + xi * parts + part * planes + plane
        row = (part * planes + plane) * length + xi * slabs
        high, low = split(in_ref[pl.ds(start, slabs, stride=stride), :] * scales[tile])
        ah_ref[row : row + slabs, tile * LANES : (tile + 1) * LANES] = high
        al_ref[row : row + slabs, tile * LANES : (tile + 1) * LANES] = low
    first_lane = lane_of((rows, HALF)) == 0
    turned = dot3((ah_ref[...], al_ref[...]), (y_ref[0:NY, :], y_ref[NY : 2 * NY, :]))
    even = (turned[:rows, :HALF], turned[rows:, :HALF])
    odd = (turned[:rows, HALF:], turned[rows:, HALF:])
    zero_odd = [jnp.where(first_lane, 0.0, values) for values in odd]
    real = jnp.concatenate(
        [even[0] + zero_odd[1], jnp.where(first_lane, odd[0], even[0] - zero_odd[1])], axis=1
    )
    imag = jnp.concatenate(
        [even[1] - zero_odd[0], jnp.where(first_lane, odd[1], even[1] + zero_odd[0])], axis=1
    )
    size = 2 * length

    def along_x(values, first):
        high, low = split(values)
        table = x_ref[first * size : (first + 1) * size, :]
        rest = x_ref[(first + 1) * size : (first + 2) * size, :]
        both = dot(jnp.concatenate([table, table], axis=1), jnp.concatenate([high, low], axis=0))
        return both + dot(rest, high)

    for plane in range(planes):
        here = slice(plane * length, (plane + 1) * length)
        there = slice(rows + plane * length, rows + (plane + 1) * length)
        values = along_x(jnp.concatenate([real[here], imag[here]], axis=0), 0)
        values = values * jnp.concatenate([hat_ref[plane], hat_ref[plane]], axis=0)
        values = along_x(values, 2)
        low, high = values[:, :HALF], values[:, HALF:]
        lane = first_lane[:length]
        even_r = jnp.where(lane, low[:length], low[:length] + high[:length])
        even_i = jnp.where(lane, low[length:], low[length:] + high[length:])
        odd_r = jnp.where(lane, high[:length], high[length:] - low[length:])
        odd_i = jnp.where(lane, high[length:], low[:length] - high[:length])
        ah_ref[here, :], al_ref[here, :] = split(jnp.concatenate([even_r, odd_r], axis=1))
        ah_ref[there, :], al_ref[there, :] = split(jnp.concatenate([even_i, odd_i], axis=1))
    turned = dot3((ah_ref[...], al_ref[...]), (y_ref[2 * NY : 3 * NY, :], y_ref[3 * NY : 4 * NY, :]))
    tops = [
        jnp.max(in_ref[pl.ds(tile * slabs * stride + 4 * parts, slabs, stride=stride), :], axis=0, keepdims=True)
        for tile in range(2)
    ]
    exponent = jnp.broadcast_to(jnp.maximum(*tops) + BOUND - HEADROOM + math.ceil(math.log2(length * NY) / 2), (8, LANES))
    exponent_ref[...] = exponent
    scale = jnp.exp2(-exponent[0:1, 0:1])
    for tile, part, plane, xi in pieces():
        here = slice((part * planes + plane) * length + xi * slabs, (part * planes + plane) * length + (xi + 1) * slabs)
        start = tile * slabs * stride + xi * parts + part * planes + plane
        out_ref[pl.ds(start, slabs, stride=stride), :] = (
            turned[here, tile * LANES : (tile + 1) * LANES] * scale
        )


def potential_kernel(slabs, in_ref, exponent_ref, v_ref, p0, p1, p2, p3, edge_ref):
    half = slabs // 2
    parts = NZ // (2 * slabs)
    planes = parts // 2
    stride = 4 * parts
    sums = []
    for parity in range(2):
        columns = []
        for plane in range(4):
            rows = []
            for part in range(parts):
                upper = (part % planes + parity) % 2
                for tile in range(2):
                    start = (tile * slabs + upper * half) * stride + plane * parts + part
                    rows.append(in_ref[pl.ds(start, half, stride=stride), :])
            columns.append(jnp.concatenate(rows, axis=0))
        sums.append(dot3(quarter(v_ref, parity), split(jnp.concatenate(columns, axis=1))))
    scale = jnp.exp2(exponent_ref[0:1, 0:1])
    shape = (LANES, LANES)
    edges = [jnp.zeros(shape, F32)] * 4
    halves_of_z = [((sums[0] + sums[1]) * scale), ((sums[0] - sums[1]) * scale)]
    for plane, pot in enumerate((p0, p1, p2, p3)):
        at_edge = edge_codes((plane,), shape) < 2
        for upper in range(2):
            result = halves_of_z[upper][:, plane * LANES : (plane + 1) * LANES].astype(BF16).astype(F32)
            if plane:
                result = pltpu.roll(result, 8 * plane, 1)
            pot[upper * (NZ // 2) : (upper + 1) * (NZ // 2), :] = result
            for block in range(2):
                edges[2 * upper + block] = jnp.where(
                    at_edge, result[block * LANES : (block + 1) * LANES, :], edges[2 * upper + block]
                )
        pot[NZ:ZROWS, :] = pot[0:8, :]
    edge = pltpu.roll(edges[0], 2, 1)
    for block in range(1, 4):
        edge += pltpu.roll(edges[block], 32 * block + 2, 1)
    edge_ref[...] = edge.astype(BF16)


def widen_edge(edge_ref, wide_ref):
    for block in range(4):
        wide_ref[block * LANES : (block + 1) * LANES, :] = pltpu.roll(
            edge_ref[...].astype(F32), (LANES - 2 - 32 * block) % LANES, 1
        )
    wide_ref[NZ:ZROWS, :] = wide_ref[0:8, :]


def masked(values, live):
    return jnp.where(lane_of(values.shape) < live, values, 0.0)


def own_sample_kernel(facts_ref, p0, p1, p2, p3, edge_ref, kinds_ref, stk_ref, out_ref, wide_ref, sp_ref):
    widen_edge(edge_ref, wide_ref)
    live = facts_ref[3, 0]
    slots = kinds_ref.shape[1]
    sample_columns((p0, p1, p2, p3), wide_ref, place_in_facts(facts_ref), live, sp_ref, 0, OWN[0])

    @pl.when(live > LANES)
    def _():
        out_ref[...] = masked(far_sums(sp_ref, kinds_ref[2:3, :], stk_ref, 0), live)

    @pl.when(live <= LANES)
    def _():
        out_ref[:, 0:LANES] = masked(far_sums(sp_ref, kinds_ref[2:3, 0:LANES], stk_ref, 0), live)
        out_ref[:, LANES:slots] = jnp.zeros((PANELS, slots - LANES), F32)


def beside_sample_kernel(odd_ref, facts_ref, p0, p1, p2, p3, edge_ref, kinds_ref, stk_ref, out0, out1, wide_ref, sp_ref):
    widen_edge(edge_ref, wide_ref)
    slots = kinds_ref.shape[1] // 2
    outs = (out0, out1)
    for first, counts in chunks_beside(facts_ref, slots):
        here = slice(first, first + LANES)
        for side, (planes, _) in enumerate(BESIDE):
            sample_columns((p0, p1, p2, p3), wide_ref, place_in_facts(facts_ref, side * slots + first),
                           counts[side], sp_ref, 2 * first + side * LANES, planes)

        @pl.when(counts[0] + counts[1] > 0)
        def _(first=first, counts=counts, here=here):
            kinds = both_sides(kinds_ref.at[2:3, :], slots, first)
            result = far_sums(sp_ref, kinds, stk_ref, 2 * first)
            sums = [masked(result[:, side * LANES : (side + 1) * LANES], counts[side]) for side in range(2)]
            even = jnp.broadcast_to(odd_ref[0], sums[0].shape) == 0
            out0[:, here] = jnp.where(even, sums[1], sums[0])
            out1[:, here] = jnp.where(even, sums[0], sums[1])

        @pl.when(counts[0] + counts[1] <= 0)
        def _(here=here):
            for out in outs:
                out[:, here] = jnp.zeros((PANELS, LANES), F32)


def near_kernel(live_ref, here_ref, there_ref, source_ref, block_ref, table_ref, out_ref):
    live = live_ref[0]
    fanout, slots = source_ref.shape
    height = here_ref.shape[0] // 3
    pool = jnp.concatenate(
        [ref[step * height : step * height + PANELS, :] for step in range(3) for ref in (here_ref, there_ref)],
        axis=1,
    )
    total = pool.shape[1]
    for first in range(0, slots, LANES):
        where = slice(first, first + LANES)

        @pl.when(live > first)
        def _(where=where, first=first):
            index = lax.broadcasted_iota(jnp.int32, (total, LANES), 0)
            result = jnp.zeros((PANELS, LANES), F32)
            for j in range(fanout):
                chosen = jnp.where(index == source_ref[j : j + 1, where], 1.0, 0.0).astype(BF16)
                gathered = dot(pool, chosen)
                result += dot(
                    table_ref[...], by_kind(gathered, block_ref[j : j + 1, where]).astype(BF16)
                )
            column = first + lane_of((PANELS, LANES))
            out_ref[:, where] = jnp.where(column < live, result, 0.0)

        @pl.when(live <= first)
        def _(where=where):
            out_ref[:, where] = jnp.zeros((PANELS, LANES), F32)


def shape_of(*dims, dtype=F32):
    return jax.ShapeDtypeStruct(dims, dtype)


def body(slabs, tiles, charges, live_count, slot_brick, slot_stencil, stencils, near_source,
         near_block, near_blocks, kernel_hat):
    slots = charges.shape[1]
    owners = slabs * tiles
    planes = kernel_hat.shape[0] // 2
    length = kernel_hat.shape[1]
    parts = NZ // owners
    axes = ("tile", "slab")
    both = ("slab", "tile")

    def moved(values, step_of, swap=0):
        pairs = [
            (a * tiles + b, (a + step_of(a)) % slabs * tiles + (b + swap) % tiles)
            for a in range(slabs)
            for b in range(tiles)
        ]
        return lax.ppermute(values, both, pairs)

    def to_first(values):
        return moved(values, lambda a: 1 - 2 * (a % 2))

    def to_second(values):
        return moved(values, lambda a: 2 * (a % 2) - 1)

    def to_other_tile(values):
        return moved(values, lambda a: 0, 1)

    odd = (lax.axis_index("slab") % 2)[None]
    row = lax.broadcasted_iota(jnp.int32, (PANELS + 16, slots), 0)
    column = lax.broadcasted_iota(jnp.int32, (PANELS + 16, slots), 1)
    live = jnp.broadcast_to(live_count[0], row.shape)
    brick = jnp.broadcast_to(slot_brick[None, :], row.shape)
    facts = lax.shift_right_logical(brick, jnp.where(row == PANELS, 7, 0)) & (NZ // 4 - 1)
    facts = jnp.where(row == PANELS + 2, slot_stencil[None, :], jnp.where(row == PANELS + 3, live, facts))
    held = jnp.where(column < live, jnp.pad(charges, ((0, 16), (0, 0))), jnp.zeros((), BF16))
    packed = jnp.where(row < PANELS, held, facts.astype(BF16))
    from_second = to_second(packed)
    from_first = to_first(packed)

    grid = shape_of(ZROWS, LANES)
    *grids, stk, facts = pl.pallas_call(
        own_kernel,
        out_shape=(grid,) * 5 + (shape_of(KS * PANELS, POINTS, dtype=BF16), shape_of(8, slots, dtype=jnp.int32)),
        in_specs=[VMEM, pl.BlockSpec(memory_space=pl.ANY)],
        out_specs=(VMEM,) * 7,
        scratch_shapes=[
            pltpu.VMEM((slots * 8, LANES), F32),
            pltpu.VMEM((KS * PANELS, POINTS), BF16),
            pltpu.SMEM((8, slots), jnp.int32),
            pltpu.SemaphoreType.DMA((2,)),
        ],
        compiler_params=PARAMS,
        name="own_scatter",
    )(packed, stencils.reshape(KS * PANELS, POINTS))

    g = pl.pallas_call(
        beside_kernel,
        out_shape=(grid,) * 5
        + (
            shape_of(LANES, LANES),
            shape_of(8, 2 * slots, dtype=jnp.int32),
            shape_of(3 * (PANELS + 16), slots, dtype=BF16),
        ),
        in_specs=[SMEM] + [VMEM] * 9,
        out_specs=(VMEM,) * 8,
        scratch_shapes=[
            pltpu.VMEM((2 * slots * 8, LANES), F32),
            pltpu.SMEM((8, 2 * slots), jnp.int32),
            pltpu.SemaphoreType.DMA,
        ],
        input_output_aliases={5: 0, 6: 1, 7: 2, 8: 3, 9: 4},
        compiler_params=PARAMS,
        name="beside_scatter",
    )(odd, packed, from_first, from_second, stk, *grids)
    facts2 = g[6]
    edge = to_other_tile(g[5])

    forward, inverse = z_tables(slabs, tiles)
    rows = owners * (4 * parts + SCALE_ROWS)
    sent = pl.pallas_call(
        functools.partial(z_kernel, slabs),
        out_shape=shape_of(rows, LANES),
        in_specs=[VMEM] * 6,
        out_specs=VMEM,
        scratch_shapes=[pltpu.VMEM((ZROWS, LANES), F32)],
        compiler_params=PARAMS,
        name="z_forward",
    )(*g[:4], edge, jnp.asarray(halves(*forward)))

    def exchanged(values, kept):
        values = values.reshape(owners, -1, LANES)[:, :kept].astype(jnp.float16)
        values = lax.all_to_all(values, axes, 0, 0, tiled=True)
        return values

    def widened(values):
        return values.astype(F32).reshape(-1, LANES)

    hat, sent = lax.optimization_barrier((kernel_hat, sent))
    got = exchanged(sent, 4 * parts + SCALE_ROWS)
    me = lax.axis_index("slab") * tiles + lax.axis_index("tile")
    offset = (me >= owners // 2).astype(jnp.int32)[None]
    hat = pl.pallas_call(
        functools.partial(hat_kernel, planes),
        out_shape=shape_of(planes, length, NY),
        in_specs=[SMEM] + [VMEM] * 2,
        out_specs=VMEM,
        compiler_params=PARAMS,
        name="hat_order",
    )(offset, hat, jnp.asarray(reversal()))

    got, hat = lax.optimization_barrier((got, hat))
    pool = (g[7], to_other_tile(g[7]))
    direction = near_source // slots
    pool_index = (direction // 3 * 2 + (direction % 3 != 1).astype(jnp.int32)) * slots + near_source % slots
    near = pl.pallas_call(
        near_kernel,
        out_shape=shape_of(PANELS, slots),
        in_specs=[SMEM] + [VMEM] * 5,
        out_specs=VMEM,
        compiler_params=PARAMS,
        name="near_field",
    )(live_count, *pool, pool_index.T, near_block.T, near_blocks.reshape(PANELS, KN * PANELS))

    back, exponent = pl.pallas_call(
        functools.partial(plane_kernel, slabs, planes),
        out_shape=(shape_of(rows, LANES), shape_of(8, LANES)),
        in_specs=[VMEM] * 4,
        out_specs=(VMEM, VMEM),
        scratch_shapes=[pltpu.VMEM((2 * planes * length, NY), BF16)] * 2,
        compiler_params=PARAMS,
        name="plane_filter",
    )(widened(got), hat, jnp.asarray(halves(y_table(), y_table().T)), jnp.asarray(halves(*x_tables(slabs))))
    back, near = lax.optimization_barrier((exchanged(back, 4 * parts), near))

    pot = pl.pallas_call(
        functools.partial(potential_kernel, slabs),
        out_shape=(grid,) * 4 + (shape_of(LANES, LANES, dtype=BF16),),
        in_specs=[VMEM] * 3,
        out_specs=(VMEM,) * 5,
        compiler_params=PARAMS,
        name="z_inverse",
    )(widened(back), exponent, jnp.asarray(halves(*inverse)))
    edge = to_other_tile(pot[4])

    def sample_scratch(width):
        return [pltpu.VMEM((ZROWS, LANES), F32), pltpu.VMEM((width * 8, LANES), F32)]

    sums = shape_of(PANELS, slots)
    others = pl.pallas_call(
        beside_sample_kernel,
        out_shape=(sums, sums),
        in_specs=[SMEM] * 2 + [VMEM] * 7,
        out_specs=(VMEM, VMEM),
        scratch_shapes=sample_scratch(2 * slots),
        compiler_params=PARAMS,
        name="beside_sample",
    )(odd, facts2, *pot[:4], edge, facts2, stk)
    second = to_second(others[1])
    first = to_first(others[0])
    own = pl.pallas_call(
        own_sample_kernel,
        out_shape=sums,
        in_specs=[SMEM] + [VMEM] * 7,
        out_specs=VMEM,
        scratch_shapes=sample_scratch(slots),
        compiler_params=PARAMS,
        name="own_sample",
    )(facts, *pot[:4], edge, facts, stk)
    return own + near + first + second


def solution(mesh):
    both = ("slab", "tile")
    in_specs = (
        P(None, both),
        P(both),
        P(both),
        P(both),
        P(),
        P(both, None),
        P(both, None),
        P(),
        P(both, None, None),
    )
    return jax.shard_map(
        functools.partial(body, mesh.shape["slab"], mesh.shape["tile"]),
        mesh=mesh,
        in_specs=in_specs,
        out_specs=P(None, both),
        check_vma=False,
    )
```

```python
import functools
import math

import jax
import jax.numpy as jnp
import ml_dtypes
import numpy as np
from jax import lax
from jax.experimental import pallas as pl
from jax.experimental.pallas import tpu as pltpu
from jax.sharding import PartitionSpec as P

PANELS = 64
POINTS = 512
NY = 256
NZ = 512
KS = 16
KN = 16
LANES = 128
ZROWS = NZ + 8
UNROLL = 16
HALF = NY // 2
SCALE_ROWS = 8
BOUND = 12.0
HEADROOM = 15.0
F32 = jnp.float32
BF16 = jnp.bfloat16
SMEM = pl.BlockSpec(memory_space=pltpu.SMEM)
VMEM = pl.BlockSpec(memory_space=pltpu.VMEM)
PARAMS = pltpu.CompilerParams(vmem_limit_bytes=48 * 1024 * 1024)


def halves(*tables):
    parts = []
    for table in tables:
        high = table.astype(ml_dtypes.bfloat16)
        parts += [high, (table - high.astype(np.float64)).astype(ml_dtypes.bfloat16)]
    return np.concatenate(parts, axis=0)


def z_tables(slabs, tiles):
    half = slabs // 2
    planes = NZ // (slabs * tiles) // 2
    plane = np.arange(planes + 1)[:, None, None]
    tile = np.arange(tiles)[None, :, None]
    slab = np.arange(half)[None, None, :]
    owner = slab * tiles + tile
    freq = (owner * 2 * planes + plane).reshape(-1)
    forward, inverse = [], []
    for parity in range(2):
        cell = np.arange(parity, NZ, 2) - 2
        angle = (freq[:, None] * cell[None, :] % NZ) * (2 * np.pi / NZ)
        forward.append(np.concatenate([np.cos(angle), -np.sin(angle)], axis=0))
        upper = (plane[:-1] + parity) % 2
        back = ((upper * half * tiles + owner) * 2 * planes + plane[:-1] + upper).reshape(-1)
        cell = np.arange(NZ // 2) - 2
        angle = (back[:, None] * cell[None, :] % NZ) * (2 * np.pi / NZ)
        weight = np.where(back == 0, 1.0, 2.0)[:, None] / NZ
        inverse.append(np.concatenate([weight * np.cos(angle), -weight * np.sin(angle)], axis=0).T)
    return forward, inverse


def y_table():
    angle = (np.arange(NY)[:, None] * np.arange(HALF + 1)[None, :] % NY) * (2 * np.pi / NY)
    return np.concatenate([np.cos(angle[:, :HALF]), np.cos(angle[:, HALF:]), np.sin(angle[:, 1:HALF])], axis=1)


def reversal():
    table = np.zeros((HALF, HALF), ml_dtypes.bfloat16)
    lane = np.arange(HALF)
    table[lane, (HALF - lane) % HALF] = 1
    return table


def x_tables(slabs):
    length = 4 * slabs
    cell = (np.arange(4)[:, None] + 4 * np.arange(slabs)[None, :]).reshape(-1)
    angle = (np.arange(length)[:, None] * cell[None, :] % length) * (2 * np.pi / length)
    cosine, sine = np.cos(angle), np.sin(angle)
    forward = np.block([[cosine, sine], [-sine, cosine]])
    inverse = np.block([[cosine.T, -sine.T], [sine.T, cosine.T]])
    return forward, inverse


def split(values):
    high = values.astype(BF16)
    return high, (values - high.astype(F32)).astype(BF16)


def dot(a, b):
    return jnp.dot(a, b, preferred_element_type=F32)


def dot3(a, b):
    return dot(a[0], b[0]) + (dot(a[0], b[1]) + dot(a[1], b[0]))


def lane_of(shape):
    return lax.broadcasted_iota(jnp.int32, shape, 1)


def by_kind(values, kinds):
    zero = jnp.zeros_like(values)
    return jnp.concatenate(
        [jnp.where(kinds == kind, values, zero) for kind in range(KS)], axis=0
    )


def footprints(packed, stk_ref, fp_ref, first):
    count = packed.shape[1]
    turned = jnp.transpose(packed.astype(F32))
    kinds = turned[:, PANELS + 2 : PANELS + 3]
    charges = jnp.concatenate([turned[:, :PANELS], turned[:, :PANELS]], axis=1)
    offset = kinds - jnp.where(lane_of((count, LANES)) < PANELS, 0.0, 1.0)
    spread = jnp.concatenate(
        [jnp.where(offset == kind, charges, 0.0).astype(BF16) for kind in range(0, KS, 2)], axis=1
    )
    result = dot(spread, stk_ref[...])
    for pair in range(4):
        part = result[:, pair * LANES : (pair + 1) * LANES]
        fp_ref[pl.ds(first * 8 + 2 * pair, count, stride=8), :] = part
        fp_ref[pl.ds(first * 8 + 2 * pair + 1, count, stride=8), :] = pltpu.roll(part, 64, 1)


def lane_in(plane, shape):
    return (lane_of(shape) - 8 * plane) & (LANES - 1)


def edge_codes(planes, shape):
    code = jnp.full(shape, 3, jnp.int32)
    for plane in planes:
        lane = lane_in(plane, shape)
        code = jnp.where(lane >= LANES - 2, 0, jnp.where(lane < 2, 1, code))
    return code


def scatter_columns(fp_ref, first, place_of, count, sets, planes):
    shape = (8, LANES)
    lanes = [lane_in(plane, shape) for plane in planes]
    codes = edge_codes(planes, shape)

    def step(index, carry):
        updates = []
        for inner in range(UNROLL):
            column = index * UNROLL + inner
            row, begin, edge, turn, _ = place_of(column)
            value = fp_ref[pl.ds(pl.multiple_of((first + column) * 8, 8), 8), :]
            turned = pltpu.roll(value, turn, 1)
            terms = [jnp.where(((lane - begin) & -8) == 0, turned, 0.0) for lane in lanes]
            terms.append(jnp.where(codes == edge, turned, 0.0))
            updates.append((pl.ds(row, 8), terms))
        for inner, (where, terms) in enumerate(updates):
            grids = sets[inner % 2]
            refs = [grids[plane] for plane in planes] + [grids[4]]
            sums = [ref[where, :] + term for ref, term in zip(refs, terms)]
            for ref, total in zip(refs, sums):
                ref[where, :] = total
        return carry

    lax.fori_loop(0, lax.shift_right_logical(count + UNROLL - 1, 4), step, 0)


def sample_columns(pot_refs, edge_ref, place_of, count, sp_ref, first, planes):
    shape = (8, LANES)
    lanes = [lane_in(plane, shape) for plane in planes]
    codes = edge_codes(planes, shape)

    def step(index, carry):
        results = []
        for inner in range(UNROLL):
            column = index * UNROLL + inner
            row, begin, edge, _, turn = place_of(column)
            where = pl.ds(row, 8)
            result = jnp.where(codes == edge, edge_ref[where, :], 0.0)
            for plane, lane in zip(planes, lanes):
                result = jnp.where(((lane - begin) & -8) == 0, pot_refs[plane][where, :], result)
            turned = pltpu.roll(result, turn, 1)
            results.append((pl.ds(pl.multiple_of((first + column) * 8, 8), 8), turned))
        for where, result in results:
            sp_ref[where, :] = result
        return carry

    lax.fori_loop(0, lax.shift_right_logical(count + UNROLL - 1, 4), step, 0)


def far_sums(sp_ref, kinds, stk_ref, first):
    count = kinds.shape[1]
    lane = lane_of((count, LANES))
    pairs = []
    for pair in range(4):
        even = sp_ref[pl.ds(first * 8 + 2 * pair, count, stride=8), :]
        odd = sp_ref[pl.ds(first * 8 + 2 * pair + 1, count, stride=8), :]
        pairs.append(jnp.where(lane < 64, even, pltpu.roll(odd, 64, 1)).astype(BF16))
    samples = jnp.concatenate(pairs, axis=1)
    sums = lax.dot_general(
        stk_ref[...], samples, (((1,), (1,)), ((), ())), preferred_element_type=F32
    )
    result = jnp.zeros((PANELS, count), F32)
    for kind in range(KS):
        result += jnp.where(kinds == kind, sums[kind * PANELS : (kind + 1) * PANELS, :], 0.0)
    return result


OWN = ((0, 1, 2, 3), 2)
BESIDE = (((0, 1), 6), ((2, 3), -2))


def place_in_facts(facts_ref, start=0):
    return lambda column: [facts_ref[row, start + column] for row in (0, 1, 4, 5, 6)]


def facts_of(packed_ref, row, shift_i):
    facts = packed_ref[row : row + 16, :].astype(F32).astype(jnp.int32)
    by, bz, kinds, live = (facts[index : index + 1, :] for index in range(4))
    begin = 4 * by - 2
    edge = jnp.where(by == 0, 0, jnp.where(by == NY // 8 - 1, 1, 2))
    turn = begin - 8 * shift_i
    rows = [4 * bz, begin, kinds, live, edge, turn & (LANES - 1), -turn & (LANES - 1), by]
    return jnp.concatenate(rows, axis=0)


def own_kernel(packed_ref, stencil_ref, *refs):
    grids, (stk_ref, out_facts, fp_ref, rows_ref, facts_ref, sems) = refs[:10], refs[10:]
    copy = pltpu.make_async_copy(stencil_ref, rows_ref, sems.at[0])
    copy.start()
    out_facts[...] = facts_of(packed_ref, PANELS, OWN[1])
    facts_copy = pltpu.make_async_copy(out_facts, facts_ref, sems.at[1])
    facts_copy.start()
    for ref in grids:
        ref[...] = jnp.zeros_like(ref)
    shape = (POINTS, POINTS)
    point = lax.broadcasted_iota(jnp.int32, shape, 0)
    target = (point & 7) * 64 + lax.shift_right_logical(point, 3)
    order = jnp.where(lane_of(shape) == target, 1.0, 0.0).astype(BF16)
    facts_copy.wait()
    copy.wait()
    stk_ref[...] = dot(rows_ref[...], order).astype(BF16)
    live = facts_ref[3, 0]

    @pl.when(live > LANES)
    def _():
        footprints(packed_ref[...], stk_ref, fp_ref, 0)

    @pl.when(live <= LANES)
    def _():
        footprints(packed_ref[:, 0:LANES], stk_ref, fp_ref, 0)

    scatter_columns(fp_ref, 0, place_in_facts(facts_ref), live, (grids[:5], grids[5:]), OWN[0])


def chunks_beside(facts_ref, slots):
    for first in range(0, slots, LANES):
        counts = [jnp.clip(facts_ref[3, side * slots] - first, 0, LANES) for side in range(2)]
        yield first, counts


def both_sides(ref, slots, first):
    return jnp.concatenate(
        [ref[:, side * slots + first : side * slots + first + LANES] for side in range(2)], axis=1
    )


def beside_kernel(odd_ref, own_ref, first_ref, second_ref, stk_ref, *refs):
    grids, (out_edge, out_facts, pool_ref, fp_ref, facts_ref, sem) = refs[10:20], refs[20:]
    height, slots = own_ref.shape
    before, after = pl.ds(0, height), pl.ds(2 * height, height)
    pool_ref[height : 2 * height, :] = own_ref[...]

    @pl.when(odd_ref[0] == 0)
    def _():
        pool_ref[after, :] = first_ref[...]
        pool_ref[before, :] = second_ref[...]

    @pl.when(odd_ref[0] != 0)
    def _():
        pool_ref[before, :] = first_ref[...]
        pool_ref[after, :] = second_ref[...]

    for side, (_, shift_i) in enumerate(BESIDE):
        out_facts[:, side * slots : (side + 1) * slots] = facts_of(pool_ref, 2 * side * height + PANELS, shift_i)
    copy = pltpu.make_async_copy(out_facts, facts_ref, sem)
    copy.start()

    def project(first):
        here = slice(first, first + LANES)
        packed = jnp.concatenate(
            [pool_ref[0:height, here], pool_ref[2 * height : 3 * height, here]], axis=1
        )
        footprints(packed, stk_ref, fp_ref, 2 * first)

    project(0)
    copy.wait()
    for first, counts in chunks_beside(facts_ref, slots):
        if first:
            @pl.when(counts[0] + counts[1] > 0)
            def _(first=first):
                project(first)

        for side, (planes, _) in enumerate(BESIDE):
            scatter_columns(fp_ref, 2 * first + side * LANES, place_in_facts(facts_ref, side * slots + first),
                            counts[side], (grids[:5], grids[5:]), planes)
    for ref, other in zip(grids[:5], grids[5:]):
        ref[...] += other[...]
        ref[0:8, :] += ref[NZ:ZROWS, :]
    edge_ref = grids[4]
    total = pltpu.roll(edge_ref[0:LANES, :], 2, 1)
    for block in range(1, 4):
        total += pltpu.roll(edge_ref[block * LANES : (block + 1) * LANES, :], 32 * block + 2, 1)
    out_edge[...] = total


def exponent_of(values):
    top = functools.reduce(jnp.maximum, [jnp.max(jnp.abs(v), axis=0, keepdims=True) for v in values])
    top = jnp.maximum(jnp.max(top, axis=1, keepdims=True), 2.0**-100)
    return jnp.ceil(jnp.log2(top)) - BOUND


def quarter(table_ref, index):
    rows = table_ref.shape[0] // 4
    return tuple(table_ref[part * rows : (part + 1) * rows, :] for part in (2 * index, 2 * index + 1))


def z_kernel(slabs, g0, g1, g2, g3, edge_ref, w_ref, out_ref, wide_ref):
    widen_edge(edge_ref, wide_ref)
    half = slabs // 2
    parts = NZ // (2 * slabs)
    planes = parts // 2
    stride = 4 * parts + SCALE_ROWS
    sums = []
    for parity in range(2):
        where = pl.ds(parity, NZ // 2, stride=2)
        columns = []
        for plane, grid in enumerate((g0, g1, g2, g3)):
            at_edge = edge_codes((plane,), (NZ // 2, LANES)) < 2
            values = grid[where, :] + jnp.where(at_edge, wide_ref[where, :], 0.0)
            columns.append(pltpu.roll(values, LANES - 8 * plane, 1) if plane else values)
        sums.append(dot3(quarter(w_ref, parity), split(jnp.concatenate(columns, axis=1))))
    results = (sums[0] + sums[1], sums[0] - sums[1])
    exponent = exponent_of(results)
    scale = jnp.exp2(-exponent)
    results = [result * scale for result in results]
    for upper, result in enumerate(results):
        for part in range(parts):
            index = part // planes * (planes + 1) + part % planes + upper
            for tile in range(2):
                rows = result[(index * 2 + tile) * half : (index * 2 + tile + 1) * half, :]
                start = (tile * slabs + upper * half) * stride + part
                for plane in range(4):
                    out_ref[pl.ds(start + plane * parts, half, stride=stride), :] = rows[
                        :, plane * LANES : (plane + 1) * LANES
                    ]
    for row in range(SCALE_ROWS):
        out_ref[pl.ds(4 * parts + row, 2 * slabs, stride=stride), :] = jnp.broadcast_to(
            exponent, (2 * slabs, LANES)
        )


def hat_kernel(planes, offset_ref, hat_ref, turn_ref, out_ref):
    length = hat_ref.shape[1]
    values = jnp.concatenate([hat_ref[offset_ref[0] + plane] for plane in range(planes)], axis=0)
    values = values * (1.0 / (length * NY))
    upper = values[:, HALF:]
    high, low = split(upper)
    rest = (upper - high.astype(F32) - low.astype(F32)).astype(BF16)
    turn = turn_ref[...]
    upper = dot(high, turn) + (dot(low, turn) + dot(rest, turn))
    for plane in range(planes):
        here = slice(plane * length, (plane + 1) * length)
        out_ref[plane] = jnp.concatenate([values[here, :HALF], upper[here, :]], axis=1)


def plane_kernel(slabs, planes, in_ref, hat_ref, y_ref, x_ref, out_ref, exponent_ref, ah_ref, al_ref):
    length = 4 * slabs
    rows = planes * length
    parts = 2 * planes
    stride = 4 * parts + SCALE_ROWS

    def pieces():
        for tile in range(2):
            for part in range(2):
                for xi in range(4):
                    for plane in range(planes):
                        yield tile, part, plane, xi

    scales = [
        jnp.exp2(in_ref[pl.ds(tile * slabs * stride + 4 * parts, slabs, stride=stride), :])
        for tile in range(2)
    ]
    for tile, part, plane, xi in pieces():
        start = tile * slabs * stride + xi * parts + part * planes + plane
        row = (part * planes + plane) * length + xi * slabs
        high, low = split(in_ref[pl.ds(start, slabs, stride=stride), :] * scales[tile])
        ah_ref[row : row + slabs, tile * LANES : (tile + 1) * LANES] = high
        al_ref[row : row + slabs, tile * LANES : (tile + 1) * LANES] = low
    first_lane = lane_of((rows, HALF)) == 0
    turned = dot3((ah_ref[...], al_ref[...]), (y_ref[0:NY, :], y_ref[NY : 2 * NY, :]))
    even = (turned[:rows, :HALF], turned[rows:, :HALF])
    odd = (turned[:rows, HALF:], turned[rows:, HALF:])
    zero_odd = [jnp.where(first_lane, 0.0, values) for values in odd]
    real = jnp.concatenate(
        [even[0] + zero_odd[1], jnp.where(first_lane, odd[0], even[0] - zero_odd[1])], axis=1
    )
    imag = jnp.concatenate(
        [even[1] - zero_odd[0], jnp.where(first_lane, odd[1], even[1] + zero_odd[0])], axis=1
    )
    size = 2 * length

    def along_x(values, first):
        high, low = split(values)
        table = x_ref[first * size : (first + 1) * size, :]
        rest = x_ref[(first + 1) * size : (first + 2) * size, :]
        both = dot(jnp.concatenate([table, table], axis=1), jnp.concatenate([high, low], axis=0))
        return both + dot(rest, high)

    for plane in range(planes):
        here = slice(plane * length, (plane + 1) * length)
        there = slice(rows + plane * length, rows + (plane + 1) * length)
        values = along_x(jnp.concatenate([real[here], imag[here]], axis=0), 0)
        values = values * jnp.concatenate([hat_ref[plane], hat_ref[plane]], axis=0)
        values = along_x(values, 2)
        low, high = values[:, :HALF], values[:, HALF:]
        lane = first_lane[:length]
        even_r = jnp.where(lane, low[:length], low[:length] + high[:length])
        even_i = jnp.where(lane, low[length:], low[length:] + high[length:])
        odd_r = jnp.where(lane, high[:length], high[length:] - low[length:])
        odd_i = jnp.where(lane, high[length:], low[:length] - high[:length])
        ah_ref[here, :], al_ref[here, :] = split(jnp.concatenate([even_r, odd_r], axis=1))
        ah_ref[there, :], al_ref[there, :] = split(jnp.concatenate([even_i, odd_i], axis=1))
    turned = dot3((ah_ref[...], al_ref[...]), (y_ref[2 * NY : 3 * NY, :], y_ref[3 * NY : 4 * NY, :]))
    tops = [
        jnp.max(in_ref[pl.ds(tile * slabs * stride + 4 * parts, slabs, stride=stride), :], axis=0, keepdims=True)
        for tile in range(2)
    ]
    exponent = jnp.broadcast_to(jnp.maximum(*tops) + BOUND - HEADROOM + math.ceil(math.log2(length * NY) / 2), (8, LANES))
    exponent_ref[...] = exponent
    scale = jnp.exp2(-exponent[0:1, 0:1])
    for tile, part, plane, xi in pieces():
        here = slice((part * planes + plane) * length + xi * slabs, (part * planes + plane) * length + (xi + 1) * slabs)
        start = tile * slabs * stride + xi * parts + part * planes + plane
        out_ref[pl.ds(start, slabs, stride=stride), :] = (
            turned[here, tile * LANES : (tile + 1) * LANES] * scale
        )


def potential_kernel(slabs, in_ref, exponent_ref, v_ref, p0, p1, p2, p3, edge_ref):
    half = slabs // 2
    parts = NZ // (2 * slabs)
    planes = parts // 2
    stride = 4 * parts
    sums = []
    for parity in range(2):
        columns = []
        for plane in range(4):
            rows = []
            for part in range(parts):
                upper = (part % planes + parity) % 2
                for tile in range(2):
                    start = (tile * slabs + upper * half) * stride + plane * parts + part
                    rows.append(in_ref[pl.ds(start, half, stride=stride), :])
            columns.append(jnp.concatenate(rows, axis=0))
        sums.append(dot3(quarter(v_ref, parity), split(jnp.concatenate(columns, axis=1))))
    scale = jnp.exp2(exponent_ref[0:1, 0:1])
    shape = (LANES, LANES)
    edges = [jnp.zeros(shape, F32)] * 4
    halves_of_z = [((sums[0] + sums[1]) * scale), ((sums[0] - sums[1]) * scale)]
    for plane, pot in enumerate((p0, p1, p2, p3)):
        at_edge = edge_codes((plane,), shape) < 2
        for upper in range(2):
            result = halves_of_z[upper][:, plane * LANES : (plane + 1) * LANES].astype(BF16).astype(F32)
            if plane:
                result = pltpu.roll(result, 8 * plane, 1)
            pot[upper * (NZ // 2) : (upper + 1) * (NZ // 2), :] = result
            for block in range(2):
                edges[2 * upper + block] = jnp.where(
                    at_edge, result[block * LANES : (block + 1) * LANES, :], edges[2 * upper + block]
                )
        pot[NZ:ZROWS, :] = pot[0:8, :]
    edge = pltpu.roll(edges[0], 2, 1)
    for block in range(1, 4):
        edge += pltpu.roll(edges[block], 32 * block + 2, 1)
    edge_ref[...] = edge.astype(BF16)


def widen_edge(edge_ref, wide_ref):
    for block in range(4):
        wide_ref[block * LANES : (block + 1) * LANES, :] = pltpu.roll(
            edge_ref[...].astype(F32), (LANES - 2 - 32 * block) % LANES, 1
        )
    wide_ref[NZ:ZROWS, :] = wide_ref[0:8, :]


def masked(values, live):
    return jnp.where(lane_of(values.shape) < live, values, 0.0)


def own_sample_kernel(facts_ref, p0, p1, p2, p3, edge_ref, kinds_ref, stk_ref, out_ref, wide_ref, sp_ref):
    widen_edge(edge_ref, wide_ref)
    live = facts_ref[3, 0]
    slots = kinds_ref.shape[1]
    sample_columns((p0, p1, p2, p3), wide_ref, place_in_facts(facts_ref), live, sp_ref, 0, OWN[0])

    @pl.when(live > LANES)
    def _():
        out_ref[...] = masked(far_sums(sp_ref, kinds_ref[2:3, :], stk_ref, 0), live)

    @pl.when(live <= LANES)
    def _():
        out_ref[:, 0:LANES] = masked(far_sums(sp_ref, kinds_ref[2:3, 0:LANES], stk_ref, 0), live)
        out_ref[:, LANES:slots] = jnp.zeros((PANELS, slots - LANES), F32)


def beside_sample_kernel(odd_ref, facts_ref, p0, p1, p2, p3, edge_ref, kinds_ref, stk_ref, out0, out1, wide_ref, sp_ref):
    widen_edge(edge_ref, wide_ref)
    slots = kinds_ref.shape[1] // 2
    outs = (out0, out1)
    for first, counts in chunks_beside(facts_ref, slots):
        here = slice(first, first + LANES)
        for side, (planes, _) in enumerate(BESIDE):
            sample_columns((p0, p1, p2, p3), wide_ref, place_in_facts(facts_ref, side * slots + first),
                           counts[side], sp_ref, 2 * first + side * LANES, planes)

        @pl.when(counts[0] + counts[1] > 0)
        def _(first=first, counts=counts, here=here):
            kinds = both_sides(kinds_ref.at[2:3, :], slots, first)
            result = far_sums(sp_ref, kinds, stk_ref, 2 * first)
            sums = [masked(result[:, side * LANES : (side + 1) * LANES], counts[side]) for side in range(2)]
            even = jnp.broadcast_to(odd_ref[0], sums[0].shape) == 0
            out0[:, here] = jnp.where(even, sums[1], sums[0])
            out1[:, here] = jnp.where(even, sums[0], sums[1])

        @pl.when(counts[0] + counts[1] <= 0)
        def _(here=here):
            for out in outs:
                out[:, here] = jnp.zeros((PANELS, LANES), F32)


def near_kernel(live_ref, here_ref, there_ref, source_ref, block_ref, table_ref, out_ref):
    live = live_ref[0]
    fanout, slots = source_ref.shape
    height = here_ref.shape[0] // 3
    pool = jnp.concatenate(
        [ref[step * height : step * height + PANELS, :] for step in range(3) for ref in (here_ref, there_ref)],
        axis=1,
    )
    total = pool.shape[1]
    for first in range(0, slots, LANES):
        where = slice(first, first + LANES)

        @pl.when(live > first)
        def _(where=where, first=first):
            index = lax.broadcasted_iota(jnp.int32, (total, LANES), 0)
            result = jnp.zeros((PANELS, LANES), F32)
            for j in range(fanout):
                chosen = jnp.where(index == source_ref[j : j + 1, where], 1.0, 0.0).astype(BF16)
                gathered = dot(pool, chosen)
                result += dot(
                    table_ref[...], by_kind(gathered, block_ref[j : j + 1, where]).astype(BF16)
                )
            column = first + lane_of((PANELS, LANES))
            out_ref[:, where] = jnp.where(column < live, result, 0.0)

        @pl.when(live <= first)
        def _(where=where):
            out_ref[:, where] = jnp.zeros((PANELS, LANES), F32)


def shape_of(*dims, dtype=F32):
    return jax.ShapeDtypeStruct(dims, dtype)


def body(slabs, tiles, charges, live_count, slot_brick, slot_stencil, stencils, near_source,
         near_block, near_blocks, kernel_hat):
    slots = charges.shape[1]
    owners = slabs * tiles
    planes = kernel_hat.shape[0] // 2
    length = kernel_hat.shape[1]
    parts = NZ // owners
    axes = ("tile", "slab")
    both = ("slab", "tile")

    def moved(values, step_of, swap=0):
        pairs = [
            (a * tiles + b, (a + step_of(a)) % slabs * tiles + (b + swap) % tiles)
            for a in range(slabs)
            for b in range(tiles)
        ]
        return lax.ppermute(values, both, pairs)

    def to_first(values):
        return moved(values, lambda a: 1 - 2 * (a % 2))

    def to_second(values):
        return moved(values, lambda a: 2 * (a % 2) - 1)

    def to_other_tile(values):
        return moved(values, lambda a: 0, 1)

    odd = (lax.axis_index("slab") % 2)[None]
    row = lax.broadcasted_iota(jnp.int32, (PANELS + 16, slots), 0)
    column = lax.broadcasted_iota(jnp.int32, (PANELS + 16, slots), 1)
    live = jnp.broadcast_to(live_count[0], row.shape)
    brick = jnp.broadcast_to(slot_brick[None, :], row.shape)
    facts = lax.shift_right_logical(brick, jnp.where(row == PANELS, 7, 0)) & (NZ // 4 - 1)
    facts = jnp.where(row == PANELS + 2, slot_stencil[None, :], jnp.where(row == PANELS + 3, live, facts))
    held = jnp.where(column < live, jnp.pad(charges, ((0, 16), (0, 0))), jnp.zeros((), BF16))
    packed = jnp.where(row < PANELS, held, facts.astype(BF16))
    from_second = to_second(packed)
    from_first = to_first(packed)

    grid = shape_of(ZROWS, LANES)
    *grids, stk, facts = pl.pallas_call(
        own_kernel,
        out_shape=(grid,) * 10 + (shape_of(KS * PANELS, POINTS, dtype=BF16), shape_of(8, slots, dtype=jnp.int32)),
        in_specs=[VMEM, pl.BlockSpec(memory_space=pl.ANY)],
        out_specs=(VMEM,) * 12,
        scratch_shapes=[
            pltpu.VMEM((slots * 8, LANES), F32),
            pltpu.VMEM((KS * PANELS, POINTS), BF16),
            pltpu.SMEM((8, slots), jnp.int32),
            pltpu.SemaphoreType.DMA((2,)),
        ],
        compiler_params=PARAMS,
        name="own_scatter",
    )(packed, stencils.reshape(KS * PANELS, POINTS))

    g = pl.pallas_call(
        beside_kernel,
        out_shape=(grid,) * 10
        + (
            shape_of(LANES, LANES),
            shape_of(8, 2 * slots, dtype=jnp.int32),
            shape_of(3 * (PANELS + 16), slots, dtype=BF16),
        ),
        in_specs=[SMEM] + [VMEM] * 14,
        out_specs=(VMEM,) * 13,
        scratch_shapes=[
            pltpu.VMEM((2 * slots * 8, LANES), F32),
            pltpu.SMEM((8, 2 * slots), jnp.int32),
            pltpu.SemaphoreType.DMA,
        ],
        input_output_aliases={5 + index: index for index in range(10)},
        compiler_params=PARAMS,
        name="beside_scatter",
    )(odd, packed, from_first, from_second, stk, *grids)
    facts2 = g[11]
    edge = to_other_tile(g[10])

    forward, inverse = z_tables(slabs, tiles)
    rows = owners * (4 * parts + SCALE_ROWS)
    sent = pl.pallas_call(
        functools.partial(z_kernel, slabs),
        out_shape=shape_of(rows, LANES),
        in_specs=[VMEM] * 6,
        out_specs=VMEM,
        scratch_shapes=[pltpu.VMEM((ZROWS, LANES), F32)],
        compiler_params=PARAMS,
        name="z_forward",
    )(*g[:4], edge, jnp.asarray(halves(*forward)))

    def exchanged(values, kept):
        values = values.reshape(owners, -1, LANES)[:, :kept].astype(jnp.float16)
        values = lax.all_to_all(values, axes, 0, 0, tiled=True)
        return values

    def widened(values):
        return values.astype(F32).reshape(-1, LANES)

    hat, sent = lax.optimization_barrier((kernel_hat, sent))
    got = exchanged(sent, 4 * parts + SCALE_ROWS)
    me = lax.axis_index("slab") * tiles + lax.axis_index("tile")
    offset = (me >= owners // 2).astype(jnp.int32)[None]
    hat = pl.pallas_call(
        functools.partial(hat_kernel, planes),
        out_shape=shape_of(planes, length, NY),
        in_specs=[SMEM] + [VMEM] * 2,
        out_specs=VMEM,
        compiler_params=PARAMS,
        name="hat_order",
    )(offset, hat, jnp.asarray(reversal()))

    got, hat = lax.optimization_barrier((got, hat))
    pool = (g[12], to_other_tile(g[12]))
    direction = near_source // slots
    pool_index = (direction // 3 * 2 + (direction % 3 != 1).astype(jnp.int32)) * slots + near_source % slots
    near = pl.pallas_call(
        near_kernel,
        out_shape=shape_of(PANELS, slots),
        in_specs=[SMEM] + [VMEM] * 5,
        out_specs=VMEM,
        compiler_params=PARAMS,
        name="near_field",
    )(live_count, *pool, pool_index.T, near_block.T, near_blocks.reshape(PANELS, KN * PANELS))

    back, exponent = pl.pallas_call(
        functools.partial(plane_kernel, slabs, planes),
        out_shape=(shape_of(rows, LANES), shape_of(8, LANES)),
        in_specs=[VMEM] * 4,
        out_specs=(VMEM, VMEM),
        scratch_shapes=[pltpu.VMEM((2 * planes * length, NY), BF16)] * 2,
        compiler_params=PARAMS,
        name="plane_filter",
    )(widened(got), hat, jnp.asarray(halves(y_table(), y_table().T)), jnp.asarray(halves(*x_tables(slabs))))
    back, near = lax.optimization_barrier((exchanged(back, 4 * parts), near))

    pot = pl.pallas_call(
        functools.partial(potential_kernel, slabs),
        out_shape=(grid,) * 4 + (shape_of(LANES, LANES, dtype=BF16),),
        in_specs=[VMEM] * 3,
        out_specs=(VMEM,) * 5,
        compiler_params=PARAMS,
        name="z_inverse",
    )(widened(back), exponent, jnp.asarray(halves(*inverse)))
    edge = to_other_tile(pot[4])

    def sample_scratch(width):
        return [pltpu.VMEM((ZROWS, LANES), F32), pltpu.VMEM((width * 8, LANES), F32)]

    sums = shape_of(PANELS, slots)
    others = pl.pallas_call(
        beside_sample_kernel,
        out_shape=(sums, sums),
        in_specs=[SMEM] * 2 + [VMEM] * 7,
        out_specs=(VMEM, VMEM),
        scratch_shapes=sample_scratch(2 * slots),
        compiler_params=PARAMS,
        name="beside_sample",
    )(odd, facts2, *pot[:4], edge, facts2, stk)
    second = to_second(others[1])
    first = to_first(others[0])
    own = pl.pallas_call(
        own_sample_kernel,
        out_shape=sums,
        in_specs=[SMEM] + [VMEM] * 7,
        out_specs=VMEM,
        scratch_shapes=sample_scratch(slots),
        compiler_params=PARAMS,
        name="own_sample",
    )(facts, *pot[:4], edge, facts, stk)
    return own + near + first + second


def solution(mesh):
    both = ("slab", "tile")
    in_specs = (
        P(None, both),
        P(both),
        P(both),
        P(both),
        P(),
        P(both, None),
        P(both, None),
        P(),
        P(both, None, None),
    )
    return jax.shard_map(
        functools.partial(body, mesh.shape["slab"], mesh.shape["tile"]),
        mesh=mesh,
        in_specs=in_specs,
        out_specs=P(None, both),
        check_vma=False,
    )
```

```python
import functools
import math

import jax
import jax.numpy as jnp
import ml_dtypes
import numpy as np
from jax import lax
from jax.experimental import pallas as pl
from jax.experimental.pallas import tpu as pltpu
from jax.sharding import PartitionSpec as P

PANELS = 64
POINTS = 512
NY = 256
NZ = 512
KS = 16
KN = 16
LANES = 128
ZROWS = NZ + 8
UNROLL = 32
HALF = NY // 2
SCALE_ROWS = 8
BOUND = 12.0
HEADROOM = 15.0
F32 = jnp.float32
BF16 = jnp.bfloat16
SMEM = pl.BlockSpec(memory_space=pltpu.SMEM)
VMEM = pl.BlockSpec(memory_space=pltpu.VMEM)
PARAMS = pltpu.CompilerParams(vmem_limit_bytes=48 * 1024 * 1024)


def halves(*tables):
    parts = []
    for table in tables:
        high = table.astype(ml_dtypes.bfloat16)
        parts += [high, (table - high.astype(np.float64)).astype(ml_dtypes.bfloat16)]
    return np.concatenate(parts, axis=0)


def z_tables(slabs, tiles):
    half = slabs // 2
    planes = NZ // (slabs * tiles) // 2
    plane = np.arange(planes + 1)[:, None, None]
    tile = np.arange(tiles)[None, :, None]
    slab = np.arange(half)[None, None, :]
    owner = slab * tiles + tile
    freq = (owner * 2 * planes + plane).reshape(-1)
    forward, inverse = [], []
    for parity in range(2):
        cell = np.arange(parity, NZ, 2) - 2
        angle = (freq[:, None] * cell[None, :] % NZ) * (2 * np.pi / NZ)
        forward.append(np.concatenate([np.cos(angle), -np.sin(angle)], axis=0))
        upper = (plane[:-1] + parity) % 2
        back = ((upper * half * tiles + owner) * 2 * planes + plane[:-1] + upper).reshape(-1)
        cell = np.arange(NZ // 2) - 2
        angle = (back[:, None] * cell[None, :] % NZ) * (2 * np.pi / NZ)
        weight = np.where(back == 0, 1.0, 2.0)[:, None] / NZ
        inverse.append(np.concatenate([weight * np.cos(angle), -weight * np.sin(angle)], axis=0).T)
    return forward, inverse


def y_table():
    angle = (np.arange(NY)[:, None] * np.arange(HALF + 1)[None, :] % NY) * (2 * np.pi / NY)
    return np.concatenate([np.cos(angle[:, :HALF]), np.cos(angle[:, HALF:]), np.sin(angle[:, 1:HALF])], axis=1)


def reversal():
    table = np.zeros((HALF, HALF), ml_dtypes.bfloat16)
    lane = np.arange(HALF)
    table[lane, (HALF - lane) % HALF] = 1
    return table


def x_tables(slabs):
    length = 4 * slabs
    cell = (np.arange(4)[:, None] + 4 * np.arange(slabs)[None, :]).reshape(-1)
    angle = (np.arange(length)[:, None] * cell[None, :] % length) * (2 * np.pi / length)
    cosine, sine = np.cos(angle), np.sin(angle)
    forward = np.block([[cosine, sine], [-sine, cosine]])
    inverse = np.block([[cosine.T, -sine.T], [sine.T, cosine.T]])
    return forward, inverse


def split(values):
    high = values.astype(BF16)
    return high, (values - high.astype(F32)).astype(BF16)


def dot(a, b):
    return jnp.dot(a, b, preferred_element_type=F32)


def dot3(a, b):
    return dot(a[0], b[0]) + (dot(a[0], b[1]) + dot(a[1], b[0]))


def lane_of(shape):
    return lax.broadcasted_iota(jnp.int32, shape, 1)


def by_kind(values, kinds):
    zero = jnp.zeros_like(values)
    return jnp.concatenate(
        [jnp.where(kinds == kind, values, zero) for kind in range(KS)], axis=0
    )


def footprints(packed, stk_ref, fp_ref, first):
    count = packed.shape[1]
    turned = jnp.transpose(packed.astype(F32))
    kinds = turned[:, PANELS + 2 : PANELS + 3]
    charges = jnp.concatenate([turned[:, :PANELS], turned[:, :PANELS]], axis=1)
    offset = kinds - jnp.where(lane_of((count, LANES)) < PANELS, 0.0, 1.0)
    spread = jnp.concatenate(
        [jnp.where(offset == kind, charges, 0.0).astype(BF16) for kind in range(0, KS, 2)], axis=1
    )
    result = dot(spread, stk_ref[...])
    for pair in range(4):
        part = result[:, pair * LANES : (pair + 1) * LANES]
        fp_ref[pl.ds(first * 8 + 2 * pair, count, stride=8), :] = part
        fp_ref[pl.ds(first * 8 + 2 * pair + 1, count, stride=8), :] = pltpu.roll(part, 64, 1)


def lane_in(plane, shape):
    return (lane_of(shape) - 8 * plane) & (LANES - 1)


def edge_codes(planes, shape):
    code = jnp.full(shape, 3, jnp.int32)
    for plane in planes:
        lane = lane_in(plane, shape)
        code = jnp.where(lane >= LANES - 2, 0, jnp.where(lane < 2, 1, code))
    return code


def scatter_columns(fp_ref, first, place_of, count, grids, edge_ref, planes):
    shape = (8, LANES)
    lanes = [lane_in(plane, shape) for plane in planes]
    codes = edge_codes(planes, shape)

    def step(index, carry):
        updates = []
        for inner in range(UNROLL):
            column = index * UNROLL + inner
            row, begin, edge, turn, _ = place_of(column)
            value = fp_ref[pl.ds(pl.multiple_of((first + column) * 8, 8), 8), :]
            turned = pltpu.roll(value, turn, 1)
            terms = [jnp.where(((lane - begin) & -8) == 0, turned, 0.0) for lane in lanes]
            terms.append(jnp.where(codes == edge, turned, 0.0))
            updates.append((pl.ds(row, 8), terms))
        refs = [grids[plane] for plane in planes] + [edge_ref]
        for where, terms in updates:
            sums = [ref[where, :] + term for ref, term in zip(refs, terms)]
            for ref, total in zip(refs, sums):
                ref[where, :] = total
        return carry

    lax.fori_loop(0, lax.shift_right_logical(count + UNROLL - 1, 5), step, 0)


def sample_columns(pot_refs, edge_ref, place_of, count, sp_ref, first, planes):
    shape = (8, LANES)
    lanes = [lane_in(plane, shape) for plane in planes]
    codes = edge_codes(planes, shape)

    def step(index, carry):
        results = []
        for inner in range(UNROLL):
            column = index * UNROLL + inner
            row, begin, edge, _, turn = place_of(column)
            where = pl.ds(row, 8)
            result = jnp.where(codes == edge, edge_ref[where, :], 0.0)
            for plane, lane in zip(planes, lanes):
                result = jnp.where(((lane - begin) & -8) == 0, pot_refs[plane][where, :], result)
            turned = pltpu.roll(result, turn, 1)
            results.append((pl.ds(pl.multiple_of((first + column) * 8, 8), 8), turned))
        for where, result in results:
            sp_ref[where, :] = result
        return carry

    lax.fori_loop(0, lax.shift_right_logical(count + UNROLL - 1, 5), step, 0)


def far_sums(sp_ref, kinds, stk_ref, first):
    count = kinds.shape[1]
    lane = lane_of((count, LANES))
    pairs = []
    for pair in range(4):
        even = sp_ref[pl.ds(first * 8 + 2 * pair, count, stride=8), :]
        odd = sp_ref[pl.ds(first * 8 + 2 * pair + 1, count, stride=8), :]
        pairs.append(jnp.where(lane < 64, even, pltpu.roll(odd, 64, 1)).astype(BF16))
    samples = jnp.concatenate(pairs, axis=1)
    sums = lax.dot_general(
        stk_ref[...], samples, (((1,), (1,)), ((), ())), preferred_element_type=F32
    )
    result = jnp.zeros((PANELS, count), F32)
    for kind in range(KS):
        result += jnp.where(kinds == kind, sums[kind * PANELS : (kind + 1) * PANELS, :], 0.0)
    return result


OWN = ((0, 1, 2, 3), 2)
BESIDE = (((0, 1), 6), ((2, 3), -2))


def place_in_facts(facts_ref, start=0):
    return lambda column: [facts_ref[row, start + column] for row in (0, 1, 4, 5, 6)]


def facts_of(packed_ref, row, shift_i):
    facts = packed_ref[row : row + 16, :].astype(F32).astype(jnp.int32)
    by, bz, kinds, live = (facts[index : index + 1, :] for index in range(4))
    begin = 4 * by - 2
    edge = jnp.where(by == 0, 0, jnp.where(by == NY // 8 - 1, 1, 2))
    turn = begin - 8 * shift_i
    rows = [4 * bz, begin, kinds, live, edge, turn & (LANES - 1), -turn & (LANES - 1), by]
    return jnp.concatenate(rows, axis=0)


def own_kernel(packed_ref, stencil_ref,
               g0, g1, g2, g3, edge_ref, stk_ref, out_facts, fp_ref, rows_ref, facts_ref, sems):
    copy = pltpu.make_async_copy(stencil_ref, rows_ref, sems.at[0])
    copy.start()
    out_facts[...] = facts_of(packed_ref, PANELS, OWN[1])
    facts_copy = pltpu.make_async_copy(out_facts, facts_ref, sems.at[1])
    facts_copy.start()
    for ref in (g0, g1, g2, g3, edge_ref):
        ref[...] = jnp.zeros_like(ref)
    shape = (POINTS, POINTS)
    point = lax.broadcasted_iota(jnp.int32, shape, 0)
    target = (point & 7) * 64 + lax.shift_right_logical(point, 3)
    order = jnp.where(lane_of(shape) == target, 1.0, 0.0).astype(BF16)
    facts_copy.wait()
    copy.wait()
    stk_ref[...] = dot(rows_ref[...], order).astype(BF16)
    live = facts_ref[3, 0]

    @pl.when(live > LANES)
    def _():
        footprints(packed_ref[...], stk_ref, fp_ref, 0)

    @pl.when(live <= LANES)
    def _():
        footprints(packed_ref[:, 0:LANES], stk_ref, fp_ref, 0)

    scatter_columns(fp_ref, 0, place_in_facts(facts_ref), live, (g0, g1, g2, g3), edge_ref, OWN[0])


def chunks_beside(facts_ref, slots):
    for first in range(0, slots, LANES):
        counts = [jnp.clip(facts_ref[3, side * slots] - first, 0, LANES) for side in range(2)]
        yield first, counts


def both_sides(ref, slots, first):
    return jnp.concatenate(
        [ref[:, side * slots + first : side * slots + first + LANES] for side in range(2)], axis=1
    )


def beside_kernel(odd_ref, own_ref, first_ref, second_ref, stk_ref, i0, i1, i2, i3, iedge,
                  g0, g1, g2, g3, edge_ref, out_edge, out_facts, pool_ref, fp_ref, facts_ref, sem):
    height, slots = own_ref.shape
    before, after = pl.ds(0, height), pl.ds(2 * height, height)
    pool_ref[height : 2 * height, :] = own_ref[...]

    @pl.when(odd_ref[0] == 0)
    def _():
        pool_ref[after, :] = first_ref[...]
        pool_ref[before, :] = second_ref[...]

    @pl.when(odd_ref[0] != 0)
    def _():
        pool_ref[before, :] = first_ref[...]
        pool_ref[after, :] = second_ref[...]

    for side, (_, shift_i) in enumerate(BESIDE):
        out_facts[:, side * slots : (side + 1) * slots] = facts_of(pool_ref, 2 * side * height + PANELS, shift_i)
    copy = pltpu.make_async_copy(out_facts, facts_ref, sem)
    copy.start()

    def project(first):
        here = slice(first, first + LANES)
        packed = jnp.concatenate(
            [pool_ref[0:height, here], pool_ref[2 * height : 3 * height, here]], axis=1
        )
        footprints(packed, stk_ref, fp_ref, 2 * first)

    project(0)
    copy.wait()
    for first, counts in chunks_beside(facts_ref, slots):
        if first:
            @pl.when(counts[0] + counts[1] > 0)
            def _(first=first):
                project(first)

        for side, (planes, _) in enumerate(BESIDE):
            scatter_columns(fp_ref, 2 * first + side * LANES, place_in_facts(facts_ref, side * slots + first),
                            counts[side], (g0, g1, g2, g3), edge_ref, planes)
    for ref in (g0, g1, g2, g3, edge_ref):
        ref[0:8, :] += ref[NZ:ZROWS, :]
    total = pltpu.roll(edge_ref[0:LANES, :], 2, 1)
    for block in range(1, 4):
        total += pltpu.roll(edge_ref[block * LANES : (block + 1) * LANES, :], 32 * block + 2, 1)
    out_edge[...] = total


def exponent_of(values):
    top = functools.reduce(jnp.maximum, [jnp.max(jnp.abs(v), axis=0, keepdims=True) for v in values])
    top = jnp.maximum(jnp.max(top, axis=1, keepdims=True), 2.0**-100)
    return jnp.ceil(jnp.log2(top)) - BOUND


def quarter(table_ref, index):
    rows = table_ref.shape[0] // 4
    return tuple(table_ref[part * rows : (part + 1) * rows, :] for part in (2 * index, 2 * index + 1))


def z_kernel(slabs, g0, g1, g2, g3, edge_ref, w_ref, out_ref, wide_ref):
    widen_edge(edge_ref, wide_ref)
    half = slabs // 2
    parts = NZ // (2 * slabs)
    planes = parts // 2
    stride = 4 * parts + SCALE_ROWS
    sums = []
    for parity in range(2):
        where = pl.ds(parity, NZ // 2, stride=2)
        columns = []
        for plane, grid in enumerate((g0, g1, g2, g3)):
            at_edge = edge_codes((plane,), (NZ // 2, LANES)) < 2
            values = grid[where, :] + jnp.where(at_edge, wide_ref[where, :], 0.0)
            columns.append(pltpu.roll(values, LANES - 8 * plane, 1) if plane else values)
        sums.append(dot3(quarter(w_ref, parity), split(jnp.concatenate(columns, axis=1))))
    results = (sums[0] + sums[1], sums[0] - sums[1])
    exponent = exponent_of(results)
    scale = jnp.exp2(-exponent)
    results = [result * scale for result in results]
    for upper, result in enumerate(results):
        for part in range(parts):
            index = part // planes * (planes + 1) + part % planes + upper
            for tile in range(2):
                rows = result[(index * 2 + tile) * half : (index * 2 + tile + 1) * half, :]
                start = (tile * slabs + upper * half) * stride + part
                for plane in range(4):
                    out_ref[pl.ds(start + plane * parts, half, stride=stride), :] = rows[
                        :, plane * LANES : (plane + 1) * LANES
                    ]
    for row in range(SCALE_ROWS):
        out_ref[pl.ds(4 * parts + row, 2 * slabs, stride=stride), :] = jnp.broadcast_to(
            exponent, (2 * slabs, LANES)
        )


def hat_kernel(planes, offset_ref, hat_ref, turn_ref, out_ref):
    length = hat_ref.shape[1]
    values = jnp.concatenate([hat_ref[offset_ref[0] + plane] for plane in range(planes)], axis=0)
    values = values * (1.0 / (length * NY))
    upper = values[:, HALF:]
    high, low = split(upper)
    rest = (upper - high.astype(F32) - low.astype(F32)).astype(BF16)
    turn = turn_ref[...]
    upper = dot(high, turn) + (dot(low, turn) + dot(rest, turn))
    for plane in range(planes):
        here = slice(plane * length, (plane + 1) * length)
        out_ref[plane] = jnp.concatenate([values[here, :HALF], upper[here, :]], axis=1)


def plane_kernel(slabs, planes, in_ref, hat_ref, y_ref, x_ref, out_ref, exponent_ref, ah_ref, al_ref):
    length = 4 * slabs
    rows = planes * length
    parts = 2 * planes
    stride = 4 * parts + SCALE_ROWS

    def pieces():
        for tile in range(2):
            for part in range(2):
                for xi in range(4):
                    for plane in range(planes):
                        yield tile, part, plane, xi

    scales = [
        jnp.exp2(in_ref[pl.ds(tile * slabs * stride + 4 * parts, slabs, stride=stride), :])
        for tile in range(2)
    ]
    for tile, part, plane, xi in pieces():
        start = tile * slabs * stride + xi * parts + part * planes + plane
        row = (part * planes + plane) * length + xi * slabs
        high, low = split(in_ref[pl.ds(start, slabs, stride=stride), :] * scales[tile])
        ah_ref[row : row + slabs, tile * LANES : (tile + 1) * LANES] = high
        al_ref[row : row + slabs, tile * LANES : (tile + 1) * LANES] = low
    first_lane = lane_of((rows, HALF)) == 0
    turned = dot3((ah_ref[...], al_ref[...]), (y_ref[0:NY, :], y_ref[NY : 2 * NY, :]))
    even = (turned[:rows, :HALF], turned[rows:, :HALF])
    odd = (turned[:rows, HALF:], turned[rows:, HALF:])
    zero_odd = [jnp.where(first_lane, 0.0, values) for values in odd]
    real = jnp.concatenate(
        [even[0] + zero_odd[1], jnp.where(first_lane, odd[0], even[0] - zero_odd[1])], axis=1
    )
    imag = jnp.concatenate(
        [even[1] - zero_odd[0], jnp.where(first_lane, odd[1], even[1] + zero_odd[0])], axis=1
    )
    size = 2 * length

    def along_x(values, first):
        high, low = split(values)
        table = x_ref[first * size : (first + 1) * size, :]
        rest = x_ref[(first + 1) * size : (first + 2) * size, :]
        both = dot(jnp.concatenate([table, table], axis=1), jnp.concatenate([high, low], axis=0))
        return both + dot(rest, high)

    for plane in range(planes):
        here = slice(plane * length, (plane + 1) * length)
        there = slice(rows + plane * length, rows + (plane + 1) * length)
        values = along_x(jnp.concatenate([real[here], imag[here]], axis=0), 0)
        values = values * jnp.concatenate([hat_ref[plane], hat_ref[plane]], axis=0)
        values = along_x(values, 2)
        low, high = values[:, :HALF], values[:, HALF:]
        lane = first_lane[:length]
        even_r = jnp.where(lane, low[:length], low[:length] + high[:length])
        even_i = jnp.where(lane, low[length:], low[length:] + high[length:])
        odd_r = jnp.where(lane, high[:length], high[length:] - low[length:])
        odd_i = jnp.where(lane, high[length:], low[:length] - high[:length])
        ah_ref[here, :], al_ref[here, :] = split(jnp.concatenate([even_r, odd_r], axis=1))
        ah_ref[there, :], al_ref[there, :] = split(jnp.concatenate([even_i, odd_i], axis=1))
    turned = dot3((ah_ref[...], al_ref[...]), (y_ref[2 * NY : 3 * NY, :], y_ref[3 * NY : 4 * NY, :]))
    tops = [
        jnp.max(in_ref[pl.ds(tile * slabs * stride + 4 * parts, slabs, stride=stride), :], axis=0, keepdims=True)
        for tile in range(2)
    ]
    exponent = jnp.broadcast_to(jnp.maximum(*tops) + BOUND - HEADROOM + math.ceil(math.log2(length * NY) / 2), (8, LANES))
    exponent_ref[...] = exponent
    scale = jnp.exp2(-exponent[0:1, 0:1])
    for tile, part, plane, xi in pieces():
        here = slice((part * planes + plane) * length + xi * slabs, (part * planes + plane) * length + (xi + 1) * slabs)
        start = tile * slabs * stride + xi * parts + part * planes + plane
        out_ref[pl.ds(start, slabs, stride=stride), :] = (
            turned[here, tile * LANES : (tile + 1) * LANES] * scale
        )


def potential_kernel(slabs, in_ref, exponent_ref, v_ref, p0, p1, p2, p3, edge_ref):
    half = slabs // 2
    parts = NZ // (2 * slabs)
    planes = parts // 2
    stride = 4 * parts
    sums = []
    for parity in range(2):
        columns = []
        for plane in range(4):
            rows = []
            for part in range(parts):
                upper = (part % planes + parity) % 2
                for tile in range(2):
                    start = (tile * slabs + upper * half) * stride + plane * parts + part
                    rows.append(in_ref[pl.ds(start, half, stride=stride), :])
            columns.append(jnp.concatenate(rows, axis=0))
        sums.append(dot3(quarter(v_ref, parity), split(jnp.concatenate(columns, axis=1))))
    scale = jnp.exp2(exponent_ref[0:1, 0:1])
    shape = (LANES, LANES)
    edges = [jnp.zeros(shape, F32)] * 4
    halves_of_z = [((sums[0] + sums[1]) * scale), ((sums[0] - sums[1]) * scale)]
    for plane, pot in enumerate((p0, p1, p2, p3)):
        at_edge = edge_codes((plane,), shape) < 2
        for upper in range(2):
            result = halves_of_z[upper][:, plane * LANES : (plane + 1) * LANES].astype(BF16).astype(F32)
            if plane:
                result = pltpu.roll(result, 8 * plane, 1)
            pot[upper * (NZ // 2) : (upper + 1) * (NZ // 2), :] = result
            for block in range(2):
                edges[2 * upper + block] = jnp.where(
                    at_edge, result[block * LANES : (block + 1) * LANES, :], edges[2 * upper + block]
                )
        pot[NZ:ZROWS, :] = pot[0:8, :]
    edge = pltpu.roll(edges[0], 2, 1)
    for block in range(1, 4):
        edge += pltpu.roll(edges[block], 32 * block + 2, 1)
    edge_ref[...] = edge.astype(BF16)


def widen_edge(edge_ref, wide_ref):
    for block in range(4):
        wide_ref[block * LANES : (block + 1) * LANES, :] = pltpu.roll(
            edge_ref[...].astype(F32), (LANES - 2 - 32 * block) % LANES, 1
        )
    wide_ref[NZ:ZROWS, :] = wide_ref[0:8, :]


def masked(values, live):
    return jnp.where(lane_of(values.shape) < live, values, 0.0)


def own_sample_kernel(facts_ref, p0, p1, p2, p3, edge_ref, kinds_ref, stk_ref, out_ref, wide_ref, sp_ref):
    widen_edge(edge_ref, wide_ref)
    live = facts_ref[3, 0]
    slots = kinds_ref.shape[1]
    sample_columns((p0, p1, p2, p3), wide_ref, place_in_facts(facts_ref), live, sp_ref, 0, OWN[0])

    @pl.when(live > LANES)
    def _():
        out_ref[...] = masked(far_sums(sp_ref, kinds_ref[2:3, :], stk_ref, 0), live)

    @pl.when(live <= LANES)
    def _():
        out_ref[:, 0:LANES] = masked(far_sums(sp_ref, kinds_ref[2:3, 0:LANES], stk_ref, 0), live)
        out_ref[:, LANES:slots] = jnp.zeros((PANELS, slots - LANES), F32)


def beside_sample_kernel(odd_ref, facts_ref, p0, p1, p2, p3, edge_ref, kinds_ref, stk_ref, out0, out1, wide_ref, sp_ref):
    widen_edge(edge_ref, wide_ref)
    slots = kinds_ref.shape[1] // 2
    outs = (out0, out1)
    for first, counts in chunks_beside(facts_ref, slots):
        here = slice(first, first + LANES)
        for side, (planes, _) in enumerate(BESIDE):
            sample_columns((p0, p1, p2, p3), wide_ref, place_in_facts(facts_ref, side * slots + first),
                           counts[side], sp_ref, 2 * first + side * LANES, planes)

        @pl.when(counts[0] + counts[1] > 0)
        def _(first=first, counts=counts, here=here):
            kinds = both_sides(kinds_ref.at[2:3, :], slots, first)
            result = far_sums(sp_ref, kinds, stk_ref, 2 * first)
            sums = [masked(result[:, side * LANES : (side + 1) * LANES], counts[side]) for side in range(2)]
            even = jnp.broadcast_to(odd_ref[0], sums[0].shape) == 0
            out0[:, here] = jnp.where(even, sums[1], sums[0])
            out1[:, here] = jnp.where(even, sums[0], sums[1])

        @pl.when(counts[0] + counts[1] <= 0)
        def _(here=here):
            for out in outs:
                out[:, here] = jnp.zeros((PANELS, LANES), F32)


def near_kernel(live_ref, here_ref, there_ref, source_ref, block_ref, table_ref, out_ref):
    live = live_ref[0]
    fanout, slots = source_ref.shape
    height = here_ref.shape[0] // 3
    pool = jnp.concatenate(
        [ref[step * height : step * height + PANELS, :] for step in range(3) for ref in (here_ref, there_ref)],
        axis=1,
    )
    total = pool.shape[1]
    for first in range(0, slots, LANES):
        where = slice(first, first + LANES)

        @pl.when(live > first)
        def _(where=where, first=first):
            index = lax.broadcasted_iota(jnp.int32, (total, LANES), 0)
            result = jnp.zeros((PANELS, LANES), F32)
            for j in range(fanout):
                chosen = jnp.where(index == source_ref[j : j + 1, where], 1.0, 0.0).astype(BF16)
                gathered = dot(pool, chosen)
                result += dot(
                    table_ref[...], by_kind(gathered, block_ref[j : j + 1, where]).astype(BF16)
                )
            column = first + lane_of((PANELS, LANES))
            out_ref[:, where] = jnp.where(column < live, result, 0.0)

        @pl.when(live <= first)
        def _(where=where):
            out_ref[:, where] = jnp.zeros((PANELS, LANES), F32)


def shape_of(*dims, dtype=F32):
    return jax.ShapeDtypeStruct(dims, dtype)


def body(slabs, tiles, charges, live_count, slot_brick, slot_stencil, stencils, near_source,
         near_block, near_blocks, kernel_hat):
    slots = charges.shape[1]
    owners = slabs * tiles
    planes = kernel_hat.shape[0] // 2
    length = kernel_hat.shape[1]
    parts = NZ // owners
    axes = ("tile", "slab")
    both = ("slab", "tile")

    def moved(values, step_of, swap=0):
        pairs = [
            (a * tiles + b, (a + step_of(a)) % slabs * tiles + (b + swap) % tiles)
            for a in range(slabs)
            for b in range(tiles)
        ]
        return lax.ppermute(values, both, pairs)

    def to_first(values):
        return moved(values, lambda a: 1 - 2 * (a % 2))

    def to_second(values):
        return moved(values, lambda a: 2 * (a % 2) - 1)

    def to_other_tile(values):
        return moved(values, lambda a: 0, 1)

    odd = (lax.axis_index("slab") % 2)[None]
    row = lax.broadcasted_iota(jnp.int32, (PANELS + 16, slots), 0)
    column = lax.broadcasted_iota(jnp.int32, (PANELS + 16, slots), 1)
    live = jnp.broadcast_to(live_count[0], row.shape)
    brick = jnp.broadcast_to(slot_brick[None, :], row.shape)
    facts = lax.shift_right_logical(brick, jnp.where(row == PANELS, 7, 0)) & (NZ // 4 - 1)
    facts = jnp.where(row == PANELS + 2, slot_stencil[None, :], jnp.where(row == PANELS + 3, live, facts))
    held = jnp.where(column < live, jnp.pad(charges, ((0, 16), (0, 0))), jnp.zeros((), BF16))
    packed = jnp.where(row < PANELS, held, facts.astype(BF16))
    from_second = to_second(packed)
    from_first = to_first(packed)

    grid = shape_of(ZROWS, LANES)
    *grids, stk, facts = pl.pallas_call(
        own_kernel,
        out_shape=(grid,) * 5 + (shape_of(KS * PANELS, POINTS, dtype=BF16), shape_of(8, slots, dtype=jnp.int32)),
        in_specs=[VMEM, pl.BlockSpec(memory_space=pl.ANY)],
        out_specs=(VMEM,) * 7,
        scratch_shapes=[
            pltpu.VMEM((slots * 8, LANES), F32),
            pltpu.VMEM((KS * PANELS, POINTS), BF16),
            pltpu.SMEM((8, slots), jnp.int32),
            pltpu.SemaphoreType.DMA((2,)),
        ],
        compiler_params=PARAMS,
        name="own_scatter",
    )(packed, stencils.reshape(KS * PANELS, POINTS))

    g = pl.pallas_call(
        beside_kernel,
        out_shape=(grid,) * 5
        + (
            shape_of(LANES, LANES),
            shape_of(8, 2 * slots, dtype=jnp.int32),
            shape_of(3 * (PANELS + 16), slots, dtype=BF16),
        ),
        in_specs=[SMEM] + [VMEM] * 9,
        out_specs=(VMEM,) * 8,
        scratch_shapes=[
            pltpu.VMEM((2 * slots * 8, LANES), F32),
            pltpu.SMEM((8, 2 * slots), jnp.int32),
            pltpu.SemaphoreType.DMA,
        ],
        input_output_aliases={5: 0, 6: 1, 7: 2, 8: 3, 9: 4},
        compiler_params=PARAMS,
        name="beside_scatter",
    )(odd, packed, from_first, from_second, stk, *grids)
    facts2 = g[6]
    edge = to_other_tile(g[5])

    forward, inverse = z_tables(slabs, tiles)
    rows = owners * (4 * parts + SCALE_ROWS)
    sent = pl.pallas_call(
        functools.partial(z_kernel, slabs),
        out_shape=shape_of(rows, LANES),
        in_specs=[VMEM] * 6,
        out_specs=VMEM,
        scratch_shapes=[pltpu.VMEM((ZROWS, LANES), F32)],
        compiler_params=PARAMS,
        name="z_forward",
    )(*g[:4], edge, jnp.asarray(halves(*forward)))

    def exchanged(values, kept):
        values = values.reshape(owners, -1, LANES)[:, :kept].astype(jnp.float16)
        values = lax.all_to_all(values, axes, 0, 0, tiled=True)
        return values

    def widened(values):
        return values.astype(F32).reshape(-1, LANES)

    hat, sent = lax.optimization_barrier((kernel_hat, sent))
    got = exchanged(sent, 4 * parts + SCALE_ROWS)
    me = lax.axis_index("slab") * tiles + lax.axis_index("tile")
    offset = (me >= owners // 2).astype(jnp.int32)[None]
    hat = pl.pallas_call(
        functools.partial(hat_kernel, planes),
        out_shape=shape_of(planes, length, NY),
        in_specs=[SMEM] + [VMEM] * 2,
        out_specs=VMEM,
        compiler_params=PARAMS,
        name="hat_order",
    )(offset, hat, jnp.asarray(reversal()))

    got, hat = lax.optimization_barrier((got, hat))
    pool = (g[7], to_other_tile(g[7]))
    direction = near_source // slots
    pool_index = (direction // 3 * 2 + (direction % 3 != 1).astype(jnp.int32)) * slots + near_source % slots
    near = pl.pallas_call(
        near_kernel,
        out_shape=shape_of(PANELS, slots),
        in_specs=[SMEM] + [VMEM] * 5,
        out_specs=VMEM,
        compiler_params=PARAMS,
        name="near_field",
    )(live_count, *pool, pool_index.T, near_block.T, near_blocks.reshape(PANELS, KN * PANELS))

    back, exponent = pl.pallas_call(
        functools.partial(plane_kernel, slabs, planes),
        out_shape=(shape_of(rows, LANES), shape_of(8, LANES)),
        in_specs=[VMEM] * 4,
        out_specs=(VMEM, VMEM),
        scratch_shapes=[pltpu.VMEM((2 * planes * length, NY), BF16)] * 2,
        compiler_params=PARAMS,
        name="plane_filter",
    )(widened(got), hat, jnp.asarray(halves(y_table(), y_table().T)), jnp.asarray(halves(*x_tables(slabs))))
    back, near = lax.optimization_barrier((exchanged(back, 4 * parts), near))

    pot = pl.pallas_call(
        functools.partial(potential_kernel, slabs),
        out_shape=(grid,) * 4 + (shape_of(LANES, LANES, dtype=BF16),),
        in_specs=[VMEM] * 3,
        out_specs=(VMEM,) * 5,
        compiler_params=PARAMS,
        name="z_inverse",
    )(widened(back), exponent, jnp.asarray(halves(*inverse)))
    edge = to_other_tile(pot[4])

    def sample_scratch(width):
        return [pltpu.VMEM((ZROWS, LANES), F32), pltpu.VMEM((width * 8, LANES), F32)]

    sums = shape_of(PANELS, slots)
    others = pl.pallas_call(
        beside_sample_kernel,
        out_shape=(sums, sums),
        in_specs=[SMEM] * 2 + [VMEM] * 7,
        out_specs=(VMEM, VMEM),
        scratch_shapes=sample_scratch(2 * slots),
        compiler_params=PARAMS,
        name="beside_sample",
    )(odd, facts2, *pot[:4], edge, facts2, stk)
    second = to_second(others[1])
    first = to_first(others[0])
    own = pl.pallas_call(
        own_sample_kernel,
        out_shape=sums,
        in_specs=[SMEM] + [VMEM] * 7,
        out_specs=VMEM,
        scratch_shapes=sample_scratch(slots),
        compiler_params=PARAMS,
        name="own_sample",
    )(facts, *pot[:4], edge, facts, stk)
    return own + near + first + second


def solution(mesh):
    both = ("slab", "tile")
    in_specs = (
        P(None, both),
        P(both),
        P(both),
        P(both),
        P(),
        P(both, None),
        P(both, None),
        P(),
        P(both, None, None),
    )
    return jax.shard_map(
        functools.partial(body, mesh.shape["slab"], mesh.shape["tile"]),
        mesh=mesh,
        in_specs=in_specs,
        out_specs=P(None, both),
        check_vma=False,
    )
```

```python
import functools
import math

import jax
import jax.numpy as jnp
import ml_dtypes
import numpy as np
from jax import lax
from jax.experimental import pallas as pl
from jax.experimental.pallas import tpu as pltpu
from jax.sharding import PartitionSpec as P

PANELS = 64
POINTS = 512
NY = 256
NZ = 512
KS = 16
KN = 16
LANES = 128
ZROWS = NZ + 8
UNROLL = 32
HALF = NY // 2
SCALE_ROWS = 8
BOUND = 12.0
HEADROOM = 15.0
F32 = jnp.float32
BF16 = jnp.bfloat16
SMEM = pl.BlockSpec(memory_space=pltpu.SMEM)
VMEM = pl.BlockSpec(memory_space=pltpu.VMEM)
PARAMS = pltpu.CompilerParams(vmem_limit_bytes=48 * 1024 * 1024)


def halves(*tables):
    parts = []
    for table in tables:
        high = table.astype(ml_dtypes.bfloat16)
        parts += [high, (table - high.astype(np.float64)).astype(ml_dtypes.bfloat16)]
    return np.concatenate(parts, axis=0)


def z_tables(slabs, tiles):
    half = slabs // 2
    planes = NZ // (slabs * tiles) // 2
    plane = np.arange(planes + 1)[:, None, None]
    tile = np.arange(tiles)[None, :, None]
    slab = np.arange(half)[None, None, :]
    owner = slab * tiles + tile
    freq = (owner * 2 * planes + plane).reshape(-1)
    forward, inverse = [], []
    for parity in range(2):
        cell = np.arange(parity, NZ, 2) - 2
        angle = (freq[:, None] * cell[None, :] % NZ) * (2 * np.pi / NZ)
        forward.append(np.concatenate([np.cos(angle), -np.sin(angle)], axis=0))
        upper = (plane[:-1] + parity) % 2
        back = ((upper * half * tiles + owner) * 2 * planes + plane[:-1] + upper).reshape(-1)
        cell = np.arange(NZ // 2) - 2
        angle = (back[:, None] * cell[None, :] % NZ) * (2 * np.pi / NZ)
        weight = np.where(back == 0, 1.0, 2.0)[:, None] / NZ
        inverse.append(np.concatenate([weight * np.cos(angle), -weight * np.sin(angle)], axis=0).T)
    return forward, inverse


def y_table():
    angle = (np.arange(NY)[:, None] * np.arange(HALF + 1)[None, :] % NY) * (2 * np.pi / NY)
    return np.concatenate([np.cos(angle[:, :HALF]), np.cos(angle[:, HALF:]), np.sin(angle[:, 1:HALF])], axis=1)


def reversal():
    table = np.zeros((HALF, HALF), ml_dtypes.bfloat16)
    lane = np.arange(HALF)
    table[lane, (HALF - lane) % HALF] = 1
    return table


def x_tables(slabs):
    length = 4 * slabs
    cell = (np.arange(4)[:, None] + 4 * np.arange(slabs)[None, :]).reshape(-1)
    angle = (np.arange(length)[:, None] * cell[None, :] % length) * (2 * np.pi / length)
    cosine, sine = np.cos(angle), np.sin(angle)
    forward = np.block([[cosine, sine], [-sine, cosine]])
    inverse = np.block([[cosine.T, -sine.T], [sine.T, cosine.T]])
    return forward, inverse


def split(values):
    high = values.astype(BF16)
    return high, (values - high.astype(F32)).astype(BF16)


def dot(a, b):
    return jnp.dot(a, b, preferred_element_type=F32)


def dot3(a, b):
    return dot(a[0], b[0]) + (dot(a[0], b[1]) + dot(a[1], b[0]))


def lane_of(shape):
    return lax.broadcasted_iota(jnp.int32, shape, 1)


def by_kind(values, kinds):
    zero = jnp.zeros_like(values)
    return jnp.concatenate(
        [jnp.where(kinds == kind, values, zero) for kind in range(KS)], axis=0
    )


def footprints(packed, stk_ref, fp_ref, first):
    count = packed.shape[1]
    turned = jnp.transpose(packed.astype(F32))
    kinds = turned[:, PANELS + 2 : PANELS + 3]
    charges = jnp.concatenate([turned[:, :PANELS], turned[:, :PANELS]], axis=1)
    offset = kinds - jnp.where(lane_of((count, LANES)) < PANELS, 0.0, 1.0)
    spread = jnp.concatenate(
        [jnp.where(offset == kind, charges, 0.0).astype(BF16) for kind in range(0, KS, 2)], axis=1
    )
    result = dot(spread, stk_ref[...])
    for pair in range(4):
        part = result[:, pair * LANES : (pair + 1) * LANES]
        fp_ref[pl.ds(first * 8 + 2 * pair, count, stride=8), :] = part
        fp_ref[pl.ds(first * 8 + 2 * pair + 1, count, stride=8), :] = pltpu.roll(part, 64, 1)


def lane_in(plane, shape):
    return (lane_of(shape) - 8 * plane) & (LANES - 1)


def edge_codes(planes, shape):
    code = jnp.full(shape, 3, jnp.int32)
    for plane in planes:
        lane = lane_in(plane, shape)
        code = jnp.where(lane >= LANES - 2, 0, jnp.where(lane < 2, 1, code))
    return code


def scatter_columns(fp_ref, first, place_of, count, grids, edge_ref, planes):
    shape = (8, LANES)
    lanes = [lane_in(plane, shape) for plane in planes]
    codes = edge_codes(planes, shape)

    def step(index, carry):
        updates = []
        for inner in range(UNROLL):
            column = index * UNROLL + inner
            row, begin, edge, turn, _ = place_of(column)
            value = fp_ref[pl.ds(pl.multiple_of((first + column) * 8, 8), 8), :]
            turned = pltpu.roll(value, turn, 1)
            terms = [jnp.where(((lane - begin) & -8) == 0, turned, 0.0) for lane in lanes]
            terms.append(jnp.where(codes == edge, turned, 0.0))
            updates.append((pl.ds(row, 8), terms))
        refs = [grids[plane] for plane in planes] + [edge_ref]
        for where, terms in updates:
            sums = [ref[where, :] + term for ref, term in zip(refs, terms)]
            for ref, total in zip(refs, sums):
                ref[where, :] = total
        return carry

    lax.fori_loop(0, lax.shift_right_logical(count + UNROLL - 1, 5), step, 0)


def sample_columns(pot_refs, edge_ref, place_of, count, sp_ref, first, planes):
    shape = (8, LANES)
    lanes = [lane_in(plane, shape) for plane in planes]
    codes = edge_codes(planes, shape)

    def step(index, carry):
        results = []
        for inner in range(UNROLL):
            column = index * UNROLL + inner
            row, begin, edge, _, turn = place_of(column)
            where = pl.ds(row, 8)
            result = jnp.where(codes == edge, edge_ref[where, :], 0.0)
            for plane, lane in zip(planes, lanes):
                result = jnp.where(((lane - begin) & -8) == 0, pot_refs[plane][where, :], result)
            turned = pltpu.roll(result, turn, 1)
            results.append((pl.ds(pl.multiple_of((first + column) * 8, 8), 8), turned))
        for where, result in results:
            sp_ref[where, :] = result
        return carry

    lax.fori_loop(0, lax.shift_right_logical(count + UNROLL - 1, 5), step, 0)


def far_sums(sp_ref, kinds, stk_ref, first):
    count = kinds.shape[1]
    lane = lane_of((count, LANES))
    pairs = []
    for pair in range(4):
        even = sp_ref[pl.ds(first * 8 + 2 * pair, count, stride=8), :]
        odd = sp_ref[pl.ds(first * 8 + 2 * pair + 1, count, stride=8), :]
        pairs.append(jnp.where(lane < 64, even, pltpu.roll(odd, 64, 1)).astype(BF16))
    samples = jnp.concatenate(pairs, axis=1)
    sums = lax.dot_general(
        stk_ref[...], samples, (((1,), (1,)), ((), ())), preferred_element_type=F32
    )
    result = jnp.zeros((PANELS, count), F32)
    for kind in range(KS):
        result += jnp.where(kinds == kind, sums[kind * PANELS : (kind + 1) * PANELS, :], 0.0)
    return result


OWN = ((0, 1, 2, 3), 2)
BESIDE = (((0, 1), 6), ((2, 3), -2))


def place_in_facts(facts_ref, start=0):
    return lambda column: [facts_ref[row, start + column] for row in (0, 1, 4, 5, 6)]


def facts_of(packed_ref, row, shift_i):
    facts = packed_ref[row : row + 16, :].astype(F32).astype(jnp.int32)
    by, bz, kinds, live = (facts[index : index + 1, :] for index in range(4))
    begin = 4 * by - 2
    edge = jnp.where(by == 0, 0, jnp.where(by == NY // 8 - 1, 1, 2))
    turn = begin - 8 * shift_i
    rows = [4 * bz, begin, kinds, live, edge, turn & (LANES - 1), -turn & (LANES - 1), by]
    return jnp.concatenate(rows, axis=0)


def own_kernel(packed_ref, stencil_ref,
               g0, g1, g2, g3, edge_ref, stk_ref, out_facts, fp_ref, rows_ref, facts_ref, sems):
    copy = pltpu.make_async_copy(stencil_ref, rows_ref, sems.at[0])
    copy.start()
    out_facts[...] = facts_of(packed_ref, PANELS, OWN[1])
    facts_copy = pltpu.make_async_copy(out_facts, facts_ref, sems.at[1])
    facts_copy.start()
    for ref in (g0, g1, g2, g3, edge_ref):
        ref[...] = jnp.zeros_like(ref)
    shape = (POINTS, POINTS)
    point = lax.broadcasted_iota(jnp.int32, shape, 0)
    target = (point & 7) * 64 + lax.shift_right_logical(point, 3)
    order = jnp.where(lane_of(shape) == target, 1.0, 0.0).astype(BF16)
    facts_copy.wait()
    copy.wait()
    stk_ref[...] = dot(rows_ref[...], order).astype(BF16)
    live = facts_ref[3, 0]

    @pl.when(live > LANES)
    def _():
        footprints(packed_ref[...], stk_ref, fp_ref, 0)

    @pl.when(live <= LANES)
    def _():
        footprints(packed_ref[:, 0:LANES], stk_ref, fp_ref, 0)

    scatter_columns(fp_ref, 0, place_in_facts(facts_ref), live, (g0, g1, g2, g3), edge_ref, OWN[0])


def chunks_beside(facts_ref, slots):
    for first in range(0, slots, LANES):
        counts = [jnp.clip(facts_ref[3, side * slots] - first, 0, LANES) for side in range(2)]
        yield first, counts


def both_sides(ref, slots, first):
    return jnp.concatenate(
        [ref[:, side * slots + first : side * slots + first + LANES] for side in range(2)], axis=1
    )


def beside_kernel(odd_ref, own_ref, first_ref, second_ref, stk_ref, i0, i1, i2, i3, iedge,
                  g0, g1, g2, g3, edge_ref, out_edge, out_facts, pool_ref, fp_ref, facts_ref, sem):
    height, slots = own_ref.shape
    before, after = pl.ds(0, height), pl.ds(2 * height, height)
    pool_ref[height : 2 * height, :] = own_ref[...]

    @pl.when(odd_ref[0] == 0)
    def _():
        pool_ref[after, :] = first_ref[...]
        pool_ref[before, :] = second_ref[...]

    @pl.when(odd_ref[0] != 0)
    def _():
        pool_ref[before, :] = first_ref[...]
        pool_ref[after, :] = second_ref[...]

    for side, (_, shift_i) in enumerate(BESIDE):
        out_facts[:, side * slots : (side + 1) * slots] = facts_of(pool_ref, 2 * side * height + PANELS, shift_i)
    copy = pltpu.make_async_copy(out_facts, facts_ref, sem)
    copy.start()

    def project(first):
        here = slice(first, first + LANES)
        packed = jnp.concatenate(
            [pool_ref[0:height, here], pool_ref[2 * height : 3 * height, here]], axis=1
        )
        footprints(packed, stk_ref, fp_ref, 2 * first)

    project(0)
    copy.wait()
    for first, counts in chunks_beside(facts_ref, slots):
        if first:
            @pl.when(counts[0] + counts[1] > 0)
            def _(first=first):
                project(first)

        for side, (planes, _) in enumerate(BESIDE):
            scatter_columns(fp_ref, 2 * first + side * LANES, place_in_facts(facts_ref, side * slots + first),
                            counts[side], (g0, g1, g2, g3), edge_ref, planes)
    for ref in (g0, g1, g2, g3, edge_ref):
        ref[0:8, :] += ref[NZ:ZROWS, :]
    total = pltpu.roll(edge_ref[0:LANES, :], 2, 1)
    for block in range(1, 4):
        total += pltpu.roll(edge_ref[block * LANES : (block + 1) * LANES, :], 32 * block + 2, 1)
    out_edge[...] = total


def exponent_of(values):
    top = functools.reduce(jnp.maximum, [jnp.max(jnp.abs(v), axis=0, keepdims=True) for v in values])
    top = jnp.maximum(jnp.max(top, axis=1, keepdims=True), 2.0**-100)
    return jnp.ceil(jnp.log2(top)) - BOUND


def quarter(table_ref, index):
    rows = table_ref.shape[0] // 4
    return tuple(table_ref[part * rows : (part + 1) * rows, :] for part in (2 * index, 2 * index + 1))


def z_kernel(slabs, g0, g1, g2, g3, edge_ref, w_ref, out_ref, wide_ref):
    widen_edge(edge_ref, wide_ref)
    half = slabs // 2
    parts = NZ // (2 * slabs)
    planes = parts // 2
    stride = 4 * parts + SCALE_ROWS
    sums = []
    for parity in range(2):
        where = pl.ds(parity, NZ // 2, stride=2)
        columns = []
        for plane, grid in enumerate((g0, g1, g2, g3)):
            at_edge = edge_codes((plane,), (NZ // 2, LANES)) < 2
            values = grid[where, :] + jnp.where(at_edge, wide_ref[where, :], 0.0)
            columns.append(pltpu.roll(values, LANES - 8 * plane, 1) if plane else values)
        sums.append(dot3(quarter(w_ref, parity), split(jnp.concatenate(columns, axis=1))))
    results = (sums[0] + sums[1], sums[0] - sums[1])
    exponent = exponent_of(results)
    scale = jnp.exp2(-exponent)
    results = [result * scale for result in results]
    for upper, result in enumerate(results):
        for part in range(parts):
            index = part // planes * (planes + 1) + part % planes + upper
            for tile in range(2):
                rows = result[(index * 2 + tile) * half : (index * 2 + tile + 1) * half, :]
                start = (tile * slabs + upper * half) * stride + part
                for plane in range(4):
                    out_ref[pl.ds(start + plane * parts, half, stride=stride), :] = rows[
                        :, plane * LANES : (plane + 1) * LANES
                    ]
    for row in range(SCALE_ROWS):
        out_ref[pl.ds(4 * parts + row, 2 * slabs, stride=stride), :] = jnp.broadcast_to(
            exponent, (2 * slabs, LANES)
        )


def hat_kernel(planes, offset_ref, hat_ref, turn_ref, out_ref):
    length = hat_ref.shape[1]
    values = jnp.concatenate([hat_ref[offset_ref[0] + plane] for plane in range(planes)], axis=0)
    values = values * (1.0 / (length * NY))
    upper = values[:, HALF:]
    high, low = split(upper)
    rest = (upper - high.astype(F32) - low.astype(F32)).astype(BF16)
    turn = turn_ref[...]
    upper = dot(high, turn) + (dot(low, turn) + dot(rest, turn))
    for plane in range(planes):
        here = slice(plane * length, (plane + 1) * length)
        out_ref[plane] = jnp.concatenate([values[here, :HALF], upper[here, :]], axis=1)


def plane_kernel(slabs, planes, in_ref, hat_ref, y_ref, x_ref, out_ref, exponent_ref, ah_ref, al_ref):
    length = 4 * slabs
    rows = planes * length
    parts = 2 * planes
    stride = 4 * parts + SCALE_ROWS

    def pieces():
        for tile in range(2):
            for part in range(2):
                for xi in range(4):
                    for plane in range(planes):
                        yield tile, part, plane, xi

    scales = [
        jnp.exp2(in_ref[pl.ds(tile * slabs * stride + 4 * parts, slabs, stride=stride), :])
        for tile in range(2)
    ]
    for tile, part, plane, xi in pieces():
        start = tile * slabs * stride + xi * parts + part * planes + plane
        row = (part * planes + plane) * length + xi * slabs
        high, low = split(in_ref[pl.ds(start, slabs, stride=stride), :] * scales[tile])
        ah_ref[row : row + slabs, tile * LANES : (tile + 1) * LANES] = high
        al_ref[row : row + slabs, tile * LANES : (tile + 1) * LANES] = low
    first_lane = lane_of((rows, HALF)) == 0
    turned = dot3((ah_ref[...], al_ref[...]), (y_ref[0:NY, :], y_ref[NY : 2 * NY, :]))
    even = (turned[:rows, :HALF], turned[rows:, :HALF])
    odd = (turned[:rows, HALF:], turned[rows:, HALF:])
    zero_odd = [jnp.where(first_lane, 0.0, values) for values in odd]
    real = jnp.concatenate(
        [even[0] + zero_odd[1], jnp.where(first_lane, odd[0], even[0] - zero_odd[1])], axis=1
    )
    imag = jnp.concatenate(
        [even[1] - zero_odd[0], jnp.where(first_lane, odd[1], even[1] + zero_odd[0])], axis=1
    )
    size = 2 * length

    def along_x(values, first):
        high, low = split(values)
        table = x_ref[first * size : (first + 1) * size, :]
        rest = x_ref[(first + 1) * size : (first + 2) * size, :]
        both = dot(jnp.concatenate([table, table], axis=1), jnp.concatenate([high, low], axis=0))
        return both + dot(rest, high)

    for plane in range(planes):
        here = slice(plane * length, (plane + 1) * length)
        there = slice(rows + plane * length, rows + (plane + 1) * length)
        values = along_x(jnp.concatenate([real[here], imag[here]], axis=0), 0)
        values = values * jnp.concatenate([hat_ref[plane], hat_ref[plane]], axis=0)
        values = along_x(values, 2)
        low, high = values[:, :HALF], values[:, HALF:]
        lane = first_lane[:length]
        even_r = jnp.where(lane, low[:length], low[:length] + high[:length])
        even_i = jnp.where(lane, low[length:], low[length:] + high[length:])
        odd_r = jnp.where(lane, high[:length], high[length:] - low[length:])
        odd_i = jnp.where(lane, high[length:], low[:length] - high[:length])
        ah_ref[here, :], al_ref[here, :] = split(jnp.concatenate([even_r, odd_r], axis=1))
        ah_ref[there, :], al_ref[there, :] = split(jnp.concatenate([even_i, odd_i], axis=1))
    turned = dot3((ah_ref[...], al_ref[...]), (y_ref[2 * NY : 3 * NY, :], y_ref[3 * NY : 4 * NY, :]))
    tops = [
        jnp.max(in_ref[pl.ds(tile * slabs * stride + 4 * parts, slabs, stride=stride), :], axis=0, keepdims=True)
        for tile in range(2)
    ]
    exponent = jnp.broadcast_to(jnp.maximum(*tops) + BOUND - HEADROOM + math.ceil(math.log2(length * NY) / 2), (8, LANES))
    exponent_ref[...] = exponent
    scale = jnp.exp2(-exponent[0:1, 0:1])
    for tile, part, plane, xi in pieces():
        here = slice((part * planes + plane) * length + xi * slabs, (part * planes + plane) * length + (xi + 1) * slabs)
        start = tile * slabs * stride + xi * parts + part * planes + plane
        out_ref[pl.ds(start, slabs, stride=stride), :] = (
            turned[here, tile * LANES : (tile + 1) * LANES] * scale
        )


def potential_kernel(slabs, in_ref, exponent_ref, v_ref, p0, p1, p2, p3, edge_ref):
    half = slabs // 2
    parts = NZ // (2 * slabs)
    planes = parts // 2
    stride = 4 * parts
    sums = []
    for parity in range(2):
        columns = []
        for plane in range(4):
            rows = []
            for part in range(parts):
                upper = (part % planes + parity) % 2
                for tile in range(2):
                    start = (tile * slabs + upper * half) * stride + plane * parts + part
                    rows.append(in_ref[pl.ds(start, half, stride=stride), :])
            columns.append(jnp.concatenate(rows, axis=0))
        sums.append(dot3(quarter(v_ref, parity), split(jnp.concatenate(columns, axis=1))))
    scale = jnp.exp2(exponent_ref[0:1, 0:1])
    shape = (LANES, LANES)
    edges = [jnp.zeros(shape, F32)] * 4
    halves_of_z = [((sums[0] + sums[1]) * scale), ((sums[0] - sums[1]) * scale)]
    for plane, pot in enumerate((p0, p1, p2, p3)):
        at_edge = edge_codes((plane,), shape) < 2
        for upper in range(2):
            result = halves_of_z[upper][:, plane * LANES : (plane + 1) * LANES].astype(BF16).astype(F32)
            if plane:
                result = pltpu.roll(result, 8 * plane, 1)
            pot[upper * (NZ // 2) : (upper + 1) * (NZ // 2), :] = result
            for block in range(2):
                edges[2 * upper + block] = jnp.where(
                    at_edge, result[block * LANES : (block + 1) * LANES, :], edges[2 * upper + block]
                )
        pot[NZ:ZROWS, :] = pot[0:8, :]
    edge = pltpu.roll(edges[0], 2, 1)
    for block in range(1, 4):
        edge += pltpu.roll(edges[block], 32 * block + 2, 1)
    edge_ref[...] = edge.astype(BF16)


def widen_edge(edge_ref, wide_ref):
    for block in range(4):
        wide_ref[block * LANES : (block + 1) * LANES, :] = pltpu.roll(
            edge_ref[...].astype(F32), (LANES - 2 - 32 * block) % LANES, 1
        )
    wide_ref[NZ:ZROWS, :] = wide_ref[0:8, :]


def masked(values, live):
    return jnp.where(lane_of(values.shape) < live, values, 0.0)


def own_sample_kernel(facts_ref, p0, p1, p2, p3, edge_ref, kinds_ref, stk_ref, out_ref, wide_ref, sp_ref):
    widen_edge(edge_ref, wide_ref)
    live = facts_ref[3, 0]
    slots = kinds_ref.shape[1]
    sample_columns((p0, p1, p2, p3), wide_ref, place_in_facts(facts_ref), live, sp_ref, 0, OWN[0])

    @pl.when(live > LANES)
    def _():
        out_ref[...] = masked(far_sums(sp_ref, kinds_ref[2:3, :], stk_ref, 0), live)

    @pl.when(live <= LANES)
    def _():
        out_ref[:, 0:LANES] = masked(far_sums(sp_ref, kinds_ref[2:3, 0:LANES], stk_ref, 0), live)
        out_ref[:, LANES:slots] = jnp.zeros((PANELS, slots - LANES), F32)


def beside_sample_kernel(odd_ref, facts_ref, p0, p1, p2, p3, edge_ref, kinds_ref, stk_ref, out0, out1, wide_ref, sp_ref):
    widen_edge(edge_ref, wide_ref)
    slots = kinds_ref.shape[1] // 2
    outs = (out0, out1)
    for first, counts in chunks_beside(facts_ref, slots):
        here = slice(first, first + LANES)
        for side, (planes, _) in enumerate(BESIDE):
            sample_columns((p0, p1, p2, p3), wide_ref, place_in_facts(facts_ref, side * slots + first),
                           counts[side], sp_ref, 2 * first + side * LANES, planes)

        @pl.when(counts[0] + counts[1] > 0)
        def _(first=first, counts=counts, here=here):
            kinds = both_sides(kinds_ref.at[2:3, :], slots, first)
            result = far_sums(sp_ref, kinds, stk_ref, 2 * first)
            sums = [masked(result[:, side * LANES : (side + 1) * LANES], counts[side]) for side in range(2)]
            even = jnp.broadcast_to(odd_ref[0], sums[0].shape) == 0
            out0[:, here] = jnp.where(even, sums[1], sums[0])
            out1[:, here] = jnp.where(even, sums[0], sums[1])

        @pl.when(counts[0] + counts[1] <= 0)
        def _(here=here):
            for out in outs:
                out[:, here] = jnp.zeros((PANELS, LANES), F32)


def near_kernel(live_ref, here_ref, there_ref, source_ref, block_ref, table_ref, out_ref):
    live = live_ref[0]
    fanout, slots = source_ref.shape
    height = here_ref.shape[0] // 3
    pool = jnp.concatenate(
        [ref[step * height : step * height + PANELS, :] for step in range(3) for ref in (here_ref, there_ref)],
        axis=1,
    )
    total = pool.shape[1]
    for first in range(0, slots, LANES):
        where = slice(first, first + LANES)

        @pl.when(live > first)
        def _(where=where, first=first):
            index = lax.broadcasted_iota(jnp.int32, (total, LANES), 0)
            result = jnp.zeros((PANELS, LANES), F32)
            for j in range(fanout):
                chosen = jnp.where(index == source_ref[j : j + 1, where], 1.0, 0.0).astype(BF16)
                gathered = dot(pool, chosen)
                result += dot(
                    table_ref[...], by_kind(gathered, block_ref[j : j + 1, where]).astype(BF16)
                )
            column = first + lane_of((PANELS, LANES))
            out_ref[:, where] = jnp.where(column < live, result, 0.0)

        @pl.when(live <= first)
        def _(where=where):
            out_ref[:, where] = jnp.zeros((PANELS, LANES), F32)


def shape_of(*dims, dtype=F32):
    return jax.ShapeDtypeStruct(dims, dtype)


def body(slabs, tiles, charges, live_count, slot_brick, slot_stencil, stencils, near_source,
         near_block, near_blocks, kernel_hat):
    slots = charges.shape[1]
    owners = slabs * tiles
    planes = kernel_hat.shape[0] // 2
    length = kernel_hat.shape[1]
    parts = NZ // owners
    axes = ("tile", "slab")
    both = ("slab", "tile")

    def moved(values, step_of, swap=0):
        pairs = [
            (a * tiles + b, (a + step_of(a)) % slabs * tiles + (b + swap) % tiles)
            for a in range(slabs)
            for b in range(tiles)
        ]
        return lax.ppermute(values, both, pairs)

    def to_first(values):
        return moved(values, lambda a: 1 - 2 * (a % 2))

    def to_second(values):
        return moved(values, lambda a: 2 * (a % 2) - 1)

    def to_other_tile(values):
        return moved(values, lambda a: 0, 1)

    odd = (lax.axis_index("slab") % 2)[None]
    row = lax.broadcasted_iota(jnp.int32, (PANELS + 16, slots), 0)
    column = lax.broadcasted_iota(jnp.int32, (PANELS + 16, slots), 1)
    live = jnp.broadcast_to(live_count[0], row.shape)
    brick = jnp.broadcast_to(slot_brick[None, :], row.shape)
    facts = lax.shift_right_logical(brick, jnp.where(row == PANELS, 7, 0)) & (NZ // 4 - 1)
    facts = jnp.where(row == PANELS + 2, slot_stencil[None, :], jnp.where(row == PANELS + 3, live, facts))
    held = jnp.where(column < live, jnp.pad(charges, ((0, 16), (0, 0))), jnp.zeros((), BF16))
    packed = jnp.where(row < PANELS, held, facts.astype(BF16))
    from_second = to_second(packed)
    from_first = to_first(packed)

    grid = shape_of(ZROWS, LANES)
    *grids, stk, facts = pl.pallas_call(
        own_kernel,
        out_shape=(grid,) * 5 + (shape_of(KS * PANELS, POINTS, dtype=BF16), shape_of(8, slots, dtype=jnp.int32)),
        in_specs=[VMEM, pl.BlockSpec(memory_space=pl.ANY)],
        out_specs=(VMEM,) * 7,
        scratch_shapes=[
            pltpu.VMEM((slots * 8, LANES), F32),
            pltpu.VMEM((KS * PANELS, POINTS), BF16),
            pltpu.SMEM((8, slots), jnp.int32),
            pltpu.SemaphoreType.DMA((2,)),
        ],
        compiler_params=PARAMS,
        name="own_scatter",
    )(packed, stencils.reshape(KS * PANELS, POINTS))

    g = pl.pallas_call(
        beside_kernel,
        out_shape=(grid,) * 5
        + (
            shape_of(LANES, LANES),
            shape_of(8, 2 * slots, dtype=jnp.int32),
            shape_of(3 * (PANELS + 16), slots, dtype=BF16),
        ),
        in_specs=[SMEM] + [VMEM] * 9,
        out_specs=(VMEM,) * 8,
        scratch_shapes=[
            pltpu.VMEM((2 * slots * 8, LANES), F32),
            pltpu.SMEM((8, 2 * slots), jnp.int32),
            pltpu.SemaphoreType.DMA,
        ],
        input_output_aliases={5: 0, 6: 1, 7: 2, 8: 3, 9: 4},
        compiler_params=PARAMS,
        name="beside_scatter",
    )(odd, packed, from_first, from_second, stk, *grids)
    facts2 = g[6]
    edge = to_other_tile(g[5])

    forward, inverse = z_tables(slabs, tiles)
    rows = owners * (4 * parts + SCALE_ROWS)
    sent = pl.pallas_call(
        functools.partial(z_kernel, slabs),
        out_shape=shape_of(rows, LANES),
        in_specs=[VMEM] * 6,
        out_specs=VMEM,
        scratch_shapes=[pltpu.VMEM((ZROWS, LANES), F32)],
        compiler_params=PARAMS,
        name="z_forward",
    )(*g[:4], edge, jnp.asarray(halves(*forward)))

    def exchanged(values, kept):
        values = values.reshape(owners, -1, LANES)[:, :kept].astype(jnp.float16)
        values = lax.all_to_all(values, axes, 0, 0, tiled=True)
        return values

    def widened(values):
        return values.astype(F32).reshape(-1, LANES)

    hat, sent = lax.optimization_barrier((kernel_hat, sent))
    got = exchanged(sent, 4 * parts + SCALE_ROWS)
    me = lax.axis_index("slab") * tiles + lax.axis_index("tile")
    offset = (me >= owners // 2).astype(jnp.int32)[None]
    hat = pl.pallas_call(
        functools.partial(hat_kernel, planes),
        out_shape=shape_of(planes, length, NY),
        in_specs=[SMEM] + [VMEM] * 2,
        out_specs=VMEM,
        compiler_params=PARAMS,
        name="hat_order",
    )(offset, hat, jnp.asarray(reversal()))

    got, hat = lax.optimization_barrier((got, hat))
    pool = (g[7], to_other_tile(g[7]))
    direction = near_source // slots
    pool_index = (direction // 3 * 2 + (direction % 3 != 1).astype(jnp.int32)) * slots + near_source % slots
    near = pl.pallas_call(
        near_kernel,
        out_shape=shape_of(PANELS, slots),
        in_specs=[SMEM] + [VMEM] * 5,
        out_specs=VMEM,
        compiler_params=PARAMS,
        name="near_field",
    )(live_count, *pool, pool_index.T, near_block.T, near_blocks.reshape(PANELS, KN * PANELS))

    back, exponent = pl.pallas_call(
        functools.partial(plane_kernel, slabs, planes),
        out_shape=(shape_of(rows, LANES), shape_of(8, LANES)),
        in_specs=[VMEM] * 4,
        out_specs=(VMEM, VMEM),
        scratch_shapes=[pltpu.VMEM((2 * planes * length, NY), BF16)] * 2,
        compiler_params=PARAMS,
        name="plane_filter",
    )(widened(got), hat, jnp.asarray(halves(y_table(), y_table().T)), jnp.asarray(halves(*x_tables(slabs))))
    back, near = lax.optimization_barrier((exchanged(back, 4 * parts), near))

    pot = pl.pallas_call(
        functools.partial(potential_kernel, slabs),
        out_shape=(grid,) * 4 + (shape_of(LANES, LANES, dtype=BF16),),
        in_specs=[VMEM] * 3,
        out_specs=(VMEM,) * 5,
        compiler_params=PARAMS,
        name="z_inverse",
    )(widened(back), exponent, jnp.asarray(halves(*inverse)))
    edge = to_other_tile(pot[4])

    def sample_scratch(width):
        return [pltpu.VMEM((ZROWS, LANES), F32), pltpu.VMEM((width * 8, LANES), F32)]

    sums = shape_of(PANELS, slots)
    others = pl.pallas_call(
        beside_sample_kernel,
        out_shape=(sums, sums),
        in_specs=[SMEM] * 2 + [VMEM] * 7,
        out_specs=(VMEM, VMEM),
        scratch_shapes=sample_scratch(2 * slots),
        compiler_params=PARAMS,
        name="beside_sample",
    )(odd, facts2, *pot[:4], edge, facts2, stk)
    first = to_first(others[0])
    second = to_second(others[1])
    own = pl.pallas_call(
        own_sample_kernel,
        out_shape=sums,
        in_specs=[SMEM] + [VMEM] * 7,
        out_specs=VMEM,
        scratch_shapes=sample_scratch(slots),
        compiler_params=PARAMS,
        name="own_sample",
    )(facts, *pot[:4], edge, facts, stk)
    return own + near + first + second


def solution(mesh):
    both = ("slab", "tile")
    in_specs = (
        P(None, both),
        P(both),
        P(both),
        P(both),
        P(),
        P(both, None),
        P(both, None),
        P(),
        P(both, None, None),
    )
    return jax.shard_map(
        functools.partial(body, mesh.shape["slab"], mesh.shape["tile"]),
        mesh=mesh,
        in_specs=in_specs,
        out_specs=P(None, both),
        check_vma=False,
    )
```

```python
import functools
import math

import jax
import jax.numpy as jnp
import ml_dtypes
import numpy as np
from jax import lax
from jax.experimental import pallas as pl
from jax.experimental.pallas import tpu as pltpu
from jax.sharding import PartitionSpec as P

PANELS = 64
POINTS = 512
NY = 256
NZ = 512
KS = 16
KN = 16
LANES = 128
ZROWS = NZ + 8
UNROLL = 32
HALF = NY // 2
SCALE_ROWS = 8
BOUND = 12.0
HEADROOM = 15.0
F32 = jnp.float32
BF16 = jnp.bfloat16
SMEM = pl.BlockSpec(memory_space=pltpu.SMEM)
VMEM = pl.BlockSpec(memory_space=pltpu.VMEM)
PARAMS = pltpu.CompilerParams(vmem_limit_bytes=48 * 1024 * 1024)


def halves(*tables):
    parts = []
    for table in tables:
        high = table.astype(ml_dtypes.bfloat16)
        parts += [high, (table - high.astype(np.float64)).astype(ml_dtypes.bfloat16)]
    return np.concatenate(parts, axis=0)


def z_tables(slabs, tiles):
    half = slabs // 2
    planes = NZ // (slabs * tiles) // 2
    plane = np.arange(planes + 1)[:, None, None]
    tile = np.arange(tiles)[None, :, None]
    slab = np.arange(half)[None, None, :]
    owner = slab * tiles + tile
    freq = (owner * 2 * planes + plane).reshape(-1)
    forward, inverse = [], []
    for parity in range(2):
        cell = np.arange(parity, NZ, 2) - 2
        angle = (freq[:, None] * cell[None, :] % NZ) * (2 * np.pi / NZ)
        forward.append(np.concatenate([np.cos(angle), -np.sin(angle)], axis=0))
        upper = (plane[:-1] + parity) % 2
        back = ((upper * half * tiles + owner) * 2 * planes + plane[:-1] + upper).reshape(-1)
        cell = np.arange(NZ // 2) - 2
        angle = (back[:, None] * cell[None, :] % NZ) * (2 * np.pi / NZ)
        weight = np.where(back == 0, 1.0, 2.0)[:, None] / NZ
        inverse.append(np.concatenate([weight * np.cos(angle), -weight * np.sin(angle)], axis=0).T)
    return forward, inverse


def y_table():
    angle = (np.arange(NY)[:, None] * np.arange(HALF + 1)[None, :] % NY) * (2 * np.pi / NY)
    return np.concatenate([np.cos(angle[:, :HALF]), np.cos(angle[:, HALF:]), np.sin(angle[:, 1:HALF])], axis=1)


def reversal():
    table = np.zeros((HALF, HALF), ml_dtypes.bfloat16)
    lane = np.arange(HALF)
    table[lane, (HALF - lane) % HALF] = 1
    return table


def x_tables(slabs):
    length = 4 * slabs
    cell = (np.arange(4)[:, None] + 4 * np.arange(slabs)[None, :]).reshape(-1)
    angle = (np.arange(length)[:, None] * cell[None, :] % length) * (2 * np.pi / length)
    cosine, sine = np.cos(angle), np.sin(angle)
    forward = np.block([[cosine, sine], [-sine, cosine]])
    inverse = np.block([[cosine.T, -sine.T], [sine.T, cosine.T]])
    return forward, inverse


def split(values):
    high = values.astype(BF16)
    return high, (values - high.astype(F32)).astype(BF16)


def dot(a, b):
    return jnp.dot(a, b, preferred_element_type=F32)


def dot3(a, b):
    return dot(a[0], b[0]) + (dot(a[0], b[1]) + dot(a[1], b[0]))


def lane_of(shape):
    return lax.broadcasted_iota(jnp.int32, shape, 1)


def by_kind(values, kinds):
    zero = jnp.zeros_like(values)
    return jnp.concatenate(
        [jnp.where(kinds == kind, values, zero) for kind in range(KS)], axis=0
    )


def footprints(packed, stk_ref, fp_ref, first):
    count = packed.shape[1]
    turned = jnp.transpose(packed.astype(F32))
    kinds = turned[:, PANELS + 2 : PANELS + 3]
    charges = jnp.concatenate([turned[:, :PANELS], turned[:, :PANELS]], axis=1)
    offset = kinds - jnp.where(lane_of((count, LANES)) < PANELS, 0.0, 1.0)
    spread = jnp.concatenate(
        [jnp.where(offset == kind, charges, 0.0).astype(BF16) for kind in range(0, KS, 2)], axis=1
    )
    result = dot(spread, stk_ref[...])
    for pair in range(4):
        part = result[:, pair * LANES : (pair + 1) * LANES]
        fp_ref[pl.ds(first * 8 + 2 * pair, count, stride=8), :] = part
        fp_ref[pl.ds(first * 8 + 2 * pair + 1, count, stride=8), :] = pltpu.roll(part, 64, 1)


def lane_in(plane, shape):
    return (lane_of(shape) - 8 * plane) & (LANES - 1)


def edge_codes(planes, shape):
    code = jnp.full(shape, 3, jnp.int32)
    for plane in planes:
        lane = lane_in(plane, shape)
        code = jnp.where(lane >= LANES - 2, 0, jnp.where(lane < 2, 1, code))
    return code


def scatter_columns(fp_ref, first, place_of, count, grids, edge_ref, planes):
    shape = (8, LANES)
    lanes = [lane_in(plane, shape) for plane in planes]
    codes = edge_codes(planes, shape)

    def step(index, carry):
        updates = []
        for inner in range(UNROLL):
            column = index * UNROLL + inner
            row, begin, edge, turn, _ = place_of(column)
            value = fp_ref[pl.ds(pl.multiple_of((first + column) * 8, 8), 8), :]
            turned = pltpu.roll(value, turn, 1)
            terms = [jnp.where(((lane - begin) & -8) == 0, turned, 0.0) for lane in lanes]
            terms.append(jnp.where(codes == edge, turned, 0.0))
            updates.append((pl.ds(row, 8), terms))
        refs = [grids[plane] for plane in planes] + [edge_ref]
        for where, terms in updates:
            sums = [ref[where, :] + term for ref, term in zip(refs, terms)]
            for ref, total in zip(refs, sums):
                ref[where, :] = total
        return carry

    lax.fori_loop(0, lax.shift_right_logical(count + UNROLL - 1, 5), step, 0)


def sample_columns(pot_refs, edge_ref, place_of, count, sp_ref, first, planes):
    shape = (8, LANES)
    lanes = [lane_in(plane, shape) for plane in planes]
    codes = edge_codes(planes, shape)

    def step(index, carry):
        results = []
        for inner in range(UNROLL):
            column = index * UNROLL + inner
            row, begin, edge, _, turn = place_of(column)
            where = pl.ds(row, 8)
            result = jnp.where(codes == edge, edge_ref[where, :], 0.0)
            for plane, lane in zip(planes, lanes):
                result = jnp.where(((lane - begin) & -8) == 0, pot_refs[plane][where, :], result)
            turned = pltpu.roll(result, turn, 1)
            results.append((pl.ds(pl.multiple_of((first + column) * 8, 8), 8), turned))
        for where, result in results:
            sp_ref[where, :] = result
        return carry

    lax.fori_loop(0, lax.shift_right_logical(count + UNROLL - 1, 5), step, 0)


def far_sums(sp_ref, kinds, stk_ref, first):
    count = kinds.shape[1]
    lane = lane_of((count, LANES))
    pairs = []
    for pair in range(4):
        even = sp_ref[pl.ds(first * 8 + 2 * pair, count, stride=8), :]
        odd = sp_ref[pl.ds(first * 8 + 2 * pair + 1, count, stride=8), :]
        pairs.append(jnp.where(lane < 64, even, pltpu.roll(odd, 64, 1)).astype(BF16))
    samples = jnp.concatenate(pairs, axis=1)
    sums = lax.dot_general(
        stk_ref[...], samples, (((1,), (1,)), ((), ())), preferred_element_type=F32
    )
    result = jnp.zeros((PANELS, count), F32)
    for kind in range(KS):
        result += jnp.where(kinds == kind, sums[kind * PANELS : (kind + 1) * PANELS, :], 0.0)
    return result


OWN = ((0, 1, 2, 3), 2)
BESIDE = (((0, 1), 6), ((2, 3), -2))


def place_in_facts(facts_ref, start=0):
    return lambda column: [facts_ref[row, start + column] for row in (0, 1, 4, 5, 6)]


def facts_of(packed_ref, row, shift_i):
    facts = packed_ref[row : row + 16, :].astype(F32).astype(jnp.int32)
    by, bz, kinds, live = (facts[index : index + 1, :] for index in range(4))
    begin = 4 * by - 2
    edge = jnp.where(by == 0, 0, jnp.where(by == NY // 8 - 1, 1, 2))
    turn = begin - 8 * shift_i
    rows = [4 * bz, begin, kinds, live, edge, turn & (LANES - 1), -turn & (LANES - 1), by]
    return jnp.concatenate(rows, axis=0)


def own_kernel(packed_ref, stencil_ref,
               g0, g1, g2, g3, edge_ref, stk_ref, out_facts, fp_ref, rows_ref, facts_ref, sems):
    copy = pltpu.make_async_copy(stencil_ref, rows_ref, sems.at[0])
    copy.start()
    out_facts[...] = facts_of(packed_ref, PANELS, OWN[1])
    facts_copy = pltpu.make_async_copy(out_facts, facts_ref, sems.at[1])
    facts_copy.start()
    for ref in (g0, g1, g2, g3, edge_ref):
        ref[...] = jnp.zeros_like(ref)
    shape = (POINTS, POINTS)
    point = lax.broadcasted_iota(jnp.int32, shape, 0)
    target = (point & 7) * 64 + lax.shift_right_logical(point, 3)
    order = jnp.where(lane_of(shape) == target, 1.0, 0.0).astype(BF16)
    facts_copy.wait()
    copy.wait()
    stk_ref[...] = dot(rows_ref[...], order).astype(BF16)
    live = facts_ref[3, 0]

    @pl.when(live > LANES)
    def _():
        footprints(packed_ref[...], stk_ref, fp_ref, 0)

    @pl.when(live <= LANES)
    def _():
        footprints(packed_ref[:, 0:LANES], stk_ref, fp_ref, 0)

    scatter_columns(fp_ref, 0, place_in_facts(facts_ref), live, (g0, g1, g2, g3), edge_ref, OWN[0])


def chunks_beside(facts_ref, slots):
    for first in range(0, slots, LANES):
        counts = [jnp.clip(facts_ref[3, side * slots] - first, 0, LANES) for side in range(2)]
        yield first, counts


def both_sides(ref, slots, first):
    return jnp.concatenate(
        [ref[:, side * slots + first : side * slots + first + LANES] for side in range(2)], axis=1
    )


def beside_kernel(odd_ref, own_ref, first_ref, second_ref, stk_ref, i0, i1, i2, i3, iedge,
                  g0, g1, g2, g3, edge_ref, out_edge, out_facts, pool_ref, fp_ref, facts_ref, sem):
    height, slots = own_ref.shape
    before, after = pl.ds(0, height), pl.ds(2 * height, height)
    pool_ref[height : 2 * height, :] = own_ref[...]

    @pl.when(odd_ref[0] == 0)
    def _():
        pool_ref[after, :] = first_ref[...]
        pool_ref[before, :] = second_ref[...]

    @pl.when(odd_ref[0] != 0)
    def _():
        pool_ref[before, :] = first_ref[...]
        pool_ref[after, :] = second_ref[...]

    for side, (_, shift_i) in enumerate(BESIDE):
        out_facts[:, side * slots : (side + 1) * slots] = facts_of(pool_ref, 2 * side * height + PANELS, shift_i)
    copy = pltpu.make_async_copy(out_facts, facts_ref, sem)
    copy.start()

    def project(first):
        here = slice(first, first + LANES)
        packed = jnp.concatenate(
            [pool_ref[0:height, here], pool_ref[2 * height : 3 * height, here]], axis=1
        )
        footprints(packed, stk_ref, fp_ref, 2 * first)

    project(0)
    copy.wait()
    for first, counts in chunks_beside(facts_ref, slots):
        if first:
            @pl.when(counts[0] + counts[1] > 0)
            def _(first=first):
                project(first)

        for side, (planes, _) in enumerate(BESIDE):
            scatter_columns(fp_ref, 2 * first + side * LANES, place_in_facts(facts_ref, side * slots + first),
                            counts[side], (g0, g1, g2, g3), edge_ref, planes)
    for ref in (g0, g1, g2, g3, edge_ref):
        ref[0:8, :] += ref[NZ:ZROWS, :]
    total = pltpu.roll(edge_ref[0:LANES, :], 2, 1)
    for block in range(1, 4):
        total += pltpu.roll(edge_ref[block * LANES : (block + 1) * LANES, :], 32 * block + 2, 1)
    out_edge[...] = total


def exponent_of(values):
    top = functools.reduce(jnp.maximum, [jnp.max(jnp.abs(v), axis=0, keepdims=True) for v in values])
    top = jnp.maximum(jnp.max(top, axis=1, keepdims=True), 2.0**-100)
    return jnp.ceil(jnp.log2(top)) - BOUND


def quarter(table_ref, index):
    rows = table_ref.shape[0] // 4
    return tuple(table_ref[part * rows : (part + 1) * rows, :] for part in (2 * index, 2 * index + 1))


def z_kernel(slabs, g0, g1, g2, g3, edge_ref, w_ref, out_ref, wide_ref):
    widen_edge(edge_ref, wide_ref)
    half = slabs // 2
    parts = NZ // (2 * slabs)
    planes = parts // 2
    stride = 4 * parts + SCALE_ROWS
    sums = []
    for parity in range(2):
        where = pl.ds(parity, NZ // 2, stride=2)
        columns = []
        for plane, grid in enumerate((g0, g1, g2, g3)):
            at_edge = edge_codes((plane,), (NZ // 2, LANES)) < 2
            values = grid[where, :] + jnp.where(at_edge, wide_ref[where, :], 0.0)
            columns.append(pltpu.roll(values, LANES - 8 * plane, 1) if plane else values)
        sums.append(dot3(quarter(w_ref, parity), split(jnp.concatenate(columns, axis=1))))
    results = (sums[0] + sums[1], sums[0] - sums[1])
    exponent = exponent_of(results)
    scale = jnp.exp2(-exponent)
    results = [result * scale for result in results]
    for upper, result in enumerate(results):
        for part in range(parts):
            index = part // planes * (planes + 1) + part % planes + upper
            for tile in range(2):
                rows = result[(index * 2 + tile) * half : (index * 2 + tile + 1) * half, :]
                start = (tile * slabs + upper * half) * stride + part
                for plane in range(4):
                    out_ref[pl.ds(start + plane * parts, half, stride=stride), :] = rows[
                        :, plane * LANES : (plane + 1) * LANES
                    ]
    for row in range(SCALE_ROWS):
        out_ref[pl.ds(4 * parts + row, 2 * slabs, stride=stride), :] = jnp.broadcast_to(
            exponent, (2 * slabs, LANES)
        )


def hat_kernel(planes, offset_ref, hat_ref, turn_ref, out_ref):
    length = hat_ref.shape[1]
    values = jnp.concatenate([hat_ref[offset_ref[0] + plane] for plane in range(planes)], axis=0)
    values = values * (1.0 / (length * NY))
    upper = values[:, HALF:]
    high, low = split(upper)
    rest = (upper - high.astype(F32) - low.astype(F32)).astype(BF16)
    turn = turn_ref[...]
    upper = dot(high, turn) + (dot(low, turn) + dot(rest, turn))
    for plane in range(planes):
        here = slice(plane * length, (plane + 1) * length)
        out_ref[plane] = jnp.concatenate([values[here, :HALF], upper[here, :]], axis=1)


def plane_kernel(slabs, planes, in_ref, hat_ref, y_ref, x_ref, out_ref, exponent_ref, ah_ref, al_ref):
    length = 4 * slabs
    rows = planes * length
    parts = 2 * planes
    stride = 4 * parts + SCALE_ROWS

    def pieces():
        for tile in range(2):
            for part in range(2):
                for xi in range(4):
                    for plane in range(planes):
                        yield tile, part, plane, xi

    scales = [
        jnp.exp2(in_ref[pl.ds(tile * slabs * stride + 4 * parts, slabs, stride=stride), :])
        for tile in range(2)
    ]
    for tile, part, plane, xi in pieces():
        start = tile * slabs * stride + xi * parts + part * planes + plane
        row = (part * planes + plane) * length + xi * slabs
        high, low = split(in_ref[pl.ds(start, slabs, stride=stride), :] * scales[tile])
        ah_ref[row : row + slabs, tile * LANES : (tile + 1) * LANES] = high
        al_ref[row : row + slabs, tile * LANES : (tile + 1) * LANES] = low
    first_lane = lane_of((rows, HALF)) == 0
    turned = dot3((ah_ref[...], al_ref[...]), (y_ref[0:NY, :], y_ref[NY : 2 * NY, :]))
    even = (turned[:rows, :HALF], turned[rows:, :HALF])
    odd = (turned[:rows, HALF:], turned[rows:, HALF:])
    zero_odd = [jnp.where(first_lane, 0.0, values) for values in odd]
    real = jnp.concatenate(
        [even[0] + zero_odd[1], jnp.where(first_lane, odd[0], even[0] - zero_odd[1])], axis=1
    )
    imag = jnp.concatenate(
        [even[1] - zero_odd[0], jnp.where(first_lane, odd[1], even[1] + zero_odd[0])], axis=1
    )
    size = 2 * length

    def along_x(values, first):
        high, low = split(values)
        table = x_ref[first * size : (first + 1) * size, :]
        rest = x_ref[(first + 1) * size : (first + 2) * size, :]
        both = dot(jnp.concatenate([table, table], axis=1), jnp.concatenate([high, low], axis=0))
        return both + dot(rest, high)

    for plane in range(planes):
        here = slice(plane * length, (plane + 1) * length)
        there = slice(rows + plane * length, rows + (plane + 1) * length)
        values = along_x(jnp.concatenate([real[here], imag[here]], axis=0), 0)
        values = values * jnp.concatenate([hat_ref[plane], hat_ref[plane]], axis=0)
        values = along_x(values, 2)
        low, high = values[:, :HALF], values[:, HALF:]
        lane = first_lane[:length]
        even_r = jnp.where(lane, low[:length], low[:length] + high[:length])
        even_i = jnp.where(lane, low[length:], low[length:] + high[length:])
        odd_r = jnp.where(lane, high[:length], high[length:] - low[length:])
        odd_i = jnp.where(lane, high[length:], low[:length] - high[:length])
        ah_ref[here, :], al_ref[here, :] = split(jnp.concatenate([even_r, odd_r], axis=1))
        ah_ref[there, :], al_ref[there, :] = split(jnp.concatenate([even_i, odd_i], axis=1))
    turned = dot3((ah_ref[...], al_ref[...]), (y_ref[2 * NY : 3 * NY, :], y_ref[3 * NY : 4 * NY, :]))
    tops = [
        jnp.max(in_ref[pl.ds(tile * slabs * stride + 4 * parts, slabs, stride=stride), :], axis=0, keepdims=True)
        for tile in range(2)
    ]
    exponent = jnp.broadcast_to(jnp.maximum(*tops) + BOUND - HEADROOM + math.ceil(math.log2(length * NY) / 2), (8, LANES))
    exponent_ref[...] = exponent
    scale = jnp.exp2(-exponent[0:1, 0:1])
    for tile, part, plane, xi in pieces():
        here = slice((part * planes + plane) * length + xi * slabs, (part * planes + plane) * length + (xi + 1) * slabs)
        start = tile * slabs * stride + xi * parts + part * planes + plane
        out_ref[pl.ds(start, slabs, stride=stride), :] = (
            turned[here, tile * LANES : (tile + 1) * LANES] * scale
        )


def potential_kernel(slabs, in_ref, exponent_ref, v_ref, p0, p1, p2, p3, edge_ref):
    half = slabs // 2
    parts = NZ // (2 * slabs)
    planes = parts // 2
    stride = 4 * parts
    sums = []
    for parity in range(2):
        columns = []
        for plane in range(4):
            rows = []
            for part in range(parts):
                upper = (part % planes + parity) % 2
                for tile in range(2):
                    start = (tile * slabs + upper * half) * stride + plane * parts + part
                    rows.append(in_ref[pl.ds(start, half, stride=stride), :])
            columns.append(jnp.concatenate(rows, axis=0))
        sums.append(dot3(quarter(v_ref, parity), split(jnp.concatenate(columns, axis=1))))
    scale = jnp.exp2(exponent_ref[0:1, 0:1])
    shape = (LANES, LANES)
    edges = [jnp.zeros(shape, F32)] * 4
    halves_of_z = [((sums[0] + sums[1]) * scale), ((sums[0] - sums[1]) * scale)]
    for plane, pot in enumerate((p0, p1, p2, p3)):
        at_edge = edge_codes((plane,), shape) < 2
        for upper in range(2):
            result = halves_of_z[upper][:, plane * LANES : (plane + 1) * LANES].astype(BF16).astype(F32)
            if plane:
                result = pltpu.roll(result, 8 * plane, 1)
            pot[upper * (NZ // 2) : (upper + 1) * (NZ // 2), :] = result
            for block in range(2):
                edges[2 * upper + block] = jnp.where(
                    at_edge, result[block * LANES : (block + 1) * LANES, :], edges[2 * upper + block]
                )
        pot[NZ:ZROWS, :] = pot[0:8, :]
    edge = pltpu.roll(edges[0], 2, 1)
    for block in range(1, 4):
        edge += pltpu.roll(edges[block], 32 * block + 2, 1)
    edge_ref[...] = edge.astype(BF16)


def widen_edge(edge_ref, wide_ref):
    for block in range(4):
        wide_ref[block * LANES : (block + 1) * LANES, :] = pltpu.roll(
            edge_ref[...].astype(F32), (LANES - 2 - 32 * block) % LANES, 1
        )
    wide_ref[NZ:ZROWS, :] = wide_ref[0:8, :]


def masked(values, live):
    return jnp.where(lane_of(values.shape) < live, values, 0.0)


def own_sample_kernel(facts_ref, p0, p1, p2, p3, edge_ref, kinds_ref, stk_ref, out_ref, wide_ref, sp_ref):
    widen_edge(edge_ref, wide_ref)
    live = facts_ref[3, 0]
    slots = kinds_ref.shape[1]
    sample_columns((p0, p1, p2, p3), wide_ref, place_in_facts(facts_ref), live, sp_ref, 0, OWN[0])

    @pl.when(live > LANES)
    def _():
        out_ref[...] = masked(far_sums(sp_ref, kinds_ref[2:3, :], stk_ref, 0), live)

    @pl.when(live <= LANES)
    def _():
        out_ref[:, 0:LANES] = masked(far_sums(sp_ref, kinds_ref[2:3, 0:LANES], stk_ref, 0), live)
        out_ref[:, LANES:slots] = jnp.zeros((PANELS, slots - LANES), F32)


def beside_sample_kernel(odd_ref, facts_ref, p0, p1, p2, p3, edge_ref, kinds_ref, stk_ref, out0, out1, wide_ref, sp_ref):
    widen_edge(edge_ref, wide_ref)
    slots = kinds_ref.shape[1] // 2
    outs = (out0, out1)
    for first, counts in chunks_beside(facts_ref, slots):
        here = slice(first, first + LANES)
        for side, (planes, _) in enumerate(BESIDE):
            sample_columns((p0, p1, p2, p3), wide_ref, place_in_facts(facts_ref, side * slots + first),
                           counts[side], sp_ref, 2 * first + side * LANES, planes)

        @pl.when(counts[0] + counts[1] > 0)
        def _(first=first, counts=counts, here=here):
            kinds = both_sides(kinds_ref.at[2:3, :], slots, first)
            result = far_sums(sp_ref, kinds, stk_ref, 2 * first)
            sums = [masked(result[:, side * LANES : (side + 1) * LANES], counts[side]) for side in range(2)]
            even = jnp.broadcast_to(odd_ref[0], sums[0].shape) == 0
            out0[:, here] = jnp.where(even, sums[1], sums[0])
            out1[:, here] = jnp.where(even, sums[0], sums[1])

        @pl.when(counts[0] + counts[1] <= 0)
        def _(here=here):
            for out in outs:
                out[:, here] = jnp.zeros((PANELS, LANES), F32)


def near_kernel(live_ref, here_ref, there_ref, source_ref, block_ref, table_ref, out_ref):
    live = live_ref[0]
    fanout, slots = source_ref.shape
    height = here_ref.shape[0] // 3
    pool = jnp.concatenate(
        [ref[step * height : step * height + PANELS, :] for step in range(3) for ref in (here_ref, there_ref)],
        axis=1,
    )
    total = pool.shape[1]
    for first in range(0, slots, LANES):
        where = slice(first, first + LANES)

        @pl.when(live > first)
        def _(where=where, first=first):
            index = lax.broadcasted_iota(jnp.int32, (total, LANES), 0)
            result = jnp.zeros((PANELS, LANES), F32)
            for j in range(fanout):
                chosen = jnp.where(index == source_ref[j : j + 1, where], 1.0, 0.0).astype(BF16)
                gathered = dot(pool, chosen)
                result += dot(
                    table_ref[...], by_kind(gathered, block_ref[j : j + 1, where]).astype(BF16)
                )
            column = first + lane_of((PANELS, LANES))
            out_ref[:, where] = jnp.where(column < live, result, 0.0)

        @pl.when(live <= first)
        def _(where=where):
            out_ref[:, where] = jnp.zeros((PANELS, LANES), F32)


def shape_of(*dims, dtype=F32):
    return jax.ShapeDtypeStruct(dims, dtype)


def body(slabs, tiles, charges, live_count, slot_brick, slot_stencil, stencils, near_source,
         near_block, near_blocks, kernel_hat):
    slots = charges.shape[1]
    owners = slabs * tiles
    planes = kernel_hat.shape[0] // 2
    length = kernel_hat.shape[1]
    parts = NZ // owners
    axes = ("tile", "slab")
    both = ("slab", "tile")

    def moved(values, step_of, swap=0):
        pairs = [
            (a * tiles + b, (a + step_of(a)) % slabs * tiles + (b + swap) % tiles)
            for a in range(slabs)
            for b in range(tiles)
        ]
        return lax.ppermute(values, both, pairs)

    def to_first(values):
        return moved(values, lambda a: 1 - 2 * (a % 2))

    def to_second(values):
        return moved(values, lambda a: 2 * (a % 2) - 1)

    def to_other_tile(values):
        return moved(values, lambda a: 0, 1)

    odd = (lax.axis_index("slab") % 2)[None]
    row = lax.broadcasted_iota(jnp.int32, (PANELS + 16, slots), 0)
    column = lax.broadcasted_iota(jnp.int32, (PANELS + 16, slots), 1)
    live = jnp.broadcast_to(live_count[0], row.shape)
    brick = jnp.broadcast_to(slot_brick[None, :], row.shape)
    facts = lax.shift_right_logical(brick, jnp.where(row == PANELS, 7, 0)) & (NZ // 4 - 1)
    facts = jnp.where(row == PANELS + 2, slot_stencil[None, :], jnp.where(row == PANELS + 3, live, facts))
    held = jnp.where(column < live, jnp.pad(charges, ((0, 16), (0, 0))), jnp.zeros((), BF16))
    packed = jnp.where(row < PANELS, held, facts.astype(BF16))
    from_first = to_first(packed)
    from_second = to_second(packed)

    grid = shape_of(ZROWS, LANES)
    *grids, stk, facts = pl.pallas_call(
        own_kernel,
        out_shape=(grid,) * 5 + (shape_of(KS * PANELS, POINTS, dtype=BF16), shape_of(8, slots, dtype=jnp.int32)),
        in_specs=[VMEM, pl.BlockSpec(memory_space=pl.ANY)],
        out_specs=(VMEM,) * 7,
        scratch_shapes=[
            pltpu.VMEM((slots * 8, LANES), F32),
            pltpu.VMEM((KS * PANELS, POINTS), BF16),
            pltpu.SMEM((8, slots), jnp.int32),
            pltpu.SemaphoreType.DMA((2,)),
        ],
        compiler_params=PARAMS,
        name="own_scatter",
    )(packed, stencils.reshape(KS * PANELS, POINTS))

    g = pl.pallas_call(
        beside_kernel,
        out_shape=(grid,) * 5
        + (
            shape_of(LANES, LANES),
            shape_of(8, 2 * slots, dtype=jnp.int32),
            shape_of(3 * (PANELS + 16), slots, dtype=BF16),
        ),
        in_specs=[SMEM] + [VMEM] * 9,
        out_specs=(VMEM,) * 8,
        scratch_shapes=[
            pltpu.VMEM((2 * slots * 8, LANES), F32),
            pltpu.SMEM((8, 2 * slots), jnp.int32),
            pltpu.SemaphoreType.DMA,
        ],
        input_output_aliases={5: 0, 6: 1, 7: 2, 8: 3, 9: 4},
        compiler_params=PARAMS,
        name="beside_scatter",
    )(odd, packed, from_first, from_second, stk, *grids)
    facts2 = g[6]
    edge = to_other_tile(g[5])

    forward, inverse = z_tables(slabs, tiles)
    rows = owners * (4 * parts + SCALE_ROWS)
    sent = pl.pallas_call(
        functools.partial(z_kernel, slabs),
        out_shape=shape_of(rows, LANES),
        in_specs=[VMEM] * 6,
        out_specs=VMEM,
        scratch_shapes=[pltpu.VMEM((ZROWS, LANES), F32)],
        compiler_params=PARAMS,
        name="z_forward",
    )(*g[:4], edge, jnp.asarray(halves(*forward)))

    def exchanged(values, kept):
        values = values.reshape(owners, -1, LANES)[:, :kept].astype(jnp.float16)
        values = lax.all_to_all(values, axes, 0, 0, tiled=True)
        return values

    def widened(values):
        return values.astype(F32).reshape(-1, LANES)

    hat, sent = lax.optimization_barrier((kernel_hat, sent))
    got = exchanged(sent, 4 * parts + SCALE_ROWS)
    me = lax.axis_index("slab") * tiles + lax.axis_index("tile")
    offset = (me >= owners // 2).astype(jnp.int32)[None]
    hat = pl.pallas_call(
        functools.partial(hat_kernel, planes),
        out_shape=shape_of(planes, length, NY),
        in_specs=[SMEM] + [VMEM] * 2,
        out_specs=VMEM,
        compiler_params=PARAMS,
        name="hat_order",
    )(offset, hat, jnp.asarray(reversal()))

    got, hat = lax.optimization_barrier((got, hat))
    pool = (g[7], to_other_tile(g[7]))
    direction = near_source // slots
    pool_index = (direction // 3 * 2 + (direction % 3 != 1).astype(jnp.int32)) * slots + near_source % slots
    near = pl.pallas_call(
        near_kernel,
        out_shape=shape_of(PANELS, slots),
        in_specs=[SMEM] + [VMEM] * 5,
        out_specs=VMEM,
        compiler_params=PARAMS,
        name="near_field",
    )(live_count, *pool, pool_index.T, near_block.T, near_blocks.reshape(PANELS, KN * PANELS))

    back, exponent = pl.pallas_call(
        functools.partial(plane_kernel, slabs, planes),
        out_shape=(shape_of(rows, LANES), shape_of(8, LANES)),
        in_specs=[VMEM] * 4,
        out_specs=(VMEM, VMEM),
        scratch_shapes=[pltpu.VMEM((2 * planes * length, NY), BF16)] * 2,
        compiler_params=PARAMS,
        name="plane_filter",
    )(widened(got), hat, jnp.asarray(halves(y_table(), y_table().T)), jnp.asarray(halves(*x_tables(slabs))))
    back, near = lax.optimization_barrier((exchanged(back, 4 * parts), near))

    pot = pl.pallas_call(
        functools.partial(potential_kernel, slabs),
        out_shape=(grid,) * 4 + (shape_of(LANES, LANES, dtype=BF16),),
        in_specs=[VMEM] * 3,
        out_specs=(VMEM,) * 5,
        compiler_params=PARAMS,
        name="z_inverse",
    )(widened(back), exponent, jnp.asarray(halves(*inverse)))
    edge = to_other_tile(pot[4])

    def sample_scratch(width):
        return [pltpu.VMEM((ZROWS, LANES), F32), pltpu.VMEM((width * 8, LANES), F32)]

    sums = shape_of(PANELS, slots)
    others = pl.pallas_call(
        beside_sample_kernel,
        out_shape=(sums, sums),
        in_specs=[SMEM] * 2 + [VMEM] * 7,
        out_specs=(VMEM, VMEM),
        scratch_shapes=sample_scratch(2 * slots),
        compiler_params=PARAMS,
        name="beside_sample",
    )(odd, facts2, *pot[:4], edge, facts2, stk)
    first = to_first(others[0])
    second = to_second(others[1])
    own = pl.pallas_call(
        own_sample_kernel,
        out_shape=sums,
        in_specs=[SMEM] + [VMEM] * 7,
        out_specs=VMEM,
        scratch_shapes=sample_scratch(slots),
        compiler_params=PARAMS,
        name="own_sample",
    )(facts, *pot[:4], edge, facts, stk)
    return own + near + first + second


def solution(mesh):
    both = ("slab", "tile")
    in_specs = (
        P(None, both),
        P(both),
        P(both),
        P(both),
        P(),
        P(both, None),
        P(both, None),
        P(),
        P(both, None, None),
    )
    return jax.shard_map(
        functools.partial(body, mesh.shape["slab"], mesh.shape["tile"]),
        mesh=mesh,
        in_specs=in_specs,
        out_specs=P(None, both),
        check_vma=False,
    )
```

```python
import functools
import math

import jax
import jax.numpy as jnp
import ml_dtypes
import numpy as np
from jax import lax
from jax.experimental import pallas as pl
from jax.experimental.pallas import tpu as pltpu
from jax.sharding import PartitionSpec as P

PANELS = 64
POINTS = 512
NY = 256
NZ = 512
KS = 16
KN = 16
LANES = 128
ZROWS = NZ + 8
UNROLL = 32
HALF = NY // 2
SCALE_ROWS = 8
BOUND = 12.0
HEADROOM = 15.0
F32 = jnp.float32
BF16 = jnp.bfloat16
SMEM = pl.BlockSpec(memory_space=pltpu.SMEM)
VMEM = pl.BlockSpec(memory_space=pltpu.VMEM)
PARAMS = pltpu.CompilerParams(vmem_limit_bytes=48 * 1024 * 1024)


def halves(*tables):
    parts = []
    for table in tables:
        high = table.astype(ml_dtypes.bfloat16)
        parts += [high, (table - high.astype(np.float64)).astype(ml_dtypes.bfloat16)]
    return np.concatenate(parts, axis=0)


def z_tables(slabs, tiles):
    half = slabs // 2
    planes = NZ // (slabs * tiles) // 2
    plane = np.arange(planes + 1)[:, None, None]
    tile = np.arange(tiles)[None, :, None]
    slab = np.arange(half)[None, None, :]
    owner = slab * tiles + tile
    freq = (owner * 2 * planes + plane).reshape(-1)
    forward, inverse = [], []
    for parity in range(2):
        cell = np.arange(parity, NZ, 2) - 2
        angle = (freq[:, None] * cell[None, :] % NZ) * (2 * np.pi / NZ)
        forward.append(np.concatenate([np.cos(angle), -np.sin(angle)], axis=0))
        upper = (plane[:-1] + parity) % 2
        back = ((upper * half * tiles + owner) * 2 * planes + plane[:-1] + upper).reshape(-1)
        cell = np.arange(NZ // 2) - 2
        angle = (back[:, None] * cell[None, :] % NZ) * (2 * np.pi / NZ)
        weight = np.where(back == 0, 1.0, 2.0)[:, None] / NZ
        inverse.append(np.concatenate([weight * np.cos(angle), -weight * np.sin(angle)], axis=0).T)
    return forward, inverse


def y_table():
    angle = (np.arange(NY)[:, None] * np.arange(HALF + 1)[None, :] % NY) * (2 * np.pi / NY)
    return np.concatenate([np.cos(angle[:, :HALF]), np.cos(angle[:, HALF:]), np.sin(angle[:, 1:HALF])], axis=1)


def reversal():
    table = np.zeros((HALF, HALF), ml_dtypes.bfloat16)
    lane = np.arange(HALF)
    table[lane, (HALF - lane) % HALF] = 1
    return table


def x_tables(slabs):
    length = 4 * slabs
    cell = (np.arange(4)[:, None] + 4 * np.arange(slabs)[None, :]).reshape(-1)
    angle = (np.arange(length)[:, None] * cell[None, :] % length) * (2 * np.pi / length)
    cosine, sine = np.cos(angle), np.sin(angle)
    forward = np.block([[cosine, sine], [-sine, cosine]])
    inverse = np.block([[cosine.T, -sine.T], [sine.T, cosine.T]])
    return forward, inverse


def joined(tables):
    result = []
    for table in tables:
        high, low = np.split(halves(table), 2)
        result.append(np.block([[high, high], [low, np.zeros_like(low)]]))
    return np.concatenate(result, axis=0)


def split(values):
    high = values.astype(BF16)
    return high, (values - high.astype(F32)).astype(BF16)


def dot(a, b):
    return jnp.dot(a, b, preferred_element_type=F32)


def dot3(a, b):
    return dot(a[0], b[0]) + (dot(a[0], b[1]) + dot(a[1], b[0]))


def lane_of(shape):
    return lax.broadcasted_iota(jnp.int32, shape, 1)


def by_kind(values, kinds):
    zero = jnp.zeros_like(values)
    return jnp.concatenate(
        [jnp.where(kinds == kind, values, zero) for kind in range(KS)], axis=0
    )


def footprints(packed, stk_ref, fp_ref, first):
    count = packed.shape[1]
    turned = jnp.transpose(packed.astype(F32))
    kinds = turned[:, PANELS + 2 : PANELS + 3]
    charges = jnp.concatenate([turned[:, :PANELS], turned[:, :PANELS]], axis=1)
    offset = kinds - jnp.where(lane_of((count, LANES)) < PANELS, 0.0, 1.0)
    spread = jnp.concatenate(
        [jnp.where(offset == kind, charges, 0.0).astype(BF16) for kind in range(0, KS, 2)], axis=1
    )
    result = dot(spread, stk_ref[...])
    for pair in range(4):
        part = result[:, pair * LANES : (pair + 1) * LANES]
        fp_ref[pl.ds(first * 8 + 2 * pair, count, stride=8), :] = part
        fp_ref[pl.ds(first * 8 + 2 * pair + 1, count, stride=8), :] = pltpu.roll(part, 64, 1)


def lane_in(plane, shape):
    return (lane_of(shape) - 8 * plane) & (LANES - 1)


def edge_codes(planes, shape):
    code = jnp.full(shape, 3, jnp.int32)
    for plane in planes:
        lane = lane_in(plane, shape)
        code = jnp.where(lane >= LANES - 2, 0, jnp.where(lane < 2, 1, code))
    return code


def scatter_columns(fp_ref, first, place_of, count, grids, edge_ref, planes):
    shape = (8, LANES)
    lanes = [lane_in(plane, shape) for plane in planes]
    codes = edge_codes(planes, shape)

    def step(index, carry):
        updates = []
        for inner in range(UNROLL):
            column = index * UNROLL + inner
            row, begin, edge, turn, _ = place_of(column)
            value = fp_ref[pl.ds(pl.multiple_of((first + column) * 8, 8), 8), :]
            turned = pltpu.roll(value, turn, 1)
            terms = [jnp.where(((lane - begin) & -8) == 0, turned, 0.0) for lane in lanes]
            terms.append(jnp.where(codes == edge, turned, 0.0))
            updates.append((pl.ds(row, 8), terms))
        refs = [grids[plane] for plane in planes] + [edge_ref]
        for where, terms in updates:
            sums = [ref[where, :] + term for ref, term in zip(refs, terms)]
            for ref, total in zip(refs, sums):
                ref[where, :] = total
        return carry

    lax.fori_loop(0, lax.shift_right_logical(count + UNROLL - 1, 5), step, 0)


def sample_columns(pot_refs, edge_ref, place_of, count, sp_ref, first, planes):
    shape = (8, LANES)
    lanes = [lane_in(plane, shape) for plane in planes]
    codes = edge_codes(planes, shape)

    def step(index, carry):
        results = []
        for inner in range(UNROLL):
            column = index * UNROLL + inner
            row, begin, edge, _, turn = place_of(column)
            where = pl.ds(row, 8)
            result = jnp.where(codes == edge, edge_ref[where, :], 0.0)
            for plane, lane in zip(planes, lanes):
                result = jnp.where(((lane - begin) & -8) == 0, pot_refs[plane][where, :], result)
            turned = pltpu.roll(result, turn, 1)
            results.append((pl.ds(pl.multiple_of((first + column) * 8, 8), 8), turned))
        for where, result in results:
            sp_ref[where, :] = result
        return carry

    lax.fori_loop(0, lax.shift_right_logical(count + UNROLL - 1, 5), step, 0)


def far_sums(sp_ref, kinds, stk_ref, first):
    count = kinds.shape[1]
    lane = lane_of((count, LANES))
    pairs = []
    for pair in range(4):
        even = sp_ref[pl.ds(first * 8 + 2 * pair, count, stride=8), :]
        odd = sp_ref[pl.ds(first * 8 + 2 * pair + 1, count, stride=8), :]
        pairs.append(jnp.where(lane < 64, even, pltpu.roll(odd, 64, 1)).astype(BF16))
    samples = jnp.concatenate(pairs, axis=1)
    sums = lax.dot_general(
        stk_ref[...], samples, (((1,), (1,)), ((), ())), preferred_element_type=F32
    )
    result = jnp.zeros((PANELS, count), F32)
    for kind in range(KS):
        result += jnp.where(kinds == kind, sums[kind * PANELS : (kind + 1) * PANELS, :], 0.0)
    return result


OWN = ((0, 1, 2, 3), 2)
BESIDE = (((0, 1), 6), ((2, 3), -2))


def place_in_facts(facts_ref, start=0):
    return lambda column: [facts_ref[row, start + column] for row in (0, 1, 4, 5, 6)]


def facts_of(packed_ref, row, shift_i):
    facts = packed_ref[row : row + 16, :].astype(F32).astype(jnp.int32)
    by, bz, kinds, live = (facts[index : index + 1, :] for index in range(4))
    begin = 4 * by - 2
    edge = jnp.where(by == 0, 0, jnp.where(by == NY // 8 - 1, 1, 2))
    turn = begin - 8 * shift_i
    rows = [4 * bz, begin, kinds, live, edge, turn & (LANES - 1), -turn & (LANES - 1), by]
    return jnp.concatenate(rows, axis=0)


def own_kernel(packed_ref, stencil_ref,
               g0, g1, g2, g3, edge_ref, stk_ref, out_facts, fp_ref, rows_ref, facts_ref, sems):
    copy = pltpu.make_async_copy(stencil_ref, rows_ref, sems.at[0])
    copy.start()
    out_facts[...] = facts_of(packed_ref, PANELS, OWN[1])
    facts_copy = pltpu.make_async_copy(out_facts, facts_ref, sems.at[1])
    facts_copy.start()
    for ref in (g0, g1, g2, g3, edge_ref):
        ref[...] = jnp.zeros_like(ref)
    shape = (POINTS, POINTS)
    point = lax.broadcasted_iota(jnp.int32, shape, 0)
    target = (point & 7) * 64 + lax.shift_right_logical(point, 3)
    order = jnp.where(lane_of(shape) == target, 1.0, 0.0).astype(BF16)
    facts_copy.wait()
    copy.wait()
    stk_ref[...] = dot(rows_ref[...], order).astype(BF16)
    live = facts_ref[3, 0]

    @pl.when(live > LANES)
    def _():
        footprints(packed_ref[...], stk_ref, fp_ref, 0)

    @pl.when(live <= LANES)
    def _():
        footprints(packed_ref[:, 0:LANES], stk_ref, fp_ref, 0)

    scatter_columns(fp_ref, 0, place_in_facts(facts_ref), live, (g0, g1, g2, g3), edge_ref, OWN[0])


def chunks_beside(facts_ref, slots):
    for first in range(0, slots, LANES):
        counts = [jnp.clip(facts_ref[3, side * slots] - first, 0, LANES) for side in range(2)]
        yield first, counts


def both_sides(ref, slots, first):
    return jnp.concatenate(
        [ref[:, side * slots + first : side * slots + first + LANES] for side in range(2)], axis=1
    )


def beside_kernel(odd_ref, own_ref, first_ref, second_ref, stk_ref, i0, i1, i2, i3, iedge,
                  g0, g1, g2, g3, edge_ref, out_edge, out_facts, pool_ref, fp_ref, facts_ref, sem):
    height, slots = own_ref.shape
    before, after = pl.ds(0, height), pl.ds(2 * height, height)
    pool_ref[height : 2 * height, :] = own_ref[...]

    @pl.when(odd_ref[0] == 0)
    def _():
        pool_ref[after, :] = first_ref[...]
        pool_ref[before, :] = second_ref[...]

    @pl.when(odd_ref[0] != 0)
    def _():
        pool_ref[before, :] = first_ref[...]
        pool_ref[after, :] = second_ref[...]

    for side, (_, shift_i) in enumerate(BESIDE):
        out_facts[:, side * slots : (side + 1) * slots] = facts_of(pool_ref, 2 * side * height + PANELS, shift_i)
    copy = pltpu.make_async_copy(out_facts, facts_ref, sem)
    copy.start()

    def project(first):
        here = slice(first, first + LANES)
        packed = jnp.concatenate(
            [pool_ref[0:height, here], pool_ref[2 * height : 3 * height, here]], axis=1
        )
        footprints(packed, stk_ref, fp_ref, 2 * first)

    project(0)
    copy.wait()
    for first, counts in chunks_beside(facts_ref, slots):
        if first:
            @pl.when(counts[0] + counts[1] > 0)
            def _(first=first):
                project(first)

        for side, (planes, _) in enumerate(BESIDE):
            scatter_columns(fp_ref, 2 * first + side * LANES, place_in_facts(facts_ref, side * slots + first),
                            counts[side], (g0, g1, g2, g3), edge_ref, planes)
    for ref in (g0, g1, g2, g3, edge_ref):
        ref[0:8, :] += ref[NZ:ZROWS, :]
    total = pltpu.roll(edge_ref[0:LANES, :], 2, 1)
    for block in range(1, 4):
        total += pltpu.roll(edge_ref[block * LANES : (block + 1) * LANES, :], 32 * block + 2, 1)
    out_edge[...] = total


def exponent_of(values):
    top = functools.reduce(jnp.maximum, [jnp.max(jnp.abs(v), axis=0, keepdims=True) for v in values])
    top = jnp.maximum(jnp.max(top, axis=1, keepdims=True), 2.0**-100)
    return jnp.ceil(jnp.log2(top)) - BOUND


def quarter(table_ref, index):
    rows = table_ref.shape[0] // 4
    return tuple(table_ref[part * rows : (part + 1) * rows, :] for part in (2 * index, 2 * index + 1))


def z_kernel(slabs, g0, g1, g2, g3, edge_ref, w_ref, out_ref, wide_ref):
    widen_edge(edge_ref, wide_ref)
    half = slabs // 2
    parts = NZ // (2 * slabs)
    planes = parts // 2
    stride = 4 * parts + SCALE_ROWS
    sums = []
    for parity in range(2):
        where = pl.ds(parity, NZ // 2, stride=2)
        columns = []
        for plane, grid in enumerate((g0, g1, g2, g3)):
            at_edge = edge_codes((plane,), (NZ // 2, LANES)) < 2
            values = grid[where, :] + jnp.where(at_edge, wide_ref[where, :], 0.0)
            columns.append(pltpu.roll(values, LANES - 8 * plane, 1) if plane else values)
        sums.append(dot3(quarter(w_ref, parity), split(jnp.concatenate(columns, axis=1))))
    results = (sums[0] + sums[1], sums[0] - sums[1])
    exponent = exponent_of(results)
    scale = jnp.exp2(-exponent)
    results = [result * scale for result in results]
    for upper, result in enumerate(results):
        for part in range(parts):
            index = part // planes * (planes + 1) + part % planes + upper
            for tile in range(2):
                rows = result[(index * 2 + tile) * half : (index * 2 + tile + 1) * half, :]
                start = (tile * slabs + upper * half) * stride + part
                for plane in range(4):
                    out_ref[pl.ds(start + plane * parts, half, stride=stride), :] = rows[
                        :, plane * LANES : (plane + 1) * LANES
                    ]
    for row in range(SCALE_ROWS):
        out_ref[pl.ds(4 * parts + row, 2 * slabs, stride=stride), :] = jnp.broadcast_to(
            exponent, (2 * slabs, LANES)
        )


def hat_kernel(planes, offset_ref, hat_ref, turn_ref, out_ref):
    length = hat_ref.shape[1]
    values = jnp.concatenate([hat_ref[offset_ref[0] + plane] for plane in range(planes)], axis=0)
    values = values * (1.0 / (length * NY))
    upper = values[:, HALF:]
    high, low = split(upper)
    rest = (upper - high.astype(F32) - low.astype(F32)).astype(BF16)
    turn = turn_ref[...]
    upper = dot(high, turn) + (dot(low, turn) + dot(rest, turn))
    for plane in range(planes):
        here = slice(plane * length, (plane + 1) * length)
        out_ref[plane] = jnp.concatenate([values[here, :HALF], upper[here, :]], axis=1)


def plane_kernel(slabs, planes, in_ref, hat_ref, y_ref, x_ref, out_ref, exponent_ref, ah_ref, al_ref):
    length = 4 * slabs
    rows = planes * length
    parts = 2 * planes
    stride = 4 * parts + SCALE_ROWS

    def pieces():
        for tile in range(2):
            for part in range(2):
                for xi in range(4):
                    for plane in range(planes):
                        yield tile, part, plane, xi

    scales = [
        jnp.exp2(in_ref[pl.ds(tile * slabs * stride + 4 * parts, slabs, stride=stride), :])
        for tile in range(2)
    ]
    for tile, part, plane, xi in pieces():
        start = tile * slabs * stride + xi * parts + part * planes + plane
        row = (part * planes + plane) * length + xi * slabs
        high, low = split(in_ref[pl.ds(start, slabs, stride=stride), :] * scales[tile])
        ah_ref[row : row + slabs, tile * LANES : (tile + 1) * LANES] = high
        al_ref[row : row + slabs, tile * LANES : (tile + 1) * LANES] = low
    first_lane = lane_of((rows, HALF)) == 0
    turned = dot3((ah_ref[...], al_ref[...]), (y_ref[0:NY, :], y_ref[NY : 2 * NY, :]))
    even = (turned[:rows, :HALF], turned[rows:, :HALF])
    odd = (turned[:rows, HALF:], turned[rows:, HALF:])
    zero_odd = [jnp.where(first_lane, 0.0, values) for values in odd]
    real = jnp.concatenate(
        [even[0] + zero_odd[1], jnp.where(first_lane, odd[0], even[0] - zero_odd[1])], axis=1
    )
    imag = jnp.concatenate(
        [even[1] - zero_odd[0], jnp.where(first_lane, odd[1], even[1] + zero_odd[0])], axis=1
    )
    size = 2 * length

    def along_x(values, first):
        high, low = split(values)
        table = x_ref[first * size : (first + 2) * size, :]
        both = dot(table, jnp.concatenate([high, low], axis=0))
        return both[:size] + both[size:]

    for plane in range(planes):
        here = slice(plane * length, (plane + 1) * length)
        there = slice(rows + plane * length, rows + (plane + 1) * length)
        values = along_x(jnp.concatenate([real[here], imag[here]], axis=0), 0)
        values = values * jnp.concatenate([hat_ref[plane], hat_ref[plane]], axis=0)
        values = along_x(values, 2)
        low, high = values[:, :HALF], values[:, HALF:]
        lane = first_lane[:length]
        even_r = jnp.where(lane, low[:length], low[:length] + high[:length])
        even_i = jnp.where(lane, low[length:], low[length:] + high[length:])
        odd_r = jnp.where(lane, high[:length], high[length:] - low[length:])
        odd_i = jnp.where(lane, high[length:], low[:length] - high[:length])
        ah_ref[here, :], al_ref[here, :] = split(jnp.concatenate([even_r, odd_r], axis=1))
        ah_ref[there, :], al_ref[there, :] = split(jnp.concatenate([even_i, odd_i], axis=1))
    turned = dot3((ah_ref[...], al_ref[...]), (y_ref[2 * NY : 3 * NY, :], y_ref[3 * NY : 4 * NY, :]))
    tops = [
        jnp.max(in_ref[pl.ds(tile * slabs * stride + 4 * parts, slabs, stride=stride), :], axis=0, keepdims=True)
        for tile in range(2)
    ]
    exponent = jnp.broadcast_to(jnp.maximum(*tops) + BOUND - HEADROOM + math.ceil(math.log2(length * NY) / 2), (8, LANES))
    exponent_ref[...] = exponent
    scale = jnp.exp2(-exponent[0:1, 0:1])
    for tile, part, plane, xi in pieces():
        here = slice((part * planes + plane) * length + xi * slabs, (part * planes + plane) * length + (xi + 1) * slabs)
        start = tile * slabs * stride + xi * parts + part * planes + plane
        out_ref[pl.ds(start, slabs, stride=stride), :] = (
            turned[here, tile * LANES : (tile + 1) * LANES] * scale
        )


def potential_kernel(slabs, in_ref, exponent_ref, v_ref, p0, p1, p2, p3, edge_ref):
    half = slabs // 2
    parts = NZ // (2 * slabs)
    planes = parts // 2
    stride = 4 * parts
    sums = []
    for parity in range(2):
        columns = []
        for plane in range(4):
            rows = []
            for part in range(parts):
                upper = (part % planes + parity) % 2
                for tile in range(2):
                    start = (tile * slabs + upper * half) * stride + plane * parts + part
                    rows.append(in_ref[pl.ds(start, half, stride=stride), :])
            columns.append(jnp.concatenate(rows, axis=0))
        sums.append(dot3(quarter(v_ref, parity), split(jnp.concatenate(columns, axis=1))))
    scale = jnp.exp2(exponent_ref[0:1, 0:1])
    shape = (LANES, LANES)
    edges = [jnp.zeros(shape, F32)] * 4
    halves_of_z = [((sums[0] + sums[1]) * scale), ((sums[0] - sums[1]) * scale)]
    for plane, pot in enumerate((p0, p1, p2, p3)):
        at_edge = edge_codes((plane,), shape) < 2
        for upper in range(2):
            result = halves_of_z[upper][:, plane * LANES : (plane + 1) * LANES].astype(BF16).astype(F32)
            if plane:
                result = pltpu.roll(result, 8 * plane, 1)
            pot[upper * (NZ // 2) : (upper + 1) * (NZ // 2), :] = result
            for block in range(2):
                edges[2 * upper + block] = jnp.where(
                    at_edge, result[block * LANES : (block + 1) * LANES, :], edges[2 * upper + block]
                )
        pot[NZ:ZROWS, :] = pot[0:8, :]
    edge = pltpu.roll(edges[0], 2, 1)
    for block in range(1, 4):
        edge += pltpu.roll(edges[block], 32 * block + 2, 1)
    edge_ref[...] = edge.astype(BF16)


def widen_edge(edge_ref, wide_ref):
    for block in range(4):
        wide_ref[block * LANES : (block + 1) * LANES, :] = pltpu.roll(
            edge_ref[...].astype(F32), (LANES - 2 - 32 * block) % LANES, 1
        )
    wide_ref[NZ:ZROWS, :] = wide_ref[0:8, :]


def masked(values, live):
    return jnp.where(lane_of(values.shape) < live, values, 0.0)


def own_sample_kernel(facts_ref, p0, p1, p2, p3, edge_ref, kinds_ref, stk_ref, out_ref, wide_ref, sp_ref):
    widen_edge(edge_ref, wide_ref)
    live = facts_ref[3, 0]
    slots = kinds_ref.shape[1]
    sample_columns((p0, p1, p2, p3), wide_ref, place_in_facts(facts_ref), live, sp_ref, 0, OWN[0])

    @pl.when(live > LANES)
    def _():
        out_ref[...] = masked(far_sums(sp_ref, kinds_ref[2:3, :], stk_ref, 0), live)

    @pl.when(live <= LANES)
    def _():
        out_ref[:, 0:LANES] = masked(far_sums(sp_ref, kinds_ref[2:3, 0:LANES], stk_ref, 0), live)
        out_ref[:, LANES:slots] = jnp.zeros((PANELS, slots - LANES), F32)


def beside_sample_kernel(odd_ref, facts_ref, p0, p1, p2, p3, edge_ref, kinds_ref, stk_ref, out0, out1, wide_ref, sp_ref):
    widen_edge(edge_ref, wide_ref)
    slots = kinds_ref.shape[1] // 2
    outs = (out0, out1)
    for first, counts in chunks_beside(facts_ref, slots):
        here = slice(first, first + LANES)
        for side, (planes, _) in enumerate(BESIDE):
            sample_columns((p0, p1, p2, p3), wide_ref, place_in_facts(facts_ref, side * slots + first),
                           counts[side], sp_ref, 2 * first + side * LANES, planes)

        @pl.when(counts[0] + counts[1] > 0)
        def _(first=first, counts=counts, here=here):
            kinds = both_sides(kinds_ref.at[2:3, :], slots, first)
            result = far_sums(sp_ref, kinds, stk_ref, 2 * first)
            sums = [masked(result[:, side * LANES : (side + 1) * LANES], counts[side]) for side in range(2)]
            even = jnp.broadcast_to(odd_ref[0], sums[0].shape) == 0
            out0[:, here] = jnp.where(even, sums[1], sums[0])
            out1[:, here] = jnp.where(even, sums[0], sums[1])

        @pl.when(counts[0] + counts[1] <= 0)
        def _(here=here):
            for out in outs:
                out[:, here] = jnp.zeros((PANELS, LANES), F32)


def near_kernel(live_ref, here_ref, there_ref, source_ref, block_ref, table_ref, out_ref):
    live = live_ref[0]
    fanout, slots = source_ref.shape
    height = here_ref.shape[0] // 3
    pool = jnp.concatenate(
        [ref[step * height : step * height + PANELS, :] for step in range(3) for ref in (here_ref, there_ref)],
        axis=1,
    )
    total = pool.shape[1]
    for first in range(0, slots, LANES):
        where = slice(first, first + LANES)

        @pl.when(live > first)
        def _(where=where, first=first):
            index = lax.broadcasted_iota(jnp.int32, (total, LANES), 0)
            result = jnp.zeros((PANELS, LANES), F32)
            for j in range(fanout):
                chosen = jnp.where(index == source_ref[j : j + 1, where], 1.0, 0.0).astype(BF16)
                gathered = dot(pool, chosen)
                result += dot(
                    table_ref[...], by_kind(gathered, block_ref[j : j + 1, where]).astype(BF16)
                )
            column = first + lane_of((PANELS, LANES))
            out_ref[:, where] = jnp.where(column < live, result, 0.0)

        @pl.when(live <= first)
        def _(where=where):
            out_ref[:, where] = jnp.zeros((PANELS, LANES), F32)


def shape_of(*dims, dtype=F32):
    return jax.ShapeDtypeStruct(dims, dtype)


def body(slabs, tiles, charges, live_count, slot_brick, slot_stencil, stencils, near_source,
         near_block, near_blocks, kernel_hat):
    slots = charges.shape[1]
    owners = slabs * tiles
    planes = kernel_hat.shape[0] // 2
    length = kernel_hat.shape[1]
    parts = NZ // owners
    axes = ("tile", "slab")
    both = ("slab", "tile")

    def moved(values, step_of, swap=0):
        pairs = [
            (a * tiles + b, (a + step_of(a)) % slabs * tiles + (b + swap) % tiles)
            for a in range(slabs)
            for b in range(tiles)
        ]
        return lax.ppermute(values, both, pairs)

    def to_first(values):
        return moved(values, lambda a: 1 - 2 * (a % 2))

    def to_second(values):
        return moved(values, lambda a: 2 * (a % 2) - 1)

    def to_other_tile(values):
        return moved(values, lambda a: 0, 1)

    odd = (lax.axis_index("slab") % 2)[None]
    row = lax.broadcasted_iota(jnp.int32, (PANELS + 16, slots), 0)
    column = lax.broadcasted_iota(jnp.int32, (PANELS + 16, slots), 1)
    live = jnp.broadcast_to(live_count[0], row.shape)
    brick = jnp.broadcast_to(slot_brick[None, :], row.shape)
    facts = lax.shift_right_logical(brick, jnp.where(row == PANELS, 7, 0)) & (NZ // 4 - 1)
    facts = jnp.where(row == PANELS + 2, slot_stencil[None, :], jnp.where(row == PANELS + 3, live, facts))
    held = jnp.where(column < live, jnp.pad(charges, ((0, 16), (0, 0))), jnp.zeros((), BF16))
    packed = jnp.where(row < PANELS, held, facts.astype(BF16))
    from_second = to_second(packed)
    from_first = to_first(packed)

    grid = shape_of(ZROWS, LANES)
    *grids, stk, facts = pl.pallas_call(
        own_kernel,
        out_shape=(grid,) * 5 + (shape_of(KS * PANELS, POINTS, dtype=BF16), shape_of(8, slots, dtype=jnp.int32)),
        in_specs=[VMEM, pl.BlockSpec(memory_space=pl.ANY)],
        out_specs=(VMEM,) * 7,
        scratch_shapes=[
            pltpu.VMEM((slots * 8, LANES), F32),
            pltpu.VMEM((KS * PANELS, POINTS), BF16),
            pltpu.SMEM((8, slots), jnp.int32),
            pltpu.SemaphoreType.DMA((2,)),
        ],
        compiler_params=PARAMS,
        name="own_scatter",
    )(packed, stencils.reshape(KS * PANELS, POINTS))

    g = pl.pallas_call(
        beside_kernel,
        out_shape=(grid,) * 5
        + (
            shape_of(LANES, LANES),
            shape_of(8, 2 * slots, dtype=jnp.int32),
            shape_of(3 * (PANELS + 16), slots, dtype=BF16),
        ),
        in_specs=[SMEM] + [VMEM] * 9,
        out_specs=(VMEM,) * 8,
        scratch_shapes=[
            pltpu.VMEM((2 * slots * 8, LANES), F32),
            pltpu.SMEM((8, 2 * slots), jnp.int32),
            pltpu.SemaphoreType.DMA,
        ],
        input_output_aliases={5: 0, 6: 1, 7: 2, 8: 3, 9: 4},
        compiler_params=PARAMS,
        name="beside_scatter",
    )(odd, packed, from_first, from_second, stk, *grids)
    facts2 = g[6]
    edge = to_other_tile(g[5])

    forward, inverse = z_tables(slabs, tiles)
    rows = owners * (4 * parts + SCALE_ROWS)
    sent = pl.pallas_call(
        functools.partial(z_kernel, slabs),
        out_shape=shape_of(rows, LANES),
        in_specs=[VMEM] * 6,
        out_specs=VMEM,
        scratch_shapes=[pltpu.VMEM((ZROWS, LANES), F32)],
        compiler_params=PARAMS,
        name="z_forward",
    )(*g[:4], edge, jnp.asarray(halves(*forward)))

    def exchanged(values, kept):
        values = values.reshape(owners, -1, LANES)[:, :kept].astype(jnp.float16)
        values = lax.all_to_all(values, axes, 0, 0, tiled=True)
        return values

    def widened(values):
        return values.astype(F32).reshape(-1, LANES)

    hat, sent = lax.optimization_barrier((kernel_hat, sent))
    got = exchanged(sent, 4 * parts + SCALE_ROWS)
    me = lax.axis_index("slab") * tiles + lax.axis_index("tile")
    offset = (me >= owners // 2).astype(jnp.int32)[None]
    hat = pl.pallas_call(
        functools.partial(hat_kernel, planes),
        out_shape=shape_of(planes, length, NY),
        in_specs=[SMEM] + [VMEM] * 2,
        out_specs=VMEM,
        compiler_params=PARAMS,
        name="hat_order",
    )(offset, hat, jnp.asarray(reversal()))

    got, hat = lax.optimization_barrier((got, hat))
    pool = (g[7], to_other_tile(g[7]))
    direction = near_source // slots
    pool_index = (direction // 3 * 2 + (direction % 3 != 1).astype(jnp.int32)) * slots + near_source % slots
    near = pl.pallas_call(
        near_kernel,
        out_shape=shape_of(PANELS, slots),
        in_specs=[SMEM] + [VMEM] * 5,
        out_specs=VMEM,
        compiler_params=PARAMS,
        name="near_field",
    )(live_count, *pool, pool_index.T, near_block.T, near_blocks.reshape(PANELS, KN * PANELS))

    back, exponent = pl.pallas_call(
        functools.partial(plane_kernel, slabs, planes),
        out_shape=(shape_of(rows, LANES), shape_of(8, LANES)),
        in_specs=[VMEM] * 4,
        out_specs=(VMEM, VMEM),
        scratch_shapes=[pltpu.VMEM((2 * planes * length, NY), BF16)] * 2,
        compiler_params=PARAMS,
        name="plane_filter",
    )(widened(got), hat, jnp.asarray(halves(y_table(), y_table().T)), jnp.asarray(joined(x_tables(slabs))))
    back, near = lax.optimization_barrier((exchanged(back, 4 * parts), near))

    pot = pl.pallas_call(
        functools.partial(potential_kernel, slabs),
        out_shape=(grid,) * 4 + (shape_of(LANES, LANES, dtype=BF16),),
        in_specs=[VMEM] * 3,
        out_specs=(VMEM,) * 5,
        compiler_params=PARAMS,
        name="z_inverse",
    )(widened(back), exponent, jnp.asarray(halves(*inverse)))
    edge = to_other_tile(pot[4])

    def sample_scratch(width):
        return [pltpu.VMEM((ZROWS, LANES), F32), pltpu.VMEM((width * 8, LANES), F32)]

    sums = shape_of(PANELS, slots)
    others = pl.pallas_call(
        beside_sample_kernel,
        out_shape=(sums, sums),
        in_specs=[SMEM] * 2 + [VMEM] * 7,
        out_specs=(VMEM, VMEM),
        scratch_shapes=sample_scratch(2 * slots),
        compiler_params=PARAMS,
        name="beside_sample",
    )(odd, facts2, *pot[:4], edge, facts2, stk)
    first = to_first(others[0])
    second = to_second(others[1])
    own = pl.pallas_call(
        own_sample_kernel,
        out_shape=sums,
        in_specs=[SMEM] + [VMEM] * 7,
        out_specs=VMEM,
        scratch_shapes=sample_scratch(slots),
        compiler_params=PARAMS,
        name="own_sample",
    )(facts, *pot[:4], edge, facts, stk)
    return own + near + first + second


def solution(mesh):
    both = ("slab", "tile")
    in_specs = (
        P(None, both),
        P(both),
        P(both),
        P(both),
        P(),
        P(both, None),
        P(both, None),
        P(),
        P(both, None, None),
    )
    return jax.shard_map(
        functools.partial(body, mesh.shape["slab"], mesh.shape["tile"]),
        mesh=mesh,
        in_specs=in_specs,
        out_specs=P(None, both),
        check_vma=False,
    )
```
